32 devices in a mesh: dp: 8 (over z, y), mp: 4 (over x, core).
Axes of the slice: x: 2, y: 2, z: 4, core: 2. Of those that a mesh axis runs over, the one named last changes fastest.
Arguments:
- block_input: bfloat16 [8192, 1024], P('dp')
- out_cotangent: bfloat16 [8192, 1024], P('dp')
- sigmas: float32 [32], replicated, may hold values from 0.02 to 80
- class_labels: int32 [32], replicated, may hold values from 0 to 999
- image_lengths: int32 [32], replicated, may hold values from 0 to 1024, as said below
- fourier_freqs: float32 [384], replicated, may hold values from -4 to 4
- inproj_state: float32 [4, 1024, 3, 1024], P(None, 'dp', None, 'mp'), as said below
- outproj_state: float32 [4, 1024, 1024], P(None, 'mp', 'dp'), as said below
- upproj_state: float32 [4, 1024, 2, 3072], P(None, 'dp', None, 'mp'), as said below
- downproj_state: float32 [4, 3072, 1024], P(None, 'mp', 'dp'), as said below
- timeproj_state: float32 [4, 768, 768], P(None, 'dp'), as said below
- classemb_state: float32 [4, 1000, 768], P(None, None, 'dp'), as said below
- mapup_state: float32 [4, 768, 2, 2304], P(None, 'dp', None, 'mp'), as said below
- mapdown_state: float32 [4, 2304, 768], P(None, 'mp', 'dp'), as said below
- modproj_state: float32 [4, 768, 2, 1024], P(None, 'dp'), as said below
- gains_state: float32 [4, 3, 768], P(None, None, 'dp'), as said below
- headscale_state: float32 [4, 16], P(None, 'mp'), as said below
Outputs:
- layer_out: bfloat16 [8192, 1024], P('dp')
- input_grad: float32 [8192, 1024], P('dp')
- grad_norm: float32 [], replicated
- new_inproj: float32 [2, 1024, 3, 1024], P(None, 'dp', None, 'mp')
- inproj_first: float32 [1024, 3, 1024], P('dp', None, 'mp')
- inproj_second: float32 [1024, 3, 1024], P('dp', None, 'mp')
- new_outproj: float32 [2, 1024, 1024], P(None, 'mp', 'dp')
- outproj_first: float32 [1024, 1024], P('mp', 'dp')
- outproj_second: float32 [1024, 1024], P('mp', 'dp')
- new_upproj: float32 [2, 1024, 2, 3072], P(None, 'dp', None, 'mp')
- upproj_first: float32 [1024, 2, 3072], P('dp', None, 'mp')
- upproj_second: float32 [1024, 2, 3072], P('dp', None, 'mp')
- new_downproj: float32 [2, 3072, 1024], P(None, 'mp', 'dp')
- downproj_first: float32 [3072, 1024], P('mp', 'dp')
- downproj_second: float32 [3072, 1024], P('mp', 'dp')
- new_timeproj: float32 [2, 768, 768], P(None, 'dp')
- timeproj_first: float32 [768, 768], P('dp')
- timeproj_second: float32 [768, 768], P('dp')
- new_classemb: float32 [2, 1000, 768], P(None, None, 'dp')
- classemb_first: float32 [1000, 768], P(None, 'dp')
- classemb_second: float32 [1000, 768], P(None, 'dp')
- new_mapup: float32 [2, 768, 2, 2304], P(None, 'dp', None, 'mp')
- mapup_first: float32 [768, 2, 2304], P('dp', None, 'mp')
- mapup_second: float32 [768, 2, 2304], P('dp', None, 'mp')
- new_mapdown: float32 [2, 2304, 768], P(None, 'mp', 'dp')
- mapdown_first: float32 [2304, 768], P('mp', 'dp')
- mapdown_second: float32 [2304, 768], P('mp', 'dp')
- new_modproj: float32 [2, 768, 2, 1024], P(None, 'dp')
- modproj_first: float32 [768, 2, 1024], P('dp')
- modproj_second: float32 [768, 2, 1024], P('dp')
- new_gains: float32 [2, 3, 768], P(None, None, 'dp')
- gains_first: float32 [3, 768], P(None, 'dp')
- gains_second: float32 [3, 768], P(None, 'dp')
- new_headscale: float32 [2, 16], P(None, 'mp')
- headscale_first: float32 [16], P('mp')
- headscale_second: float32 [16], P('mp')
The draws below stay inside these ranges and needn't reach their ends.
Inputs may be any that keep to these rules, and one draw needn't show every extreme that they name: `image_lengths`: each data shard's 4 entries are either 1024 followed by zeros, or k >= 1 entries of 256 followed by zeros; in every draw some shard holds one image of 1024 tokens and another holds 4 images of 256. `inproj_state`: second moments are positive. `outproj_state`: second moments are positive. `upproj_state`: second moments are positive. `downproj_state`: second moments are positive. `timeproj_state`: second moments are positive. `classemb_state`: second moments are positive. `mapup_state`: second moments are positive. `mapdown_state`: second moments are positive. `modproj_state`: second moments are positive. `gains_state`: second moments are positive. `headscale_state`: second moments and scales are positive.
All inputs are finite; a program needn't handle non-finite values.
Results may differ from the reference program's by a relative error of at most 0.02.
The reference program's roundings to bfloat16 on the way count: a program that leaves them out, or rounds other values in their place, can miss the bound.
Values may be sent and summed in bfloat16 or wider, within the bound.
A program may use at most 256 MiB of HBM per device.

```python
import math
import jax
import jax.numpy as jnp
from jax import lax

D = 1024
H = 16
FF = 3072
DM = 768
MFF = 2304
NCLASS = 1000
SHORT = 256
IMG_DEV = 4
STEP = 10
LONG = 1024
SLOTS = 1024
IMAGES = 32
TOKENS = 8192
PARAMS = 21872912


def draw_noise(key, shape):
    return jax.random.normal(key, shape, jnp.float32)


def gradient_size(factor):
    return factor * 1.0 / math.sqrt(PARAMS)


def state_stack(key, weight, spread, grad_size):
    first = 0.1 / 0.9 * grad_size * draw_noise(jax.random.fold_in(key, 11), weight.shape)
    second = 0.05 / 0.95 * grad_size * grad_size * jax.random.uniform(jax.random.fold_in(key, 12), weight.shape, jnp.float32, 1.0, 4.0)
    average = weight + 0.3 * spread * draw_noise(jax.random.fold_in(key, 13), weight.shape)
    return jnp.stack([weight, first, second, average])


def matrix_state(base_key, tag, shape, spread, factor):
    key = jax.random.fold_in(base_key, tag)
    weight = spread * draw_noise(jax.random.fold_in(key, 10), shape)
    return state_stack(key, weight, spread, gradient_size(factor))


def rising_rows(key, rows):
    upper = 3.0
    rise = 1.0 + (upper - 1.0) * jnp.arange(D, dtype=jnp.float32) / (D - 1)
    return draw_noise(key, (rows, D)) * rise[None, :]


def draw_block_input(key, part):
    return rising_rows(jax.random.fold_in(key, 1), TOKENS).astype(jnp.bfloat16)


def draw_out_cotangent(key, part):
    return rising_rows(jax.random.fold_in(key, 2), TOKENS).astype(jnp.bfloat16)


def draw_image_lengths(key, part):
    groups = IMAGES // IMG_DEV
    kind = jax.random.randint(jax.random.fold_in(key, 1), (groups,), 0, 2)
    count = jax.random.randint(jax.random.fold_in(key, 2), (groups,), 1, IMG_DEV + 1)
    order = jax.random.permutation(jax.random.fold_in(key, 3), groups)
    shard_ids = jnp.arange(groups, dtype=jnp.int32)
    kind = jnp.where(shard_ids == order[0], 1, jnp.where(shard_ids == order[1], 0, kind))
    count = jnp.where(shard_ids == order[1], IMG_DEV, count)
    slot_ids = jnp.arange(IMG_DEV, dtype=jnp.int32)
    short_rows = jnp.where(slot_ids[None, :] < count[:, None], SHORT, 0)
    long_rows = jnp.where(slot_ids[None, :] == 0, LONG, 0) + jnp.zeros((groups, 1), jnp.int32)
    lengths_all = jnp.where(kind[:, None] == 1, long_rows, short_rows)
    return lengths_all.reshape(-1).astype(jnp.int32)


def draw_inproj_state(key, part):
    return matrix_state(key, 101, (D, 3, D), D ** (-0.5), 1.0)


def draw_outproj_state(key, part):
    return matrix_state(key, 102, (D, D), (D // 64) ** (-0.5), 1.0)


def draw_upproj_state(key, part):
    return matrix_state(key, 103, (D, 2, FF), D ** (-0.5), 1.0)


def draw_downproj_state(key, part):
    return matrix_state(key, 104, (FF, D), FF ** (-0.5), 1.0)


def draw_timeproj_state(key, part):
    return matrix_state(key, 105, (DM, DM), DM ** (-0.5), 1.0)


def draw_classemb_state(key, part):
    return matrix_state(key, 106, (NCLASS, DM), 1.0, 2.0)


def draw_mapup_state(key, part):
    return matrix_state(key, 107, (DM, 2, MFF), DM ** (-0.5), 1.0)


def draw_mapdown_state(key, part):
    return matrix_state(key, 108, (MFF, DM), MFF ** (-0.5), 1.0)


def draw_modproj_state(key, part):
    return matrix_state(key, 109, (DM, 2, D), 0.5 * DM ** (-0.5), 1.0)


def draw_gains_state(key, part):
    own_key = jax.random.fold_in(key, 110)
    rising = 0.6 + 1.2 * jnp.arange(DM, dtype=jnp.float32) / (DM - 1)
    weight = rising[None, :] * (1.0 + 0.1 * draw_noise(jax.random.fold_in(own_key, 10), (3, DM)))
    return state_stack(own_key, weight, 0.1, gradient_size(1.5))


def draw_headscale_state(key, part):
    own_key = jax.random.fold_in(key, 111)
    weight = jnp.exp(jax.random.uniform(jax.random.fold_in(own_key, 10), (H,), jnp.float32, math.log(8.0), math.log(20.0)))
    return state_stack(own_key, weight, 3.0, gradient_size(5.0))


def touch_ends(values, key, low, top_value):
    longest = values.shape.index(max(values.shape))
    spots = []
    for shift in (0, 1):
        where = [jax.random.randint(jax.random.fold_in(key, axis), (), 0, length) for axis, length in enumerate(values.shape)]
        where[longest] = (where[longest] + shift) % values.shape[longest]
        spots.append(tuple(where))
    return values.at[spots[0]].set(low).at[spots[1]].set(top_value)


def scatter_about(key, shape, scale, bound, kind=jnp.bfloat16):
    result = scale * jax.random.normal(key, shape, jnp.float32)
    return jnp.clip(result, min=-bound, max=bound).astype(kind)


def setup_inputs(seed: int = 0) -> dict:
    streams_of = jax.random.split(jax.random.key(seed), 18)
    return {
        "block_input": draw_block_input(jax.random.fold_in(streams_of[17], 71), 0),
        "out_cotangent": draw_out_cotangent(jax.random.fold_in(streams_of[17], 71), 0),
        "sigmas": jnp.clip(jnp.exp(jax.random.uniform(streams_of[2], (IMAGES,), jnp.float32, math.log(0.02), math.log(80.0))), 0.02, 80.0),
        "class_labels": touch_ends(jax.random.randint(streams_of[3], (IMAGES,), 0, NCLASS), jax.random.fold_in(streams_of[3], 1), 0, NCLASS - 1).astype(jnp.int32),
        "image_lengths": draw_image_lengths(jax.random.fold_in(streams_of[17], 71), 0),
        "fourier_freqs": scatter_about(streams_of[5], (DM // 2,), 1.0, 4.0, jnp.float32),
        "inproj_state": draw_inproj_state(jax.random.fold_in(streams_of[17], 71), 0),
        "outproj_state": draw_outproj_state(jax.random.fold_in(streams_of[17], 71), 0),
        "upproj_state": draw_upproj_state(jax.random.fold_in(streams_of[17], 71), 0),
        "downproj_state": draw_downproj_state(jax.random.fold_in(streams_of[17], 71), 0),
        "timeproj_state": draw_timeproj_state(jax.random.fold_in(streams_of[17], 71), 0),
        "classemb_state": draw_classemb_state(jax.random.fold_in(streams_of[17], 71), 0),
        "mapup_state": draw_mapup_state(jax.random.fold_in(streams_of[17], 71), 0),
        "mapdown_state": draw_mapdown_state(jax.random.fold_in(streams_of[17], 71), 0),
        "modproj_state": draw_modproj_state(jax.random.fold_in(streams_of[17], 71), 0),
        "gains_state": draw_gains_state(jax.random.fold_in(streams_of[17], 71), 0),
        "headscale_state": draw_headscale_state(jax.random.fold_in(streams_of[17], 71), 0),
    }


@jax.custom_vjp
def low(v):
    return lax.optimization_barrier(v.astype(jnp.bfloat16)).astype(jnp.float32)

@jax.custom_vjp
def low_back(v):
    return v

def low_keep(v):
    return (low(v), None)

def low_pass(kept, grad):
    return (grad,)

def back_keep(v):
    return (v, None)

def back_low(kept, grad):
    return (low(grad),)
low.defvjp(low_keep, low_pass)
low_back.defvjp(back_keep, back_low)
EPSILON = 1e-06
HIGHEST = lax.Precision.HIGHEST
BETA_ONE = 0.9
BETA_TWO = 0.95
ADAM_EPSILON = 1e-08
CLIP_NORM = 1.0
MASKED = -1e+30
NAMES = ('inproj', 'outproj', 'upproj', 'downproj', 'timeproj', 'classemb', 'mapup', 'mapdown', 'modproj', 'gains', 'headscale')

def rms_scale(values, scales):
    return values * lax.rsqrt(lax.optimization_barrier(jnp.mean(values * values, axis=-1, keepdims=True)) + EPSILON) * scales

def geglu_gate(hidden):
    return hidden[:, 0] * jax.nn.gelu(hidden[:, 1], approximate=False)

def fourier(sigmas, fourier_freqs):
    angles = 2.0 * math.pi * (jnp.log(sigmas) / 4.0)[:, None] * fourier_freqs[None, :]
    return jnp.concatenate([jnp.cos(angles), jnp.sin(angles)], axis=1)

def cosine(queries, key_rows, head_scale):
    query_unit = queries * lax.rsqrt(lax.optimization_barrier(jnp.sum(queries * queries, axis=-1, keepdims=True)) + EPSILON) * head_scale[None, :, None]
    key_unit = key_rows * lax.rsqrt(lax.optimization_barrier(jnp.sum(key_rows * key_rows, axis=-1, keepdims=True)) + EPSILON)
    return (query_unit, key_unit)

def learn_rates():
    return (2.5 * D ** (-0.5), 2.5 * (D // 64) ** (-0.5), 2.5 * D ** (-0.5), 2.5 * FF ** (-0.5), 2.5 * DM ** (-0.5), 2.5, 2.5 * DM ** (-0.5), 2.5 * MFF ** (-0.5), 1.25 * DM ** (-0.5), 0.25, 7.5)

def decay_rates():
    return (0.01, 0.01, 0.01, 0.01, 0.01, 0.01, 0.01, 0.01, 0.01, 0.0, 0.0)

def adamw_step(state, gradient, rate, decay):
    keep_rate = 1.0 - (1.0 + STEP) ** (-0.75)
    first = BETA_ONE * state[1] + (1.0 - BETA_ONE) * gradient
    second = BETA_TWO * state[2] + (1.0 - BETA_TWO) * gradient * gradient
    first_hat = first / (1.0 - BETA_ONE ** STEP)
    second_hat = second / (1.0 - BETA_TWO ** STEP)
    weight = state[0] * (1.0 - rate * decay) - rate * first_hat / (jnp.sqrt(second_hat) + ADAM_EPSILON)
    average = keep_rate * state[3] + (1.0 - keep_rate) * weight
    return (jnp.stack([weight, average]), first, second)

def layer_shard(inputs, mods, lengths_here, w_in, w_out, w_up, w_down, head_scale):
    slot_count = inputs.shape[0]
    image_ends = jnp.cumsum(lengths_here).astype(jnp.int32)
    position = jnp.arange(slot_count, dtype=jnp.int32)
    slot_of = lax.optimization_barrier(jnp.sum((position[:, None] >= image_ends[None, :]).astype(jnp.int32), axis=1)).astype(jnp.int32)
    live_rows = (position < image_ends[-1]).astype(jnp.float32)[:, None]
    member = (slot_of[:, None] == jnp.arange(IMG_DEV, dtype=jnp.int32)[None, :]).astype(jnp.float32)
    same_image = slot_of[:, None] == slot_of[None, :]
    attn_mod = 1.0 + jnp.dot(member, mods[:, 0], precision=HIGHEST)
    ff_mod = 1.0 + jnp.dot(member, mods[:, 1], precision=HIGHEST)
    normed = low(rms_scale(inputs, attn_mod))
    projected = low_back(jnp.einsum('td,dcf->tcf', normed, w_in, precision=HIGHEST))
    head_count = head_scale.shape[0]
    queries = projected[:, 0].reshape(slot_count, head_count, -1)
    key_rows = projected[:, 1].reshape(slot_count, head_count, -1)
    value_rows = projected[:, 2].reshape(slot_count, head_count, -1)
    query_unit, key_unit = cosine(queries, key_rows, head_scale)
    query_low = low(query_unit)
    key_low = low(key_unit)
    value_low = low(value_rows)
    scores = low_back(jnp.einsum('thd,uhd->htu', query_low, key_low, precision=HIGHEST))
    scores = jnp.where(same_image[None], scores, MASKED)
    probabilities = jax.nn.softmax(scores, axis=-1)
    attended = low(low_back(jnp.einsum('htu,uhd->thd', low(probabilities), value_low, precision=HIGHEST)))
    attended = attended.reshape(slot_count, -1)
    middle = inputs + low_back(jnp.dot(attended, w_out, precision=HIGHEST))
    normed_mid = low(rms_scale(middle, ff_mod))
    hidden = low_back(jnp.einsum('td,dcf->tcf', normed_mid, w_up, precision=HIGHEST))
    gated_vals = low(geglu_gate(hidden))
    branch = low_back(jnp.dot(gated_vals, w_down, precision=HIGHEST))
    return live_rows * (middle + branch)

def forward(params, inputs, sigmas, class_labels, image_lengths, fourier_freqs):
    gain_values = low(params['gains'])
    feats = low(fourier(sigmas, fourier_freqs))
    onehot = (class_labels[:, None] == jnp.arange(NCLASS, dtype=jnp.int32)[None, :]).astype(jnp.float32)
    embedded = jnp.dot(feats, low(params['timeproj']), precision=HIGHEST) + jnp.dot(onehot, low(params['classemb']), precision=HIGHEST)
    unit_rms = rms_scale(embedded, gain_values[0])
    pre_up = low(rms_scale(unit_rms, gain_values[1]))
    map_hidden = jnp.einsum('id,dcf->icf', pre_up, low(params['mapup']), precision=HIGHEST)
    map_gated = low(geglu_gate(map_hidden))
    mixed = unit_rms + jnp.dot(map_gated, low(params['mapdown']), precision=HIGHEST)
    cond_low = low(rms_scale(mixed, gain_values[2]))
    mods = jnp.einsum('id,dcf->icf', cond_low, low(params['modproj']), precision=HIGHEST)
    groups = IMAGES // IMG_DEV
    w_in = low(params['inproj'])
    w_out = low(params['outproj'])
    w_up = low(params['upproj'])
    w_down = low(params['downproj'])
    head_scale = params['headscale']

    def one_shard(carried, pieces):
        return (carried, layer_shard(pieces[0], pieces[1], pieces[2], w_in, w_out, w_up, w_down, head_scale))
    unused_carry, outputs = lax.scan(jax.checkpoint(one_shard), jnp.zeros((), jnp.float32), (inputs.reshape(groups, SLOTS, D), mods.reshape(groups, IMG_DEV, 2, D), image_lengths.reshape(groups, IMG_DEV)))
    return outputs.reshape(groups * SLOTS, D)

def reference(block_input, out_cotangent, sigmas, class_labels, image_lengths, fourier_freqs, inproj_state, outproj_state, upproj_state, downproj_state, timeproj_state, classemb_state, mapup_state, mapdown_state, modproj_state, gains_state, headscale_state):
    states = (inproj_state, outproj_state, upproj_state, downproj_state, timeproj_state, classemb_state, mapup_state, mapdown_state, modproj_state, gains_state, headscale_state)
    params = {name: state[0] for name, state in zip(NAMES, states)}

    def run_layer(weights, inputs):
        return forward(weights, inputs, sigmas, class_labels, image_lengths, fourier_freqs)
    layer_out, back = jax.vjp(run_layer, params, block_input.astype(jnp.float32))
    gradients, input_grad = back(out_cotangent.astype(jnp.float32))
    squares = jnp.zeros((), jnp.float32)
    for name in NAMES:
        squares = squares + jnp.sum(gradients[name] * gradients[name])
    grad_norm = jnp.sqrt(squares)
    factor = CLIP_NORM / jnp.maximum(grad_norm, CLIP_NORM)
    rates = learn_rates()
    decays = decay_rates()
    updated = [adamw_step(states[index], factor * gradients[NAMES[index]], rates[index], decays[index]) for index in range(len(NAMES))]
    return (layer_out.astype(jnp.bfloat16), input_grad, grad_norm, updated[0][0], updated[0][1], updated[0][2], updated[1][0], updated[1][1], updated[1][2], updated[2][0], updated[2][1], updated[2][2], updated[3][0], updated[3][1], updated[3][2], updated[4][0], updated[4][1], updated[4][2], updated[5][0], updated[5][1], updated[5][2], updated[6][0], updated[6][1], updated[6][2], updated[7][0], updated[7][1], updated[7][2], updated[8][0], updated[8][1], updated[8][2], updated[9][0], updated[9][1], updated[9][2], updated[10][0], updated[10][1], updated[10][2])
```

```python
import functools
import math

import jax
import jax.numpy as jnp
from jax import lax
from jax.experimental import pallas as pl
from jax.experimental.pallas import tpu as pltpu
from jax.sharding import PartitionSpec as P

D = 1024
H = 16
FF = 3072
DM = 768
MFF = 2304
NCLASS = 1000
IMG_DEV = 4
STEP = 10

EPSILON = 1e-06
BETA_ONE = 0.9
BETA_TWO = 0.95
ADAM_EPSILON = 1e-08
CLIP_NORM = 1.0
MASKED = -1e30
MESH = pl.DeviceIdType.MESH
VMEM_BYTES = 60 * 2**20
F32 = jnp.float32
BF16 = jnp.bfloat16


def minor_size(count):
    return 1 << ((count.bit_length() - 1) // 2)


def fourier(sigmas, fourier_freqs):
    angles = 2.0 * math.pi * (jnp.log(sigmas) / 4.0)[:, None] * fourier_freqs[None, :]
    return jnp.concatenate([jnp.cos(angles), jnp.sin(angles)], axis=1)


def learn_rates():
    return (
        2.5 * D ** (-0.5),
        2.5 * (D // 64) ** (-0.5),
        2.5 * D ** (-0.5),
        2.5 * FF ** (-0.5),
        2.5 * DM ** (-0.5),
        2.5,
        2.5 * DM ** (-0.5),
        2.5 * MFF ** (-0.5),
        1.25 * DM ** (-0.5),
        0.25,
        7.5,
    )


def decay_rates():
    return (0.01, 0.01, 0.01, 0.01, 0.01, 0.01, 0.01, 0.01, 0.01, 0.0, 0.0)


def adamw_step(state, gradient, rate, decay):
    keep_rate = 1.0 - (1.0 + STEP) ** (-0.75)
    first = BETA_ONE * state[1] + (1.0 - BETA_ONE) * gradient
    second = BETA_TWO * state[2] + (1.0 - BETA_TWO) * gradient * gradient
    first_hat = first / (1.0 - BETA_ONE**STEP)
    second_hat = second / (1.0 - BETA_TWO**STEP)
    weight = state[0] * (1.0 - rate * decay) - rate * first_hat / (
        jnp.sqrt(second_hat) + ADAM_EPSILON
    )
    average = keep_rate * state[3] + (1.0 - keep_rate) * weight
    return (jnp.stack([weight, average]), first, second)


def dot_nn(a, b):
    return lax.dot_general(a, b, (((1,), (0,)), ((), ())), preferred_element_type=F32)


def dot_nt(a, b):
    return lax.dot_general(a, b, (((1,), (1,)), ((), ())), preferred_element_type=F32)


def dot_tn(a, b):
    return lax.dot_general(a, b, (((0,), (0,)), ((), ())), preferred_element_type=F32)


def two_part(dot, exact, wide):
    high = wide.astype(BF16)
    low = (wide - high.astype(F32)).astype(BF16)
    return dot(exact, high) + dot(exact, low)


def two_part_left(dot, wide, exact):
    high = wide.astype(BF16)
    low = (wide - high.astype(F32)).astype(BF16)
    return dot(high, exact) + dot(low, exact)


def gelu_parts(b):
    cdf = 0.5 * (1.0 + lax.erf(b * (1.0 / math.sqrt(2.0))))
    pdf = jnp.exp(-0.5 * b * b) * (1.0 / math.sqrt(2.0 * math.pi))
    return b * cdf, cdf + b * pdf


def greet(peers):
    barrier = pltpu.get_barrier_semaphore()
    total = 0
    for count, peer_of in peers:

        def say(k, carry, peer_of=peer_of):
            pl.semaphore_signal(barrier, inc=1, device_id=peer_of(k), device_id_type=MESH)
            return carry

        lax.fori_loop(1, count, say, 0)
        total += count - 1
    pl.semaphore_wait(barrier, total)


class Exchange:
    def __init__(self, count, me, device_of, send_sem, recv_sem):
        self.count, self.me, self.device_of = count, me, device_of
        self.send_sem, self.recv_sem = send_sem, recv_sem

    def _copy(self, k, src_of, dst, slot):
        peer = lax.rem(self.me + k, self.count)
        return pltpu.make_async_remote_copy(
            src_ref=src_of(peer),
            dst_ref=dst.at[slot],
            send_sem=self.send_sem.at[k],
            recv_sem=self.recv_sem.at[k],
            device_id=self.device_of(peer),
            device_id_type=MESH,
        )

    def start(self, src_of, dst):
        def body(k, carry):
            self._copy(k, src_of, dst, self.me).start()
            return carry

        lax.fori_loop(1, self.count, body, 0)

    def wait(self, src_of, dst):
        def body(k, carry):
            self._copy(k, src_of, dst, lax.rem(self.me + self.count - k, self.count)).wait()
            return carry

        lax.fori_loop(1, self.count, body, 0)

    def run(self, src_of, dst):
        self.start(src_of, dst)
        self.wait(src_of, dst)


def total_of(ref, count):
    value = ref[0]
    for index in range(1, count):
        value = value + ref[index]
    return value


def mean_square(blocks):
    sums = jnp.sum(jnp.sum(blocks, axis=0), axis=-1, keepdims=True)
    return sums * (1.0 / DM)


def rms_blocks(blocks):
    factor = lax.rsqrt(mean_square(blocks * blocks) + EPSILON)
    return factor


def rms_blocks_back(blocks, factor, gain_grad):
    inner = mean_square(blocks * gain_grad)
    return factor[None] * gain_grad - blocks * (factor * factor * factor * inner)[None]


def front_kernel(
    n_dp, n_mp,
    shard_ref, feats_ref, wt_ref, ecols_ref, gains_ref, wmu_ref, wmd_ref, wmod_ref,
    wg_ref, mods_ref, emb_ref, hid_ref, gated_ref, mixed_ref,
    send_a, recv_a, own_a, send_h, recv_h, own_g, recv_g, own_x, recv_x, own_m, send_o, recv_o,
    dp_ss, dp_rs, mp_ss, mp_rs, z_ss, z_rs, y_ss, y_rs,
):
    d, m = lax.axis_index("dp"), lax.axis_index("mp")
    n_y = minor_size(n_dp)
    n_z = n_dp // n_y
    z, y = lax.div(d, n_y), lax.rem(d, n_y)
    images = feats_ref.shape[0]
    rows = shard_ref.shape[1]
    greet(
        [
            (n_dp, lambda k: (lax.rem(d + k, n_dp), m)),
            (n_mp, lambda k: (d, lax.rem(m + k, n_mp))),
        ]
    )

    def block(dd):
        return wg_ref.at[:, pl.ds(pl.multiple_of(dd * rows, rows), rows), :]

    wg_ref[:, pl.ds(pl.multiple_of(d * rows, rows), rows), :] = shard_ref[...]

    def z_copy(kz, from_z):
        to = lax.rem(z + kz, n_z) * n_y + y
        return pltpu.make_async_remote_copy(
            src_ref=block(d), dst_ref=block(from_z * n_y + y), send_sem=z_ss.at[kz],
            recv_sem=z_rs.at[kz], device_id=(to, m), device_id_type=MESH)

    def y_copy(kz, ky, out_block, in_block):
        to = z * n_y + lax.rem(y + ky, n_y)
        return pltpu.make_async_remote_copy(
            src_ref=block(out_block), dst_ref=block(in_block), send_sem=y_ss.at[kz, ky],
            recv_sem=y_rs.at[kz, ky], device_id=(to, m), device_id_type=MESH)

    def z_start(kz, carry):
        z_copy(kz, z).start()
        return carry

    def y_start(kz):
        mine = lax.rem(z + n_z - kz, n_z) * n_y + y

        def body(ky, carry):
            y_copy(kz, ky, mine, mine).start()
            return carry

        lax.fori_loop(1, n_y, body, 0)

    def forward(kz):
        z_copy(kz, lax.rem(z + n_z - kz, n_z)).wait_recv()
        y_start(kz)

    def finish(kz, carry):
        z_from = lax.rem(z + n_z - kz, n_z)

        def body(ky, inner):
            y_copy(kz, ky, z_from * n_y + y, z_from * n_y + lax.rem(y + n_y - ky, n_y)).wait()
            return inner

        lax.fori_loop(1, n_y, body, 0)
        return carry

    lax.fori_loop(1, n_z, z_start, 0)
    y_start(0)

    def dp_ex(stage):
        return Exchange(n_dp, d, lambda p: (p, m), dp_ss.at[stage], dp_rs.at[stage])

    feats = feats_ref[...]
    for p in range(n_dp):
        send_a[p] = dot_nn(feats, wt_ref[p])
    ex = dp_ex(0)
    ex.start(lambda p: send_a.at[p], recv_a)
    recv_a[d] = send_a[d]
    ex.wait(lambda p: send_a.at[p], recv_a)
    own_a[0:images, :] = total_of(recv_a, n_dp) + ecols_ref[...]
    own_a[images:, :] = gains_ref[...]
    ex = dp_ex(1)
    ex.start(lambda p: own_a, emb_ref)
    emb_ref[d] = own_a[...]
    ex.wait(lambda p: own_a, emb_ref)
    gains = emb_ref[:, images:, :]
    emb = emb_ref[:, 0:images, :]
    unit = emb * rms_blocks(emb)[None] * gains[:, 0:1, :]
    unit_factor = rms_blocks(unit)
    own_x[0] = (emb_ref[d][0:images] * rms_blocks(emb)) * emb_ref[d][images : images + 1]
    unit_own = own_x[0]
    pre_own = (unit_own * unit_factor * emb_ref[d][images + 1 : images + 2]).astype(BF16)
    for c in range(2):
        part = dot_nn(pre_own, wmu_ref[c])
        for p in range(n_dp):
            send_h[p, c] = part[p * IMG_DEV : (p + 1) * IMG_DEV, :]
    ex = dp_ex(2)
    ex.start(lambda p: send_h.at[p], recv_h)
    recv_h[d] = send_h[d]
    ex.wait(lambda p: send_h.at[p], recv_h)
    hidden = total_of(recv_h, n_dp)
    hid_ref[...] = hidden
    own_g[...] = (hidden[0] * gelu_parts(hidden[1])[0]).astype(BF16).astype(F32)
    ex = dp_ex(3)
    ex.start(lambda p: own_g, recv_g)
    recv_g[d] = own_g[...]
    ex.wait(lambda p: own_g, recv_g)
    for p in range(n_dp):
        gated_ref[p * IMG_DEV : (p + 1) * IMG_DEV, :] = recv_g[p]
    own_x[0] = dot_nt(gated_ref[...].astype(BF16), wmd_ref[...])
    ex = Exchange(n_mp, m, lambda p: (d, p), mp_ss.at[0], mp_rs.at[0])
    ex.start(lambda p: own_x.at[0], recv_x)
    recv_x[m] = own_x[0]
    ex.wait(lambda p: own_x.at[0], recv_x)
    own_m[...] = total_of(recv_x, n_mp) + unit_own
    ex = dp_ex(4)
    ex.start(lambda p: own_m, mixed_ref)
    mixed_ref[d] = own_m[...]
    ex.wait(lambda p: own_m, mixed_ref)
    mixed_factor = rms_blocks(mixed_ref[...])
    cond_own = (own_m[...] * mixed_factor * emb_ref[d][images + 2 : images + 3]).astype(BF16)
    for c in range(2):
        part = dot_nn(cond_own, wmod_ref[c])
        for p in range(n_dp):
            send_o[p, c] = part[p * IMG_DEV : (p + 1) * IMG_DEV, :]
    ex = dp_ex(5)
    ex.start(lambda p: send_o.at[p], recv_o)
    for kz in range(1, n_z):
        forward(kz)
    recv_o[d] = send_o[d]
    ex.wait(lambda p: send_o.at[p], recv_o)
    mods_ref[...] = total_of(recv_o, n_dp)

    def z_done(kz, carry):
        z_copy(kz, z).wait_send()
        return carry

    lax.fori_loop(0, n_z, finish, 0)
    lax.fori_loop(1, n_z, z_done, 0)


def vmem_specs(count):
    return [pl.BlockSpec(memory_space=pltpu.VMEM)] * count


def front(n_dp, n_mp, shard, feats_own, w_time, e_cols, gains_own, w_mapup, w_mapdown, w_mod):
    images, part = feats_own.shape
    units = w_mapup.shape[2]
    n_y = minor_size(n_dp)
    n_z = n_dp // n_y
    shape = lambda *dims: jax.ShapeDtypeStruct(dims, F32)
    return pl.pallas_call(
        functools.partial(front_kernel, n_dp, n_mp),
        out_shape=(
            jax.ShapeDtypeStruct((shard.shape[0], shard.shape[1] * n_dp, shard.shape[2]), BF16),
            shape(2, IMG_DEV, D),
            shape(n_dp, images + 8, part),
            shape(2, IMG_DEV, units),
            shape(images, units),
            shape(n_dp, images, part),
        ),
        in_specs=vmem_specs(8),
        out_specs=tuple(vmem_specs(6)),
        scratch_shapes=[
            pltpu.VMEM((n_dp, images, part), F32),
            pltpu.VMEM((n_dp, images, part), F32),
            pltpu.VMEM((images + 8, part), F32),
            pltpu.VMEM((n_dp, 2, IMG_DEV, units), F32),
            pltpu.VMEM((n_dp, 2, IMG_DEV, units), F32),
            pltpu.VMEM((IMG_DEV, units), F32),
            pltpu.VMEM((n_dp, IMG_DEV, units), F32),
            pltpu.VMEM((1, images, part), F32),
            pltpu.VMEM((n_mp, images, part), F32),
            pltpu.VMEM((images, part), F32),
            pltpu.VMEM((n_dp, 2, IMG_DEV, D), F32),
            pltpu.VMEM((n_dp, 2, IMG_DEV, D), F32),
            pltpu.SemaphoreType.DMA((6, n_dp)),
            pltpu.SemaphoreType.DMA((6, n_dp)),
            pltpu.SemaphoreType.DMA((1, n_mp)),
            pltpu.SemaphoreType.DMA((1, n_mp)),
            pltpu.SemaphoreType.DMA((n_z,)),
            pltpu.SemaphoreType.DMA((n_z,)),
            pltpu.SemaphoreType.DMA((n_z, n_y)),
            pltpu.SemaphoreType.DMA((n_z, n_y)),
        ],
        compiler_params=pltpu.CompilerParams(
            collective_id=0, has_side_effects=True, vmem_limit_bytes=VMEM_BYTES
        ),
        name="front",
    )(shard, feats_own, w_time, e_cols, gains_own, w_mapup, w_mapdown, w_mod)


def back_kernel(
    n_dp, n_mp,
    grads_ref, dmods_ref, feats_ref, onehot_ref, wmu_ref, wmd_ref, wmod_ref,
    emb_ref, hid_ref, gated_ref, mixed_ref,
    gshard_ref, gmod_ref, gmd_ref, gmu_ref, gtime_ref, gclass_ref, ggain_ref,
    recv_q, own_q, recv_d, full_d, own_c, recv_c, send_g, recv_g, own_h, recv_h, full_h,
    own_p, recv_p, own_s, recv_s,
    recv_y, send_z, recv_z,
    dp_ss, dp_rs, mp_ss, mp_rs, z_ss, z_rs, y_ss, y_rs,
):
    d, m = lax.axis_index("dp"), lax.axis_index("mp")
    n_y = minor_size(n_dp)
    n_z = n_dp // n_y
    z, y = lax.div(d, n_y), lax.rem(d, n_y)
    images = feats_ref.shape[0]
    rows = gshard_ref.shape[1]
    greet(
        [
            (n_dp, lambda k: (lax.rem(d + k, n_dp), m)),
            (n_mp, lambda k: (d, lax.rem(m + k, n_mp))),
        ]
    )

    def piece(dd):
        return grads_ref.at[:, pl.ds(pl.multiple_of(dd * rows, rows), rows), :]

    def y_copy(kz, ky):
        to_y = lax.rem(y + ky, n_y)
        return pltpu.make_async_remote_copy(
            src_ref=piece(lax.rem(z + kz, n_z) * n_y + to_y), dst_ref=recv_y.at[kz, ky - 1],
            send_sem=y_ss.at[kz, ky], recv_sem=y_rs.at[kz, ky],
            device_id=(z * n_y + to_y, m), device_id_type=MESH)

    def z_copy(kz):
        return pltpu.make_async_remote_copy(
            src_ref=send_z.at[kz - 1], dst_ref=recv_z.at[kz - 1], send_sem=z_ss.at[kz],
            recv_sem=z_rs.at[kz], device_id=(lax.rem(z + kz, n_z) * n_y + y, m),
            device_id_type=MESH)

    for kz in list(range(1, n_z)) + [0]:
        for ky in range(1, n_y):
            y_copy(kz, ky).start()

    def dp_ex(stage):
        return Exchange(n_dp, d, lambda p: (p, m), dp_ss.at[stage], dp_rs.at[stage])

    def mp_ex(stage):
        return Exchange(n_mp, m, lambda p: (d, p), mp_ss.at[stage], mp_rs.at[stage])

    def pair_sum(kz):
        for ky in range(1, n_y):
            y_copy(kz, ky).wait_recv()
        target = lax.rem(z + kz, n_z) * n_y + y
        value = grads_ref[:, pl.ds(pl.multiple_of(target * rows, rows), rows), :].astype(F32)
        for ky in range(1, n_y):
            value = value + recv_y[kz, ky - 1].astype(F32)
        return value

    def send_on(kz):
        send_z[kz - 1] = pair_sum(kz).astype(BF16)
        z_copy(kz).start()

    ex = mp_ex(0)
    ex.start(lambda p: dmods_ref, recv_q)
    recv_q[m] = dmods_ref[...]
    ex.wait(lambda p: dmods_ref, recv_q)
    own_q[...] = total_of(recv_q, n_mp)
    ex = dp_ex(0)
    ex.start(lambda p: own_q, recv_d)
    recv_d[d] = own_q[...]
    gains_own = emb_ref[d][images:]
    emb = emb_ref[:, 0:images, :]
    emb_factor = rms_blocks(emb)
    unit = emb * emb_factor[None] * emb_ref[:, images : images + 1, :]
    unit_factor = rms_blocks(unit)
    emb_own = emb_ref[d][0:images]
    unit_own = emb_own * emb_factor * gains_own[0:1]
    pre_own = (unit_own * unit_factor * gains_own[1:2]).astype(BF16)
    mixed = mixed_ref[...]
    mixed_factor = rms_blocks(mixed)
    mixed_own = mixed_ref[d]
    cond_own = (mixed_own * mixed_factor * gains_own[2:3]).astype(BF16)
    ex.wait(lambda p: own_q, recv_d)
    for p in range(n_dp):
        for c in range(2):
            full_d[c, p * IMG_DEV : (p + 1) * IMG_DEV, :] = recv_d[p, c]
    own_c[...] = two_part_left(dot_nt, full_d[0], wmod_ref[0]) + two_part_left(
        dot_nt, full_d[1], wmod_ref[1]
    )
    ex = dp_ex(1)
    ex.start(lambda p: own_c, recv_c)
    recv_c[d] = own_c[...]
    for c in range(2):
        gmod_ref[c] = two_part(dot_tn, cond_own, full_d[c])
    if n_z > 1:
        send_on(1)
    ex.wait(lambda p: own_c, recv_c)
    ggain_ref[2:3, :] = jnp.sum(own_c[...] * mixed_own * mixed_factor, axis=0, keepdims=True)
    d_mixed = rms_blocks_back(
        mixed, mixed_factor, recv_c[...] * emb_ref[:, images + 2 : images + 3, :]
    )
    recv_c[...] = d_mixed
    mix_own = recv_c[d]
    part = two_part_left(dot_nn, mix_own, wmd_ref[...])
    for p in range(n_dp):
        send_g[p] = part[p * IMG_DEV : (p + 1) * IMG_DEV, :]
    ex = dp_ex(2)
    ex.start(lambda p: send_g.at[p], recv_g)
    recv_g[d] = send_g[d]
    gmd_ref[...] = two_part_left(dot_tn, mix_own, gated_ref[...].astype(BF16))
    for kz in range(2, n_z):
        send_on(kz)
    ex.wait(lambda p: send_g.at[p], recv_g)
    d_gated = total_of(recv_g, n_dp)
    value, slope = gelu_parts(hid_ref[1])
    own_h[0] = d_gated * value
    own_h[1] = d_gated * hid_ref[0] * slope
    ex = dp_ex(3)
    ex.start(lambda p: own_h, recv_h)
    recv_h[d] = own_h[...]
    ex.wait(lambda p: own_h, recv_h)
    for p in range(n_dp):
        for c in range(2):
            full_h[c, p * IMG_DEV : (p + 1) * IMG_DEV, :] = recv_h[p, c]
    own_p[...] = two_part_left(dot_nt, full_h[0], wmu_ref[0]) + two_part_left(
        dot_nt, full_h[1], wmu_ref[1]
    )
    ex = mp_ex(1)
    ex.start(lambda p: own_p, recv_p)
    recv_p[m] = own_p[...]
    for c in range(2):
        gmu_ref[c] = two_part(dot_tn, pre_own, full_h[c])
    ex.wait(lambda p: own_p, recv_p)
    own_s[...] = total_of(recv_p, n_mp)
    ex = dp_ex(4)
    ex.start(lambda p: own_s, recv_s)
    recv_s[d] = own_s[...]
    gshard_ref[...] = pair_sum(0)
    ex.wait(lambda p: own_s, recv_s)
    ggain_ref[1:2, :] = jnp.sum(own_s[...] * unit_own * unit_factor, axis=0, keepdims=True)
    d_unit = recv_c[...] + rms_blocks_back(
        unit, unit_factor, recv_s[...] * emb_ref[:, images + 1 : images + 2, :]
    )
    recv_s[...] = d_unit
    ggain_ref[0:1, :] = jnp.sum(recv_s[d] * emb_own * emb_factor, axis=0, keepdims=True)
    d_emb = rms_blocks_back(emb, emb_factor, d_unit * emb_ref[:, images : images + 1, :])
    recv_s[...] = d_emb
    ggain_ref[3:8, :] = jnp.zeros_like(ggain_ref[3:8, :])
    for p in range(n_dp):
        gtime_ref[p] = two_part(dot_tn, feats_ref[...], recv_s[p])
    gclass_ref[...] = two_part_left(dot_tn, recv_s[d], onehot_ref[...])
    for kz in range(1, n_z):
        z_copy(kz).wait_recv()
        gshard_ref[...] = gshard_ref[...] + recv_z[kz - 1].astype(F32)
    for kz in range(1, n_z):
        z_copy(kz).wait_send()
    for kz in range(n_z):
        for ky in range(1, n_y):
            y_copy(kz, ky).wait_send()


def back(n_dp, n_mp, grads, dmods, feats_own, onehot, w_mapup, w_mapdown, w_mod, emb, hid, gated, mixed):
    images, part = feats_own.shape
    units = w_mapup.shape[2]
    n_y = minor_size(n_dp)
    n_z = n_dp // n_y
    rows = grads.shape[1] // n_dp
    slab = (grads.shape[0], rows, grads.shape[2])
    shape = lambda *dims: jax.ShapeDtypeStruct(dims, F32)
    return pl.pallas_call(
        functools.partial(back_kernel, n_dp, n_mp),
        out_shape=(
            shape(*slab),
            shape(2, part, D),
            shape(part, units),
            shape(2, part, units),
            shape(n_dp, part, part),
            shape(part, NCLASS),
            shape(8, part),
        ),
        in_specs=vmem_specs(11),
        out_specs=tuple(vmem_specs(7)),
        scratch_shapes=[
            pltpu.VMEM((n_mp, 2, IMG_DEV, D), F32),
            pltpu.VMEM((2, IMG_DEV, D), F32),
            pltpu.VMEM((n_dp, 2, IMG_DEV, D), F32),
            pltpu.VMEM((2, images, D), F32),
            pltpu.VMEM((images, part), F32),
            pltpu.VMEM((n_dp, images, part), F32),
            pltpu.VMEM((n_dp, IMG_DEV, units), F32),
            pltpu.VMEM((n_dp, IMG_DEV, units), F32),
            pltpu.VMEM((2, IMG_DEV, units), F32),
            pltpu.VMEM((n_dp, 2, IMG_DEV, units), F32),
            pltpu.VMEM((2, images, units), F32),
            pltpu.VMEM((images, part), F32),
            pltpu.VMEM((n_mp, images, part), F32),
            pltpu.VMEM((images, part), F32),
            pltpu.VMEM((n_dp, images, part), F32),
            pltpu.VMEM((n_z, max(n_y - 1, 1)) + slab, BF16),
            pltpu.VMEM((max(n_z - 1, 1),) + slab, BF16),
            pltpu.VMEM((max(n_z - 1, 1),) + slab, BF16),
            pltpu.SemaphoreType.DMA((5, n_dp)),
            pltpu.SemaphoreType.DMA((5, n_dp)),
            pltpu.SemaphoreType.DMA((2, n_mp)),
            pltpu.SemaphoreType.DMA((2, n_mp)),
            pltpu.SemaphoreType.DMA((n_z,)),
            pltpu.SemaphoreType.DMA((n_z,)),
            pltpu.SemaphoreType.DMA((n_z, n_y)),
            pltpu.SemaphoreType.DMA((n_z, n_y)),
        ],
        compiler_params=pltpu.CompilerParams(
            collective_id=1, has_side_effects=True, vmem_limit_bytes=VMEM_BYTES
        ),
        name="back",
    )(grads, dmods, feats_own, onehot, w_mapup, w_mapdown, w_mod, emb, hid, gated, mixed)


def norm_kernel(n_dp, n_mp, heads, v_ref, o_ref, own, recv_dp, recv_mp, dp_ss, dp_rs, mp_ss, mp_rs):
    d, m = lax.axis_index("dp"), lax.axis_index("mp")
    greet(
        [
            (n_dp, lambda k: (lax.rem(d + k, n_dp), m)),
            (n_mp, lambda k: (d, lax.rem(m + k, n_mp))),
        ]
    )
    ex = Exchange(n_dp, d, lambda p: (p, m), dp_ss, dp_rs)
    ex.start(lambda p: v_ref, recv_dp)
    recv_dp[d] = v_ref[...]
    ex.wait(lambda p: v_ref, recv_dp)
    summed = total_of(recv_dp, n_dp)
    head = summed[1:2]
    squares = summed[0:1] + head * head
    own[...] = jnp.zeros_like(own)
    own[0:1, :] = squares
    ex = Exchange(n_mp, m, lambda p: (d, p), mp_ss, mp_rs)
    ex.start(lambda p: own, recv_mp)
    recv_mp[m] = own[...]
    ex.wait(lambda p: own, recv_mp)
    norm = jnp.sqrt(jnp.sum(total_of(recv_mp, n_mp)[0:1], axis=-1, keepdims=True))
    o_ref[...] = jnp.zeros_like(o_ref)
    o_ref[0:1, :] = jnp.broadcast_to(norm, (1, o_ref.shape[1]))
    o_ref[1:2, :] = head


def norm_all(n_dp, n_mp, heads, values):
    return pl.pallas_call(
        functools.partial(norm_kernel, n_dp, n_mp, heads),
        out_shape=jax.ShapeDtypeStruct(values.shape, F32),
        in_specs=vmem_specs(1),
        out_specs=vmem_specs(1)[0],
        scratch_shapes=[
            pltpu.VMEM(values.shape, F32),
            pltpu.VMEM((n_dp,) + values.shape, F32),
            pltpu.VMEM((n_mp,) + values.shape, F32),
            pltpu.SemaphoreType.DMA((n_dp,)),
            pltpu.SemaphoreType.DMA((n_dp,)),
            pltpu.SemaphoreType.DMA((n_mp,)),
            pltpu.SemaphoreType.DMA((n_mp,)),
        ],
        compiler_params=pltpu.CompilerParams(collective_id=2, has_side_effects=True),
        name="norm_all",
    )(values)


def rms_scale(values, scales):
    return values * lax.rsqrt(jnp.mean(values * values, axis=-1, keepdims=True) + EPSILON) * scales


def geglu_gate(hidden):
    return hidden[:, 0] * jax.nn.gelu(hidden[:, 1], approximate=False)


def cosine(queries, key_rows, head_scale):
    query_unit = (
        queries
        * lax.rsqrt(jnp.sum(queries * queries, axis=-1, keepdims=True) + EPSILON)
        * head_scale[None, :, None]
    )
    key_unit = key_rows * lax.rsqrt(jnp.sum(key_rows * key_rows, axis=-1, keepdims=True) + EPSILON)
    return (query_unit, key_unit)


def middle_part(block_input, out_cotangent, mods, my_lengths, wg, wf, head_scale):
    n_dp = lax.axis_size("dp")
    w_in = jnp.transpose(wg[:3], (1, 0, 2))
    w_out = wg[3].T
    rows = D // n_dp
    w_up = jnp.transpose(wf.reshape(n_dp, 3, rows, -1)[:, :2], (0, 2, 1, 3)).reshape(D, 2, -1)
    w_down = wf.reshape(n_dp, 3, rows, -1)[:, 2].reshape(D, -1).T
    slot_count = block_input.shape[0]
    image_ends = jnp.cumsum(my_lengths)
    position = jnp.arange(slot_count, dtype=jnp.int32)
    slot_of = jnp.sum((position[:, None] >= image_ends[None, :]).astype(jnp.int32), axis=1)
    live_rows = (position < image_ends[-1]).astype(jnp.float32)[:, None]
    member = (slot_of[:, None] == jnp.arange(IMG_DEV, dtype=jnp.int32)[None, :]).astype(jnp.float32)
    same_image = slot_of[:, None] == slot_of[None, :]
    hi = lax.Precision.HIGHEST
    attn_mod = 1.0 + jnp.dot(member, mods[0], precision=hi)
    ff_mod = 1.0 + jnp.dot(member, mods[1], precision=hi)
    heads_here = head_scale.shape[0]
    width_here = w_in.shape[2]
    head_size = width_here // heads_here
    inputs = block_input.astype(jnp.float32)
    normed_in, in_back = jax.vjp(rms_scale, inputs, attn_mod)
    low_in = normed_in.astype(jnp.bfloat16)
    projected = jnp.einsum("td,dcf->tcf", low_in, w_in, preferred_element_type=jnp.float32)
    queries = projected[:, 0].reshape(slot_count, heads_here, head_size)
    key_rows = projected[:, 1].reshape(slot_count, heads_here, head_size)
    (query_unit, key_unit), cosine_back = jax.vjp(cosine, queries, key_rows, head_scale)
    query_low = query_unit.astype(jnp.bfloat16)
    key_low = key_unit.astype(jnp.bfloat16)
    value_low = projected[:, 2].reshape(slot_count, heads_here, head_size).astype(jnp.bfloat16)
    scores = jnp.einsum("thd,uhd->htu", query_low, key_low, preferred_element_type=jnp.float32)
    scores = jnp.where(same_image[None], scores, MASKED)
    row_max = jnp.max(scores, axis=-1, keepdims=True)
    expon = jnp.exp(scores - row_max)
    row_total = jnp.sum(expon, axis=-1, keepdims=True)
    probabilities = expon / row_total
    log_total = row_max + jnp.log(row_total)
    attended = jnp.einsum(
        "htu,uhd->thd",
        probabilities.astype(jnp.bfloat16),
        value_low,
        preferred_element_type=jnp.float32,
    )
    attended_low = attended.reshape(slot_count, width_here).astype(jnp.bfloat16)
    branch_attn = lax.psum(jnp.dot(attended_low, w_out, preferred_element_type=jnp.float32), "mp")
    middle = inputs + branch_attn
    normed_mid, mid_back = jax.vjp(rms_scale, middle, ff_mod)
    low_mid = normed_mid.astype(jnp.bfloat16)
    hidden = jnp.einsum("td,dcf->tcf", low_mid, w_up, preferred_element_type=jnp.float32)
    gated_vals, gate_back = jax.vjp(geglu_gate, hidden)
    gated_low = gated_vals.astype(jnp.bfloat16)
    branch_ff = lax.psum(
        jnp.dot(gated_low, w_down, preferred_element_type=jnp.float32).astype(jnp.bfloat16), "mp"
    ).astype(jnp.float32)
    layer_out = (live_rows * (middle + branch_ff)).astype(jnp.bfloat16)
    out_grad = live_rows * out_cotangent.astype(jnp.float32)
    grad_branch = out_grad.astype(jnp.bfloat16)
    grad_downproj = jnp.dot(gated_low.T, grad_branch, preferred_element_type=jnp.float32)
    grad_gated = jnp.dot(grad_branch, w_down.T, preferred_element_type=jnp.float32)
    (grad_hidden,) = gate_back(grad_gated)
    grad_hidden_low = grad_hidden.astype(jnp.bfloat16)
    grad_upproj = jnp.einsum(
        "td,tcf->dcf", low_mid, grad_hidden_low, preferred_element_type=jnp.float32
    )
    grad_low_mid = lax.psum(
        jnp.einsum("tcf,dcf->td", grad_hidden_low, w_up, preferred_element_type=jnp.float32), "mp"
    )
    grad_mid_norm, grad_ff_mod = mid_back(grad_low_mid)
    grad_middle = out_grad + grad_mid_norm
    grad_y = grad_middle.astype(jnp.bfloat16)
    grad_outproj = jnp.dot(attended_low.T, grad_y, preferred_element_type=jnp.float32)
    grad_att = (
        jnp.dot(grad_y, w_out.T, preferred_element_type=jnp.float32)
        .astype(jnp.bfloat16)
        .reshape(slot_count, heads_here, head_size)
    )
    again = jnp.einsum("thd,uhd->htu", query_low, key_low, preferred_element_type=jnp.float32)
    again = jnp.where(same_image[None], again, MASKED)
    probs_again = jnp.exp(again - log_total)
    grad_values = jnp.einsum(
        "htu,thd->uhd",
        probs_again.astype(jnp.bfloat16),
        grad_att,
        preferred_element_type=jnp.float32,
    )
    grad_probs = jnp.einsum("thd,uhd->htu", grad_att, value_low, preferred_element_type=jnp.float32)
    inner = jnp.sum(grad_probs * probs_again, axis=-1, keepdims=True)
    grad_scores = (probs_again * (grad_probs - inner)).astype(jnp.bfloat16)
    grad_qunit = jnp.einsum(
        "htu,uhd->thd", grad_scores, key_low, preferred_element_type=jnp.float32
    )
    grad_kunit = jnp.einsum(
        "htu,thd->uhd", grad_scores, query_low, preferred_element_type=jnp.float32
    )
    grad_queries, grad_keys, grad_headscale = cosine_back((grad_qunit, grad_kunit))
    grad_projected = jnp.stack(
        [
            grad_queries.reshape(slot_count, width_here),
            grad_keys.reshape(slot_count, width_here),
            grad_values.reshape(slot_count, width_here),
        ],
        axis=1,
    ).astype(jnp.bfloat16)
    grad_inproj = jnp.einsum(
        "td,tcf->dcf", low_in, grad_projected, preferred_element_type=jnp.float32
    )
    grad_low_in = lax.psum(
        jnp.einsum("tcf,dcf->td", grad_projected, w_in, preferred_element_type=jnp.float32), "mp"
    )
    grad_in_norm, grad_attn_mod = in_back(grad_low_in)
    input_grad = grad_middle + grad_in_norm
    grad_mods = jnp.stack(
        [
            jnp.dot(member.T, grad_attn_mod, precision=hi),
            jnp.dot(member.T, grad_ff_mod, precision=hi),
        ],
        axis=0,
    ) / lax.axis_size("mp")
    grad_attn_w = jnp.concatenate(
        [jnp.transpose(grad_inproj, (1, 0, 2)), grad_outproj.T[None]], axis=0
    ).astype(BF16)
    grad_ffn_w = jnp.concatenate(
        [
            jnp.transpose(grad_upproj, (1, 0, 2)).reshape(2, n_dp, rows, -1),
            grad_downproj.T.reshape(1, n_dp, rows, -1),
        ],
        axis=0,
    ).astype(BF16)
    grad_ffn_w = jnp.transpose(grad_ffn_w, (1, 0, 2, 3)).reshape(n_dp, 3 * rows, -1)
    return layer_out, input_grad, grad_mods, grad_attn_w, grad_ffn_w, grad_headscale


def per_device(
    block_input,
    out_cotangent,
    sigmas,
    class_labels,
    image_lengths,
    fourier_freqs,
    inproj_state,
    outproj_state,
    upproj_state,
    downproj_state,
    timeproj_state,
    classemb_state,
    mapup_state,
    mapdown_state,
    modproj_state,
    gains_state,
    headscale_state,
):
    n_dp, n_mp = lax.axis_size("dp"), lax.axis_size("mp")
    d = lax.axis_index("dp")
    my_lengths = lax.dynamic_slice_in_dim(image_lengths, d * IMG_DEV, IMG_DEV)
    rows, _, width = inproj_state.shape[1:]
    units = upproj_state.shape[3]
    part = timeproj_state.shape[1]
    ffn_shard = jnp.concatenate(
        [
            jnp.transpose(upproj_state[0].astype(BF16), (1, 0, 2)).reshape(2 * rows, units),
            downproj_state[0].astype(BF16).T,
        ],
        axis=0,
    )
    wf = lax.all_gather(ffn_shard, "dp", axis=0)
    attn_shard = jnp.concatenate(
        [
            jnp.transpose(inproj_state[0].astype(BF16), (1, 0, 2)),
            outproj_state[0].astype(BF16).T[None],
        ],
        axis=0,
    )
    feats_low = fourier(sigmas, fourier_freqs).astype(BF16)
    feats_own = lax.dynamic_slice_in_dim(feats_low, d * part, part, axis=1)
    onehot = (class_labels[:, None] == jnp.arange(NCLASS, dtype=jnp.int32)[None, :]).astype(BF16)
    e_cols = dot_nt(onehot, classemb_state[0].astype(BF16).T)
    gains_own = jnp.pad(gains_state[0].astype(BF16).astype(F32), ((0, 5), (0, 0)))
    w_time = jnp.transpose(timeproj_state[0].astype(BF16).reshape(part, n_dp, part), (1, 0, 2))
    w_mapup = jnp.transpose(mapup_state[0].astype(BF16), (1, 0, 2))
    w_mapdown = mapdown_state[0].astype(BF16).T
    w_mod = jnp.transpose(modproj_state[0].astype(BF16), (1, 0, 2))
    wg, mods, emb, hid, gated, mixed = front(
        n_dp, n_mp, attn_shard, feats_own, w_time, e_cols, gains_own, w_mapup, w_mapdown, w_mod
    )
    layer_out, input_grad, grad_mods, grad_attn_w, grad_ffn_w, grad_headscale = middle_part(
        block_input, out_cotangent, mods, my_lengths, wg, wf, headscale_state[0]
    )
    g_ffn = lax.psum_scatter(grad_ffn_w, "dp", scatter_dimension=0).astype(F32)
    g_attn, g_mod, g_md, g_mu, g_time, g_class, g_gain = back(
        n_dp, n_mp, grad_attn_w, grad_mods, feats_own, onehot, w_mapup, w_mapdown, w_mod, emb, hid, gated, mixed
    )
    g_gain = g_gain[:3]
    g_ffn = g_ffn.reshape(3, rows, units)
    split = jnp.sum(g_attn * g_attn) + jnp.sum(g_ffn * g_ffn) + jnp.sum(g_mu * g_mu) + jnp.sum(g_md * g_md)
    shared = (
        jnp.sum(g_mod * g_mod) + jnp.sum(g_time * g_time) + jnp.sum(g_class * g_class) + jnp.sum(g_gain * g_gain)
    )
    heads_here = headscale_state.shape[1]
    packed = jnp.zeros((8, 128), F32).at[0, 0].set(split + shared / n_mp).at[1, :heads_here].set(grad_headscale)
    normed = norm_all(n_dp, n_mp, heads_here, packed)
    grad_norm = normed[0, 0]
    factor = CLIP_NORM / jnp.maximum(grad_norm, CLIP_NORM)
    gradients = (
        jnp.transpose(g_attn[:3], (1, 0, 2)),
        g_attn[3].T,
        jnp.transpose(g_ffn[:2], (1, 0, 2)),
        g_ffn[2].T,
        jnp.transpose(g_time, (1, 0, 2)).reshape(part, DM),
        g_class.T,
        jnp.transpose(g_mu, (1, 0, 2)),
        g_md.T,
        jnp.transpose(g_mod, (1, 0, 2)),
        g_gain,
        normed[1, :heads_here],
    )
    states = (
        inproj_state,
        outproj_state,
        upproj_state,
        downproj_state,
        timeproj_state,
        classemb_state,
        mapup_state,
        mapdown_state,
        modproj_state,
        gains_state,
        headscale_state,
    )
    rates = learn_rates()
    decays = decay_rates()
    results = [layer_out, input_grad, grad_norm]
    for index in range(11):
        results += adamw_step(states[index], factor * gradients[index], rates[index], decays[index])
    return tuple(results)


def solution(mesh):
    return jax.shard_map(
        per_device,
        mesh=mesh,
        in_specs=(
            P("dp", None),
            P("dp", None),
            P(),
            P(),
            P(),
            P(),
            P(None, "dp", None, "mp"),
            P(None, "mp", "dp"),
            P(None, "dp", None, "mp"),
            P(None, "mp", "dp"),
            P(None, "dp", None),
            P(None, None, "dp"),
            P(None, "dp", None, "mp"),
            P(None, "mp", "dp"),
            P(None, "dp", None, None),
            P(None, None, "dp"),
            P(None, "mp"),
        ),
        out_specs=(
            P("dp", None),
            P("dp", None),
            P(),
            P(None, "dp", None, "mp"),
            P("dp", None, "mp"),
            P("dp", None, "mp"),
            P(None, "mp", "dp"),
            P("mp", "dp"),
            P("mp", "dp"),
            P(None, "dp", None, "mp"),
            P("dp", None, "mp"),
            P("dp", None, "mp"),
            P(None, "mp", "dp"),
            P("mp", "dp"),
            P("mp", "dp"),
            P(None, "dp", None),
            P("dp", None),
            P("dp", None),
            P(None, None, "dp"),
            P(None, "dp"),
            P(None, "dp"),
            P(None, "dp", None, "mp"),
            P("dp", None, "mp"),
            P("dp", None, "mp"),
            P(None, "mp", "dp"),
            P("mp", "dp"),
            P("mp", "dp"),
            P(None, "dp", None, None),
            P("dp", None, None),
            P("dp", None, None),
            P(None, None, "dp"),
            P(None, "dp"),
            P(None, "dp"),
            P(None, "mp"),
            P("mp"),
            P("mp"),
        ),
        check_vma=False,
    )
```

```python
import functools
import math

import jax
import jax.numpy as jnp
from jax import lax
from jax.experimental import pallas as pl
from jax.experimental.pallas import tpu as pltpu
from jax.sharding import PartitionSpec as P

D = 1024
H = 16
FF = 3072
DM = 768
MFF = 2304
NCLASS = 1000
IMG_DEV = 4
STEP = 10

EPSILON = 1e-06
BETA_ONE = 0.9
BETA_TWO = 0.95
ADAM_EPSILON = 1e-08
CLIP_NORM = 1.0
MASKED = -1e30
MESH = pl.DeviceIdType.MESH
VMEM_BYTES = 60 * 2**20
F32 = jnp.float32
BF16 = jnp.bfloat16


def minor_size(count):
    return 1 << ((count.bit_length() - 1) // 2)


def fourier(sigmas, fourier_freqs):
    angles = 2.0 * math.pi * (jnp.log(sigmas) / 4.0)[:, None] * fourier_freqs[None, :]
    return jnp.concatenate([jnp.cos(angles), jnp.sin(angles)], axis=1)


def learn_rates():
    return (
        2.5 * D ** (-0.5),
        2.5 * (D // 64) ** (-0.5),
        2.5 * D ** (-0.5),
        2.5 * FF ** (-0.5),
        2.5 * DM ** (-0.5),
        2.5,
        2.5 * DM ** (-0.5),
        2.5 * MFF ** (-0.5),
        1.25 * DM ** (-0.5),
        0.25,
        7.5,
    )


def decay_rates():
    return (0.01, 0.01, 0.01, 0.01, 0.01, 0.01, 0.01, 0.01, 0.01, 0.0, 0.0)


def adamw_step(state, gradient, rate, decay):
    keep_rate = 1.0 - (1.0 + STEP) ** (-0.75)
    first = BETA_ONE * state[1] + (1.0 - BETA_ONE) * gradient
    second = BETA_TWO * state[2] + (1.0 - BETA_TWO) * gradient * gradient
    first_hat = first / (1.0 - BETA_ONE**STEP)
    second_hat = second / (1.0 - BETA_TWO**STEP)
    weight = state[0] * (1.0 - rate * decay) - rate * first_hat / (
        jnp.sqrt(second_hat) + ADAM_EPSILON
    )
    average = keep_rate * state[3] + (1.0 - keep_rate) * weight
    return (jnp.stack([weight, average]), first, second)


def dot_nn(a, b):
    return lax.dot_general(a, b, (((1,), (0,)), ((), ())), preferred_element_type=F32)


def dot_nt(a, b):
    return lax.dot_general(a, b, (((1,), (1,)), ((), ())), preferred_element_type=F32)


def dot_tn(a, b):
    return lax.dot_general(a, b, (((0,), (0,)), ((), ())), preferred_element_type=F32)


def two_part(dot, exact, wide):
    high = wide.astype(BF16)
    low = (wide - high.astype(F32)).astype(BF16)
    return dot(exact, high) + dot(exact, low)


def two_part_left(dot, wide, exact):
    high = wide.astype(BF16)
    low = (wide - high.astype(F32)).astype(BF16)
    return dot(high, exact) + dot(low, exact)


def gelu_parts(b):
    cdf = 0.5 * (1.0 + lax.erf(b * (1.0 / math.sqrt(2.0))))
    pdf = jnp.exp(-0.5 * b * b) * (1.0 / math.sqrt(2.0 * math.pi))
    return b * cdf, cdf + b * pdf


def greet(peers):
    barrier = pltpu.get_barrier_semaphore()
    total = 0
    for count, peer_of in peers:

        def say(k, carry, peer_of=peer_of):
            pl.semaphore_signal(barrier, inc=1, device_id=peer_of(k), device_id_type=MESH)
            return carry

        lax.fori_loop(1, count, say, 0)
        total += count - 1
    pl.semaphore_wait(barrier, total)


class Exchange:
    def __init__(self, count, me, device_of, send_sem, recv_sem):
        self.count, self.me, self.device_of = count, me, device_of
        self.send_sem, self.recv_sem = send_sem, recv_sem

    def _copy(self, k, src_of, dst, slot):
        peer = lax.rem(self.me + k, self.count)
        return pltpu.make_async_remote_copy(
            src_ref=src_of(peer),
            dst_ref=dst.at[slot],
            send_sem=self.send_sem.at[k],
            recv_sem=self.recv_sem.at[k],
            device_id=self.device_of(peer),
            device_id_type=MESH,
        )

    def start(self, src_of, dst):
        def body(k, carry):
            self._copy(k, src_of, dst, self.me).start()
            return carry

        lax.fori_loop(1, self.count, body, 0)

    def wait(self, src_of, dst):
        def body(k, carry):
            self._copy(k, src_of, dst, lax.rem(self.me + self.count - k, self.count)).wait()
            return carry

        lax.fori_loop(1, self.count, body, 0)

    def run(self, src_of, dst):
        self.start(src_of, dst)
        self.wait(src_of, dst)


def total_of(ref, count):
    value = ref[0]
    for index in range(1, count):
        value = value + ref[index]
    return value


def mean_square(blocks):
    sums = jnp.sum(jnp.sum(blocks, axis=0), axis=-1, keepdims=True)
    return sums * (1.0 / DM)


def rms_blocks(blocks):
    factor = lax.rsqrt(mean_square(blocks * blocks) + EPSILON)
    return factor


def rms_blocks_back(blocks, factor, gain_grad):
    inner = mean_square(blocks * gain_grad)
    return factor[None] * gain_grad - blocks * (factor * factor * factor * inner)[None]


def front_kernel(
    n_dp, n_mp,
    shard_ref, feats_ref, wt_ref, ecols_ref, gains_ref, wmu_ref, wmd_ref, wmod_ref,
    wg_ref, mods_ref, emb_ref, hid_ref, gated_ref, mixed_ref,
    send_a, recv_a, own_a, send_h, recv_h, own_g, recv_g, own_x, recv_x, own_m, send_o, recv_o,
    dp_ss, dp_rs, mp_ss, mp_rs, z_ss, z_rs, y_ss, y_rs,
):
    d, m = lax.axis_index("dp"), lax.axis_index("mp")
    n_y = minor_size(n_dp)
    n_z = n_dp // n_y
    z, y = lax.div(d, n_y), lax.rem(d, n_y)
    images = feats_ref.shape[0]
    rows = shard_ref.shape[1]
    greet(
        [
            (n_dp, lambda k: (lax.rem(d + k, n_dp), m)),
            (n_mp, lambda k: (d, lax.rem(m + k, n_mp))),
        ]
    )

    def block(dd):
        return wg_ref.at[:, pl.ds(pl.multiple_of(dd * rows, rows), rows), :]

    wg_ref[:, pl.ds(pl.multiple_of(d * rows, rows), rows), :] = shard_ref[...]

    def z_copy(kz, from_z):
        to = lax.rem(z + kz, n_z) * n_y + y
        return pltpu.make_async_remote_copy(
            src_ref=block(d), dst_ref=block(from_z * n_y + y), send_sem=z_ss.at[kz],
            recv_sem=z_rs.at[kz], device_id=(to, m), device_id_type=MESH)

    def y_copy(kz, ky, out_block, in_block):
        to = z * n_y + lax.rem(y + ky, n_y)
        return pltpu.make_async_remote_copy(
            src_ref=block(out_block), dst_ref=block(in_block), send_sem=y_ss.at[kz, ky],
            recv_sem=y_rs.at[kz, ky], device_id=(to, m), device_id_type=MESH)

    def z_start(kz, carry):
        z_copy(kz, z).start()
        return carry

    def y_start(kz):
        mine = lax.rem(z + n_z - kz, n_z) * n_y + y

        def body(ky, carry):
            y_copy(kz, ky, mine, mine).start()
            return carry

        lax.fori_loop(1, n_y, body, 0)

    def forward(kz):
        z_copy(kz, lax.rem(z + n_z - kz, n_z)).wait_recv()
        y_start(kz)

    def finish(kz, carry):
        z_from = lax.rem(z + n_z - kz, n_z)

        def body(ky, inner):
            y_copy(kz, ky, z_from * n_y + y, z_from * n_y + lax.rem(y + n_y - ky, n_y)).wait()
            return inner

        lax.fori_loop(1, n_y, body, 0)
        return carry

    lax.fori_loop(1, n_z, z_start, 0)
    y_start(0)

    def dp_ex(stage):
        return Exchange(n_dp, d, lambda p: (p, m), dp_ss.at[stage], dp_rs.at[stage])

    feats = feats_ref[...]
    for p in range(n_dp):
        send_a[p] = dot_nn(feats, wt_ref[p])
    ex = dp_ex(0)
    ex.start(lambda p: send_a.at[p], recv_a)
    recv_a[d] = send_a[d]
    ex.wait(lambda p: send_a.at[p], recv_a)
    own_a[0:images, :] = total_of(recv_a, n_dp) + ecols_ref[...]
    own_a[images:, :] = gains_ref[...]
    ex = dp_ex(1)
    ex.start(lambda p: own_a, emb_ref)
    emb_ref[d] = own_a[...]
    ex.wait(lambda p: own_a, emb_ref)
    gains = emb_ref[:, images:, :]
    emb = emb_ref[:, 0:images, :]
    unit = emb * rms_blocks(emb)[None] * gains[:, 0:1, :]
    unit_factor = rms_blocks(unit)
    own_x[0] = (emb_ref[d][0:images] * rms_blocks(emb)) * emb_ref[d][images : images + 1]
    unit_own = own_x[0]
    pre_own = (unit_own * unit_factor * emb_ref[d][images + 1 : images + 2]).astype(BF16)
    for c in range(2):
        part = dot_nn(pre_own, wmu_ref[c])
        for p in range(n_dp):
            send_h[p, c] = part[p * IMG_DEV : (p + 1) * IMG_DEV, :]
    ex = dp_ex(2)
    ex.start(lambda p: send_h.at[p], recv_h)
    recv_h[d] = send_h[d]
    ex.wait(lambda p: send_h.at[p], recv_h)
    hidden = total_of(recv_h, n_dp)
    hid_ref[...] = hidden
    own_g[...] = (hidden[0] * gelu_parts(hidden[1])[0]).astype(BF16).astype(F32)
    ex = dp_ex(3)
    ex.start(lambda p: own_g, recv_g)
    recv_g[d] = own_g[...]
    ex.wait(lambda p: own_g, recv_g)
    for p in range(n_dp):
        gated_ref[p * IMG_DEV : (p + 1) * IMG_DEV, :] = recv_g[p]
    own_x[0] = dot_nt(gated_ref[...].astype(BF16), wmd_ref[...])
    ex = Exchange(n_mp, m, lambda p: (d, p), mp_ss.at[0], mp_rs.at[0])
    ex.start(lambda p: own_x.at[0], recv_x)
    recv_x[m] = own_x[0]
    ex.wait(lambda p: own_x.at[0], recv_x)
    own_m[...] = total_of(recv_x, n_mp) + unit_own
    ex = dp_ex(4)
    ex.start(lambda p: own_m, mixed_ref)
    mixed_ref[d] = own_m[...]
    ex.wait(lambda p: own_m, mixed_ref)
    mixed_factor = rms_blocks(mixed_ref[...])
    cond_own = (own_m[...] * mixed_factor * emb_ref[d][images + 2 : images + 3]).astype(BF16)
    for c in range(2):
        part = dot_nn(cond_own, wmod_ref[c])
        for p in range(n_dp):
            send_o[p, c] = part[p * IMG_DEV : (p + 1) * IMG_DEV, :]
    ex = dp_ex(5)
    ex.start(lambda p: send_o.at[p], recv_o)
    for kz in range(1, n_z):
        forward(kz)
    recv_o[d] = send_o[d]
    ex.wait(lambda p: send_o.at[p], recv_o)
    mods_ref[...] = total_of(recv_o, n_dp)

    def z_done(kz, carry):
        z_copy(kz, z).wait_send()
        return carry

    lax.fori_loop(0, n_z, finish, 0)
    lax.fori_loop(1, n_z, z_done, 0)


def vmem_specs(count):
    return [pl.BlockSpec(memory_space=pltpu.VMEM)] * count


def front(n_dp, n_mp, shard, feats_own, w_time, e_cols, gains_own, w_mapup, w_mapdown, w_mod):
    images, part = feats_own.shape
    units = w_mapup.shape[2]
    n_y = minor_size(n_dp)
    n_z = n_dp // n_y
    shape = lambda *dims: jax.ShapeDtypeStruct(dims, F32)
    return pl.pallas_call(
        functools.partial(front_kernel, n_dp, n_mp),
        out_shape=(
            jax.ShapeDtypeStruct((shard.shape[0], shard.shape[1] * n_dp, shard.shape[2]), BF16),
            shape(2, IMG_DEV, D),
            shape(n_dp, images + 8, part),
            shape(2, IMG_DEV, units),
            shape(images, units),
            shape(n_dp, images, part),
        ),
        in_specs=vmem_specs(8),
        out_specs=tuple(vmem_specs(6)),
        scratch_shapes=[
            pltpu.VMEM((n_dp, images, part), F32),
            pltpu.VMEM((n_dp, images, part), F32),
            pltpu.VMEM((images + 8, part), F32),
            pltpu.VMEM((n_dp, 2, IMG_DEV, units), F32),
            pltpu.VMEM((n_dp, 2, IMG_DEV, units), F32),
            pltpu.VMEM((IMG_DEV, units), F32),
            pltpu.VMEM((n_dp, IMG_DEV, units), F32),
            pltpu.VMEM((1, images, part), F32),
            pltpu.VMEM((n_mp, images, part), F32),
            pltpu.VMEM((images, part), F32),
            pltpu.VMEM((n_dp, 2, IMG_DEV, D), F32),
            pltpu.VMEM((n_dp, 2, IMG_DEV, D), F32),
            pltpu.SemaphoreType.DMA((6, n_dp)),
            pltpu.SemaphoreType.DMA((6, n_dp)),
            pltpu.SemaphoreType.DMA((1, n_mp)),
            pltpu.SemaphoreType.DMA((1, n_mp)),
            pltpu.SemaphoreType.DMA((n_z,)),
            pltpu.SemaphoreType.DMA((n_z,)),
            pltpu.SemaphoreType.DMA((n_z, n_y)),
            pltpu.SemaphoreType.DMA((n_z, n_y)),
        ],
        compiler_params=pltpu.CompilerParams(
            collective_id=0, has_side_effects=True, vmem_limit_bytes=VMEM_BYTES
        ),
        name="front",
    )(shard, feats_own, w_time, e_cols, gains_own, w_mapup, w_mapdown, w_mod)


def back_kernel(
    n_dp, n_mp,
    grads_ref, dmods_ref, feats_ref, onehot_ref, wmu_ref, wmd_ref, wmod_ref,
    emb_ref, hid_ref, gated_ref, mixed_ref,
    gshard_ref, gmod_ref, gmd_ref, gmu_ref, gtime_ref, gclass_ref, ggain_ref,
    recv_q, own_q, recv_d, full_d, own_c, recv_c, send_g, recv_g, own_h, recv_h, full_h,
    own_p, recv_p, own_s, recv_s,
    recv_y, send_z, recv_z,
    dp_ss, dp_rs, mp_ss, mp_rs, z_ss, z_rs, y_ss, y_rs,
):
    d, m = lax.axis_index("dp"), lax.axis_index("mp")
    n_y = minor_size(n_dp)
    n_z = n_dp // n_y
    z, y = lax.div(d, n_y), lax.rem(d, n_y)
    images = feats_ref.shape[0]
    rows = gshard_ref.shape[1]
    greet(
        [
            (n_dp, lambda k: (lax.rem(d + k, n_dp), m)),
            (n_mp, lambda k: (d, lax.rem(m + k, n_mp))),
        ]
    )

    def piece(dd):
        return grads_ref.at[:, pl.ds(pl.multiple_of(dd * rows, rows), rows), :]

    def y_copy(kz, ky):
        to_y = lax.rem(y + ky, n_y)
        return pltpu.make_async_remote_copy(
            src_ref=piece(lax.rem(z + kz, n_z) * n_y + to_y), dst_ref=recv_y.at[kz, ky - 1],
            send_sem=y_ss.at[kz, ky], recv_sem=y_rs.at[kz, ky],
            device_id=(z * n_y + to_y, m), device_id_type=MESH)

    def z_copy(kz):
        return pltpu.make_async_remote_copy(
            src_ref=send_z.at[kz - 1], dst_ref=recv_z.at[kz - 1], send_sem=z_ss.at[kz],
            recv_sem=z_rs.at[kz], device_id=(lax.rem(z + kz, n_z) * n_y + y, m),
            device_id_type=MESH)

    for kz in list(range(1, n_z)) + [0]:
        for ky in range(1, n_y):
            y_copy(kz, ky).start()

    def dp_ex(stage):
        return Exchange(n_dp, d, lambda p: (p, m), dp_ss.at[stage], dp_rs.at[stage])

    def mp_ex(stage):
        return Exchange(n_mp, m, lambda p: (d, p), mp_ss.at[stage], mp_rs.at[stage])

    def pair_sum(kz):
        for ky in range(1, n_y):
            y_copy(kz, ky).wait_recv()
        target = lax.rem(z + kz, n_z) * n_y + y
        value = grads_ref[:, pl.ds(pl.multiple_of(target * rows, rows), rows), :].astype(F32)
        for ky in range(1, n_y):
            value = value + recv_y[kz, ky - 1].astype(F32)
        return value

    def send_on(kz):
        send_z[kz - 1] = pair_sum(kz).astype(BF16)
        z_copy(kz).start()

    ex = mp_ex(0)
    ex.start(lambda p: dmods_ref, recv_q)
    recv_q[m] = dmods_ref[...]
    ex.wait(lambda p: dmods_ref, recv_q)
    own_q[...] = total_of(recv_q, n_mp)
    ex = dp_ex(0)
    ex.start(lambda p: own_q, recv_d)
    recv_d[d] = own_q[...]
    gains_own = emb_ref[d][images:]
    emb = emb_ref[:, 0:images, :]
    emb_factor = rms_blocks(emb)
    unit = emb * emb_factor[None] * emb_ref[:, images : images + 1, :]
    unit_factor = rms_blocks(unit)
    emb_own = emb_ref[d][0:images]
    unit_own = emb_own * emb_factor * gains_own[0:1]
    pre_own = (unit_own * unit_factor * gains_own[1:2]).astype(BF16)
    mixed = mixed_ref[...]
    mixed_factor = rms_blocks(mixed)
    mixed_own = mixed_ref[d]
    cond_own = (mixed_own * mixed_factor * gains_own[2:3]).astype(BF16)
    ex.wait(lambda p: own_q, recv_d)
    for p in range(n_dp):
        for c in range(2):
            full_d[c, p * IMG_DEV : (p + 1) * IMG_DEV, :] = recv_d[p, c]
    own_c[...] = two_part_left(dot_nt, full_d[0], wmod_ref[0]) + two_part_left(
        dot_nt, full_d[1], wmod_ref[1]
    )
    ex = dp_ex(1)
    ex.start(lambda p: own_c, recv_c)
    recv_c[d] = own_c[...]
    for c in range(2):
        gmod_ref[c] = two_part(dot_tn, cond_own, full_d[c])
    if n_z > 1:
        send_on(1)
    ex.wait(lambda p: own_c, recv_c)
    ggain_ref[2:3, :] = jnp.sum(own_c[...] * mixed_own * mixed_factor, axis=0, keepdims=True)
    d_mixed = rms_blocks_back(
        mixed, mixed_factor, recv_c[...] * emb_ref[:, images + 2 : images + 3, :]
    )
    recv_c[...] = d_mixed
    mix_own = recv_c[d]
    part = two_part_left(dot_nn, mix_own, wmd_ref[...])
    for p in range(n_dp):
        send_g[p] = part[p * IMG_DEV : (p + 1) * IMG_DEV, :]
    ex = dp_ex(2)
    ex.start(lambda p: send_g.at[p], recv_g)
    recv_g[d] = send_g[d]
    gmd_ref[...] = two_part_left(dot_tn, mix_own, gated_ref[...].astype(BF16))
    for kz in range(2, n_z):
        send_on(kz)
    ex.wait(lambda p: send_g.at[p], recv_g)
    d_gated = total_of(recv_g, n_dp)
    value, slope = gelu_parts(hid_ref[1])
    own_h[0] = d_gated * value
    own_h[1] = d_gated * hid_ref[0] * slope
    ex = dp_ex(3)
    ex.start(lambda p: own_h, recv_h)
    recv_h[d] = own_h[...]
    ex.wait(lambda p: own_h, recv_h)
    for p in range(n_dp):
        for c in range(2):
            full_h[c, p * IMG_DEV : (p + 1) * IMG_DEV, :] = recv_h[p, c]
    own_p[...] = two_part_left(dot_nt, full_h[0], wmu_ref[0]) + two_part_left(
        dot_nt, full_h[1], wmu_ref[1]
    )
    ex = mp_ex(1)
    ex.start(lambda p: own_p, recv_p)
    recv_p[m] = own_p[...]
    for c in range(2):
        gmu_ref[c] = two_part(dot_tn, pre_own, full_h[c])
    ex.wait(lambda p: own_p, recv_p)
    own_s[...] = total_of(recv_p, n_mp)
    ex = dp_ex(4)
    ex.start(lambda p: own_s, recv_s)
    recv_s[d] = own_s[...]
    gshard_ref[...] = pair_sum(0)
    ex.wait(lambda p: own_s, recv_s)
    ggain_ref[1:2, :] = jnp.sum(own_s[...] * unit_own * unit_factor, axis=0, keepdims=True)
    d_unit = recv_c[...] + rms_blocks_back(
        unit, unit_factor, recv_s[...] * emb_ref[:, images + 1 : images + 2, :]
    )
    recv_s[...] = d_unit
    ggain_ref[0:1, :] = jnp.sum(recv_s[d] * emb_own * emb_factor, axis=0, keepdims=True)
    d_emb = rms_blocks_back(emb, emb_factor, d_unit * emb_ref[:, images : images + 1, :])
    recv_s[...] = d_emb
    ggain_ref[3:8, :] = jnp.zeros_like(ggain_ref[3:8, :])
    for p in range(n_dp):
        gtime_ref[p] = two_part(dot_tn, feats_ref[...], recv_s[p])
    gclass_ref[...] = two_part_left(dot_tn, recv_s[d], onehot_ref[...])
    for kz in range(1, n_z):
        z_copy(kz).wait_recv()
        gshard_ref[...] = gshard_ref[...] + recv_z[kz - 1].astype(F32)
    for kz in range(1, n_z):
        z_copy(kz).wait_send()
    for kz in range(n_z):
        for ky in range(1, n_y):
            y_copy(kz, ky).wait_send()


def back(n_dp, n_mp, grads, dmods, feats_own, onehot, w_mapup, w_mapdown, w_mod, emb, hid, gated, mixed):
    images, part = feats_own.shape
    units = w_mapup.shape[2]
    n_y = minor_size(n_dp)
    n_z = n_dp // n_y
    rows = grads.shape[1] // n_dp
    slab = (grads.shape[0], rows, grads.shape[2])
    shape = lambda *dims: jax.ShapeDtypeStruct(dims, F32)
    return pl.pallas_call(
        functools.partial(back_kernel, n_dp, n_mp),
        out_shape=(
            shape(*slab),
            shape(2, part, D),
            shape(part, units),
            shape(2, part, units),
            shape(n_dp, part, part),
            shape(part, NCLASS),
            shape(8, part),
        ),
        in_specs=vmem_specs(11),
        out_specs=tuple(vmem_specs(7)),
        scratch_shapes=[
            pltpu.VMEM((n_mp, 2, IMG_DEV, D), F32),
            pltpu.VMEM((2, IMG_DEV, D), F32),
            pltpu.VMEM((n_dp, 2, IMG_DEV, D), F32),
            pltpu.VMEM((2, images, D), F32),
            pltpu.VMEM((images, part), F32),
            pltpu.VMEM((n_dp, images, part), F32),
            pltpu.VMEM((n_dp, IMG_DEV, units), F32),
            pltpu.VMEM((n_dp, IMG_DEV, units), F32),
            pltpu.VMEM((2, IMG_DEV, units), F32),
            pltpu.VMEM((n_dp, 2, IMG_DEV, units), F32),
            pltpu.VMEM((2, images, units), F32),
            pltpu.VMEM((images, part), F32),
            pltpu.VMEM((n_mp, images, part), F32),
            pltpu.VMEM((images, part), F32),
            pltpu.VMEM((n_dp, images, part), F32),
            pltpu.VMEM((n_z, max(n_y - 1, 1)) + slab, BF16),
            pltpu.VMEM((max(n_z - 1, 1),) + slab, BF16),
            pltpu.VMEM((max(n_z - 1, 1),) + slab, BF16),
            pltpu.SemaphoreType.DMA((5, n_dp)),
            pltpu.SemaphoreType.DMA((5, n_dp)),
            pltpu.SemaphoreType.DMA((2, n_mp)),
            pltpu.SemaphoreType.DMA((2, n_mp)),
            pltpu.SemaphoreType.DMA((n_z,)),
            pltpu.SemaphoreType.DMA((n_z,)),
            pltpu.SemaphoreType.DMA((n_z, n_y)),
            pltpu.SemaphoreType.DMA((n_z, n_y)),
        ],
        compiler_params=pltpu.CompilerParams(
            collective_id=1, has_side_effects=True, vmem_limit_bytes=VMEM_BYTES
        ),
        name="back",
    )(grads, dmods, feats_own, onehot, w_mapup, w_mapdown, w_mod, emb, hid, gated, mixed)


def norm_kernel(n_dp, n_mp, heads, v_ref, o_ref, own, recv_dp, recv_mp, dp_ss, dp_rs, mp_ss, mp_rs):
    d, m = lax.axis_index("dp"), lax.axis_index("mp")
    greet(
        [
            (n_dp, lambda k: (lax.rem(d + k, n_dp), m)),
            (n_mp, lambda k: (d, lax.rem(m + k, n_mp))),
        ]
    )
    ex = Exchange(n_dp, d, lambda p: (p, m), dp_ss, dp_rs)
    ex.start(lambda p: v_ref, recv_dp)
    recv_dp[d] = v_ref[...]
    ex.wait(lambda p: v_ref, recv_dp)
    summed = total_of(recv_dp, n_dp)
    head = summed[1:2]
    squares = summed[0:1] + head * head
    own[...] = jnp.zeros_like(own)
    own[0:1, :] = squares
    ex = Exchange(n_mp, m, lambda p: (d, p), mp_ss, mp_rs)
    ex.start(lambda p: own, recv_mp)
    recv_mp[m] = own[...]
    ex.wait(lambda p: own, recv_mp)
    norm = jnp.sqrt(jnp.sum(total_of(recv_mp, n_mp)[0:1], axis=-1, keepdims=True))
    o_ref[...] = jnp.zeros_like(o_ref)
    o_ref[0:1, :] = jnp.broadcast_to(norm, (1, o_ref.shape[1]))
    o_ref[1:2, :] = head


def norm_all(n_dp, n_mp, heads, values):
    return pl.pallas_call(
        functools.partial(norm_kernel, n_dp, n_mp, heads),
        out_shape=jax.ShapeDtypeStruct(values.shape, F32),
        in_specs=vmem_specs(1),
        out_specs=vmem_specs(1)[0],
        scratch_shapes=[
            pltpu.VMEM(values.shape, F32),
            pltpu.VMEM((n_dp,) + values.shape, F32),
            pltpu.VMEM((n_mp,) + values.shape, F32),
            pltpu.SemaphoreType.DMA((n_dp,)),
            pltpu.SemaphoreType.DMA((n_dp,)),
            pltpu.SemaphoreType.DMA((n_mp,)),
            pltpu.SemaphoreType.DMA((n_mp,)),
        ],
        compiler_params=pltpu.CompilerParams(collective_id=2, has_side_effects=True),
        name="norm_all",
    )(values)


class Ranks:
    def __init__(self, n_mp):
        self.d, self.m = lax.axis_index("dp"), lax.axis_index("mp")
        self.n_x = n_mp // 2
        self.x, self.c = lax.div(self.m, 2), lax.rem(self.m, 2)
        self.sibling = (self.d, self.x * 2 + 1 - self.c)

    def rank(self, kx, same):
        core = jnp.where(same == 1, self.c, 1 - self.c)
        return lax.rem(self.x + kx, self.n_x) * 2 + core

    def chip(self, kx):
        return (self.d, lax.rem(self.x + kx, self.n_x) * 2 + self.c)

    def greet(self):
        greet([(2, lambda k: self.sibling), (self.n_x, self.chip)])


class Reduce:
    def __init__(self, ranks, core_send, core_recv, x_send, x_recv, sems):
        self.r = ranks
        self.core_send, self.core_recv, self.x_send, self.x_recv = core_send, core_recv, x_send, x_recv
        self.sems = sems

    def core_copy(self, kx):
        return pltpu.make_async_remote_copy(
            src_ref=self.core_send.at[kx], dst_ref=self.core_recv.at[kx], send_sem=self.sems.at[0, kx],
            recv_sem=self.sems.at[1, kx], device_id=self.r.sibling, device_id_type=MESH)

    def x_copy(self, kx):
        return pltpu.make_async_remote_copy(
            src_ref=self.x_send.at[kx], dst_ref=self.x_recv.at[kx], send_sem=self.sems.at[2, kx],
            recv_sem=self.sems.at[3, kx], device_id=self.r.chip(kx), device_id_type=MESH)

    def other(self, kx, part):
        self.core_send[kx] = part.astype(BF16)
        self.core_copy(kx).start()

    def same(self, kx, part):
        self.core_copy(kx).wait_recv()
        self.x_send[kx] = (part + self.core_recv[kx].astype(F32)).astype(BF16)
        self.x_copy(kx).start()

    def finish(self, part):
        self.core_copy(0).wait_recv()
        total = part + self.core_recv[0].astype(F32)
        for kx in range(1, self.r.n_x):
            self.x_copy(kx).wait_recv()
            total = total + self.x_recv[kx].astype(F32)
        return total

    def drain(self):
        self.core_copy(0).wait_send()
        for kx in range(1, self.r.n_x):
            self.core_copy(kx).wait_send()
            self.x_copy(kx).wait_send()


def reduce_scratch(n_mp, rows):
    slots = pltpu.VMEM((n_mp // 2, rows, D), BF16)
    return [slots, slots, slots, slots, pltpu.SemaphoreType.DMA((4, n_mp // 2))]


class Gather:
    def __init__(self, ranks, rows, buffer, sems):
        self.r, self.rows, self.buffer, self.sems = ranks, rows, buffer, sems

    def at(self, rank):
        return self.buffer.at[pl.ds(pl.multiple_of(rank * self.rows, self.rows), self.rows), :]

    def x_copy(self, kx, slot):
        return pltpu.make_async_remote_copy(
            src_ref=self.at(self.r.m), dst_ref=self.at(slot), send_sem=self.sems.at[0, kx],
            recv_sem=self.sems.at[1, kx], device_id=self.r.chip(kx), device_id_type=MESH)

    def core_copy(self, kx, out_slot, in_slot):
        return pltpu.make_async_remote_copy(
            src_ref=self.at(out_slot), dst_ref=self.at(in_slot), send_sem=self.sems.at[2, kx],
            recv_sem=self.sems.at[3, kx], device_id=self.r.sibling, device_id_type=MESH)

    def start(self):
        for kx in range(1, self.r.n_x):
            self.x_copy(kx, self.r.m).start()
        self.core_copy(0, self.r.m, self.r.m).start()

    def from_chip(self, kx):
        return lax.rem(self.r.x + self.r.n_x - kx, self.r.n_x) * 2 + self.r.c

    def from_core(self, kx):
        return lax.rem(self.r.x + self.r.n_x - kx, self.r.n_x) * 2 + 1 - self.r.c

    def forward(self, kx):
        slot = self.from_chip(kx)
        self.x_copy(kx, slot).wait_recv()
        self.core_copy(kx, slot, slot).start()

    def arrived(self, kx):
        self.core_copy(kx, self.r.m, self.from_core(kx)).wait_recv()

    def drain(self):
        for kx in range(1, self.r.n_x):
            self.x_copy(kx, self.r.m).wait_send()
        for kx in range(self.r.n_x):
            self.core_copy(kx, self.r.m, self.r.m).wait_send()


def gather_sems(n_mp):
    return pltpu.SemaphoreType.DMA((4, n_mp // 2))


def head_sums(values, ones):
    return two_part_left(dot_nn, values, ones)


def row_sums_factor(values):
    return lax.rsqrt(jnp.mean(values * values, axis=-1, keepdims=True) + EPSILON)


def image_scale(info_ref, mods_ref, which, image):
    is_long = info_ref[0]
    row = mods_ref[which, pl.ds(image, 1), :]
    return 1.0 + (is_long * mods_ref[which, 0:1, :] + (1.0 - is_long) * row)


def column_bias(info_ref, image, columns_shape, short):
    keys = lax.broadcasted_iota(jnp.int32, columns_shape, 0)
    own = (keys >= image * short) & (keys < (image + 1) * short)
    return jnp.where(own, 0.0, info_ref[1])


SHORT = 256


def attn_forward_kernel(
    n_mp, heads, info_ref, x_ref, mods_ref, scale_ref, ones_ref, wg_ref,
    q_ref, k_ref, v_ref, normed_ref, att_ref, stats_ref, mid_ref, nm_ref,
    qu_s, ku_s, vt_s, part_s, core_send, core_recv, x_send, x_recv, sems,
):
    r = Ranks(n_mp)
    tokens = x_ref.shape[0]
    rows = tokens // n_mp
    width = q_ref.shape[1]
    size = width // heads
    r.greet()
    red = Reduce(r, core_send, core_recv, x_send, x_recv, sems)
    at = lambda b: pl.ds(pl.multiple_of(b * rows, rows), rows)
    image_of = lambda b: lax.div(b * rows, SHORT)

    def project(b, carry):
        xb = x_ref[at(b), :].astype(F32)
        normed = (xb * row_sums_factor(xb) * image_scale(info_ref, mods_ref, 0, image_of(b))).astype(BF16)
        normed_ref[at(b), :] = normed
        q = dot_nn(normed, wg_ref[0])
        q_ref[at(b), :] = q
        qu_s[at(b), :] = (q * lax.rsqrt(head_sums(q * q, ones_ref[...]) + EPSILON) * scale_ref[...]).astype(BF16)
        k = dot_nn(normed, wg_ref[1])
        k_ref[at(b), :] = k
        ku_s[at(b), :] = (k * lax.rsqrt(head_sums(k * k, ones_ref[...]) + EPSILON)).astype(BF16)
        v = dot_nn(normed, wg_ref[2])
        v_ref[at(b), :] = v.astype(BF16)
        vt_s[:, at(b)] = v.T.astype(BF16)
        return carry

    lax.fori_loop(0, n_mp, project, 0)
    lanes = lax.broadcasted_iota(jnp.int32, (1, width), 1)

    def block(j, carry):
        kx, same = lax.rem(1 + lax.div(j, 2), r.n_x), lax.rem(j, 2)
        b = r.rank(kx, same)
        bias = column_bias(info_ref, image_of(b), (tokens, 1), SHORT)
        qu = qu_s[at(b), :]
        outs = []
        for h in range(heads):
            mask = ((lanes >= h * size) & (lanes < (h + 1) * size)).astype(F32).astype(BF16)
            scores = dot_nt(ku_s[...], qu * mask) + bias
            top = jnp.max(scores, axis=0, keepdims=True)
            expon = jnp.exp(scores - top)
            total = jnp.sum(expon, axis=0, keepdims=True)
            stats_ref[h : h + 1, at(b)] = top + jnp.log(total)
            outs.append(dot_nn(vt_s[h * size : (h + 1) * size, :], expon.astype(BF16)) / total)
        att = jnp.concatenate(outs, axis=0).T.astype(BF16)
        att_ref[at(b), :] = att
        part_s[...] = dot_nt(att, wg_ref[3])

        @pl.when(same == 0)
        def _():
            red.other(kx, part_s[...])

        @pl.when((same == 1) & (kx > 0))
        def _():
            red.same(kx, part_s[...])

        return carry

    lax.fori_loop(0, n_mp, block, 0)
    if heads < 8:
        stats_ref[heads:8, :] = jnp.zeros((8 - heads, tokens), F32)
    middle = x_ref[at(r.m), :].astype(F32) + red.finish(part_s[...])
    mid_ref[...] = middle
    nm_ref[...] = (middle * row_sums_factor(middle) * image_scale(info_ref, mods_ref, 1, image_of(r.m))).astype(BF16)
    red.drain()


SMEM_SPEC = pl.BlockSpec(memory_space=pltpu.SMEM)


def attn_forward(n_mp, heads, info, x, mods, scale, ones, wg):
    tokens = x.shape[0]
    width = wg.shape[2]
    rows = tokens // n_mp
    shape = jax.ShapeDtypeStruct
    return pl.pallas_call(
        functools.partial(attn_forward_kernel, n_mp, heads),
        out_shape=(
            shape((tokens, width), F32),
            shape((tokens, width), F32),
            shape((tokens, width), BF16),
            shape((tokens, D), BF16),
            shape((tokens, width), BF16),
            shape((8, tokens), F32),
            shape((rows, D), F32),
            shape((rows, D), BF16),
        ),
        in_specs=[SMEM_SPEC] + vmem_specs(5),
        out_specs=tuple(vmem_specs(8)),
        scratch_shapes=[
            pltpu.VMEM((tokens, width), BF16),
            pltpu.VMEM((tokens, width), BF16),
            pltpu.VMEM((width, tokens), BF16),
            pltpu.VMEM((rows, D), F32),
        ]
        + reduce_scratch(n_mp, rows),
        compiler_params=pltpu.CompilerParams(
            collective_id=3, has_side_effects=True, vmem_limit_bytes=VMEM_BYTES
        ),
        name="attn_forward",
    )(info, x, mods, scale, ones, wg)


def ffn_kernel(
    n_dp, n_mp, info_ref, nm_ref, cot_ref, mods_ref, mid_ref, wf_ref,
    gw_ref, dmid_ref, out_ref, fmod_ref,
    w_s, nm_s, gated_s, gate_s, slope_s, dh_s, dz_s, part_s, ff_s, w_sem, gather_sem,
    f_core_send, f_core_recv, f_x_send, f_x_recv, f_sems,
    b_core_send, b_core_recv, b_x_send, b_x_recv, b_sems,
):
    r = Ranks(n_mp)
    rows = nm_ref.shape[0]
    tokens = rows * n_mp
    shard = D // n_dp
    at = lambda b: pl.ds(pl.multiple_of(b * rows, rows), rows)
    image_of = lambda b: lax.div(b * rows, SHORT)

    def w_copy(dd, c):
        return pltpu.make_async_copy(
            wf_ref.at[dd, pl.ds(c * shard, shard), :],
            w_s.at[c, pl.ds(pl.multiple_of(dd * shard, shard), shard), :],
            w_sem.at[dd, c],
        )

    def w_start(dd, carry):
        for c in range(3):
            w_copy(dd, c).start()
        return carry

    def w_wait(dd, carry):
        for c in range(3):
            w_copy(dd, c).wait()
        return carry

    lax.fori_loop(0, n_dp, w_start, 0)
    r.greet()
    nm_s[at(r.m), :] = nm_ref[...]
    gather = Gather(r, rows, nm_s, gather_sem)
    gather.start()
    fwd = Reduce(r, f_core_send, f_core_recv, f_x_send, f_x_recv, f_sems)
    bwd = Reduce(r, b_core_send, b_core_recv, b_x_send, b_x_recv, b_sems)
    lax.fori_loop(0, n_dp, w_wait, 0)

    def forward(j, carry):
        kx = lax.div(j, 2)
        same = jnp.where(kx == 0, 1 - lax.rem(j, 2), lax.rem(j, 2))
        b = r.rank(kx, same)
        back_kx = lax.rem(r.n_x - kx, r.n_x)

        @pl.when((same == 0) & (kx > 0))
        def _():
            gather.forward(back_kx)

        @pl.when(same == 0)
        def _():
            gather.arrived(back_kx)

        nm = nm_s[at(b), :]
        hidden = dot_nn(nm, w_s[0])
        gate = dot_nn(nm, w_s[1])
        value, slope = gelu_parts(gate)
        gated = (hidden * value).astype(BF16)
        gated_s[at(b), :] = gated
        gate_s[at(b), :] = value
        slope_s[at(b), :] = hidden * slope
        part_s[...] = dot_nt(gated, w_s[2])

        @pl.when((same == 1) & (kx == 0))
        def _():
            ff_s[...] = part_s[...]

        @pl.when(same == 0)
        def _():
            fwd.other(kx, part_s[...])

        @pl.when((same == 1) & (kx > 0))
        def _():
            fwd.same(kx, part_s[...])

        return carry

    lax.fori_loop(0, n_mp, forward, 0)

    def live_rows(b):
        position = lax.broadcasted_iota(jnp.int32, (rows, 1), 0) + b * rows
        return (position.astype(F32) < info_ref[2]).astype(F32)

    def backward(j, carry):
        kx, same = lax.rem(1 + lax.div(j, 2), r.n_x), lax.rem(j, 2)
        b = r.rank(kx, same)
        dz = (cot_ref[at(b), :].astype(F32) * live_rows(b)).astype(BF16)
        dz_s[at(b), :] = dz
        d_gated = dot_nn(dz, w_s[2])
        d_value = (d_gated * gate_s[at(b), :]).astype(BF16)
        d_gate = (d_gated * slope_s[at(b), :]).astype(BF16)
        dh_s[0, at(b), :] = d_value
        dh_s[1, at(b), :] = d_gate
        part_s[...] = dot_nt(d_value, w_s[0]) + dot_nt(d_gate, w_s[1])

        @pl.when(same == 0)
        def _():
            bwd.other(kx, part_s[...])

        @pl.when((same == 1) & (kx > 0))
        def _():
            bwd.same(kx, part_s[...])

        return carry

    lax.fori_loop(0, n_mp, backward, 0)

    step = 512

    def weights(i, carry):
        cols = pl.ds(pl.multiple_of(i * step, step), step)
        for c in range(3):
            left = nm_s[:, cols] if c < 2 else dz_s[:, cols]
            right = dh_s[c] if c < 2 else gated_s[...]
            value = dot_tn(left, right).astype(BF16)
            for s in range(step // shard):
                gw_ref[i * (step // shard) + s, c * shard : (c + 1) * shard, :] = value[
                    s * shard : (s + 1) * shard
                ]
        return carry

    lax.fori_loop(0, D // step, weights, 0)

    d_nm = bwd.finish(part_s[...])
    middle = mid_ref[...]
    live = live_rows(r.m)
    scale = image_scale(info_ref, mods_ref, 1, image_of(r.m))
    factor = row_sums_factor(middle)
    inner = jnp.mean(middle * scale * d_nm, axis=-1, keepdims=True)
    dmid_ref[...] = cot_ref[at(r.m), :].astype(F32) * live + (
        factor * scale * d_nm - middle * (factor * factor * factor * inner)
    )
    fmod_ref[...] = jnp.sum(d_nm * middle * factor, axis=0, keepdims=True)
    out_ref[...] = ((middle + fwd.finish(ff_s[...])) * live).astype(BF16)
    gather.drain()
    fwd.drain()
    bwd.drain()


def ffn(n_dp, n_mp, info, nm, cot, mods, mid, wf):
    rows = nm.shape[0]
    tokens = rows * n_mp
    units = wf.shape[2]
    shape = jax.ShapeDtypeStruct
    return pl.pallas_call(
        functools.partial(ffn_kernel, n_dp, n_mp),
        out_shape=(
            shape(wf.shape, BF16),
            shape((rows, D), F32),
            shape((rows, D), BF16),
            shape((1, D), F32),
        ),
        in_specs=[SMEM_SPEC] + vmem_specs(4) + [pl.BlockSpec(memory_space=pl.ANY)],
        out_specs=tuple(vmem_specs(4)),
        scratch_shapes=[
            pltpu.VMEM((3, D, units), BF16),
            pltpu.VMEM((tokens, D), BF16),
            pltpu.VMEM((tokens, units), BF16),
            pltpu.VMEM((tokens, units), F32),
            pltpu.VMEM((tokens, units), F32),
            pltpu.VMEM((2, tokens, units), BF16),
            pltpu.VMEM((tokens, D), BF16),
            pltpu.VMEM((rows, D), F32),
            pltpu.VMEM((rows, D), F32),
            pltpu.SemaphoreType.DMA((n_dp, 3)),
            gather_sems(n_mp),
        ]
        + reduce_scratch(n_mp, rows)
        + reduce_scratch(n_mp, rows),
        compiler_params=pltpu.CompilerParams(
            collective_id=4, has_side_effects=True, vmem_limit_bytes=VMEM_BYTES
        ),
        name="ffn",
    )(info, nm, cot, mods, mid, wf)


def attn_backward_kernel(
    n_mp, heads, info_ref, dmid_ref, x_ref, mods_ref, scale_ref, ones_ref, wg_ref,
    q_ref, k_ref, v_ref, normed_ref, att_ref, stats_ref,
    gw_ref, gin_ref, amod_ref, gscale_ref,
    qu_s, ku_s, kt_s, dy_s, dq_s, dk_s, dv_s, low_s, part_s, gather_sem,
    core_send, core_recv, x_send, x_recv, sems,
):
    r = Ranks(n_mp)
    rows = dmid_ref.shape[0]
    tokens = rows * n_mp
    width = q_ref.shape[1]
    size = width // heads
    at = lambda b: pl.ds(pl.multiple_of(b * rows, rows), rows)
    image_of = lambda b: lax.div(b * rows, SHORT)
    dy_s[at(r.m), :] = dmid_ref[...].astype(BF16)
    r.greet()
    gather = Gather(r, rows, dy_s, gather_sem)
    gather.start()
    red = Reduce(r, core_send, core_recv, x_send, x_recv, sems)

    def units(b, carry):
        q, k = q_ref[at(b), :], k_ref[at(b), :]
        qu_s[at(b), :] = (q * lax.rsqrt(head_sums(q * q, ones_ref[...]) + EPSILON) * scale_ref[...]).astype(BF16)
        k_unit = k * lax.rsqrt(head_sums(k * k, ones_ref[...]) + EPSILON)
        ku_s[at(b), :] = k_unit.astype(BF16)
        kt_s[:, at(b)] = k_unit.T.astype(BF16)
        return carry

    lax.fori_loop(0, n_mp, units, 0)
    dk_s[...] = jnp.zeros_like(dk_s)
    dv_s[...] = jnp.zeros_like(dv_s)
    lanes = lax.broadcasted_iota(jnp.int32, (1, width), 1)

    def block(j, carry):
        kx = lax.div(j, 2)
        same = 1 - lax.rem(j, 2)
        b = r.rank(kx, same)
        back_kx = lax.rem(r.n_x - kx, r.n_x)

        @pl.when((same == 1) & (kx > 0))
        def _():
            gather.forward(back_kx)

        @pl.when(same == 0)
        def _():
            gather.arrived(back_kx)

        d_att = dot_nn(dy_s[at(b), :], wg_ref[3]).astype(BF16)
        bias = column_bias(info_ref, image_of(b), (tokens, 1), SHORT)
        qu = qu_s[at(b), :]
        outs = []
        for h in range(heads):
            mask = ((lanes >= h * size) & (lanes < (h + 1) * size)).astype(F32).astype(BF16)
            qh = qu * mask
            dh = d_att * mask
            probs = jnp.exp(dot_nt(ku_s[...], qh) + bias - stats_ref[h : h + 1, at(b)])
            d_probs = dot_nt(v_ref[...], dh)
            inner = jnp.sum(probs * d_probs, axis=0, keepdims=True)
            d_scores = (probs * (d_probs - inner)).astype(BF16)
            dv_s[...] = dv_s[...] + dot_nn(probs.astype(BF16), dh)
            dk_s[...] = dk_s[...] + dot_nn(d_scores, qh)
            outs.append(dot_nn(kt_s[h * size : (h + 1) * size, :], d_scores))
        dq_s[at(b), :] = jnp.concatenate(outs, axis=0).T
        return carry

    lax.fori_loop(0, n_mp, block, 0)

    def inputs(j, scale_grad):
        kx, same = lax.rem(1 + lax.div(j, 2), r.n_x), lax.rem(j, 2)
        b = r.rank(kx, same)
        q, k = q_ref[at(b), :], k_ref[at(b), :]
        q_factor = lax.rsqrt(head_sums(q * q, ones_ref[...]) + EPSILON)
        k_factor = lax.rsqrt(head_sums(k * k, ones_ref[...]) + EPSILON)
        dqu, dku = dq_s[at(b), :], dk_s[at(b), :]
        q_unit, k_unit = q * q_factor, k * k_factor
        q_along = dqu * q_unit
        d_q = (scale_ref[...] * q_factor * (dqu - q_unit * head_sums(q_along, ones_ref[...]))).astype(BF16)
        d_k = (k_factor * (dku - k_unit * head_sums(dku * k_unit, ones_ref[...]))).astype(BF16)
        d_v = dv_s[at(b), :].astype(BF16)
        low_s[at(b), 0:width] = d_q
        low_s[at(b), width : 2 * width] = d_k
        low_s[at(b), 2 * width : 3 * width] = d_v
        part_s[...] = dot_nt(d_q, wg_ref[0]) + dot_nt(d_k, wg_ref[1]) + dot_nt(d_v, wg_ref[2])

        @pl.when(same == 0)
        def _():
            red.other(kx, part_s[...])

        @pl.when((same == 1) & (kx > 0))
        def _():
            red.same(kx, part_s[...])

        return scale_grad + jnp.sum(q_along, axis=0, keepdims=True)

    gscale_ref[...] = lax.fori_loop(0, n_mp, inputs, jnp.zeros((1, width), F32))

    step = 512

    def weights(i, carry):
        cols = pl.ds(pl.multiple_of(i * step, step), step)
        value = dot_tn(normed_ref[:, cols], low_s[...]).astype(BF16)
        for c in range(3):
            gw_ref[c, cols, :] = value[:, c * width : (c + 1) * width]
        gw_ref[3, cols, :] = dot_tn(dy_s[:, cols], att_ref[...]).astype(BF16)
        return carry

    lax.fori_loop(0, D // step, weights, 0)

    d_normed = red.finish(part_s[...])
    x = x_ref[at(r.m), :].astype(F32)
    scale = image_scale(info_ref, mods_ref, 0, image_of(r.m))
    factor = row_sums_factor(x)
    inner = jnp.mean(x * scale * d_normed, axis=-1, keepdims=True)
    gin_ref[...] = dmid_ref[...] + (factor * scale * d_normed - x * (factor * factor * factor * inner))
    amod_ref[...] = jnp.sum(d_normed * x * factor, axis=0, keepdims=True)
    gather.drain()
    red.drain()


def attn_backward(n_mp, heads, info, dmid, x, mods, scale, ones, wg, q, k, v, normed, att, stats):
    rows = dmid.shape[0]
    tokens = rows * n_mp
    width = q.shape[1]
    shape = jax.ShapeDtypeStruct
    return pl.pallas_call(
        functools.partial(attn_backward_kernel, n_mp, heads),
        out_shape=(
            shape(wg.shape, BF16),
            shape((rows, D), F32),
            shape((1, D), F32),
            shape((1, width), F32),
        ),
        in_specs=[SMEM_SPEC] + vmem_specs(12),
        out_specs=tuple(vmem_specs(4)),
        scratch_shapes=[
            pltpu.VMEM((tokens, width), BF16),
            pltpu.VMEM((tokens, width), BF16),
            pltpu.VMEM((width, tokens), BF16),
            pltpu.VMEM((tokens, D), BF16),
            pltpu.VMEM((tokens, width), F32),
            pltpu.VMEM((tokens, width), F32),
            pltpu.VMEM((tokens, width), F32),
            pltpu.VMEM((tokens, 3 * width), BF16),
            pltpu.VMEM((rows, D), F32),
            gather_sems(n_mp),
        ]
        + reduce_scratch(n_mp, rows),
        compiler_params=pltpu.CompilerParams(
            collective_id=5, has_side_effects=True, vmem_limit_bytes=VMEM_BYTES
        ),
        name="attn_backward",
    )(info, dmid, x, mods, scale, ones, wg, q, k, v, normed, att, stats)


def spread_kernel(n_mp, out_ref, gin_ref, out_all, gin_all, gin_s, out_sem, gin_sem):
    r = Ranks(n_mp)
    rows = out_ref.shape[0]
    at = lambda b: pl.ds(pl.multiple_of(b * rows, rows), rows)
    r.greet()
    out_all[at(r.m), :] = out_ref[...]
    gin_s[at(r.m), :] = gin_ref[...].astype(BF16)
    one = Gather(r, rows, out_all, out_sem)
    two = Gather(r, rows, gin_s, gin_sem)
    one.start()
    two.start()
    gin_all[at(r.m), :] = gin_ref[...]
    for kx in range(1, r.n_x):
        one.forward(kx)
        two.forward(kx)
        gin_all[at(two.from_chip(kx)), :] = gin_s[at(two.from_chip(kx)), :].astype(F32)
    for kx in range(r.n_x):
        one.arrived(kx)
        two.arrived(kx)
        gin_all[at(two.from_core(kx)), :] = gin_s[at(two.from_core(kx)), :].astype(F32)
    one.drain()
    two.drain()


def spread(n_mp, out, gin):
    rows = out.shape[0]
    tokens = rows * n_mp
    return pl.pallas_call(
        functools.partial(spread_kernel, n_mp),
        out_shape=(
            jax.ShapeDtypeStruct((tokens, D), BF16),
            jax.ShapeDtypeStruct((tokens, D), F32),
        ),
        in_specs=vmem_specs(2),
        out_specs=tuple(vmem_specs(2)),
        scratch_shapes=[pltpu.VMEM((tokens, D), BF16), gather_sems(n_mp), gather_sems(n_mp)],
        compiler_params=pltpu.CompilerParams(
            collective_id=6, has_side_effects=True, vmem_limit_bytes=VMEM_BYTES
        ),
        name="spread",
    )(out, gin)


def middle_part(block_input, out_cotangent, mods, my_lengths, wg, wf, head_scale):
    n_dp, n_mp = lax.axis_size("dp"), lax.axis_size("mp")
    m = lax.axis_index("mp")
    tokens = block_input.shape[0]
    rows = tokens // n_mp
    heads = head_scale.shape[0]
    width = wg.shape[2]
    size = width // heads
    is_long = (my_lengths[0] > SHORT).astype(F32)
    live = jnp.sum(my_lengths).astype(F32)
    info = jnp.stack([is_long, (1.0 - is_long) * MASKED, live, live])
    scale = jnp.repeat(head_scale, size)[None, :]
    group = jnp.arange(width, dtype=jnp.int32) // size
    ones = (group[:, None] == group[None, :]).astype(BF16)
    q, k, v, normed, att, stats, mid, nm = attn_forward(
        n_mp, heads, info, block_input, mods, scale, ones, wg
    )
    gw_ffn, dmid, out_own, fmod = ffn(n_dp, n_mp, info, nm, out_cotangent, mods, mid, wf)
    gw_attn, gin_own, amod, gscale = attn_backward(
        n_mp, heads, info, dmid, block_input, mods, scale, ones, wg, q, k, v, normed, att, stats
    )
    layer_out, input_grad = spread(n_mp, out_own, gin_own)
    image = jnp.where(is_long > 0, 0, m * rows // SHORT)
    chosen = (jnp.arange(IMG_DEV, dtype=jnp.int32) == image).astype(F32)
    grad_mods = chosen[None, :, None] * jnp.stack([amod, fmod])
    grad_headscale = jnp.sum(gscale.reshape(heads, size), axis=1)
    return layer_out, input_grad, grad_mods, gw_attn, gw_ffn, grad_headscale


def per_device(
    block_input,
    out_cotangent,
    sigmas,
    class_labels,
    image_lengths,
    fourier_freqs,
    inproj_state,
    outproj_state,
    upproj_state,
    downproj_state,
    timeproj_state,
    classemb_state,
    mapup_state,
    mapdown_state,
    modproj_state,
    gains_state,
    headscale_state,
):
    n_dp, n_mp = lax.axis_size("dp"), lax.axis_size("mp")
    d = lax.axis_index("dp")
    my_lengths = lax.dynamic_slice_in_dim(image_lengths, d * IMG_DEV, IMG_DEV)
    rows, _, width = inproj_state.shape[1:]
    units = upproj_state.shape[3]
    part = timeproj_state.shape[1]
    ffn_shard = jnp.concatenate(
        [
            jnp.transpose(upproj_state[0].astype(BF16), (1, 0, 2)).reshape(2 * rows, units),
            downproj_state[0].astype(BF16).T,
        ],
        axis=0,
    )
    wf = lax.all_gather(ffn_shard, "dp", axis=0)
    attn_shard = jnp.concatenate(
        [
            jnp.transpose(inproj_state[0].astype(BF16), (1, 0, 2)),
            outproj_state[0].astype(BF16).T[None],
        ],
        axis=0,
    )
    feats_low = fourier(sigmas, fourier_freqs).astype(BF16)
    feats_own = lax.dynamic_slice_in_dim(feats_low, d * part, part, axis=1)
    onehot = (class_labels[:, None] == jnp.arange(NCLASS, dtype=jnp.int32)[None, :]).astype(BF16)
    e_cols = dot_nt(onehot, classemb_state[0].astype(BF16).T)
    gains_own = jnp.pad(gains_state[0].astype(BF16).astype(F32), ((0, 5), (0, 0)))
    w_time = jnp.transpose(timeproj_state[0].astype(BF16).reshape(part, n_dp, part), (1, 0, 2))
    w_mapup = jnp.transpose(mapup_state[0].astype(BF16), (1, 0, 2))
    w_mapdown = mapdown_state[0].astype(BF16).T
    w_mod = jnp.transpose(modproj_state[0].astype(BF16), (1, 0, 2))
    wg, mods, emb, hid, gated, mixed = front(
        n_dp, n_mp, attn_shard, feats_own, w_time, e_cols, gains_own, w_mapup, w_mapdown, w_mod
    )
    layer_out, input_grad, grad_mods, grad_attn_w, grad_ffn_w, grad_headscale = middle_part(
        block_input, out_cotangent, mods, my_lengths, wg, wf, headscale_state[0]
    )
    g_ffn = lax.psum_scatter(grad_ffn_w, "dp", scatter_dimension=0).astype(F32)
    g_attn, g_mod, g_md, g_mu, g_time, g_class, g_gain = back(
        n_dp, n_mp, grad_attn_w, grad_mods, feats_own, onehot, w_mapup, w_mapdown, w_mod, emb, hid, gated, mixed
    )
    g_gain = g_gain[:3]
    g_ffn = g_ffn.reshape(3, rows, units)
    split = jnp.sum(g_attn * g_attn) + jnp.sum(g_ffn * g_ffn) + jnp.sum(g_mu * g_mu) + jnp.sum(g_md * g_md)
    shared = (
        jnp.sum(g_mod * g_mod) + jnp.sum(g_time * g_time) + jnp.sum(g_class * g_class) + jnp.sum(g_gain * g_gain)
    )
    heads_here = headscale_state.shape[1]
    packed = jnp.zeros((8, 128), F32).at[0, 0].set(split + shared / n_mp).at[1, :heads_here].set(grad_headscale)
    normed = norm_all(n_dp, n_mp, heads_here, packed)
    grad_norm = normed[0, 0]
    factor = CLIP_NORM / jnp.maximum(grad_norm, CLIP_NORM)
    gradients = (
        jnp.transpose(g_attn[:3], (1, 0, 2)),
        g_attn[3].T,
        jnp.transpose(g_ffn[:2], (1, 0, 2)),
        g_ffn[2].T,
        jnp.transpose(g_time, (1, 0, 2)).reshape(part, DM),
        g_class.T,
        jnp.transpose(g_mu, (1, 0, 2)),
        g_md.T,
        jnp.transpose(g_mod, (1, 0, 2)),
        g_gain,
        normed[1, :heads_here],
    )
    states = (
        inproj_state,
        outproj_state,
        upproj_state,
        downproj_state,
        timeproj_state,
        classemb_state,
        mapup_state,
        mapdown_state,
        modproj_state,
        gains_state,
        headscale_state,
    )
    rates = learn_rates()
    decays = decay_rates()
    results = [layer_out, input_grad, grad_norm]
    for index in range(11):
        results += adamw_step(states[index], factor * gradients[index], rates[index], decays[index])
    return tuple(results)


def solution(mesh):
    return jax.shard_map(
        per_device,
        mesh=mesh,
        in_specs=(
            P("dp", None),
            P("dp", None),
            P(),
            P(),
            P(),
            P(),
            P(None, "dp", None, "mp"),
            P(None, "mp", "dp"),
            P(None, "dp", None, "mp"),
            P(None, "mp", "dp"),
            P(None, "dp", None),
            P(None, None, "dp"),
            P(None, "dp", None, "mp"),
            P(None, "mp", "dp"),
            P(None, "dp", None, None),
            P(None, None, "dp"),
            P(None, "mp"),
        ),
        out_specs=(
            P("dp", None),
            P("dp", None),
            P(),
            P(None, "dp", None, "mp"),
            P("dp", None, "mp"),
            P("dp", None, "mp"),
            P(None, "mp", "dp"),
            P("mp", "dp"),
            P("mp", "dp"),
            P(None, "dp", None, "mp"),
            P("dp", None, "mp"),
            P("dp", None, "mp"),
            P(None, "mp", "dp"),
            P("mp", "dp"),
            P("mp", "dp"),
            P(None, "dp", None),
            P("dp", None),
            P("dp", None),
            P(None, None, "dp"),
            P(None, "dp"),
            P(None, "dp"),
            P(None, "dp", None, "mp"),
            P("dp", None, "mp"),
            P("dp", None, "mp"),
            P(None, "mp", "dp"),
            P("mp", "dp"),
            P("mp", "dp"),
            P(None, "dp", None, None),
            P("dp", None, None),
            P("dp", None, None),
            P(None, None, "dp"),
            P(None, "dp"),
            P(None, "dp"),
            P(None, "mp"),
            P("mp"),
            P("mp"),
        ),
        check_vma=False,
    )
```

```python
import functools
import math

import jax
import jax.numpy as jnp
from jax import lax
from jax.experimental import pallas as pl
from jax.experimental.pallas import tpu as pltpu
from jax.sharding import PartitionSpec as P

D = 1024
H = 16
FF = 3072
DM = 768
MFF = 2304
NCLASS = 1000
IMG_DEV = 4
STEP = 10

EPSILON = 1e-06
BETA_ONE = 0.9
BETA_TWO = 0.95
ADAM_EPSILON = 1e-08
CLIP_NORM = 1.0
MASKED = -1e30
MESH = pl.DeviceIdType.MESH
VMEM_BYTES = 60 * 2**20
F32 = jnp.float32
BF16 = jnp.bfloat16


def minor_size(count):
    return 1 << ((count.bit_length() - 1) // 2)


def fourier(sigmas, fourier_freqs):
    angles = 2.0 * math.pi * (jnp.log(sigmas) / 4.0)[:, None] * fourier_freqs[None, :]
    return jnp.concatenate([jnp.cos(angles), jnp.sin(angles)], axis=1)


def learn_rates():
    return (
        2.5 * D ** (-0.5),
        2.5 * (D // 64) ** (-0.5),
        2.5 * D ** (-0.5),
        2.5 * FF ** (-0.5),
        2.5 * DM ** (-0.5),
        2.5,
        2.5 * DM ** (-0.5),
        2.5 * MFF ** (-0.5),
        1.25 * DM ** (-0.5),
        0.25,
        7.5,
    )


def decay_rates():
    return (0.01, 0.01, 0.01, 0.01, 0.01, 0.01, 0.01, 0.01, 0.01, 0.0, 0.0)


def adamw_step(state, gradient, rate, decay):
    keep_rate = 1.0 - (1.0 + STEP) ** (-0.75)
    first = BETA_ONE * state(1) + (1.0 - BETA_ONE) * gradient
    second = BETA_TWO * state(2) + (1.0 - BETA_TWO) * gradient * gradient
    first_hat = first / (1.0 - BETA_ONE**STEP)
    second_hat = second / (1.0 - BETA_TWO**STEP)
    weight = state(0) * (1.0 - rate * decay) - rate * first_hat / (
        jnp.sqrt(second_hat) + ADAM_EPSILON
    )
    average = keep_rate * state(3) + (1.0 - keep_rate) * weight
    return weight, average, first, second


def dot_nn(a, b):
    return lax.dot_general(a, b, (((1,), (0,)), ((), ())), preferred_element_type=F32)


def dot_nt(a, b):
    return lax.dot_general(a, b, (((1,), (1,)), ((), ())), preferred_element_type=F32)


def dot_tn(a, b):
    return lax.dot_general(a, b, (((0,), (0,)), ((), ())), preferred_element_type=F32)


def two_part(dot, exact, wide):
    high = wide.astype(BF16)
    low = (wide - high.astype(F32)).astype(BF16)
    return dot(exact, high) + dot(exact, low)


def two_part_left(dot, wide, exact):
    high = wide.astype(BF16)
    low = (wide - high.astype(F32)).astype(BF16)
    return dot(high, exact) + dot(low, exact)


def gelu_parts(b):
    cdf = 0.5 * (1.0 + lax.erf(b * (1.0 / math.sqrt(2.0))))
    pdf = jnp.exp(-0.5 * b * b) * (1.0 / math.sqrt(2.0 * math.pi))
    return b * cdf, cdf + b * pdf


def greet(peers):
    barrier = pltpu.get_barrier_semaphore()
    total = 0
    for count, peer_of in peers:

        def say(k, carry, peer_of=peer_of):
            pl.semaphore_signal(barrier, inc=1, device_id=peer_of(k), device_id_type=MESH)
            return carry

        lax.fori_loop(1, count, say, 0)
        total += count - 1
    pl.semaphore_wait(barrier, total)


class Exchange:
    def __init__(self, count, me, device_of, send_sem, recv_sem):
        self.count, self.me, self.device_of = count, me, device_of
        self.send_sem, self.recv_sem = send_sem, recv_sem

    def _copy(self, k, src_of, dst, slot):
        peer = lax.rem(self.me + k, self.count)
        return pltpu.make_async_remote_copy(
            src_ref=src_of(peer),
            dst_ref=dst.at[slot],
            send_sem=self.send_sem.at[k],
            recv_sem=self.recv_sem.at[k],
            device_id=self.device_of(peer),
            device_id_type=MESH,
        )

    def start(self, src_of, dst):
        def body(k, carry):
            self._copy(k, src_of, dst, self.me).start()
            return carry

        lax.fori_loop(1, self.count, body, 0)

    def wait(self, src_of, dst):
        def body(k, carry):
            self._copy(k, src_of, dst, lax.rem(self.me + self.count - k, self.count)).wait()
            return carry

        lax.fori_loop(1, self.count, body, 0)

    def run(self, src_of, dst):
        self.start(src_of, dst)
        self.wait(src_of, dst)


def vmem_specs(count):
    return [pl.BlockSpec(memory_space=pltpu.VMEM)] * count


def any_specs(count):
    return [pl.BlockSpec(memory_space=pl.ANY)] * count


SMEM_SPEC = pl.BlockSpec(memory_space=pltpu.SMEM)
SHORT = 256


def total_of(ref, count):
    value = ref[0]
    for index in range(1, count):
        value = value + ref[index]
    return value


def mean_square(blocks):
    sums = jnp.sum(jnp.sum(blocks, axis=0), axis=-1, keepdims=True)
    return sums * (1.0 / DM)


def rms_blocks(blocks):
    factor = lax.rsqrt(mean_square(blocks * blocks) + EPSILON)
    return factor


def rms_blocks_back(blocks, factor, gain_grad):
    inner = mean_square(blocks * gain_grad)
    return factor[None] * gain_grad - blocks * (factor * factor * factor * inner)[None]


class Grid:
    def __init__(self, n_dp):
        self.d, self.m = lax.axis_index("dp"), lax.axis_index("mp")
        self.n_y = minor_size(n_dp)
        self.n_z = n_dp // self.n_y
        self.z, self.y = lax.div(self.d, self.n_y), lax.rem(self.d, self.n_y)

    def block(self, z, y):
        return z * self.n_y + y

    def other_y(self, ky):
        return lax.rem(self.y + ky, self.n_y)

    def before_y(self, ky):
        return lax.rem(self.y + self.n_y - ky, self.n_y)

    def above(self):
        return (self.block(jnp.minimum(self.z + 1, self.n_z - 1), self.y), self.m)

    def below(self):
        return (self.block(jnp.maximum(self.z - 1, 0), self.y), self.m)


def if_piece(act, i, low, high, also=True):
    @pl.when((i >= low) & (i < high) & also)
    def _():
        act(i)


def each_piece(act, low, high):
    def body(i, carry):
        act(i)
        return carry

    lax.fori_loop(low, high, body, 0)


def gather_bulk_sems(n_dp, pieces):
    n_y = minor_size(n_dp)
    n_z = n_dp // n_y
    return [pltpu.SemaphoreType.DMA((n_z, pieces))] * 4 + [pltpu.SemaphoreType.DMA((n_z, n_y, pieces))] * 2


class BulkGather:
    def __init__(self, grid, pieces, piece, up_ss, up_rs, down_ss, down_rs, y_ss, y_rs):
        self.g, self.pieces, self.piece = grid, pieces, piece
        self.up, self.down, self.y_ss, self.y_rs = (up_ss, up_rs), (down_ss, down_rs), y_ss, y_rs
        self.ticks = pieces + grid.n_z - 1

    def z_copy(self, sems, owner_z, i, target):
        block = self.piece(self.g.block(owner_z, self.g.y), i)
        return pltpu.make_async_remote_copy(
            src_ref=block, dst_ref=block, send_sem=sems[0].at[owner_z, i], recv_sem=sems[1].at[owner_z, i],
            device_id=target, device_id_type=MESH)

    def up_copy(self, owner_z, i):
        return self.z_copy(self.up, owner_z, i, self.g.above())

    def down_copy(self, owner_z, i):
        return self.z_copy(self.down, owner_z, i, self.g.below())

    def y_copy(self, owner_z, ky, i, in_y):
        return pltpu.make_async_remote_copy(
            src_ref=self.piece(self.g.block(owner_z, self.g.y), i), dst_ref=self.piece(self.g.block(owner_z, in_y), i),
            send_sem=self.y_ss.at[owner_z, ky, i], recv_sem=self.y_rs.at[owner_z, ky, i],
            device_id=(self.g.block(self.g.z, self.g.other_y(ky)), self.g.m), device_id_type=MESH)

    def along_y(self, owner_z, i):
        for ky in range(1, self.g.n_y):
            self.y_copy(owner_z, ky, i, self.g.y).start()

    def send(self, i):
        z, n_z = self.g.z, self.g.n_z

        @pl.when(z < n_z - 1)
        def _():
            self.up_copy(z, i).start()

        @pl.when(z > 0)
        def _():
            self.down_copy(z, i).start()

        self.along_y(z, i)

    def arrival(self, hop, i):
        z, n_z = self.g.z, self.g.n_z

        @pl.when(z - 1 - hop >= 0)
        def _():
            owner = jnp.maximum(z - 1 - hop, 0)
            self.up_copy(owner, i).wait_recv()

            @pl.when(z < n_z - 1)
            def _():
                self.up_copy(owner, i).start()

            self.along_y(owner, i)

        @pl.when(z + 1 + hop < n_z)
        def _():
            owner = jnp.minimum(z + 1 + hop, n_z - 1)
            self.down_copy(owner, i).wait_recv()

            @pl.when(z > 0)
            def _():
                self.down_copy(owner, i).start()

            self.along_y(owner, i)

    def tick(self, t):
        if_piece(self.send, t, 0, self.pieces)
        for hop in range(self.g.n_z - 1):
            if_piece(functools.partial(self.arrival, hop), t - 1 - hop, 0, self.pieces)

    def finish(self):
        z, n_z = self.g.z, self.g.n_z

        def piece_done(i):
            for owner in range(n_z):

                @pl.when((z >= owner) & (z < n_z - 1))
                def _():
                    self.up_copy(owner, i).wait_send()

                @pl.when((z <= owner) & (z > 0))
                def _():
                    self.down_copy(owner, i).wait_send()

                for ky in range(1, self.g.n_y):
                    self.y_copy(owner, ky, i, self.g.before_y(ky)).wait()

        each_piece(piece_done, 0, self.pieces)


def scatter_scratch(n_dp, pieces, rows, columns):
    n_y = minor_size(n_dp)
    n_z = n_dp // n_y
    slot = (pieces, rows, columns)
    return (
        [pltpu.VMEM((n_z, max(n_y - 1, 1)) + slot, BF16)]
        + [pltpu.VMEM((n_z,) + slot, BF16)] * 4
        + gather_bulk_sems(n_dp, pieces)
    )


class BulkScatter:
    def __init__(self, grid, pieces, piece, out, recv_y, up_out, up_in, down_out, down_in, up_ss, up_rs, down_ss, down_rs, y_ss, y_rs):
        self.g, self.pieces, self.piece, self.out, self.recv_y = grid, pieces, piece, out, recv_y
        self.up, self.down = (up_out, up_in, up_ss, up_rs), (down_out, down_in, down_ss, down_rs)
        self.y_ss, self.y_rs = y_ss, y_rs
        self.ticks = pieces + grid.n_z - 1

    def y_copy(self, owner_z, ky, i):
        to_y = self.g.other_y(ky)
        return pltpu.make_async_remote_copy(
            src_ref=self.piece(self.g.block(owner_z, to_y), i), dst_ref=self.recv_y.at[owner_z, ky - 1, i],
            send_sem=self.y_ss.at[owner_z, ky, i], recv_sem=self.y_rs.at[owner_z, ky, i],
            device_id=(self.g.block(self.g.z, to_y), self.g.m), device_id_type=MESH)

    def z_copy(self, line, owner_z, i, target):
        return pltpu.make_async_remote_copy(
            src_ref=line[0].at[owner_z, i], dst_ref=line[1].at[owner_z, i], send_sem=line[2].at[owner_z, i],
            recv_sem=line[3].at[owner_z, i], device_id=target, device_id_type=MESH)

    def up_copy(self, owner_z, i):
        return self.z_copy(self.up, owner_z, i, self.g.above())

    def down_copy(self, owner_z, i):
        return self.z_copy(self.down, owner_z, i, self.g.below())

    def send(self, i):
        for owner in range(self.g.n_z):
            for ky in range(1, self.g.n_y):
                self.y_copy(owner, ky, i).start()

    def own_sum(self, owner, i):
        value = self.piece(self.g.block(owner, self.g.y), i)[...].astype(F32)
        for ky in range(1, self.g.n_y):
            self.y_copy(owner, ky, i).wait_recv()
            value = value + self.recv_y[owner, ky - 1, i].astype(F32)
        return value

    def pass_on(self, line, copy, first, low, high, i):
        def body(owner, carry):
            line[0][owner, i] = self.own_sum(owner, i).astype(BF16)

            @pl.when(jnp.logical_not(first))
            def _():
                copy(owner, i).wait_recv()
                line[0][owner, i] = (line[0][owner, i].astype(F32) + line[1][owner, i].astype(F32)).astype(BF16)

            copy(owner, i).start()
            return carry

        lax.fori_loop(low, high, body, 0)

    def go_up(self, i):
        self.pass_on(self.up, self.up_copy, self.g.z == 0, self.g.z + 1, self.g.n_z, i)

    def go_down(self, i):
        self.pass_on(self.down, self.down_copy, self.g.z == self.g.n_z - 1, 0, self.g.z, i)

    def tick(self, t):
        z, n_z = self.g.z, self.g.n_z
        if_piece(self.send, t, 0, self.pieces)
        if_piece(self.go_up, t - 1 - z, 0, self.pieces, z < n_z - 1)
        if_piece(self.go_down, t - 1 - (n_z - 1 - z), 0, self.pieces, z > 0)

    def finish(self):
        z, n_z = self.g.z, self.g.n_z

        def piece_done(i):
            self.out(i)[...] = self.own_sum(z, i)

            @pl.when(z > 0)
            def _():
                self.up_copy(z, i).wait_recv()
                self.out(i)[...] = self.out(i)[...] + self.up[1][z, i].astype(F32)

            @pl.when(z < n_z - 1)
            def _():
                self.down_copy(z, i).wait_recv()
                self.out(i)[...] = self.out(i)[...] + self.down[1][z, i].astype(F32)

            for owner in range(n_z):

                @pl.when(owner > z)
                def _():
                    self.up_copy(owner, i).wait_send()

                @pl.when(owner < z)
                def _():
                    self.down_copy(owner, i).wait_send()

                for ky in range(1, self.g.n_y):
                    self.y_copy(owner, ky, i).wait_send()

        each_piece(piece_done, 0, self.pieces)


def cuts(rows):
    return max(rows // 32, min(rows // 16, 2))


def cut_rows(ref, shard, c):
    parts = cuts(shard)
    small = shard // parts

    def piece(owner, i):
        rows = pl.ds(pl.multiple_of(owner * shard + lax.rem(i, parts) * small, small), small)
        if c is None:
            return ref.at[lax.div(i, parts), rows, :]
        return ref.at[c, rows, :]

    return piece


def loads(pairs, sems):
    copies = [pltpu.make_async_copy(source, target, sems.at[i]) for i, (source, target) in enumerate(pairs)]
    for copy in copies:
        copy.start()
    return copies


class Ranks:
    def __init__(self, n_mp):
        self.d, self.m = lax.axis_index("dp"), lax.axis_index("mp")
        self.n_x = n_mp // 2
        self.x, self.c = lax.div(self.m, 2), lax.rem(self.m, 2)
        self.sibling = (self.d, self.x * 2 + 1 - self.c)

    def rank(self, kx, same):
        core = jnp.where(same == 1, self.c, 1 - self.c)
        return lax.rem(self.x + kx, self.n_x) * 2 + core

    def chip(self, kx):
        return (self.d, lax.rem(self.x + kx, self.n_x) * 2 + self.c)

    def greet(self):
        greet([(2, lambda k: self.sibling), (self.n_x, self.chip)])


class Reduce:
    def __init__(self, ranks, core_send, core_recv, x_send, x_recv, sems):
        self.r = ranks
        self.core_send, self.core_recv, self.x_send, self.x_recv = core_send, core_recv, x_send, x_recv
        self.sems = sems

    def core_copy(self, kx):
        return pltpu.make_async_remote_copy(
            src_ref=self.core_send.at[kx], dst_ref=self.core_recv.at[kx], send_sem=self.sems.at[0, kx],
            recv_sem=self.sems.at[1, kx], device_id=self.r.sibling, device_id_type=MESH)

    def x_copy(self, kx):
        return pltpu.make_async_remote_copy(
            src_ref=self.x_send.at[kx], dst_ref=self.x_recv.at[kx], send_sem=self.sems.at[2, kx],
            recv_sem=self.sems.at[3, kx], device_id=self.r.chip(kx), device_id_type=MESH)

    def other(self, kx, part):
        self.core_send[kx] = part.astype(BF16)
        self.core_copy(kx).start()

    def same(self, kx, part):
        self.core_copy(kx).wait_recv()
        self.x_send[kx] = (part + self.core_recv[kx].astype(F32)).astype(BF16)
        self.x_copy(kx).start()

    def finish(self, part):
        self.core_copy(0).wait_recv()
        total = part + self.core_recv[0].astype(F32)
        for kx in range(1, self.r.n_x):
            self.x_copy(kx).wait_recv()
            total = total + self.x_recv[kx].astype(F32)
        return total

    def drain(self):
        self.core_copy(0).wait_send()
        for kx in range(1, self.r.n_x):
            self.core_copy(kx).wait_send()
            self.x_copy(kx).wait_send()


def reduce_scratch(n_mp, rows):
    slots = pltpu.VMEM((n_mp // 2, rows, D), BF16)
    return [slots, slots, slots, slots, pltpu.SemaphoreType.DMA((4, n_mp // 2))]


class Gather:
    def __init__(self, ranks, rows, buffer, sems):
        self.r, self.rows, self.buffer, self.sems = ranks, rows, buffer, sems

    def at(self, rank):
        return self.buffer.at[pl.ds(pl.multiple_of(rank * self.rows, self.rows), self.rows), :]

    def x_copy(self, kx, slot):
        return pltpu.make_async_remote_copy(
            src_ref=self.at(self.r.m), dst_ref=self.at(slot), send_sem=self.sems.at[0, kx],
            recv_sem=self.sems.at[1, kx], device_id=self.r.chip(kx), device_id_type=MESH)

    def core_copy(self, kx, out_slot, in_slot):
        return pltpu.make_async_remote_copy(
            src_ref=self.at(out_slot), dst_ref=self.at(in_slot), send_sem=self.sems.at[2, kx],
            recv_sem=self.sems.at[3, kx], device_id=self.r.sibling, device_id_type=MESH)

    def start(self):
        for kx in range(1, self.r.n_x):
            self.x_copy(kx, self.r.m).start()
        self.core_copy(0, self.r.m, self.r.m).start()

    def from_chip(self, kx):
        return lax.rem(self.r.x + self.r.n_x - kx, self.r.n_x) * 2 + self.r.c

    def from_core(self, kx):
        return lax.rem(self.r.x + self.r.n_x - kx, self.r.n_x) * 2 + 1 - self.r.c

    def forward(self, kx):
        slot = self.from_chip(kx)
        self.x_copy(kx, slot).wait_recv()
        self.core_copy(kx, slot, slot).start()

    def arrived(self, kx):
        self.core_copy(kx, self.r.m, self.from_core(kx)).wait_recv()

    def drain(self):
        for kx in range(1, self.r.n_x):
            self.x_copy(kx, self.r.m).wait_send()
        for kx in range(self.r.n_x):
            self.core_copy(kx, self.r.m, self.r.m).wait_send()


def gather_sems(n_mp):
    return pltpu.SemaphoreType.DMA((4, n_mp // 2))


def head_sums(values, ones):
    return two_part_left(dot_nn, values, ones)


def row_sums_factor(values):
    return lax.rsqrt(jnp.mean(values * values, axis=-1, keepdims=True) + EPSILON)


def image_scale(info_ref, mods_ref, which, image):
    is_long = info_ref[0]
    row = mods_ref[which, pl.ds(image, 1), :]
    return 1.0 + (is_long * mods_ref[which, 0:1, :] + (1.0 - is_long) * row)


def column_bias(info_ref, image, columns_shape, short):
    keys = lax.broadcasted_iota(jnp.int32, columns_shape, 0)
    own = (keys >= image * short) & (keys < (image + 1) * short)
    return jnp.where(own, 0.0, info_ref[1])


def forward_kernel(
    n_dp, n_mp, heads,
    info_ref, feats_ref, onehot_ref, x_ref, scale_ref, ones_ref,
    in_ref, out_ref, up_ref, time_ref, class_ref, mapup_ref, mapdown_ref, mod_ref, gains_ref,
    mods_ref, emb_ref, hid_ref, gated_ref, mixed_ref, wg_ref, wf_ref,
    q_ref, k_ref, v_ref, normed_ref, att_ref, stats_ref, mid_ref, nm_ref,
    in_s, out_s, up_s, time_s, class_s, mapup_s, mapdown_s, mod_s, gains_s, load_sem,
    send_a, recv_a, own_a, send_h, recv_h, own_g, recv_g, own_x, recv_x, own_m, send_o, recv_o,
    dp_ss, dp_rs, mp_ss, mp_rs, a_us, a_ur, a_ds, a_dr, a_ys, a_yr, f_us, f_ur, f_ds, f_dr, f_ys, f_yr,
    qu_s, ku_s, vt_s, part_s, core_send, core_recv, x_send, x_recv, sems,
):
    r = Ranks(n_mp)
    grid = Grid(n_dp)
    d, m = r.d, r.m
    images, part = feats_ref.shape
    copies = loads(
        (
            (time_ref.at[0], time_s),
            (in_ref.at[0], in_s),
            (out_ref.at[0], out_s),
            (class_ref.at[0], class_s),
            (gains_ref, gains_s),
            (up_ref.at[0], up_s),
            (mapup_ref.at[0], mapup_s),
            (mapdown_ref.at[0], mapdown_s),
            (mod_ref.at[0], mod_s),
        ),
        load_sem,
    )
    map_copies = [copies[0]] + copies[3:5] + copies[6:]
    greet(
        [
            (n_dp, lambda k: (lax.rem(d + k, n_dp), m)),
            (n_mp, lambda k: (d, lax.rem(m + k, n_mp))),
        ]
    )
    shard = in_s.shape[1]
    mine = pl.ds(pl.multiple_of(d * shard, shard), shard)
    attn = BulkGather(
        grid, 4, lambda dd, i: wg_ref.at[i, pl.ds(pl.multiple_of(dd * shard, shard), shard), :],
        a_us, a_ur, a_ds, a_dr, a_ys, a_yr)
    up_w = BulkGather(
        grid, 2 * cuts(shard), cut_rows(wf_ref, shard, None), f_us, f_ur, f_ds, f_dr, f_ys, f_yr
    )

    def dp_ex(stage):
        return Exchange(n_dp, d, lambda p: (p, m), dp_ss.at[stage], dp_rs.at[stage])

    copies[1].wait()
    for c in range(3):
        wg_ref[c, mine, :] = in_s[c].astype(BF16)
    copies[2].wait()
    wg_ref[3, mine, :] = out_s[...].T.astype(BF16)
    map_copies[0].wait()
    partial = dot_nn(feats_ref[...], time_s[...].astype(BF16))
    for p in range(n_dp):
        send_a[p] = partial[:, p * part : (p + 1) * part]
    ex = dp_ex(0)
    ex.start(lambda p: send_a.at[p], recv_a)
    attn.tick(0)
    recv_a[d] = send_a[d]
    copies[5].wait()
    for c in range(2):
        wf_ref[c, mine, :] = up_s[:, c, :].astype(BF16)
    for copy in map_copies[1:]:
        copy.wait()
    e_cols = dot_nt(onehot_ref[...], class_s[...].astype(BF16))
    own_a[images:, :] = jnp.zeros((8, part), F32)
    for g in range(3):
        own_a[images + g : images + g + 1, :] = gains_s[g, 0:1, :].astype(BF16).astype(F32)
    ex.wait(lambda p: send_a.at[p], recv_a)
    own_a[0:images, :] = total_of(recv_a, n_dp) + e_cols
    ex = dp_ex(1)
    ex.start(lambda p: own_a, emb_ref)
    attn.tick(1)
    emb_ref[d] = own_a[...]
    ex.wait(lambda p: own_a, emb_ref)
    gains = emb_ref[:, images:, :]
    emb = emb_ref[:, 0:images, :]
    unit = emb * rms_blocks(emb)[None] * gains[:, 0:1, :]
    unit_factor = rms_blocks(unit)
    own_x[0] = (emb_ref[d][0:images] * rms_blocks(emb)) * emb_ref[d][images : images + 1]
    unit_own = own_x[0]
    pre_own = (unit_own * unit_factor * emb_ref[d][images + 1 : images + 2]).astype(BF16)
    for c in range(2):
        part = dot_nn(pre_own, mapup_s[:, c, :].astype(BF16))
        for p in range(n_dp):
            send_h[p, c] = part[p * IMG_DEV : (p + 1) * IMG_DEV, :]
    ex = dp_ex(2)
    ex.start(lambda p: send_h.at[p], recv_h)
    attn.tick(2)
    recv_h[d] = send_h[d]
    ex.wait(lambda p: send_h.at[p], recv_h)
    hidden = total_of(recv_h, n_dp)
    hid_ref[...] = hidden
    own_g[...] = (hidden[0] * gelu_parts(hidden[1])[0]).astype(BF16).astype(F32)
    ex = dp_ex(3)
    ex.start(lambda p: own_g, recv_g)
    attn.tick(3)
    recv_g[d] = own_g[...]
    ex.wait(lambda p: own_g, recv_g)
    for p in range(n_dp):
        gated_ref[p * IMG_DEV : (p + 1) * IMG_DEV, :] = recv_g[p]
    own_x[0] = dot_nt(gated_ref[...].astype(BF16), mapdown_s[...].astype(BF16))
    ex = Exchange(n_mp, m, lambda p: (d, p), mp_ss.at[0], mp_rs.at[0])
    ex.start(lambda p: own_x.at[0], recv_x)
    attn.tick(4)
    up_w.tick(0)
    recv_x[m] = own_x[0]
    ex.wait(lambda p: own_x.at[0], recv_x)
    own_m[...] = total_of(recv_x, n_mp) + unit_own
    ex = dp_ex(4)
    ex.start(lambda p: own_m, mixed_ref)
    attn.tick(5)
    up_w.tick(1)
    mixed_ref[d] = own_m[...]
    ex.wait(lambda p: own_m, mixed_ref)
    mixed_factor = rms_blocks(mixed_ref[...])
    cond_own = (own_m[...] * mixed_factor * emb_ref[d][images + 2 : images + 3]).astype(BF16)
    for c in range(2):
        part = dot_nn(cond_own, mod_s[:, c, :].astype(BF16))
        for p in range(n_dp):
            send_o[p, c] = part[p * IMG_DEV : (p + 1) * IMG_DEV, :]
    ex = dp_ex(5)
    ex.start(lambda p: send_o.at[p], recv_o)
    attn.tick(6)
    up_w.tick(2)
    recv_o[d] = send_o[d]
    ex.wait(lambda p: send_o.at[p], recv_o)
    mods_ref[...] = total_of(recv_o, n_dp)
    each_piece(attn.tick, 7, attn.ticks)
    attn.finish()
    tokens = x_ref.shape[0]
    rows = tokens // n_mp
    width = q_ref.shape[1]
    size = width // heads
    red = Reduce(r, core_send, core_recv, x_send, x_recv, sems)
    at = lambda b: pl.ds(pl.multiple_of(b * rows, rows), rows)
    image_of = lambda b: lax.div(b * rows, SHORT)

    def project(b, carry):
        xb = x_ref[at(b), :].astype(F32)
        normed = (xb * row_sums_factor(xb) * image_scale(info_ref, mods_ref, 0, image_of(b))).astype(BF16)
        normed_ref[at(b), :] = normed
        q = dot_nn(normed, wg_ref[0])
        q_ref[at(b), :] = q
        qu_s[at(b), :] = (q * lax.rsqrt(head_sums(q * q, ones_ref[...]) + EPSILON) * scale_ref[...]).astype(BF16)
        k = dot_nn(normed, wg_ref[1])
        k_ref[at(b), :] = k
        ku_s[at(b), :] = (k * lax.rsqrt(head_sums(k * k, ones_ref[...]) + EPSILON)).astype(BF16)
        v = dot_nn(normed, wg_ref[2])
        v_ref[at(b), :] = v.astype(BF16)
        vt_s[:, at(b)] = v.T.astype(BF16)

        @pl.when(lax.rem(b, 2) == 0)
        def _():
            up_w.tick(3 + lax.div(b, 2))

        return carry

    lax.fori_loop(0, n_mp, project, 0)
    lanes = lax.broadcasted_iota(jnp.int32, (1, width), 1)

    first_tick = 3 + (n_mp + 1) // 2

    def block(j, carry):
        up_w.tick(first_tick + 2 * j)
        kx, same = lax.rem(1 + lax.div(j, 2), r.n_x), lax.rem(j, 2)
        b = r.rank(kx, same)
        bias = column_bias(info_ref, image_of(b), (tokens, 1), SHORT)
        qu = qu_s[at(b), :]
        outs = []
        for h in range(heads):
            mask = ((lanes >= h * size) & (lanes < (h + 1) * size)).astype(F32).astype(BF16)
            scores = dot_nt(ku_s[...], qu * mask) + bias
            top = jnp.max(scores, axis=0, keepdims=True)
            expon = jnp.exp(scores - top)
            total = jnp.sum(expon, axis=0, keepdims=True)
            stats_ref[h : h + 1, at(b)] = top + jnp.log(total)
            if h == heads // 2:
                up_w.tick(first_tick + 2 * j + 1)
            outs.append(dot_nn(vt_s[h * size : (h + 1) * size, :], expon.astype(BF16)) / total)
        att = jnp.concatenate(outs, axis=0).T.astype(BF16)
        att_ref[at(b), :] = att
        part_s[...] = dot_nt(att, wg_ref[3])

        @pl.when(same == 0)
        def _():
            red.other(kx, part_s[...])

        @pl.when((same == 1) & (kx > 0))
        def _():
            red.same(kx, part_s[...])

        return carry

    lax.fori_loop(0, n_mp, block, 0)
    each_piece(up_w.tick, first_tick + 2 * n_mp, up_w.ticks)
    if heads < 8:
        stats_ref[heads:8, :] = jnp.zeros((8 - heads, tokens), F32)
    middle = x_ref[at(r.m), :].astype(F32) + red.finish(part_s[...])
    mid_ref[...] = middle
    nm_ref[...] = (middle * row_sums_factor(middle) * image_scale(info_ref, mods_ref, 1, image_of(r.m))).astype(BF16)
    red.drain()
    up_w.finish()


def forward_part(n_dp, n_mp, heads, info, feats_own, onehot, x, scale, ones, layer_states, map_states, gains_state):
    images, part = feats_own.shape
    units_map = map_states[2].shape[3]
    shard, _, units = layer_states[2].shape[1:]
    width = layer_states[0].shape[3]
    tokens = x.shape[0]
    rows = tokens // n_mp
    states = (*layer_states, *map_states)
    f32 = lambda *dims: jax.ShapeDtypeStruct(dims, F32)
    bf16 = lambda *dims: jax.ShapeDtypeStruct(dims, BF16)
    return pl.pallas_call(
        functools.partial(forward_kernel, n_dp, n_mp, heads),
        out_shape=(
            f32(2, IMG_DEV, D),
            f32(n_dp, images + 8, part),
            f32(2, IMG_DEV, units_map),
            f32(images, units_map),
            f32(n_dp, images, part),
            bf16(4, D, width),
            bf16(2, D, units),
            f32(tokens, width),
            f32(tokens, width),
            bf16(tokens, width),
            bf16(tokens, D),
            bf16(tokens, width),
            f32(8, tokens),
            f32(rows, D),
            bf16(rows, D),
        ),
        in_specs=[SMEM_SPEC] + vmem_specs(5) + any_specs(9),
        out_specs=tuple(vmem_specs(15)),
        scratch_shapes=[pltpu.VMEM(state.shape[1:], F32) for state in states]
        + [
            pltpu.VMEM(gains_state.shape, F32),
            pltpu.SemaphoreType.DMA((9,)),
            pltpu.VMEM((n_dp, images, part), F32),
            pltpu.VMEM((n_dp, images, part), F32),
            pltpu.VMEM((images + 8, part), F32),
            pltpu.VMEM((n_dp, 2, IMG_DEV, units_map), F32),
            pltpu.VMEM((n_dp, 2, IMG_DEV, units_map), F32),
            pltpu.VMEM((IMG_DEV, units_map), F32),
            pltpu.VMEM((n_dp, IMG_DEV, units_map), F32),
            pltpu.VMEM((1, images, part), F32),
            pltpu.VMEM((n_mp, images, part), F32),
            pltpu.VMEM((images, part), F32),
            pltpu.VMEM((n_dp, 2, IMG_DEV, D), F32),
            pltpu.VMEM((n_dp, 2, IMG_DEV, D), F32),
            pltpu.SemaphoreType.DMA((6, n_dp)),
            pltpu.SemaphoreType.DMA((6, n_dp)),
            pltpu.SemaphoreType.DMA((1, n_mp)),
            pltpu.SemaphoreType.DMA((1, n_mp)),
        ]
        + gather_bulk_sems(n_dp, 4)
        + gather_bulk_sems(n_dp, 2 * cuts(shard))
        + [
            pltpu.VMEM((tokens, width), BF16),
            pltpu.VMEM((tokens, width), BF16),
            pltpu.VMEM((width, tokens), BF16),
            pltpu.VMEM((rows, D), F32),
        ]
        + reduce_scratch(n_mp, rows),
        compiler_params=pltpu.CompilerParams(
            collective_id=0, has_side_effects=True, vmem_limit_bytes=VMEM_BYTES
        ),
        name="forward_part",
    )(info, feats_own, onehot, x, scale, ones, *states, gains_state)


def ffn_kernel(
    n_dp, n_mp, info_ref, nm_ref, cot_ref, mods_ref, mid_ref, w_s, down_ref,
    gw_ref, gd_ref, dmid_ref, out_ref, fmod_ref,
    nm_s, gated_s, gate_s, slope_s, dh_s, dz_s, part_s, ff_s, gather_sem,
    f_core_send, f_core_recv, f_x_send, f_x_recv, f_sems,
    b_core_send, b_core_recv, b_x_send, b_x_recv, b_sems,
    down_s, wd_s, gd_s, load_sem, w_us, w_ur, w_ds, w_dr, w_ys, w_yr,
    recv_y, up_out, up_in, down_out, down_in, g_us, g_ur, g_ds, g_dr, g_ys, g_yr,
):
    r = Ranks(n_mp)
    grid = Grid(n_dp)
    copies = loads(((down_ref.at[0], down_s),), load_sem)
    rows = nm_ref.shape[0]
    tokens = rows * n_mp
    at = lambda b: pl.ds(pl.multiple_of(b * rows, rows), rows)
    image_of = lambda b: lax.div(b * rows, SHORT)

    greet(
        [
            (n_dp, lambda k: (lax.rem(r.d + k, n_dp), r.m)),
            (2, lambda k: r.sibling),
            (r.n_x, r.chip),
        ]
    )
    shard = gd_ref.shape[0]
    parts = cuts(shard)
    small = shard // parts
    copies[0].wait()
    wd_s[0, pl.ds(pl.multiple_of(r.d * shard, shard), shard), :] = down_s[...].T.astype(BF16)
    down_w = BulkGather(grid, parts, cut_rows(wd_s, shard, 0), w_us, w_ur, w_ds, w_dr, w_ys, w_yr)
    down_g = BulkScatter(
        grid, parts, cut_rows(gd_s, shard, 0),
        lambda i: gd_ref.at[pl.ds(pl.multiple_of(i * small, small), small), :],
        recv_y, up_out, up_in, down_out, down_in, g_us, g_ur, g_ds, g_dr, g_ys, g_yr)
    nm_s[at(r.m), :] = nm_ref[...]
    gather = Gather(r, rows, nm_s, gather_sem)
    gather.start()
    fwd = Reduce(r, f_core_send, f_core_recv, f_x_send, f_x_recv, f_sems)
    bwd = Reduce(r, b_core_send, b_core_recv, b_x_send, b_x_recv, b_sems)

    def forward(j, carry):
        kx = lax.div(j, 2)
        same = jnp.where(kx == 0, 1 - lax.rem(j, 2), lax.rem(j, 2))
        b = r.rank(kx, same)
        back_kx = lax.rem(r.n_x - kx, r.n_x)

        @pl.when((same == 0) & (kx > 0))
        def _():
            gather.forward(back_kx)

        @pl.when(same == 0)
        def _():
            gather.arrived(back_kx)

        down_w.tick(2 * j)
        nm = nm_s[at(b), :]
        hidden = dot_nn(nm, w_s[0])
        gate = dot_nn(nm, w_s[1])
        value, slope = gelu_parts(gate)
        gated = (hidden * value).astype(BF16)
        gated_s[at(b), :] = gated
        gate_s[at(b), :] = value
        slope_s[at(b), :] = hidden * slope
        down_w.tick(2 * j + 1)
        return carry

    lax.fori_loop(0, n_mp, forward, 0)
    each_piece(down_w.tick, 2 * n_mp, down_w.ticks)

    def live_rows(b):
        position = lax.broadcasted_iota(jnp.int32, (rows, 1), 0) + b * rows
        return (position.astype(F32) < info_ref[2]).astype(F32)

    def live_cotangent(b, carry):
        dz_s[at(b), :] = (cot_ref[at(b), :].astype(F32) * live_rows(b)).astype(BF16)
        return carry

    lax.fori_loop(0, n_mp, live_cotangent, 0)
    step = 512

    def down_gradient(i, carry):
        cols = pl.ds(pl.multiple_of(i * step, step), step)
        gd_s[0, cols, :] = dot_tn(dz_s[:, cols], gated_s[...]).astype(BF16)
        return carry

    lax.fori_loop(0, D // step, down_gradient, 0)
    down_g.tick(0)
    down_w.finish()

    def branch(j, carry):
        kx, same = lax.rem(1 + lax.div(j, 2), r.n_x), lax.rem(j, 2)
        ff_s[...] = dot_nt(gated_s[at(r.rank(kx, same)), :], wd_s[0])

        @pl.when(same == 0)
        def _():
            fwd.other(kx, ff_s[...])

        @pl.when((same == 1) & (kx > 0))
        def _():
            fwd.same(kx, ff_s[...])

        return carry

    lax.fori_loop(0, n_mp, branch, 0)

    def backward(j, carry):
        down_g.tick(1 + 2 * j)
        kx, same = lax.rem(1 + lax.div(j, 2), r.n_x), lax.rem(j, 2)
        b = r.rank(kx, same)
        d_gated = dot_nn(dz_s[at(b), :], wd_s[0])
        d_value = (d_gated * gate_s[at(b), :]).astype(BF16)
        d_gate = (d_gated * slope_s[at(b), :]).astype(BF16)
        dh_s[0, at(b), :] = d_value
        dh_s[1, at(b), :] = d_gate
        down_g.tick(2 + 2 * j)
        part_s[...] = dot_nt(d_value, w_s[0]) + dot_nt(d_gate, w_s[1])

        @pl.when(same == 0)
        def _():
            bwd.other(kx, part_s[...])

        @pl.when((same == 1) & (kx > 0))
        def _():
            bwd.same(kx, part_s[...])

        return carry

    lax.fori_loop(0, n_mp, backward, 0)
    each_piece(down_g.tick, 1 + 2 * n_mp, down_g.ticks)

    def up_gradient(i, carry):
        cols = pl.ds(pl.multiple_of(i * step, step), step)
        left = nm_s[:, cols]
        for c in range(2):
            gw_ref[c, cols, :] = dot_tn(left, dh_s[c]).astype(BF16)
        return carry

    lax.fori_loop(0, D // step, up_gradient, 0)

    d_nm = bwd.finish(part_s[...])
    middle = mid_ref[...]
    live = live_rows(r.m)
    scale = image_scale(info_ref, mods_ref, 1, image_of(r.m))
    factor = row_sums_factor(middle)
    inner = jnp.mean(middle * scale * d_nm, axis=-1, keepdims=True)
    dmid_ref[...] = cot_ref[at(r.m), :].astype(F32) * live + (
        factor * scale * d_nm - middle * (factor * factor * factor * inner)
    )
    fmod_ref[...] = jnp.sum(d_nm * middle * factor, axis=0, keepdims=True)
    out_ref[...] = ((middle + fwd.finish(ff_s[...])) * live).astype(BF16)
    gather.drain()
    fwd.drain()
    bwd.drain()
    down_g.finish()


def ffn(n_dp, n_mp, info, nm, cot, mods, mid, wf, down_state):
    rows = nm.shape[0]
    tokens = rows * n_mp
    units = wf.shape[2]
    shard = D // n_dp
    parts = cuts(shard)
    shape = jax.ShapeDtypeStruct
    return pl.pallas_call(
        functools.partial(ffn_kernel, n_dp, n_mp),
        out_shape=(
            shape(wf.shape, BF16),
            shape((shard, units), F32),
            shape((rows, D), F32),
            shape((rows, D), BF16),
            shape((1, D), F32),
        ),
        in_specs=[SMEM_SPEC] + vmem_specs(5) + any_specs(1),
        out_specs=tuple(vmem_specs(5)),
        scratch_shapes=[
            pltpu.VMEM((tokens, D), BF16),
            pltpu.VMEM((tokens, units), BF16),
            pltpu.VMEM((tokens, units), F32),
            pltpu.VMEM((tokens, units), F32),
            pltpu.VMEM((2, tokens, units), BF16),
            pltpu.VMEM((tokens, D), BF16),
            pltpu.VMEM((rows, D), F32),
            pltpu.VMEM((rows, D), F32),
            gather_sems(n_mp),
        ]
        + reduce_scratch(n_mp, rows)
        + reduce_scratch(n_mp, rows)
        + [
            pltpu.VMEM(down_state.shape[1:], F32),
            pltpu.VMEM((1, D, units), BF16),
            pltpu.VMEM((1, D, units), BF16),
            pltpu.SemaphoreType.DMA((1,)),
        ]
        + gather_bulk_sems(n_dp, parts)
        + scatter_scratch(n_dp, parts, shard // parts, units),
        compiler_params=pltpu.CompilerParams(
            collective_id=4, has_side_effects=True, vmem_limit_bytes=VMEM_BYTES
        ),
        name="ffn",
    )(info, nm, cot, mods, mid, wf, down_state)


def attn_backward_kernel(
    n_dp, n_mp, heads, info_ref, gffn_ref, dmid_ref, x_ref, mods_ref, scale_ref, ones_ref, wg_ref,
    q_ref, k_ref, v_ref, normed_ref, att_ref, stats_ref,
    gw_ref, gf_ref, gin_ref, amod_ref, gscale_ref,
    qu_s, ku_s, kt_s, dy_s, dq_s, dk_s, dv_s, low_s, part_s, gather_sem,
    core_send, core_recv, x_send, x_recv, sems,
    recv_y, up_out, up_in, down_out, down_in, f_us, f_ur, f_ds, f_dr, f_ys, f_yr,
):
    r = Ranks(n_mp)
    rows = dmid_ref.shape[0]
    tokens = rows * n_mp
    width = q_ref.shape[1]
    size = width // heads
    at = lambda b: pl.ds(pl.multiple_of(b * rows, rows), rows)
    image_of = lambda b: lax.div(b * rows, SHORT)
    dy_s[at(r.m), :] = dmid_ref[...].astype(BF16)
    grid = Grid(n_dp)
    greet(
        [
            (n_dp, lambda k: (lax.rem(r.d + k, n_dp), r.m)),
            (2, lambda k: r.sibling),
            (r.n_x, r.chip),
        ]
    )
    gather = Gather(r, rows, dy_s, gather_sem)
    gather.start()
    shard = gf_ref.shape[1]
    parts = cuts(shard)
    small = shard // parts
    up_g = BulkScatter(
        grid, 2 * parts, cut_rows(gffn_ref, shard, None),
        lambda i: gf_ref.at[lax.div(i, parts), pl.ds(pl.multiple_of(lax.rem(i, parts) * small, small), small), :],
        recv_y, up_out, up_in, down_out, down_in, f_us, f_ur, f_ds, f_dr, f_ys, f_yr)
    red = Reduce(r, core_send, core_recv, x_send, x_recv, sems)

    def units(b, carry):
        up_g.tick(b)
        q, k = q_ref[at(b), :], k_ref[at(b), :]
        qu_s[at(b), :] = (q * lax.rsqrt(head_sums(q * q, ones_ref[...]) + EPSILON) * scale_ref[...]).astype(BF16)
        k_unit = k * lax.rsqrt(head_sums(k * k, ones_ref[...]) + EPSILON)
        ku_s[at(b), :] = k_unit.astype(BF16)
        kt_s[:, at(b)] = k_unit.T.astype(BF16)
        return carry

    lax.fori_loop(0, n_mp, units, 0)
    dk_s[...] = jnp.zeros_like(dk_s)
    dv_s[...] = jnp.zeros_like(dv_s)
    lanes = lax.broadcasted_iota(jnp.int32, (1, width), 1)

    def block(j, carry):
        kx = lax.div(j, 2)
        same = 1 - lax.rem(j, 2)
        b = r.rank(kx, same)
        back_kx = lax.rem(r.n_x - kx, r.n_x)

        @pl.when((same == 1) & (kx > 0))
        def _():
            gather.forward(back_kx)

        @pl.when(same == 0)
        def _():
            gather.arrived(back_kx)

        up_g.tick(n_mp + 2 * j)
        d_att = dot_nn(dy_s[at(b), :], wg_ref[3]).astype(BF16)
        bias = column_bias(info_ref, image_of(b), (tokens, 1), SHORT)
        qu = qu_s[at(b), :]
        outs = []
        for h in range(heads):
            mask = ((lanes >= h * size) & (lanes < (h + 1) * size)).astype(F32).astype(BF16)
            qh = qu * mask
            dh = d_att * mask
            probs = jnp.exp(dot_nt(ku_s[...], qh) + bias - stats_ref[h : h + 1, at(b)])
            if h == heads // 2:
                up_g.tick(n_mp + 2 * j + 1)
            d_probs = dot_nt(v_ref[...], dh)
            inner = jnp.sum(probs * d_probs, axis=0, keepdims=True)
            d_scores = (probs * (d_probs - inner)).astype(BF16)
            dv_s[...] = dv_s[...] + dot_nn(probs.astype(BF16), dh)
            dk_s[...] = dk_s[...] + dot_nn(d_scores, qh)
            outs.append(dot_nn(kt_s[h * size : (h + 1) * size, :], d_scores))
        dq_s[at(b), :] = jnp.concatenate(outs, axis=0).T
        return carry

    lax.fori_loop(0, n_mp, block, 0)
    each_piece(up_g.tick, 3 * n_mp, up_g.ticks)

    def inputs(j, scale_grad):
        kx, same = lax.rem(1 + lax.div(j, 2), r.n_x), lax.rem(j, 2)
        b = r.rank(kx, same)
        q, k = q_ref[at(b), :], k_ref[at(b), :]
        q_factor = lax.rsqrt(head_sums(q * q, ones_ref[...]) + EPSILON)
        k_factor = lax.rsqrt(head_sums(k * k, ones_ref[...]) + EPSILON)
        dqu, dku = dq_s[at(b), :], dk_s[at(b), :]
        q_unit, k_unit = q * q_factor, k * k_factor
        q_along = dqu * q_unit
        d_q = (scale_ref[...] * q_factor * (dqu - q_unit * head_sums(q_along, ones_ref[...]))).astype(BF16)
        d_k = (k_factor * (dku - k_unit * head_sums(dku * k_unit, ones_ref[...]))).astype(BF16)
        d_v = dv_s[at(b), :].astype(BF16)
        low_s[at(b), 0:width] = d_q
        low_s[at(b), width : 2 * width] = d_k
        low_s[at(b), 2 * width : 3 * width] = d_v
        part_s[...] = dot_nt(d_q, wg_ref[0]) + dot_nt(d_k, wg_ref[1]) + dot_nt(d_v, wg_ref[2])

        @pl.when(same == 0)
        def _():
            red.other(kx, part_s[...])

        @pl.when((same == 1) & (kx > 0))
        def _():
            red.same(kx, part_s[...])

        return scale_grad + jnp.sum(q_along, axis=0, keepdims=True)

    gscale_ref[...] = lax.fori_loop(0, n_mp, inputs, jnp.zeros((1, width), F32))

    step = 512

    def weights(i, carry):
        cols = pl.ds(pl.multiple_of(i * step, step), step)
        value = dot_tn(normed_ref[:, cols], low_s[...]).astype(BF16)
        for c in range(3):
            gw_ref[c, cols, :] = value[:, c * width : (c + 1) * width]
        gw_ref[3, cols, :] = dot_tn(dy_s[:, cols], att_ref[...]).astype(BF16)
        return carry

    lax.fori_loop(0, D // step, weights, 0)

    d_normed = red.finish(part_s[...])
    x = x_ref[at(r.m), :].astype(F32)
    scale = image_scale(info_ref, mods_ref, 0, image_of(r.m))
    factor = row_sums_factor(x)
    inner = jnp.mean(x * scale * d_normed, axis=-1, keepdims=True)
    gin_ref[...] = dmid_ref[...] + (factor * scale * d_normed - x * (factor * factor * factor * inner))
    amod_ref[...] = jnp.sum(d_normed * x * factor, axis=0, keepdims=True)
    gather.drain()
    red.drain()
    up_g.finish()


def attn_backward(n_dp, n_mp, heads, info, gffn, dmid, x, mods, scale, ones, wg, q, k, v, normed, att, stats):
    rows = dmid.shape[0]
    tokens = rows * n_mp
    width = q.shape[1]
    shard = D // n_dp
    shape = jax.ShapeDtypeStruct
    return pl.pallas_call(
        functools.partial(attn_backward_kernel, n_dp, n_mp, heads),
        out_shape=(
            shape(wg.shape, BF16),
            shape((2, shard, gffn.shape[2]), F32),
            shape((rows, D), F32),
            shape((1, D), F32),
            shape((1, width), F32),
        ),
        in_specs=[SMEM_SPEC] + vmem_specs(13),
        out_specs=tuple(vmem_specs(5)),
        scratch_shapes=[
            pltpu.VMEM((tokens, width), BF16),
            pltpu.VMEM((tokens, width), BF16),
            pltpu.VMEM((width, tokens), BF16),
            pltpu.VMEM((tokens, D), BF16),
            pltpu.VMEM((tokens, width), F32),
            pltpu.VMEM((tokens, width), F32),
            pltpu.VMEM((tokens, width), F32),
            pltpu.VMEM((tokens, 3 * width), BF16),
            pltpu.VMEM((rows, D), F32),
            gather_sems(n_mp),
        ]
        + reduce_scratch(n_mp, rows)
        + scatter_scratch(n_dp, 2 * cuts(shard), shard // cuts(shard), gffn.shape[2]),
        compiler_params=pltpu.CompilerParams(
            collective_id=5, has_side_effects=True, vmem_limit_bytes=VMEM_BYTES
        ),
        name="attn_backward",
    )(info, gffn, dmid, x, mods, scale, ones, wg, q, k, v, normed, att, stats)


def back_kernel(
    n_dp, n_mp,
    info_ref, grads_ref, amod_ref, fmod_ref, out_ref, gin_ref, feats_ref, onehot_ref, mapup_ref, mapdown_ref, mod_ref,
    emb_ref, hid_ref, gated_ref, mixed_ref,
    gattn_ref, out_all, gin_all, gmod_ref, gmd_ref, gmu_ref, gtime_ref, gclass_ref, ggain_ref,
    mapup_s, mapdown_s, mod_s, load_sem, gin_s, dmods_s, full_e, out_sem, gin_sem,
    recv_q, own_q, recv_d, full_d, own_c, recv_c, send_g, recv_g, own_h, recv_h, full_h,
    own_p, recv_p, own_s, recv_s,
    dp_ss, dp_rs, mp_ss, mp_rs, recv_y, up_out, up_in, down_out, down_in, a_us, a_ur, a_ds, a_dr, a_ys, a_yr,
):
    r = Ranks(n_mp)
    d, m = r.d, r.m
    shard = gattn_ref.shape[1]
    attn_g = BulkScatter(
        Grid(n_dp), 4, lambda dd, i: grads_ref.at[i, pl.ds(pl.multiple_of(dd * shard, shard), shard), :],
        lambda i: gattn_ref.at[i], recv_y, up_out, up_in, down_out, down_in,
        a_us, a_ur, a_ds, a_dr, a_ys, a_yr)
    images, own_cols = feats_ref.shape
    rows = out_ref.shape[0]
    copies = loads(
        ((mapup_ref.at[0], mapup_s), (mapdown_ref.at[0], mapdown_s), (mod_ref.at[0], mod_s)), load_sem
    )
    greet(
        [
            (n_dp, lambda k: (lax.rem(d + k, n_dp), m)),
            (n_mp, lambda k: (d, lax.rem(m + k, n_mp))),
        ]
    )
    at = lambda b: pl.ds(pl.multiple_of(b * rows, rows), rows)
    out_all[at(m), :] = out_ref[...]
    gin_s[at(m), :] = gin_ref[...].astype(BF16)
    one = Gather(r, rows, out_all, out_sem)
    two = Gather(r, rows, gin_s, gin_sem)
    own_image = lax.div(m * rows, SHORT)
    for image in range(IMG_DEV):
        share = (1.0 - info_ref[0]) * jnp.where(own_image == image, 1.0, 0.0)
        if image == 0:
            share = share + info_ref[0]
        dmods_s[0, image : image + 1, :] = share * amod_ref[...]
        dmods_s[1, image : image + 1, :] = share * fmod_ref[...]

    def dp_ex(stage):
        return Exchange(n_dp, d, lambda p: (p, m), dp_ss.at[stage], dp_rs.at[stage])

    def mp_ex(stage):
        return Exchange(n_mp, m, lambda p: (d, p), mp_ss.at[stage], mp_rs.at[stage])

    ex = mp_ex(0)
    ex.start(lambda p: dmods_s, recv_q)
    attn_g.tick(0)
    recv_q[m] = dmods_s[...]
    ex.wait(lambda p: dmods_s, recv_q)
    own_q[...] = total_of(recv_q, n_mp)
    one.start()
    two.start()
    ex = dp_ex(0)
    ex.start(lambda p: own_q, recv_d)
    attn_g.tick(1)
    recv_d[d] = own_q[...]
    gains_own = emb_ref[d][images:]
    emb = emb_ref[:, 0:images, :]
    emb_factor = rms_blocks(emb)
    unit = emb * emb_factor[None] * emb_ref[:, images : images + 1, :]
    unit_factor = rms_blocks(unit)
    emb_own = emb_ref[d][0:images]
    unit_own = emb_own * emb_factor * gains_own[0:1]
    pre_own = (unit_own * unit_factor * gains_own[1:2]).astype(BF16)
    mixed = mixed_ref[...]
    mixed_factor = rms_blocks(mixed)
    mixed_own = mixed_ref[d]
    cond_own = (mixed_own * mixed_factor * gains_own[2:3]).astype(BF16)
    ex.wait(lambda p: own_q, recv_d)
    for p in range(n_dp):
        for c in range(2):
            full_d[c, p * IMG_DEV : (p + 1) * IMG_DEV, :] = recv_d[p, c]
    for copy in copies:
        copy.wait()
    own_c[...] = two_part_left(dot_nt, full_d[0], mod_s[:, 0, :].astype(BF16)) + two_part_left(
        dot_nt, full_d[1], mod_s[:, 1, :].astype(BF16)
    )
    ex = dp_ex(1)
    ex.start(lambda p: own_c, recv_c)
    attn_g.tick(2)
    recv_c[d] = own_c[...]
    for c in range(2):
        gmod_ref[:, c, :] = two_part(dot_tn, cond_own, full_d[c])
    ex.wait(lambda p: own_c, recv_c)
    ggain_ref[2:3, :] = jnp.sum(own_c[...] * mixed_own * mixed_factor, axis=0, keepdims=True)
    d_mixed = rms_blocks_back(
        mixed, mixed_factor, recv_c[...] * emb_ref[:, images + 2 : images + 3, :]
    )
    recv_c[...] = d_mixed
    mix_own = recv_c[d]
    part = two_part_left(dot_nn, mix_own, mapdown_s[...].astype(BF16))
    for p in range(n_dp):
        send_g[p] = part[p * IMG_DEV : (p + 1) * IMG_DEV, :]
    ex = dp_ex(2)
    ex.start(lambda p: send_g.at[p], recv_g)
    attn_g.tick(3)
    recv_g[d] = send_g[d]
    gmd_ref[...] = two_part_left(dot_tn, mix_own, gated_ref[...].astype(BF16))
    ex.wait(lambda p: send_g.at[p], recv_g)
    d_gated = total_of(recv_g, n_dp)
    value, slope = gelu_parts(hid_ref[1])
    own_h[0] = d_gated * value
    own_h[1] = d_gated * hid_ref[0] * slope
    ex = dp_ex(3)
    ex.start(lambda p: own_h, recv_h)
    recv_h[d] = own_h[...]
    attn_g.tick(4)
    ex.wait(lambda p: own_h, recv_h)
    for p in range(n_dp):
        for c in range(2):
            full_h[c, p * IMG_DEV : (p + 1) * IMG_DEV, :] = recv_h[p, c]
    own_p[...] = two_part_left(dot_nt, full_h[0], mapup_s[:, 0, :].astype(BF16)) + two_part_left(
        dot_nt, full_h[1], mapup_s[:, 1, :].astype(BF16)
    )
    ex = mp_ex(1)
    ex.start(lambda p: own_p, recv_p)
    attn_g.tick(5)
    recv_p[m] = own_p[...]
    for c in range(2):
        gmu_ref[:, c, :] = two_part(dot_tn, pre_own, full_h[c])
    ex.wait(lambda p: own_p, recv_p)
    own_s[...] = total_of(recv_p, n_mp)
    ex = dp_ex(4)
    ex.start(lambda p: own_s, recv_s)
    attn_g.tick(6)
    recv_s[d] = own_s[...]
    ex.wait(lambda p: own_s, recv_s)
    ggain_ref[1:2, :] = jnp.sum(own_s[...] * unit_own * unit_factor, axis=0, keepdims=True)
    d_unit = recv_c[...] + rms_blocks_back(
        unit, unit_factor, recv_s[...] * emb_ref[:, images + 1 : images + 2, :]
    )
    recv_s[...] = d_unit
    ggain_ref[0:1, :] = jnp.sum(recv_s[d] * emb_own * emb_factor, axis=0, keepdims=True)
    d_emb = rms_blocks_back(emb, emb_factor, d_unit * emb_ref[:, images : images + 1, :])
    recv_s[...] = d_emb
    ggain_ref[3:8, :] = jnp.zeros_like(ggain_ref[3:8, :])
    for p in range(n_dp):
        full_e[:, p * own_cols : (p + 1) * own_cols] = recv_s[p]
    gtime_ref[...] = two_part(dot_tn, feats_ref[...], full_e[...])
    gclass_ref[...] = two_part_left(dot_tn, recv_s[d], onehot_ref[...])
    gin_all[at(m), :] = gin_ref[...]
    for kx in range(1, r.n_x):
        one.forward(kx)
        two.forward(kx)
        gin_all[at(two.from_chip(kx)), :] = gin_s[at(two.from_chip(kx)), :].astype(F32)
    for kx in range(r.n_x):
        one.arrived(kx)
        two.arrived(kx)
        gin_all[at(two.from_core(kx)), :] = gin_s[at(two.from_core(kx)), :].astype(F32)
    each_piece(attn_g.tick, 7, attn_g.ticks)
    attn_g.finish()
    one.drain()
    two.drain()


def back(n_dp, n_mp, info, grads, amod, fmod, out_own, gin_own, feats_own, onehot, mapup_state, mapdown_state, mod_state, emb, hid, gated, mixed):
    images, part = feats_own.shape
    units = mapup_state.shape[3]
    rows = out_own.shape[0]
    tokens = rows * n_mp
    states = (mapup_state, mapdown_state, mod_state)
    slab = (4, grads.shape[1] // n_dp, grads.shape[2])
    shape = lambda *dims: jax.ShapeDtypeStruct(dims, F32)
    return pl.pallas_call(
        functools.partial(back_kernel, n_dp, n_mp),
        out_shape=(
            shape(*slab),
            jax.ShapeDtypeStruct((tokens, D), BF16),
            shape(tokens, D),
            shape(part, 2, D),
            shape(part, units),
            shape(part, 2, units),
            shape(part, DM),
            shape(part, NCLASS),
            shape(8, part),
        ),
        in_specs=[SMEM_SPEC] + vmem_specs(7) + any_specs(3) + vmem_specs(4),
        out_specs=tuple(vmem_specs(9)),
        scratch_shapes=[pltpu.VMEM(state.shape[1:], F32) for state in states]
        + [
            pltpu.SemaphoreType.DMA((3,)),
            pltpu.VMEM((tokens, D), BF16),
            pltpu.VMEM((2, IMG_DEV, D), F32),
            pltpu.VMEM((images, DM), F32),
            gather_sems(n_mp),
            gather_sems(n_mp),
            pltpu.VMEM((n_mp, 2, IMG_DEV, D), F32),
            pltpu.VMEM((2, IMG_DEV, D), F32),
            pltpu.VMEM((n_dp, 2, IMG_DEV, D), F32),
            pltpu.VMEM((2, images, D), F32),
            pltpu.VMEM((images, part), F32),
            pltpu.VMEM((n_dp, images, part), F32),
            pltpu.VMEM((n_dp, IMG_DEV, units), F32),
            pltpu.VMEM((n_dp, IMG_DEV, units), F32),
            pltpu.VMEM((2, IMG_DEV, units), F32),
            pltpu.VMEM((n_dp, 2, IMG_DEV, units), F32),
            pltpu.VMEM((2, images, units), F32),
            pltpu.VMEM((images, part), F32),
            pltpu.VMEM((n_mp, images, part), F32),
            pltpu.VMEM((images, part), F32),
            pltpu.VMEM((n_dp, images, part), F32),
            pltpu.SemaphoreType.DMA((5, n_dp)),
            pltpu.SemaphoreType.DMA((5, n_dp)),
            pltpu.SemaphoreType.DMA((2, n_mp)),
            pltpu.SemaphoreType.DMA((2, n_mp)),
        ]
        + scatter_scratch(n_dp, *slab),
        compiler_params=pltpu.CompilerParams(
            collective_id=1, has_side_effects=True, vmem_limit_bytes=VMEM_BYTES
        ),
        name="back",
    )(info, grads, amod, fmod, out_own, gin_own, feats_own, onehot, *states, emb, hid, gated, mixed)


def norm_kernel(
    n_dp, n_mp, heads,
    gattn_ref, gup_ref, gdown_ref, gtime_ref, gclass_ref, gmu_ref, gmd_ref, gmod_ref, ggain_ref, gscale_ref,
    norm_ref, own, all_dp, own_sum, all_mp, dp_ss, dp_rs, mp_ss, mp_rs,
):
    d, m = lax.axis_index("dp"), lax.axis_index("mp")
    greet(
        [
            (n_dp, lambda k: (lax.rem(d + k, n_dp), m)),
            (n_mp, lambda k: (d, lax.rem(m + k, n_mp))),
        ]
    )
    def squares(value):
        value = value.astype(F32)
        return jnp.sum(jnp.sum(value * value, axis=0, keepdims=True), axis=-1, keepdims=True)

    def planes(ref):
        return sum(squares(ref[:, c, :]) for c in range(2))

    split = squares(gdown_ref[...]) + planes(gmu_ref) + squares(gmd_ref[...])
    for c in range(4):
        split = split + squares(gattn_ref[c])
    for c in range(2):
        split = split + squares(gup_ref[c])
    shared = planes(gmod_ref) + squares(gtime_ref[...]) + squares(gclass_ref[...]) + squares(ggain_ref[...])
    local = split + shared * (1.0 / n_mp)
    lane = lax.broadcasted_iota(jnp.int32, (1, 128), 1)
    width = gscale_ref.shape[1]
    column = lax.div(lax.broadcasted_iota(jnp.int32, (1, width), 1), width // heads)
    own[...] = jnp.zeros_like(own)
    own[0:1, :] = jnp.where(lane == 0, local, 0.0)
    scale_row = jnp.zeros((1, 128), F32)
    for h in range(heads):
        part = jnp.sum(jnp.where(column == h, gscale_ref[...], 0.0), axis=-1, keepdims=True)
        scale_row = jnp.where(lane == h, part, scale_row)
    own[1:2, :] = scale_row
    ex = Exchange(n_dp, d, lambda p: (p, m), dp_ss, dp_rs)
    ex.start(lambda p: own, all_dp)
    all_dp[d] = own[...]
    ex.wait(lambda p: own, all_dp)
    summed = total_of(all_dp, n_dp)
    head = summed[1:2]
    own_sum[...] = jnp.zeros_like(own_sum)
    own_sum[0:1, :] = summed[0:1] + head * head
    ex = Exchange(n_mp, m, lambda p: (d, p), mp_ss, mp_rs)
    ex.start(lambda p: own_sum, all_mp)
    all_mp[m] = own_sum[...]
    ex.wait(lambda p: own_sum, all_mp)
    norm = jnp.sqrt(jnp.sum(total_of(all_mp, n_mp)[0:1], axis=-1, keepdims=True))
    norm_ref[0:1, :] = jnp.broadcast_to(norm, (1, 128))
    norm_ref[1:2, :] = head
    norm_ref[2:8, :] = jnp.zeros((6, 128), F32)


def grad_norm_of(n_dp, n_mp, heads, grads):
    block = pltpu.VMEM((8, 128), F32)
    return pl.pallas_call(
        functools.partial(norm_kernel, n_dp, n_mp, heads),
        out_shape=jax.ShapeDtypeStruct((8, 128), F32),
        in_specs=vmem_specs(10),
        out_specs=vmem_specs(1)[0],
        scratch_shapes=[
            block,
            pltpu.VMEM((n_dp, 8, 128), F32),
            block,
            pltpu.VMEM((n_mp, 8, 128), F32),
            pltpu.SemaphoreType.DMA((n_dp,)),
            pltpu.SemaphoreType.DMA((n_dp,)),
            pltpu.SemaphoreType.DMA((n_mp,)),
            pltpu.SemaphoreType.DMA((n_mp,)),
        ],
        compiler_params=pltpu.CompilerParams(
            collective_id=2, has_side_effects=True, vmem_limit_bytes=VMEM_BYTES
        ),
        name="grad_norm",
    )(*grads)


def update_kernel(heads, *refs):
    states, refs = refs[:11], refs[11:]
    norm_ref, gattn_ref, gup_ref, gdown_ref, gtime_ref, gclass_ref, gmu_ref, gmd_ref, gmod_ref, ggain_ref = refs[:10]
    outs, refs = refs[10:43], refs[43:]
    kept, new, first, second = refs[:11], refs[11:22], refs[22:33], refs[33:44]
    gup_s, load_sem, store_sem = refs[44:]
    order = (2, 8, 0, 6, 3, 5, 4, 7, 1, 9, 10)
    copies = {i: pltpu.make_async_copy(states[i], kept[i], load_sem.at[i]) for i in order}
    for i in order:
        copies[i].start()
    for c in range(2):
        gup_s[:, c, :] = gup_ref[c]
    factor = CLIP_NORM / jnp.maximum(norm_ref[0:1, 0:1], CLIP_NORM)
    head = norm_ref[1:2, :]
    rates, decays = learn_rates(), decay_rates()
    stores = []

    def store(i):
        for k, (source, target) in enumerate(((new[i], outs[3 * i]), (first[i], outs[3 * i + 1]), (second[i], outs[3 * i + 2]))):
            stores.append(pltpu.make_async_copy(source, target, store_sem.at[i, k]))
            stores[-1].start()

    def step(i, gradient, pick=lambda ref, k: ref.at[k]):
        copies[i].wait()
        new_weight, average, m_new, v_new = adamw_step(lambda k: pick(kept[i], k)[...], gradient, rates[i], decays[i])
        pick(new[i], 0)[...] = new_weight
        pick(new[i], 1)[...] = average
        first[i][...] = m_new
        second[i][...] = v_new
        store(i)

    step(2, gup_s[...] * factor[:, None, :])
    step(8, gmod_ref[...] * factor[:, None, :])
    copies[0].wait()
    for c in range(3):
        results = adamw_step(lambda k: kept[0][k, c], gattn_ref[c] * factor, rates[0], decays[0])
        new[0][0, c], new[0][1, c], first[0][c], second[0][c] = results
    store(0)
    step(6, gmu_ref[...] * factor[:, None, :])
    step(3, gdown_ref[...].T * factor)
    step(5, gclass_ref[...] * factor)
    step(4, gtime_ref[...] * factor)
    step(7, gmd_ref[...] * factor)
    step(1, gattn_ref[3].T * factor)
    copies[9].wait()
    copies[10].wait()
    for g in range(3):
        results = adamw_step(lambda k: kept[9][g, k : k + 1, :], ggain_ref[g : g + 1, :] * factor, rates[9], decays[9])
        new[9][g, 0:1, :], new[9][g, 1:2, :], first[9][g : g + 1, :], second[9][g : g + 1, :] = results
    store(9)
    results = adamw_step(lambda k: kept[10][k : k + 1, :], head[:, 0:heads] * factor, rates[10], decays[10])
    new[10][0:1, :], new[10][1:2, :], first[10][...], second[10][...] = results
    store(10)
    for copy in stores:
        copy.wait()


def update(states, norm, grads):
    heads = states[10].shape[1]
    rows, _, units = states[2].shape[1:]
    news, moments = [], []
    for i, state in enumerate(states):
        if i == 9:
            news.append((state.shape[0], 2, state.shape[2]))
            moments.append((state.shape[0], state.shape[2]))
        else:
            news.append((2,) + state.shape[1:])
            moments.append(state.shape[1:] if i < 10 else (1, heads))
    outs = []
    for new, moment in zip(news, moments):
        outs += [new, moment, moment]
    shape = lambda dims: jax.ShapeDtypeStruct(dims, F32)
    return pl.pallas_call(
        functools.partial(update_kernel, heads),
        out_shape=tuple(shape(o) for o in outs),
        in_specs=any_specs(11) + vmem_specs(10),
        out_specs=tuple(any_specs(33)),
        scratch_shapes=[pltpu.VMEM(state.shape, F32) for state in states]
        + [pltpu.VMEM(dims, F32) for dims in news]
        + [pltpu.VMEM(dims, F32) for dims in moments]
        + [pltpu.VMEM(dims, F32) for dims in moments]
        + [
            pltpu.VMEM((rows, 2, units), F32),
            pltpu.SemaphoreType.DMA((11,)),
            pltpu.SemaphoreType.DMA((11, 3)),
        ],
        compiler_params=pltpu.CompilerParams(vmem_limit_bytes=VMEM_BYTES),
        name="update",
    )(*states, norm, *grads)


def per_device(
    block_input,
    out_cotangent,
    sigmas,
    class_labels,
    image_lengths,
    fourier_freqs,
    inproj_state,
    outproj_state,
    upproj_state,
    downproj_state,
    timeproj_state,
    classemb_state,
    mapup_state,
    mapdown_state,
    modproj_state,
    gains_state,
    headscale_state,
):
    n_dp, n_mp = lax.axis_size("dp"), lax.axis_size("mp")
    d = lax.axis_index("dp")
    my_lengths = lax.dynamic_slice_in_dim(image_lengths, d * IMG_DEV, IMG_DEV)
    part = timeproj_state.shape[1]
    heads, width = headscale_state.shape[1], inproj_state.shape[3]
    in_state = jnp.transpose(inproj_state, (0, 2, 1, 3))
    class_state = jnp.transpose(classemb_state, (0, 2, 1))
    down_map_state = jnp.transpose(mapdown_state, (0, 2, 1))
    gain_state = jnp.transpose(gains_state, (1, 0, 2))
    feats_low = fourier(sigmas, fourier_freqs).astype(BF16)
    feats_own = lax.dynamic_slice_in_dim(feats_low, d * part, part, axis=1)
    onehot = (class_labels[:, None] == jnp.arange(NCLASS, dtype=jnp.int32)[None, :]).astype(BF16)
    is_long = (my_lengths[0] > SHORT).astype(F32)
    live = jnp.sum(my_lengths).astype(F32)
    info = jnp.stack([is_long, (1.0 - is_long) * MASKED, live, live])
    size = width // heads
    scale = jnp.repeat(headscale_state[0], size)[None, :]
    group = jnp.arange(width, dtype=jnp.int32) // size
    ones = (group[:, None] == group[None, :]).astype(BF16)
    mods, emb, hid, gated, mixed, wg, wf, q, k, v, normed, att, stats, mid, nm = forward_part(
        n_dp, n_mp, heads, info, feats_own, onehot, block_input, scale, ones,
        (in_state, outproj_state, upproj_state),
        (timeproj_state, class_state, mapup_state, down_map_state, modproj_state), gain_state,
    )
    gw_up, g_down, dmid, out_own, fmod = ffn(
        n_dp, n_mp, info, nm, out_cotangent, mods, mid, wf, downproj_state
    )
    gw_attn, g_up, gin_own, amod, gscale = attn_backward(
        n_dp, n_mp, heads, info, gw_up, dmid, block_input, mods, scale, ones, wg, q, k, v, normed, att, stats
    )
    g_attn, layer_out, input_grad, g_mod, g_md, g_mu, g_time, g_class, g_gain = back(
        n_dp, n_mp, info, gw_attn, amod, fmod, out_own, gin_own, feats_own, onehot,
        mapup_state, down_map_state, modproj_state, emb, hid, gated, mixed,
    )
    states = (
        in_state,
        outproj_state,
        upproj_state,
        downproj_state,
        timeproj_state,
        class_state,
        mapup_state,
        down_map_state,
        modproj_state,
        gain_state,
        headscale_state,
    )
    grads = (g_attn, g_up, g_down, g_time, g_class, g_mu, g_md, g_mod, g_gain)
    norm = grad_norm_of(n_dp, n_mp, heads, grads + (gscale,))
    new = update(states, norm, grads)
    orders = {0: (0, 2, 1, 3), 5: (0, 2, 1), 7: (0, 2, 1), 9: (1, 0, 2)}
    moment_orders = {0: (1, 0, 2), 5: (1, 0), 7: (1, 0)}
    results = [layer_out, input_grad, norm[0, 0]]
    for i in range(11):
        stacked, first, second = new[3 * i : 3 * i + 3]
        if i in orders:
            stacked = jnp.transpose(stacked, orders[i])
        if i in moment_orders:
            first, second = jnp.transpose(first, moment_orders[i]), jnp.transpose(second, moment_orders[i])
        if i == 10:
            first, second = first[0], second[0]
        results += [stacked, first, second]
    return tuple(results)


def solution(mesh):
    return jax.shard_map(
        per_device,
        mesh=mesh,
        in_specs=(
            P("dp", None),
            P("dp", None),
            P(),
            P(),
            P(),
            P(),
            P(None, "dp", None, "mp"),
            P(None, "mp", "dp"),
            P(None, "dp", None, "mp"),
            P(None, "mp", "dp"),
            P(None, "dp", None),
            P(None, None, "dp"),
            P(None, "dp", None, "mp"),
            P(None, "mp", "dp"),
            P(None, "dp", None, None),
            P(None, None, "dp"),
            P(None, "mp"),
        ),
        out_specs=(
            P("dp", None),
            P("dp", None),
            P(),
            P(None, "dp", None, "mp"),
            P("dp", None, "mp"),
            P("dp", None, "mp"),
            P(None, "mp", "dp"),
            P("mp", "dp"),
            P("mp", "dp"),
            P(None, "dp", None, "mp"),
            P("dp", None, "mp"),
            P("dp", None, "mp"),
            P(None, "mp", "dp"),
            P("mp", "dp"),
            P("mp", "dp"),
            P(None, "dp", None),
            P("dp", None),
            P("dp", None),
            P(None, None, "dp"),
            P(None, "dp"),
            P(None, "dp"),
            P(None, "dp", None, "mp"),
            P("dp", None, "mp"),
            P("dp", None, "mp"),
            P(None, "mp", "dp"),
            P("mp", "dp"),
            P("mp", "dp"),
            P(None, "dp", None, None),
            P("dp", None, None),
            P("dp", None, None),
            P(None, None, "dp"),
            P(None, "dp"),
            P(None, "dp"),
            P(None, "mp"),
            P("mp"),
            P("mp"),
        ),
        check_vma=False,
    )
```

```python
import functools
import math

import jax
import jax.numpy as jnp
from jax import lax
from jax.experimental import pallas as pl
from jax.experimental.pallas import tpu as pltpu
from jax.sharding import PartitionSpec as P

D = 1024
H = 16
FF = 3072
DM = 768
MFF = 2304
NCLASS = 1000
IMG_DEV = 4
STEP = 10

EPSILON = 1e-06
BETA_ONE = 0.9
BETA_TWO = 0.95
ADAM_EPSILON = 1e-08
CLIP_NORM = 1.0
MASKED = -1e30
MESH = pl.DeviceIdType.MESH
VMEM_BYTES = 60 * 2**20
F32 = jnp.float32
BF16 = jnp.bfloat16


def minor_size(count):
    return 1 << ((count.bit_length() - 1) // 2)


def learn_rates():
    return (
        2.5 * D ** (-0.5),
        2.5 * (D // 64) ** (-0.5),
        2.5 * D ** (-0.5),
        2.5 * FF ** (-0.5),
        2.5 * DM ** (-0.5),
        2.5,
        2.5 * DM ** (-0.5),
        2.5 * MFF ** (-0.5),
        1.25 * DM ** (-0.5),
        0.25,
        7.5,
    )


def decay_rates():
    return (0.01, 0.01, 0.01, 0.01, 0.01, 0.01, 0.01, 0.01, 0.01, 0.0, 0.0)


def adamw_step(state, gradient, rate, decay):
    keep_rate = 1.0 - (1.0 + STEP) ** (-0.75)
    first = BETA_ONE * state(1) + (1.0 - BETA_ONE) * gradient
    second = BETA_TWO * state(2) + (1.0 - BETA_TWO) * gradient * gradient
    first_hat = first / (1.0 - BETA_ONE**STEP)
    second_hat = second / (1.0 - BETA_TWO**STEP)
    weight = state(0) * (1.0 - rate * decay) - rate * first_hat / (
        jnp.sqrt(second_hat) + ADAM_EPSILON
    )
    average = keep_rate * state(3) + (1.0 - keep_rate) * weight
    return weight, average, first, second


def dot_nn(a, b):
    return lax.dot_general(a, b, (((1,), (0,)), ((), ())), preferred_element_type=F32)


def dot_nt(a, b):
    return lax.dot_general(a, b, (((1,), (1,)), ((), ())), preferred_element_type=F32)


def dot_tn(a, b):
    return lax.dot_general(a, b, (((0,), (0,)), ((), ())), preferred_element_type=F32)


def two_part(dot, exact, wide):
    high = wide.astype(BF16)
    low = (wide - high.astype(F32)).astype(BF16)
    return dot(exact, high) + dot(exact, low)


def two_part_left(dot, wide, exact):
    high = wide.astype(BF16)
    low = (wide - high.astype(F32)).astype(BF16)
    return dot(high, exact) + dot(low, exact)


def gelu_parts(b):
    cdf = 0.5 * (1.0 + lax.erf(b * (1.0 / math.sqrt(2.0))))
    pdf = jnp.exp(-0.5 * b * b) * (1.0 / math.sqrt(2.0 * math.pi))
    return b * cdf, cdf + b * pdf


def greet(peers):
    barrier = pltpu.get_barrier_semaphore()
    total = 0
    for count, peer_of in peers:

        def say(k, carry, peer_of=peer_of):
            pl.semaphore_signal(barrier, inc=1, device_id=peer_of(k), device_id_type=MESH)
            return carry

        lax.fori_loop(1, count, say, 0)
        total += count - 1
    pl.semaphore_wait(barrier, total)


class Exchange:
    def __init__(self, count, me, device_of, send_sem, recv_sem):
        self.count, self.me, self.device_of = count, me, device_of
        self.send_sem, self.recv_sem = send_sem, recv_sem

    def _copy(self, k, src_of, dst, slot):
        peer = lax.rem(self.me + k, self.count)
        return pltpu.make_async_remote_copy(
            src_ref=src_of(peer),
            dst_ref=dst.at[slot],
            send_sem=self.send_sem.at[k],
            recv_sem=self.recv_sem.at[k],
            device_id=self.device_of(peer),
            device_id_type=MESH,
        )

    def start(self, src_of, dst):
        def body(k, carry):
            self._copy(k, src_of, dst, self.me).start()
            return carry

        lax.fori_loop(1, self.count, body, 0)

    def wait(self, src_of, dst):
        def body(k, carry):
            self._copy(k, src_of, dst, lax.rem(self.me + self.count - k, self.count)).wait()
            return carry

        lax.fori_loop(1, self.count, body, 0)

    def run(self, src_of, dst):
        self.start(src_of, dst)
        self.wait(src_of, dst)


def vmem_specs(count):
    return [pl.BlockSpec(memory_space=pltpu.VMEM)] * count


def any_specs(count):
    return [pl.BlockSpec(memory_space=pl.ANY)] * count


SMEM_SPEC = pl.BlockSpec(memory_space=pltpu.SMEM)
SHORT = 256


def total_of(ref, count):
    value = ref[0]
    for index in range(1, count):
        value = value + ref[index]
    return value


def pack_rows(rows):
    half = rows.shape[1] // 2
    return jnp.concatenate([rows[:, :half], rows[:, half:]], axis=0).astype(BF16)


def mean_square(blocks):
    sums = jnp.sum(jnp.sum(blocks, axis=0), axis=-1, keepdims=True)
    return sums * (1.0 / DM)


def rms_blocks(blocks):
    factor = lax.rsqrt(mean_square(blocks * blocks) + EPSILON)
    return factor


def rms_blocks_back(blocks, factor, gain_grad):
    inner = mean_square(blocks * gain_grad)
    return factor[None] * gain_grad - blocks * (factor * factor * factor * inner)[None]


class Grid:
    def __init__(self, n_dp):
        self.d, self.m = lax.axis_index("dp"), lax.axis_index("mp")
        self.n_y = minor_size(n_dp)
        self.n_z = n_dp // self.n_y
        self.z, self.y = lax.div(self.d, self.n_y), lax.rem(self.d, self.n_y)

    def at(self, kz, ky):
        return lax.rem(self.z + kz, self.n_z) * self.n_y + lax.rem(self.y + ky, self.n_y)

    def before(self, kz, ky):
        return lax.rem(self.z + self.n_z - kz, self.n_z) * self.n_y + lax.rem(self.y + self.n_y - ky, self.n_y)


def bulk_sems(n_dp, pieces):
    n_y = minor_size(n_dp)
    z_sem = pltpu.SemaphoreType.DMA((n_dp // n_y, pieces))
    y_sem = pltpu.SemaphoreType.DMA((n_dp // n_y, n_y, pieces))
    return [z_sem, z_sem, y_sem, y_sem]


def if_piece(act, i, low, high):
    @pl.when((i >= low) & (i < high))
    def _():
        act(i)


def each_piece(act, low, high):
    def body(i, carry):
        act(i)
        return carry

    lax.fori_loop(low, high, body, 0)


class Paced:
    def paced_send(self, u, first, num, den):
        self._at(self.send, u, first, num, den)

    def paced_forward(self, u, first, num, den):
        self._at(self.forward, u, first, num, den)

    def _at(self, act, u, first, num, den):
        far = 64 * num
        done = lambda t: lax.div((t - first) * den + far, num)
        new, old = done(u), done(u - 1)
        for step in range(-(-den // num)):
            i = old + 1 + step - 64

            @pl.when((new - 64 >= i) & (i >= 0) & (i < self.pieces))
            def _(i=i):
                act(i)

    @staticmethod
    def after(pieces, first, num, den, ticks):
        return min(pieces, max(0, (ticks - 1 - first) * den // num + 1)) if ticks > first else 0


class BulkGather(Paced):
    def __init__(self, grid, pieces, piece, z_ss, z_rs, y_ss, y_rs):
        self.g, self.pieces, self.piece = grid, pieces, piece
        self.z_ss, self.z_rs, self.y_ss, self.y_rs = z_ss, z_rs, y_ss, y_rs

    def z_copy(self, kz, i, owner):
        return pltpu.make_async_remote_copy(
            src_ref=self.piece(self.g.d, i), dst_ref=self.piece(owner, i), send_sem=self.z_ss.at[kz, i],
            recv_sem=self.z_rs.at[kz, i], device_id=(self.g.at(kz, 0), self.g.m), device_id_type=MESH)

    def y_copy(self, kz, ky, i, owner):
        return pltpu.make_async_remote_copy(
            src_ref=self.piece(self.g.before(kz, 0), i), dst_ref=self.piece(owner, i),
            send_sem=self.y_ss.at[kz, ky, i], recv_sem=self.y_rs.at[kz, ky, i],
            device_id=(self.g.at(0, ky), self.g.m), device_id_type=MESH)

    def send(self, i):
        for kz in range(1, self.g.n_z):
            self.z_copy(kz, i, self.g.d).start()
        for ky in range(1, self.g.n_y):
            self.y_copy(0, ky, i, self.g.d).start()

    def forward(self, i):
        for kz in range(1, self.g.n_z):
            self.z_copy(kz, i, self.g.before(kz, 0)).wait_recv()
            for ky in range(1, self.g.n_y):
                self.y_copy(kz, ky, i, self.g.before(kz, 0)).start()

    def finish_piece(self, i):
        for kz in range(1, self.g.n_z):
            self.z_copy(kz, i, self.g.d).wait_send()
        for kz in range(self.g.n_z):
            for ky in range(1, self.g.n_y):
                self.y_copy(kz, ky, i, self.g.before(kz, ky)).wait()

    def finish(self):
        each_piece(self.finish_piece, 0, self.pieces)


def line_sems(n_dp, pieces):
    n_y = minor_size(n_dp)
    n_z = n_dp // n_y
    return [pltpu.SemaphoreType.DMA((n_z, pieces))] * 4 + [pltpu.SemaphoreType.DMA((n_z, n_y, pieces))] * 2


class LineGather:
    def __init__(self, grid, pieces, piece, up_ss, up_rs, down_ss, down_rs, y_ss, y_rs):
        self.g, self.pieces, self.piece = grid, pieces, piece
        self.up, self.down, self.y_ss, self.y_rs = (up_ss, up_rs), (down_ss, down_rs), y_ss, y_rs
        self.ticks = pieces + grid.n_z - 1

    def block(self, z, y):
        return z * self.g.n_y + y

    def other_y(self, ky):
        return lax.rem(self.g.y + ky, self.g.n_y)

    def before_y(self, ky):
        return lax.rem(self.g.y + self.g.n_y - ky, self.g.n_y)

    def above(self):
        return (self.block(jnp.minimum(self.g.z + 1, self.g.n_z - 1), self.g.y), self.g.m)

    def below(self):
        return (self.block(jnp.maximum(self.g.z - 1, 0), self.g.y), self.g.m)

    def z_copy(self, sems, owner_z, i, target):
        block = self.piece(self.block(owner_z, self.g.y), i)
        return pltpu.make_async_remote_copy(
            src_ref=block, dst_ref=block, send_sem=sems[0].at[owner_z, i], recv_sem=sems[1].at[owner_z, i],
            device_id=target, device_id_type=MESH)

    def up_copy(self, owner_z, i):
        return self.z_copy(self.up, owner_z, i, self.above())

    def down_copy(self, owner_z, i):
        return self.z_copy(self.down, owner_z, i, self.below())

    def y_copy(self, owner_z, ky, i, in_y):
        return pltpu.make_async_remote_copy(
            src_ref=self.piece(self.block(owner_z, self.g.y), i), dst_ref=self.piece(self.block(owner_z, in_y), i),
            send_sem=self.y_ss.at[owner_z, ky, i], recv_sem=self.y_rs.at[owner_z, ky, i],
            device_id=(self.block(self.g.z, self.other_y(ky)), self.g.m), device_id_type=MESH)

    def along_y(self, owner_z, i):
        for ky in range(1, self.g.n_y):
            self.y_copy(owner_z, ky, i, self.g.y).start()

    def send(self, i):
        z, n_z = self.g.z, self.g.n_z

        @pl.when(z < n_z - 1)
        def _():
            self.up_copy(z, i).start()

        @pl.when(z > 0)
        def _():
            self.down_copy(z, i).start()

        self.along_y(z, i)

    def arrival(self, hop, i):
        z, n_z = self.g.z, self.g.n_z

        @pl.when(z - 1 - hop >= 0)
        def _():
            owner = jnp.maximum(z - 1 - hop, 0)
            self.up_copy(owner, i).wait_recv()

            @pl.when(z < n_z - 1)
            def _():
                self.up_copy(owner, i).start()

            self.along_y(owner, i)

        @pl.when(z + 1 + hop < n_z)
        def _():
            owner = jnp.minimum(z + 1 + hop, n_z - 1)
            self.down_copy(owner, i).wait_recv()

            @pl.when(z > 0)
            def _():
                self.down_copy(owner, i).start()

            self.along_y(owner, i)

    def tick(self, t):
        if_piece(self.send, t, 0, self.pieces)
        for hop in range(self.g.n_z - 1):
            if_piece(functools.partial(self.arrival, hop), t - 1 - hop, 0, self.pieces)

    def finish(self):
        z, n_z = self.g.z, self.g.n_z

        def piece_done(i):
            for owner in range(n_z):

                @pl.when((z >= owner) & (z < n_z - 1))
                def _():
                    self.up_copy(owner, i).wait_send()

                @pl.when((z <= owner) & (z > 0))
                def _():
                    self.down_copy(owner, i).wait_send()

                for ky in range(1, self.g.n_y):
                    self.y_copy(owner, ky, i, self.before_y(ky)).wait()

        each_piece(piece_done, 0, self.pieces)


def scatter_scratch(n_dp, pieces, rows, columns):
    n_y = minor_size(n_dp)
    n_z = n_dp // n_y
    slot = (pieces, rows, columns)
    return [
        pltpu.VMEM((n_z, max(n_y - 1, 1)) + slot, BF16),
        pltpu.VMEM((max(n_z - 1, 1),) + slot, BF16),
        pltpu.VMEM((max(n_z - 1, 1),) + slot, BF16),
    ] + bulk_sems(n_dp, pieces)


class BulkScatter(Paced):
    def __init__(self, grid, pieces, piece, out, recv_y, send_z, recv_z, z_ss, z_rs, y_ss, y_rs, sent=None):
        self.g, self.pieces, self.piece, self.out, self.sent = grid, pieces, piece, out, sent or piece
        self.recv_y, self.send_z, self.recv_z = recv_y, send_z, recv_z
        self.z_ss, self.z_rs, self.y_ss, self.y_rs = z_ss, z_rs, y_ss, y_rs

    def y_copy(self, kz, ky, i):
        return pltpu.make_async_remote_copy(
            src_ref=self.sent(self.g.at(kz, ky), i), dst_ref=self.recv_y.at[kz, ky - 1, i],
            send_sem=self.y_ss.at[kz, ky, i], recv_sem=self.y_rs.at[kz, ky, i],
            device_id=(self.g.at(0, ky), self.g.m), device_id_type=MESH)

    def z_copy(self, kz, i):
        return pltpu.make_async_remote_copy(
            src_ref=self.send_z.at[kz - 1, i], dst_ref=self.recv_z.at[kz - 1, i], send_sem=self.z_ss.at[kz, i],
            recv_sem=self.z_rs.at[kz, i], device_id=(self.g.at(kz, 0), self.g.m), device_id_type=MESH)

    def send(self, i):
        for kz in list(range(1, self.g.n_z)) + [0]:
            for ky in range(1, self.g.n_y):
                self.y_copy(kz, ky, i).start()

    def forward(self, i):
        for kz in list(range(1, self.g.n_z)) + [0]:
            value = self.piece(self.g.at(kz, 0), i)[...].astype(F32)
            for ky in range(1, self.g.n_y):
                self.y_copy(kz, ky, i).wait_recv()
                value = value + self.recv_y[kz, ky - 1, i].astype(F32)
            if kz == 0:
                self.out(i)[...] = value
            else:
                self.send_z[kz - 1, i] = value.astype(BF16)
                self.z_copy(kz, i).start()

    def finish_piece(self, i):
        total = self.out(i)[...]
        for kz in range(1, self.g.n_z):
            self.z_copy(kz, i).wait_recv()
            total = total + self.recv_z[kz - 1, i].astype(F32)
        self.out(i)[...] = total
        for kz in range(1, self.g.n_z):
            self.z_copy(kz, i).wait_send()
        for kz in range(self.g.n_z):
            for ky in range(1, self.g.n_y):
                self.y_copy(kz, ky, i).wait_send()

    def finish(self):
        each_piece(self.finish_piece, 0, self.pieces)


def cuts(rows):
    return max(rows // 32, min(rows // 16, 2))


def scatter_split(shard):
    parts = cuts(shard)
    return parts // 2, min(parts // 2 + 2 * parts + 1, 3 * parts - 1)


def cut_rows(ref, shard, first=0):
    parts = cuts(shard)
    small = shard // parts

    def piece(owner, i):
        rows = pl.ds(pl.multiple_of(owner * shard + lax.rem(i + first, parts) * small, small), small)
        return ref.at[lax.div(i + first, parts), rows, :]

    return piece


class Images:
    def __init__(self, lengths_ref):
        start = lax.axis_index("dp") * IMG_DEV
        self.is_long = jnp.where(lengths_ref[start] > SHORT, 1.0, 0.0)
        self.bias = (1.0 - self.is_long) * MASKED
        live = lengths_ref[start]
        for j in range(1, IMG_DEV):
            live = live + lengths_ref[start + j]
        self.live = live.astype(F32)


def fill_onehot(target, labels_ref):
    classes = lax.broadcasted_iota(jnp.int32, (1, NCLASS), 1)

    def body(i, carry):
        target[pl.ds(i, 1), :] = jnp.where(classes == labels_ref[i], 1.0, 0.0)
        return carry

    lax.fori_loop(0, target.shape[0], body, 0)


def own_features(target, sigmas_ref, freqs_ref, d):
    count, part = freqs_ref.shape[1], target.shape[1]

    def body(i, carry):
        target[pl.ds(i, 1), :] = jnp.full((1, part), sigmas_ref[i], F32)
        return carry

    lax.fori_loop(0, target.shape[0], body, 0)
    slices = count // part
    freqs = freqs_ref[0:1, 0:part]
    for k in range(1, slices):
        freqs = jnp.where(lax.rem(d, slices) == k, freqs_ref[0:1, k * part : (k + 1) * part], freqs)
    angles = 2.0 * math.pi * (jnp.log(target[...]) / 4.0) * freqs
    target[...] = jnp.where(d < slices, jnp.cos(angles), jnp.sin(angles))


def head_ones(width, heads):
    size = width // heads
    row = lax.div(lax.broadcasted_iota(jnp.int32, (width, 1), 0), size)
    column = lax.div(lax.broadcasted_iota(jnp.int32, (1, width), 1), size)
    return (row == column).astype(F32).astype(BF16)


def head_scales(scales_ref, width, heads):
    column = lax.div(lax.broadcasted_iota(jnp.int32, (1, width), 1), width // heads)
    row = jnp.full((1, width), scales_ref[0, 0], F32)
    for h in range(1, heads):
        row = jnp.where(column == h, scales_ref[0, h], row)
    return row


def loads(pairs, sems):
    copies = [pltpu.make_async_copy(source, target, sems.at[i]) for i, (source, target) in enumerate(pairs)]
    for copy in copies:
        copy.start()
    return copies


class Ranks:
    def __init__(self, n_mp):
        self.d, self.m = lax.axis_index("dp"), lax.axis_index("mp")
        self.n_x = n_mp // 2
        self.x, self.c = lax.div(self.m, 2), lax.rem(self.m, 2)
        self.sibling = (self.d, self.x * 2 + 1 - self.c)

    def rank(self, kx, same):
        core = jnp.where(same == 1, self.c, 1 - self.c)
        return lax.rem(self.x + kx, self.n_x) * 2 + core

    def chip(self, kx):
        return (self.d, lax.rem(self.x + kx, self.n_x) * 2 + self.c)

    def greet(self):
        greet([(2, lambda k: self.sibling), (self.n_x, self.chip)])


class Reduce:
    def __init__(self, ranks, core_send, core_recv, x_send, x_recv, sems):
        self.r = ranks
        self.core_send, self.core_recv, self.x_send, self.x_recv = core_send, core_recv, x_send, x_recv
        self.sems = sems

    def core_copy(self, kx):
        return pltpu.make_async_remote_copy(
            src_ref=self.core_send.at[kx], dst_ref=self.core_recv.at[kx], send_sem=self.sems.at[0, kx],
            recv_sem=self.sems.at[1, kx], device_id=self.r.sibling, device_id_type=MESH)

    def x_copy(self, kx):
        return pltpu.make_async_remote_copy(
            src_ref=self.x_send.at[kx], dst_ref=self.x_recv.at[kx], send_sem=self.sems.at[2, kx],
            recv_sem=self.sems.at[3, kx], device_id=self.r.chip(kx), device_id_type=MESH)

    def other(self, kx, part):
        self.core_send[kx] = part.astype(BF16)
        self.core_copy(kx).start()

    def same(self, kx, part):
        self.core_copy(kx).wait_recv()
        self.x_send[kx] = (part + self.core_recv[kx].astype(F32)).astype(BF16)
        self.x_copy(kx).start()

    def finish(self, part):
        self.core_copy(0).wait_recv()
        total = part + self.core_recv[0].astype(F32)
        for kx in range(1, self.r.n_x):
            self.x_copy(kx).wait_recv()
            total = total + self.x_recv[kx].astype(F32)
        return total

    def drain(self):
        self.core_copy(0).wait_send()
        for kx in range(1, self.r.n_x):
            self.core_copy(kx).wait_send()
            self.x_copy(kx).wait_send()


def reduce_scratch(n_mp, rows):
    slots = pltpu.VMEM((n_mp // 2, rows, D), BF16)
    return [slots, slots, slots, slots, pltpu.SemaphoreType.DMA((4, n_mp // 2))]


class Gather:
    def __init__(self, ranks, rows, buffer, sems):
        self.r, self.rows, self.buffer, self.sems = ranks, rows, buffer, sems

    def at(self, rank):
        return self.buffer.at[pl.ds(pl.multiple_of(rank * self.rows, self.rows), self.rows), :]

    def x_copy(self, kx, slot):
        return pltpu.make_async_remote_copy(
            src_ref=self.at(self.r.m), dst_ref=self.at(slot), send_sem=self.sems.at[0, kx],
            recv_sem=self.sems.at[1, kx], device_id=self.r.chip(kx), device_id_type=MESH)

    def core_copy(self, kx, out_slot, in_slot):
        return pltpu.make_async_remote_copy(
            src_ref=self.at(out_slot), dst_ref=self.at(in_slot), send_sem=self.sems.at[2, kx],
            recv_sem=self.sems.at[3, kx], device_id=self.r.sibling, device_id_type=MESH)

    def start(self):
        for kx in range(1, self.r.n_x):
            self.x_copy(kx, self.r.m).start()
        self.core_copy(0, self.r.m, self.r.m).start()

    def from_chip(self, kx):
        return lax.rem(self.r.x + self.r.n_x - kx, self.r.n_x) * 2 + self.r.c

    def from_core(self, kx):
        return lax.rem(self.r.x + self.r.n_x - kx, self.r.n_x) * 2 + 1 - self.r.c

    def forward(self, kx):
        slot = self.from_chip(kx)
        self.x_copy(kx, slot).wait_recv()
        self.core_copy(kx, slot, slot).start()

    def arrived(self, kx):
        self.core_copy(kx, self.r.m, self.from_core(kx)).wait_recv()

    def drain(self):
        for kx in range(1, self.r.n_x):
            self.x_copy(kx, self.r.m).wait_send()
        for kx in range(self.r.n_x):
            self.core_copy(kx, self.r.m, self.r.m).wait_send()


def gather_sems(n_mp):
    return pltpu.SemaphoreType.DMA((4, n_mp // 2))


def head_sums(values, ones):
    return two_part_left(dot_nn, values, ones)


def row_sums_factor(values):
    return lax.rsqrt(jnp.mean(values * values, axis=-1, keepdims=True) + EPSILON)


def image_scale(info, mods_ref, which, image):
    is_long = info.is_long
    row = mods_ref[which, pl.ds(image, 1), :]
    return 1.0 + (is_long * mods_ref[which, 0:1, :] + (1.0 - is_long) * row)


def column_bias(info, image, columns_shape, short):
    keys = lax.broadcasted_iota(jnp.int32, columns_shape, 0)
    own = (keys >= image * short) & (keys < (image + 1) * short)
    return jnp.where(own, 0.0, info.bias)


def forward_kernel(
    n_dp, n_mp, heads,
    lengths_ref, sigmas_ref, labels_ref, scales_ref, freqs_ref, x_ref,
    in_ref, out_ref, up_ref, time_ref, class_ref, mapup_ref, mapdown_ref, mod_ref, gains_ref,
    mods_ref, emb_ref, hid_ref, gated_ref, mixed_ref, feats_ref, wg_out, wf_out,
    q_out, k_out, v_out, normed_out, att_ref, stats_ref, mid_ref, nm_ref,
    wg_ref, q_ref, k_ref, v_ref, normed_ref, wf_ref, onehot_s, ones_ref, store_sem,
    in_s, out_s, up_s, time_s, class_s, mapup_s, mapdown_s, mod_s, gains_s, load_sem,
    send_a, recv_a, own_a, send_h, recv_h, own_g, recv_g, own_x, recv_x, own_m, send_o, recv_o,
    dp_ss, dp_rs, mp_ss, mp_rs, a_us, a_ur, a_ds, a_dr, a_ys, a_yr, f_us, f_ur, f_ds, f_dr, f_ys, f_yr,
    qu_s, ku_s, vt_s, part_s, core_send, core_recv, x_send, x_recv, sems,
):
    r = Ranks(n_mp)
    grid = Grid(n_dp)
    d, m = r.d, r.m
    images, part = feats_ref.shape
    info = Images(lengths_ref)
    copies = loads(
        (
            (time_ref.at[0], time_s),
            (in_ref.at[0], in_s),
            (out_ref.at[0], out_s),
            (class_ref.at[0], class_s),
            (gains_ref, gains_s),
            (up_ref.at[0], up_s),
            (mapup_ref.at[0], mapup_s),
            (mapdown_ref.at[0], mapdown_s),
            (mod_ref.at[0], mod_s),
        ),
        load_sem,
    )
    map_copies = [copies[0]] + copies[3:5] + copies[6:]
    greet(
        [
            (n_dp, lambda k: (lax.rem(d + k, n_dp), m)),
            (n_mp, lambda k: (d, lax.rem(m + k, n_mp))),
        ]
    )
    own_features(feats_ref, sigmas_ref, freqs_ref, d)
    shard = in_s.shape[1]
    mine = pl.ds(pl.multiple_of(d * shard, shard), shard)
    attn = LineGather(
        grid, 4, lambda dd, i: wg_ref.at[i, pl.ds(pl.multiple_of(dd * shard, shard), shard), :],
        a_us, a_ur, a_ds, a_dr, a_ys, a_yr)
    up_w = LineGather(
        grid, 2 * cuts(shard), cut_rows(wf_ref, shard), f_us, f_ur, f_ds, f_dr, f_ys, f_yr
    )

    def dp_ex(stage):
        return Exchange(n_dp, d, lambda p: (p, m), dp_ss.at[stage], dp_rs.at[stage])

    copies[1].wait()
    for c in range(3):
        wg_ref[c, mine, :] = in_s[c].astype(BF16)
    copies[2].wait()
    wg_ref[3, mine, :] = out_s[...].T.astype(BF16)
    map_copies[0].wait()
    partial = dot_nn(feats_ref[...].astype(BF16), time_s[...].astype(BF16))
    for p in range(n_dp):
        send_a[p] = partial[:, p * part : (p + 1) * part]
    ex = dp_ex(0)
    ex.start(lambda p: send_a.at[p], recv_a)
    attn.tick(0)
    recv_a[d] = send_a[d]
    copies[5].wait()
    for c in range(2):
        wf_ref[c, mine, :] = up_s[:, c, :].astype(BF16)
    fill_onehot(onehot_s, labels_ref)
    ones_ref[...] = head_ones(q_ref.shape[1], heads)
    for copy in map_copies[1:]:
        copy.wait()
    e_cols = dot_nt(onehot_s[...].astype(BF16), class_s[...].astype(BF16))
    own_a[images:, :] = jnp.zeros((8, part), F32)
    for g in range(3):
        own_a[images + g : images + g + 1, :] = gains_s[g, 0:1, :].astype(BF16).astype(F32)
    ex.wait(lambda p: send_a.at[p], recv_a)
    own_a[0:images, :] = total_of(recv_a, n_dp) + e_cols
    ex = dp_ex(1)
    ex.start(lambda p: own_a, emb_ref)
    attn.tick(1)
    emb_ref[d] = own_a[...]
    ex.wait(lambda p: own_a, emb_ref)
    gains = emb_ref[:, images:, :]
    emb = emb_ref[:, 0:images, :]
    unit = emb * rms_blocks(emb)[None] * gains[:, 0:1, :]
    unit_factor = rms_blocks(unit)
    own_x[0] = (emb_ref[d][0:images] * rms_blocks(emb)) * emb_ref[d][images : images + 1]
    unit_own = own_x[0]
    pre_own = (unit_own * unit_factor * emb_ref[d][images + 1 : images + 2]).astype(BF16)
    for c in range(2):
        part = dot_nn(pre_own, mapup_s[:, c, :].astype(BF16))
        for p in range(n_dp):
            send_h[p, c] = part[p * IMG_DEV : (p + 1) * IMG_DEV, :]
    ex = dp_ex(2)
    ex.start(lambda p: send_h.at[p], recv_h)
    attn.tick(2)
    recv_h[d] = send_h[d]
    ex.wait(lambda p: send_h.at[p], recv_h)
    hidden = total_of(recv_h, n_dp)
    hid_ref[...] = hidden
    own_g[...] = (hidden[0] * gelu_parts(hidden[1])[0]).astype(BF16).astype(F32)
    ex = dp_ex(3)
    ex.start(lambda p: own_g, recv_g)
    attn.tick(3)
    recv_g[d] = own_g[...]
    ex.wait(lambda p: own_g, recv_g)
    for p in range(n_dp):
        gated_ref[p * IMG_DEV : (p + 1) * IMG_DEV, :] = recv_g[p]
    own_x[0] = dot_nt(gated_ref[...].astype(BF16), mapdown_s[...].astype(BF16))
    ex = Exchange(n_mp, m, lambda p: (d, p), mp_ss.at[0], mp_rs.at[0])
    ex.start(lambda p: own_x.at[0], recv_x)
    attn.tick(4)
    up_w.tick(0)
    recv_x[m] = own_x[0]
    ex.wait(lambda p: own_x.at[0], recv_x)
    own_m[...] = total_of(recv_x, n_mp) + unit_own
    ex = dp_ex(4)
    ex.start(lambda p: own_m, mixed_ref)
    attn.tick(5)
    up_w.tick(1)
    mixed_ref[d] = own_m[...]
    ex.wait(lambda p: own_m, mixed_ref)
    mixed_factor = rms_blocks(mixed_ref[...])
    cond_own = (own_m[...] * mixed_factor * emb_ref[d][images + 2 : images + 3]).astype(BF16)
    for c in range(2):
        part = dot_nn(cond_own, mod_s[:, c, :].astype(BF16))
        for p in range(n_dp):
            send_o[p, c] = part[p * IMG_DEV : (p + 1) * IMG_DEV, :]
    ex = dp_ex(5)
    ex.start(lambda p: send_o.at[p], recv_o)
    attn.tick(6)
    up_w.tick(2)
    recv_o[d] = send_o[d]
    ex.wait(lambda p: send_o.at[p], recv_o)
    mods_ref[...] = total_of(recv_o, n_dp)
    each_piece(attn.tick, 7, attn.ticks)
    attn.finish()
    tokens = x_ref.shape[0]
    rows = tokens // n_mp
    width = q_ref.shape[1]
    size = width // heads
    red = Reduce(r, core_send, core_recv, x_send, x_recv, sems)
    at = lambda b: pl.ds(pl.multiple_of(b * rows, rows), rows)
    image_of = lambda b: lax.div(b * rows, SHORT)

    scale_row = head_scales(scales_ref, q_ref.shape[1], heads)

    def project(b, carry):
        xb = x_ref[at(b), :].astype(F32)
        normed = (xb * row_sums_factor(xb) * image_scale(info, mods_ref, 0, image_of(b))).astype(BF16)
        normed_ref[at(b), :] = normed
        q = dot_nn(normed, wg_ref[0])
        q_ref[at(b), :] = q
        qu_s[at(b), :] = (q * lax.rsqrt(head_sums(q * q, ones_ref[...]) + EPSILON) * scale_row).astype(BF16)
        k = dot_nn(normed, wg_ref[1])
        k_ref[at(b), :] = k
        ku_s[at(b), :] = (k * lax.rsqrt(head_sums(k * k, ones_ref[...]) + EPSILON)).astype(BF16)
        v = dot_nn(normed, wg_ref[2])
        v_ref[at(b), :] = v.astype(BF16)
        vt_s[:, at(b)] = v.T.astype(BF16)

        @pl.when(lax.rem(b, 2) == 0)
        def _():
            up_w.tick(3 + lax.div(b, 2))

        return carry

    lax.fori_loop(0, n_mp, project, 0)
    stores = [
        pltpu.make_async_copy(source, target, store_sem.at[n])
        for n, (source, target) in enumerate(
            ((wg_ref, wg_out), (q_ref, q_out), (k_ref, k_out), (v_ref, v_out), (normed_ref, normed_out))
        )
    ]
    for copy in stores:
        copy.start()
    first_tick = 3 + (n_mp + 1) // 2
    lanes = lax.broadcasted_iota(jnp.int32, (1, width), 1)

    def block(j, carry):
        up_w.tick(first_tick + 2 * j)
        kx, same = lax.rem(1 + lax.div(j, 2), r.n_x), lax.rem(j, 2)
        b = r.rank(kx, same)
        bias = column_bias(info, image_of(b), (tokens, 1), SHORT)
        qu = qu_s[at(b), :]
        outs = []
        for h in range(heads):
            mask = ((lanes >= h * size) & (lanes < (h + 1) * size)).astype(F32).astype(BF16)
            scores = dot_nt(ku_s[...], qu * mask) + bias
            top = jnp.max(scores, axis=0, keepdims=True)
            expon = jnp.exp(scores - top)
            total = jnp.sum(expon, axis=0, keepdims=True)
            stats_ref[h : h + 1, at(b)] = top + jnp.log(total)
            if h == heads // 2:
                up_w.tick(first_tick + 2 * j + 1)
            outs.append(dot_nn(vt_s[h * size : (h + 1) * size, :], expon.astype(BF16)) / total)
        att = jnp.concatenate(outs, axis=0).T.astype(BF16)
        att_ref[at(b), :] = att
        part_s[...] = dot_nt(att, wg_ref[3])

        @pl.when(same == 0)
        def _():
            red.other(kx, part_s[...])

        @pl.when((same == 1) & (kx > 0))
        def _():
            red.same(kx, part_s[...])

        return carry

    lax.fori_loop(0, n_mp, block, 0)
    each_piece(up_w.tick, first_tick + 2 * n_mp, up_w.ticks)
    if heads < 8:
        stats_ref[heads:8, :] = jnp.zeros((8 - heads, tokens), F32)
    middle = x_ref[at(r.m), :].astype(F32) + red.finish(part_s[...])
    mid_ref[...] = middle
    nm_ref[...] = (middle * row_sums_factor(middle) * image_scale(info, mods_ref, 1, image_of(r.m))).astype(BF16)
    red.drain()
    up_w.finish()
    stores.append(pltpu.make_async_copy(wf_ref, wf_out, store_sem.at[5]))
    stores[-1].start()
    for copy in stores:
        copy.wait()


def forward_part(n_dp, n_mp, lengths, sigmas, labels, scales, freqs, x, layer_states, map_states, gains_state):
    images, part = sigmas.shape[0], map_states[0].shape[1]
    units_map = map_states[2].shape[3]
    shard, _, units = layer_states[2].shape[1:]
    width, heads = layer_states[0].shape[3], scales.shape[1]
    tokens = x.shape[0]
    rows = tokens // n_mp
    states = (*layer_states, *map_states)
    f32 = lambda *dims: jax.ShapeDtypeStruct(dims, F32)
    bf16 = lambda *dims: jax.ShapeDtypeStruct(dims, BF16)
    return pl.pallas_call(
        functools.partial(forward_kernel, n_dp, n_mp, heads),
        out_shape=(
            f32(2, IMG_DEV, D),
            f32(n_dp, images + 8, part),
            f32(2, IMG_DEV, units_map),
            f32(images, units_map),
            f32(n_dp, images, part),
            f32(images, part),
            bf16(4, D, width),
            bf16(2, D, units),
            f32(tokens, width),
            f32(tokens, width),
            bf16(tokens, width),
            bf16(tokens, D),
            bf16(tokens, width),
            f32(8, tokens),
            f32(rows, D),
            bf16(rows, D),
        ),
        in_specs=[SMEM_SPEC] * 4 + vmem_specs(2) + any_specs(9),
        out_specs=tuple(vmem_specs(6) + any_specs(6) + vmem_specs(4)),
        scratch_shapes=[
            pltpu.VMEM((4, D, width), BF16),
            pltpu.VMEM((tokens, width), F32),
            pltpu.VMEM((tokens, width), F32),
            pltpu.VMEM((tokens, width), BF16),
            pltpu.VMEM((tokens, D), BF16),
            pltpu.VMEM((2, D, units), BF16),
            pltpu.VMEM((images, NCLASS), F32),
            pltpu.VMEM((width, width), BF16),
            pltpu.SemaphoreType.DMA((6,)),
        ]
        + [pltpu.VMEM(state.shape[1:], F32) for state in states]
        + [
            pltpu.VMEM(gains_state.shape, F32),
            pltpu.SemaphoreType.DMA((9,)),
            pltpu.VMEM((n_dp, images, part), F32),
            pltpu.VMEM((n_dp, images, part), F32),
            pltpu.VMEM((images + 8, part), F32),
            pltpu.VMEM((n_dp, 2, IMG_DEV, units_map), F32),
            pltpu.VMEM((n_dp, 2, IMG_DEV, units_map), F32),
            pltpu.VMEM((IMG_DEV, units_map), F32),
            pltpu.VMEM((n_dp, IMG_DEV, units_map), F32),
            pltpu.VMEM((1, images, part), F32),
            pltpu.VMEM((n_mp, images, part), F32),
            pltpu.VMEM((images, part), F32),
            pltpu.VMEM((n_dp, 2, IMG_DEV, D), F32),
            pltpu.VMEM((n_dp, 2, IMG_DEV, D), F32),
            pltpu.SemaphoreType.DMA((6, n_dp)),
            pltpu.SemaphoreType.DMA((6, n_dp)),
            pltpu.SemaphoreType.DMA((1, n_mp)),
            pltpu.SemaphoreType.DMA((1, n_mp)),
        ]
        + line_sems(n_dp, 4)
        + line_sems(n_dp, 2 * cuts(shard))
        + [
            pltpu.VMEM((tokens, width), BF16),
            pltpu.VMEM((tokens, width), BF16),
            pltpu.VMEM((width, tokens), BF16),
            pltpu.VMEM((rows, D), F32),
        ]
        + reduce_scratch(n_mp, rows),
        compiler_params=pltpu.CompilerParams(
            collective_id=0, has_side_effects=True, vmem_limit_bytes=VMEM_BYTES
        ),
        name="forward_part",
    )(lengths, sigmas, labels, scales, freqs, x, *states, gains_state)


def ffn_kernel(
    n_dp, n_mp, lengths_ref, nm_ref, mods_ref, mid_ref, cot_ref, wf_ref, down_ref,
    gd_ref, dmid_ref, fmod_ref, gated_out, wd_out, gw_out,
    w_s, cot_s, nm_s, gated_s, gate_s, slope_s, dh_s, dz_s, part_s, gw_s, gather_sem,
    b_core_send, b_core_recv, b_x_send, b_x_recv, b_sems,
    down_s, wd_s, load_sem, store_sem, w_zs, w_zr, w_ys, w_yr,
    recv_y, send_z, recv_z, g_zs, g_zr, g_ys, g_yr,
):
    r = Ranks(n_mp)
    grid = Grid(n_dp)
    info = Images(lengths_ref)
    copies = loads(((down_ref.at[0], down_s), (wf_ref, w_s), (cot_ref, cot_s)), load_sem)
    rows = nm_ref.shape[0]
    tokens = rows * n_mp
    at = lambda b: pl.ds(pl.multiple_of(b * rows, rows), rows)
    image_of = lambda b: lax.div(b * rows, SHORT)

    greet(
        [
            (n_dp, lambda k: (lax.rem(r.d + k, n_dp), r.m)),
            (2, lambda k: r.sibling),
            (r.n_x, r.chip),
        ]
    )
    shard = D // n_dp
    parts = cuts(shard)
    small = shard // parts
    copies[0].wait()
    wd_s[0, pl.ds(pl.multiple_of(r.d * shard, shard), shard), :] = down_s[...].T.astype(BF16)
    down_w = BulkGather(grid, parts, cut_rows(wd_s, shard), w_zs, w_zr, w_ys, w_yr)
    first = scatter_split(shard)[0]
    down_g = BulkScatter(
        grid, first, cut_rows(gw_s, shard), lambda i: gd_ref.at[i],
        recv_y, send_z, recv_z, g_zs, g_zr, g_ys, g_yr)
    each_piece(down_w.send, 0, parts)
    nm_s[at(r.m), :] = nm_ref[...]
    gather = Gather(r, rows, nm_s, gather_sem)
    gather.start()
    copies[1].wait()
    bwd = Reduce(r, b_core_send, b_core_recv, b_x_send, b_x_recv, b_sems)

    def forward(j, carry):
        kx = lax.div(j, 2)
        same = jnp.where(kx == 0, 1 - lax.rem(j, 2), lax.rem(j, 2))
        b = r.rank(kx, same)
        back_kx = lax.rem(r.n_x - kx, r.n_x)

        if_piece(down_w.forward, j - 1, 0, min(2, parts))

        @pl.when((same == 0) & (kx > 0))
        def _():
            gather.forward(back_kx)

        @pl.when(same == 0)
        def _():
            gather.arrived(back_kx)

        nm = nm_s[at(b), :]
        hidden = dot_nn(nm, w_s[0])
        gate = dot_nn(nm, w_s[1])
        value, slope = gelu_parts(gate)
        gated = (hidden * value).astype(BF16)
        gated_s[at(b), :] = gated
        gate_s[at(b), :] = value
        slope_s[at(b), :] = hidden * slope
        if_piece(down_w.forward, j, 2, parts)
        return carry

    lax.fori_loop(0, n_mp, forward, 0)
    copies[2].wait()

    def live_rows(b):
        position = lax.broadcasted_iota(jnp.int32, (rows, 1), 0) + b * rows
        return (position.astype(F32) < info.live).astype(F32)

    def live_cotangent(b, carry):
        dz_s[at(b), :] = (cot_s[at(b), :].astype(F32) * live_rows(b)).astype(BF16)
        return carry

    lax.fori_loop(0, n_mp, live_cotangent, 0)
    step = 512

    def down_gradient(i, carry):
        cols = pl.ds(pl.multiple_of(i * step, step), step)
        gw_s[0, cols, :] = dot_tn(dz_s[:, cols], gated_s[...]).astype(BF16)
        return carry

    lax.fori_loop(0, D // step, down_gradient, 0)
    each_piece(down_g.send, 0, first)
    each_piece(down_w.forward, n_mp, parts)
    down_w.finish()
    stores = [
        pltpu.make_async_copy(source, target, store_sem.at[n])
        for n, (source, target) in enumerate(((gated_s, gated_out), (wd_s.at[0], wd_out), (gw_s.at[0], gw_out.at[0])))
    ]
    for copy in stores:
        copy.start()

    def backward(j, carry):
        kx, same = lax.rem(1 + lax.div(j, 2), r.n_x), lax.rem(j, 2)
        b = r.rank(kx, same)
        d_gated = dot_nn(dz_s[at(b), :], wd_s[0])
        d_value = (d_gated * gate_s[at(b), :]).astype(BF16)
        d_gate = (d_gated * slope_s[at(b), :]).astype(BF16)
        dh_s[0, at(b), :] = d_value
        dh_s[1, at(b), :] = d_gate
        part_s[...] = dot_nt(d_value, w_s[0]) + dot_nt(d_gate, w_s[1])

        @pl.when(same == 0)
        def _():
            bwd.other(kx, part_s[...])

        @pl.when((same == 1) & (kx > 0))
        def _():
            bwd.same(kx, part_s[...])

        return carry

    lax.fori_loop(0, n_mp, backward, 0)

    def up_gradient(i, carry):
        if_piece(down_g.forward, i, 0, first)
        cols = pl.ds(pl.multiple_of(i * step, step), step)
        left = nm_s[:, cols]
        for c in range(2):
            gw_s[1 + c, cols, :] = dot_tn(left, dh_s[c]).astype(BF16)
        return carry

    lax.fori_loop(0, D // step, up_gradient, 0)

    each_piece(down_g.forward, D // step, first)
    up_store = pltpu.make_async_copy(gw_s.at[pl.ds(1, 2)], gw_out.at[pl.ds(1, 2)], store_sem.at[3])
    up_store.start()
    d_nm = bwd.finish(part_s[...])
    middle = mid_ref[...]
    live = live_rows(r.m)
    scale = image_scale(info, mods_ref, 1, image_of(r.m))
    factor = row_sums_factor(middle)
    inner = jnp.mean(middle * scale * d_nm, axis=-1, keepdims=True)
    dmid_ref[...] = cot_s[at(r.m), :].astype(F32) * live + (
        factor * scale * d_nm - middle * (factor * factor * factor * inner)
    )
    fmod_ref[...] = jnp.sum(d_nm * middle * factor, axis=0, keepdims=True)
    gather.drain()
    bwd.drain()
    down_g.finish()
    for copy in stores + [up_store]:
        copy.wait()


def ffn(n_dp, n_mp, lengths, nm, mods, mid, cot, wf, down_state):
    rows = nm.shape[0]
    tokens = rows * n_mp
    units = wf.shape[2]
    shard = D // n_dp
    parts = cuts(shard)
    first = scatter_split(shard)[0]
    shape = jax.ShapeDtypeStruct
    return pl.pallas_call(
        functools.partial(ffn_kernel, n_dp, n_mp),
        out_shape=(
            shape((first, shard // parts, units), F32),
            shape((rows, D), F32),
            shape((1, D), F32),
            shape((tokens, units), BF16),
            shape((D, units), BF16),
            shape((3, D, units), BF16),
        ),
        in_specs=[SMEM_SPEC] + vmem_specs(3) + any_specs(3),
        out_specs=tuple(vmem_specs(3) + any_specs(3)),
        scratch_shapes=[
            pltpu.VMEM((2, D, units), BF16),
            pltpu.VMEM((tokens, D), BF16),
            pltpu.VMEM((tokens, D), BF16),
            pltpu.VMEM((tokens, units), BF16),
            pltpu.VMEM((tokens, units), F32),
            pltpu.VMEM((tokens, units), F32),
            pltpu.VMEM((2, tokens, units), BF16),
            pltpu.VMEM((tokens, D), BF16),
            pltpu.VMEM((rows, D), F32),
            pltpu.VMEM((3, D, units), BF16),
            gather_sems(n_mp),
        ]
        + reduce_scratch(n_mp, rows)
        + [
            pltpu.VMEM(down_state.shape[1:], F32),
            pltpu.VMEM((1, D, units), BF16),
            pltpu.SemaphoreType.DMA((3,)),
            pltpu.SemaphoreType.DMA((4,)),
        ]
        + bulk_sems(n_dp, parts)
        + scatter_scratch(n_dp, first, shard // parts, units),
        compiler_params=pltpu.CompilerParams(
            collective_id=4, has_side_effects=True, vmem_limit_bytes=VMEM_BYTES
        ),
        name="ffn",
    )(lengths, nm, mods, mid, cot, wf, down_state)


def attn_backward_kernel(
    n_dp, n_mp, heads, lengths_ref, scales_ref, dmid_ref, mods_ref, q_ref, k_ref, stats_ref,
    gffn_ref, wg_any, v_any, normed_any, att_any, x_any,
    gw_ref, gf_ref, gin_ref, amod_ref, gscale_ref,
    gffn_s, wg_ref, v_ref, normed_ref, att_ref, x_ref, ones_ref, load_sem,
    qu_s, ku_s, kt_s, dy_s, dq_s, dk_s, dv_s, low_s, part_s, gather_sem,
    core_send, core_recv, x_send, x_recv, sems,
    recv_y, send_z, recv_z, f_zs, f_zr, f_ys, f_yr,
):
    r = Ranks(n_mp)
    info = Images(lengths_ref)
    rows = dmid_ref.shape[0]
    tokens = rows * n_mp
    width = q_ref.shape[1]
    size = width // heads
    at = lambda b: pl.ds(pl.multiple_of(b * rows, rows), rows)
    image_of = lambda b: lax.div(b * rows, SHORT)
    copies = loads(
        (
            (wg_any, wg_ref),
            (v_any, v_ref),
            (gffn_ref, gffn_s),
            (normed_any, normed_ref),
            (att_any, att_ref),
            (x_any.at[at(r.m), :], x_ref),
        ),
        load_sem,
    )
    dy_s[at(r.m), :] = dmid_ref[...].astype(BF16)
    grid = Grid(n_dp)
    greet(
        [
            (n_dp, lambda k: (lax.rem(r.d + k, n_dp), r.m)),
            (2, lambda k: r.sibling),
            (r.n_x, r.chip),
        ]
    )
    gather = Gather(r, rows, dy_s, gather_sem)
    gather.start()
    shard = D // n_dp
    start, end = scatter_split(shard)
    ffn_g = BulkScatter(
        grid, end - start, cut_rows(gffn_s, shard, start), lambda i: gf_ref.at[i],
        recv_y, send_z, recv_z, f_zs, f_zr, f_ys, f_yr, sent=cut_rows(gffn_ref, shard, start))
    each_piece(ffn_g.send, 0, ffn_g.pieces)
    ones_ref[...] = head_ones(width, heads)
    scale_row = head_scales(scales_ref, width, heads)
    red = Reduce(r, core_send, core_recv, x_send, x_recv, sems)

    def units(b, carry):
        q, k = q_ref[at(b), :], k_ref[at(b), :]
        qu_s[at(b), :] = (q * lax.rsqrt(head_sums(q * q, ones_ref[...]) + EPSILON) * scale_row).astype(BF16)
        k_unit = k * lax.rsqrt(head_sums(k * k, ones_ref[...]) + EPSILON)
        ku_s[at(b), :] = k_unit.astype(BF16)
        kt_s[:, at(b)] = k_unit.T.astype(BF16)
        return carry

    lax.fori_loop(0, n_mp, units, 0)
    for copy in copies[:3]:
        copy.wait()
    dk_s[...] = jnp.zeros_like(dk_s)
    dv_s[...] = jnp.zeros_like(dv_s)
    lanes = lax.broadcasted_iota(jnp.int32, (1, width), 1)

    pace = (heads * n_mp // 8, 7 * heads * n_mp, 6 * ffn_g.pieces)

    def block(j, carry):
        kx = lax.div(j, 2)
        same = 1 - lax.rem(j, 2)
        b = r.rank(kx, same)
        back_kx = lax.rem(r.n_x - kx, r.n_x)

        @pl.when((same == 1) & (kx > 0))
        def _():
            gather.forward(back_kx)

        @pl.when(same == 0)
        def _():
            gather.arrived(back_kx)

        d_att = dot_nn(dy_s[at(b), :], wg_ref[3]).astype(BF16)
        bias = column_bias(info, image_of(b), (tokens, 1), SHORT)
        qu = qu_s[at(b), :]
        outs = []
        for h in range(heads):
            mask = ((lanes >= h * size) & (lanes < (h + 1) * size)).astype(F32).astype(BF16)
            qh = qu * mask
            dh = d_att * mask
            probs = jnp.exp(dot_nt(ku_s[...], qh) + bias - stats_ref[h : h + 1, at(b)])
            ffn_g.paced_forward(heads * j + h, *pace)
            d_probs = dot_nt(v_ref[...], dh)
            inner = jnp.sum(probs * d_probs, axis=0, keepdims=True)
            d_scores = (probs * (d_probs - inner)).astype(BF16)
            dv_s[...] = dv_s[...] + dot_nn(probs.astype(BF16), dh)
            dk_s[...] = dk_s[...] + dot_nn(d_scores, qh)
            outs.append(dot_nn(kt_s[h * size : (h + 1) * size, :], d_scores))
        dq_s[at(b), :] = jnp.concatenate(outs, axis=0).T
        return carry

    lax.fori_loop(0, n_mp, block, 0)

    def inputs(j, scale_grad):
        kx, same = lax.rem(1 + lax.div(j, 2), r.n_x), lax.rem(j, 2)
        b = r.rank(kx, same)
        q, k = q_ref[at(b), :], k_ref[at(b), :]
        q_factor = lax.rsqrt(head_sums(q * q, ones_ref[...]) + EPSILON)
        k_factor = lax.rsqrt(head_sums(k * k, ones_ref[...]) + EPSILON)
        dqu, dku = dq_s[at(b), :], dk_s[at(b), :]
        q_unit, k_unit = q * q_factor, k * k_factor
        q_along = dqu * q_unit
        d_q = (scale_row * q_factor * (dqu - q_unit * head_sums(q_along, ones_ref[...]))).astype(BF16)
        d_k = (k_factor * (dku - k_unit * head_sums(dku * k_unit, ones_ref[...]))).astype(BF16)
        d_v = dv_s[at(b), :].astype(BF16)
        low_s[at(b), 0:width] = d_q
        low_s[at(b), width : 2 * width] = d_k
        low_s[at(b), 2 * width : 3 * width] = d_v
        part_s[...] = dot_nt(d_q, wg_ref[0]) + dot_nt(d_k, wg_ref[1]) + dot_nt(d_v, wg_ref[2])

        @pl.when(same == 0)
        def _():
            red.other(kx, part_s[...])

        @pl.when((same == 1) & (kx > 0))
        def _():
            red.same(kx, part_s[...])

        ffn_g.paced_forward(heads * n_mp + j, *pace)
        return scale_grad + jnp.sum(q_along, axis=0, keepdims=True)

    gscale_ref[...] = lax.fori_loop(0, n_mp, inputs, jnp.zeros((1, width), F32))

    each_piece(ffn_g.forward, ffn_g.after(ffn_g.pieces, *pace, heads * n_mp + n_mp), ffn_g.pieces)
    for copy in copies[3:]:
        copy.wait()
    step = 512

    def weights(i, carry):
        cols = pl.ds(pl.multiple_of(i * step, step), step)
        value = dot_tn(normed_ref[:, cols], low_s[...]).astype(BF16)
        for c in range(3):
            gw_ref[c, cols, :] = value[:, c * width : (c + 1) * width]
        gw_ref[3, cols, :] = dot_tn(dy_s[:, cols], att_ref[...]).astype(BF16)
        return carry

    lax.fori_loop(0, D // step, weights, 0)

    d_normed = red.finish(part_s[...])
    x = x_ref[...].astype(F32)
    scale = image_scale(info, mods_ref, 0, image_of(r.m))
    factor = row_sums_factor(x)
    inner = jnp.mean(x * scale * d_normed, axis=-1, keepdims=True)
    gin_ref[...] = dmid_ref[...] + (factor * scale * d_normed - x * (factor * factor * factor * inner))
    amod_ref[...] = jnp.sum(d_normed * x * factor, axis=0, keepdims=True)
    gather.drain()
    red.drain()
    ffn_g.finish()


def attn_backward(n_dp, n_mp, lengths, scales, dmid, mods, q, k, stats, gffn, wg, v, normed, att, x):
    rows = dmid.shape[0]
    tokens = rows * n_mp
    width, heads = q.shape[1], scales.shape[1]
    shard = D // n_dp
    small = shard // cuts(shard)
    start, end = scatter_split(shard)
    shape = jax.ShapeDtypeStruct
    return pl.pallas_call(
        functools.partial(attn_backward_kernel, n_dp, n_mp, heads),
        out_shape=(
            shape(wg.shape, BF16),
            shape((end - start, small, gffn.shape[2]), F32),
            shape((rows, D), F32),
            shape((1, D), F32),
            shape((1, width), F32),
        ),
        in_specs=[SMEM_SPEC] * 2 + vmem_specs(5) + any_specs(6),
        out_specs=tuple(vmem_specs(5)),
        scratch_shapes=[
            pltpu.VMEM(gffn.shape, BF16),
            pltpu.VMEM(wg.shape, BF16),
            pltpu.VMEM((tokens, width), BF16),
            pltpu.VMEM((tokens, D), BF16),
            pltpu.VMEM((tokens, width), BF16),
            pltpu.VMEM((rows, D), BF16),
            pltpu.VMEM((width, width), BF16),
            pltpu.SemaphoreType.DMA((6,)),
            pltpu.VMEM((tokens, width), BF16),
            pltpu.VMEM((tokens, width), BF16),
            pltpu.VMEM((width, tokens), BF16),
            pltpu.VMEM((tokens, D), BF16),
            pltpu.VMEM((tokens, width), F32),
            pltpu.VMEM((tokens, width), F32),
            pltpu.VMEM((tokens, width), F32),
            pltpu.VMEM((tokens, 3 * width), BF16),
            pltpu.VMEM((rows, D), F32),
            gather_sems(n_mp),
        ]
        + reduce_scratch(n_mp, rows)
        + scatter_scratch(n_dp, end - start, small, gffn.shape[2]),
        compiler_params=pltpu.CompilerParams(
            collective_id=5, has_side_effects=True, vmem_limit_bytes=VMEM_BYTES
        ),
        name="attn_backward",
    )(lengths, scales, dmid, mods, q, k, stats, gffn, wg, v, normed, att, x)


def squares(value):
    return jnp.sum(jnp.sum(value * value, axis=0, keepdims=True), axis=-1, keepdims=True)


def planes(ref):
    return squares(ref[:, 0, :]) + squares(ref[:, 1, :])


def back_kernel(
    n_dp, n_mp, heads,
    lengths_ref, labels_ref, grads_ref, amod_ref, fmod_ref, mid_ref, gin_ref, feats_ref, gd_ref, gu_ref, gscale_ref,
    emb_ref, hid_ref, gated_ref, mixed_ref,
    mapup_ref, mapdown_ref, mod_ref, gffn_ref, ffgated_ref, wd_ref,
    gattn_ref, gf_ref, out_all, gin_s, gmod_ref, gmd_ref, gmu_ref, gtime_ref, gclass_ref, ggain_ref, norm_ref,
    mapup_s, mapdown_s, mod_s, gffn_s, ffgated_s, wd_s, load_sem, own_r, full_e, onehot_s, out_sem, gin_sem,
    recv_q, stage_q, own_q, recv_d, full_d, own_c, recv_c, send_g, recv_g, own_h, recv_h, full_h,
    own_p, recv_p, own_s, recv_s, own_n, all_dp, own_sum, all_mp,
    dp_ss, dp_rs, mp_ss, mp_rs,
    core_send, core_recv, x_send, x_recv, sems,
    recv_y, send_z, recv_z, a_zs, a_zr, a_ys, a_yr,
    f_recv_y, f_send_z, f_recv_z, f_zs, f_zr, f_ys, f_yr,
):
    r = Ranks(n_mp)
    d, m = r.d, r.m
    info = Images(lengths_ref)
    grid = Grid(n_dp)
    shard = gattn_ref.shape[1]
    start = scatter_split(shard)[1]
    tall = shard // 2
    attn_g = BulkScatter(
        grid, 8,
        lambda dd, i: grads_ref.at[
            lax.div(i, 2), pl.ds(pl.multiple_of(dd * shard + lax.rem(i, 2) * tall, tall), tall), :
        ],
        lambda i: gattn_ref.at[lax.div(i, 2), pl.ds(pl.multiple_of(lax.rem(i, 2) * tall, tall), tall), :],
        recv_y, send_z, recv_z, a_zs, a_zr, a_ys, a_yr)
    ffn_g = BulkScatter(
        grid, 3 * cuts(shard) - start, cut_rows(gffn_s, shard, start - 2 * cuts(shard)), lambda i: gf_ref.at[i],
        f_recv_y, f_send_z, f_recv_z, f_zs, f_zr, f_ys, f_yr)
    images, own_cols = feats_ref.shape
    rows = mid_ref.shape[0]
    copies = loads(
        (
            (mod_ref.at[0], mod_s),
            (mapdown_ref.at[0], mapdown_s),
            (mapup_ref.at[0], mapup_s),
            (ffgated_ref, ffgated_s),
            (wd_ref, wd_s),
            (gffn_ref.at[pl.ds(2, 1)], gffn_s),
        ),
        load_sem,
    )
    greet(
        [
            (n_dp, lambda k: (lax.rem(d + k, n_dp), m)),
            (n_mp, lambda k: (d, lax.rem(m + k, n_mp))),
        ]
    )
    at = lambda b: pl.ds(pl.multiple_of(b * rows, rows), rows)
    gin_s[at(m), :] = gin_ref[...].astype(BF16)
    one = Gather(r, rows, out_all, out_sem)
    two = Gather(r, rows, gin_s, gin_sem)
    red = Reduce(r, core_send, core_recv, x_send, x_recv, sems)

    def branch(j):
        kx, same = (1 + j // 2) % r.n_x, j % 2
        part = dot_nt(ffgated_s[at(r.rank(kx, same)), :], wd_s[...])
        if same == 0:
            red.other(kx, part)
        elif kx > 0:
            red.same(kx, part)
        else:
            position = lax.broadcasted_iota(jnp.int32, (rows, 1), 0) + m * rows
            live = (position.astype(F32) < info.live).astype(F32)
            out_all[at(m), :] = ((mid_ref[...] + red.finish(part)) * live).astype(BF16)

    def branches(quarter):
        for j in range(quarter * n_mp // 4, (quarter + 1) * n_mp // 4):
            branch(j)

    own_r[0:1, :] = amod_ref[...]
    own_r[1:2, :] = fmod_ref[...]

    def dp_ex(stage):
        return Exchange(n_dp, d, lambda p: (p, m), dp_ss.at[stage], dp_rs.at[stage])

    def mp_ex(stage):
        return Exchange(n_mp, m, lambda p: (d, p), mp_ss.at[stage], mp_rs.at[stage])

    def local_squares():
        value = jnp.zeros((1, 1), F32)
        for i in range(gd_ref.shape[0]):
            value = value + squares(gd_ref[i])
        for i in range(gu_ref.shape[0]):
            value = value + squares(gu_ref[i])
        return value

    ex = mp_ex(0)
    ex.start(lambda p: own_r, recv_q)
    attn_g.send(0)
    copies[5].wait()
    ffn_g.send(0)
    fill_onehot(onehot_s, labels_ref)
    recv_q[m] = own_r[...]
    ex.wait(lambda p: own_r, recv_q)
    for image in range(IMG_DEV):
        for c in range(2):
            row = jnp.zeros((1, D), F32)
            for rank in range(n_mp):
                share = 1.0 - info.is_long if rank * rows // SHORT == image else 0.0
                if image == 0:
                    share = share + info.is_long
                row = row + share * recv_q[rank, c : c + 1, :]
            stage_q[c * IMG_DEV + image : c * IMG_DEV + image + 1, :] = row
    own_q[...] = pack_rows(stage_q[...])
    two.start()
    ex = dp_ex(0)
    ex.start(lambda p: own_q, recv_d)
    attn_g.send(1)
    for copy in copies[:5]:
        copy.wait()
    branches(0)
    ffn_g.forward(0)
    recv_d[d] = own_q[...]
    gains_own = emb_ref[d][images:]
    emb = emb_ref[:, 0:images, :]
    emb_factor = rms_blocks(emb)
    unit = emb * emb_factor[None] * emb_ref[:, images : images + 1, :]
    unit_factor = rms_blocks(unit)
    emb_own = emb_ref[d][0:images]
    unit_own = emb_own * emb_factor * gains_own[0:1]
    pre_own = (unit_own * unit_factor * gains_own[1:2]).astype(BF16)
    mixed = mixed_ref[...]
    mixed_factor = rms_blocks(mixed)
    mixed_own = mixed_ref[d]
    cond_own = (mixed_own * mixed_factor * gains_own[2:3]).astype(BF16)
    ex.wait(lambda p: own_q, recv_d)
    for p in range(n_dp):
        block = recv_d[p].astype(F32)
        for c in range(2):
            for half in range(2):
                first = (2 * half + c) * IMG_DEV
                full_d[c, p * IMG_DEV : (p + 1) * IMG_DEV, half * D // 2 : (half + 1) * D // 2] = block[
                    first : first + IMG_DEV
                ]
    own_c[...] = two_part_left(dot_nt, full_d[0], mod_s[:, 0, :].astype(BF16)) + two_part_left(
        dot_nt, full_d[1], mod_s[:, 1, :].astype(BF16)
    )
    ex = dp_ex(1)
    ex.start(lambda p: own_c, recv_c)
    attn_g.send(2)
    attn_g.forward(0)
    branches(1)
    recv_c[d] = own_c[...]
    for c in range(2):
        gmod_ref[:, c, :] = two_part(dot_tn, cond_own, full_d[c])
    ex.wait(lambda p: own_c, recv_c)
    ggain_ref[2:3, :] = jnp.sum(own_c[...] * mixed_own * mixed_factor, axis=0, keepdims=True)
    d_mixed = rms_blocks_back(
        mixed, mixed_factor, recv_c[...] * emb_ref[:, images + 2 : images + 3, :]
    )
    recv_c[...] = d_mixed
    mix_own = recv_c[d]
    part = two_part_left(dot_nn, mix_own, mapdown_s[...].astype(BF16))
    for p in range(n_dp):
        send_g[p] = part[p * IMG_DEV : (p + 1) * IMG_DEV, :]
    ex = dp_ex(2)
    ex.start(lambda p: send_g.at[p], recv_g)
    attn_g.send(3)
    attn_g.forward(1)
    branches(2)
    recv_g[d] = send_g[d]
    gmd_ref[...] = two_part_left(dot_tn, mix_own, gated_ref[...].astype(BF16))
    ex.wait(lambda p: send_g.at[p], recv_g)
    d_gated = total_of(recv_g, n_dp)
    value, slope = gelu_parts(hid_ref[1])
    own_h[0] = d_gated * value
    own_h[1] = d_gated * hid_ref[0] * slope
    ex = dp_ex(3)
    ex.start(lambda p: own_h, recv_h)
    recv_h[d] = own_h[...]
    attn_g.send(4)
    attn_g.forward(2)
    branches(3)
    ex.wait(lambda p: own_h, recv_h)
    for p in range(n_dp):
        for c in range(2):
            full_h[c, p * IMG_DEV : (p + 1) * IMG_DEV, :] = recv_h[p, c]
    own_p[...] = two_part_left(dot_nt, full_h[0], mapup_s[:, 0, :].astype(BF16)) + two_part_left(
        dot_nt, full_h[1], mapup_s[:, 1, :].astype(BF16)
    )
    ex = mp_ex(1)
    ex.start(lambda p: own_p, recv_p)
    one.start()
    attn_g.send(5)
    attn_g.send(6)
    attn_g.forward(3)
    squares_done = local_squares()
    recv_p[m] = own_p[...]
    for c in range(2):
        gmu_ref[:, c, :] = two_part(dot_tn, pre_own, full_h[c])
    ex.wait(lambda p: own_p, recv_p)
    own_s[...] = total_of(recv_p, n_mp)
    ex = dp_ex(4)
    ex.start(lambda p: own_s, recv_s)
    attn_g.send(7)
    attn_g.forward(4)
    attn_g.forward(5)
    recv_s[d] = own_s[...]
    ex.wait(lambda p: own_s, recv_s)
    ggain_ref[1:2, :] = jnp.sum(own_s[...] * unit_own * unit_factor, axis=0, keepdims=True)
    d_unit = recv_c[...] + rms_blocks_back(
        unit, unit_factor, recv_s[...] * emb_ref[:, images + 1 : images + 2, :]
    )
    recv_s[...] = d_unit
    ggain_ref[0:1, :] = jnp.sum(recv_s[d] * emb_own * emb_factor, axis=0, keepdims=True)
    d_emb = rms_blocks_back(emb, emb_factor, d_unit * emb_ref[:, images : images + 1, :])
    recv_s[...] = d_emb
    ggain_ref[3:8, :] = jnp.zeros_like(ggain_ref[3:8, :])
    for p in range(n_dp):
        full_e[:, p * own_cols : (p + 1) * own_cols] = recv_s[p]
    attn_g.forward(6)
    attn_g.forward(7)
    gtime_ref[...] = two_part(dot_tn, feats_ref[...].astype(BF16), full_e[...])
    gclass_ref[...] = two_part_left(dot_tn, recv_s[d], onehot_s[...].astype(BF16))
    attn_g.finish()
    ffn_g.finish()
    split = squares_done + squares(gmd_ref[...]) + planes(gmu_ref)
    for c in range(4):
        split = split + squares(gattn_ref[c])
    for i in range(ffn_g.pieces):
        split = split + squares(gf_ref[i])
    shared = planes(gmod_ref) + squares(gtime_ref[...]) + squares(gclass_ref[...]) + squares(ggain_ref[...])
    lane = lax.broadcasted_iota(jnp.int32, (1, 128), 1)
    own_n[...] = jnp.zeros_like(own_n)
    own_n[0:1, :] = jnp.where(lane == 0, split + shared * (1.0 / n_mp), 0.0)
    width = gscale_ref.shape[1]
    column = lax.div(lax.broadcasted_iota(jnp.int32, (1, width), 1), width // heads)
    scale_row = jnp.zeros((1, 128), F32)
    for h in range(heads):
        head_part = jnp.sum(jnp.where(column == h, gscale_ref[...], 0.0), axis=-1, keepdims=True)
        scale_row = jnp.where(lane == h, head_part, scale_row)
    own_n[1:2, :] = scale_row
    ex = dp_ex(5)
    ex.start(lambda p: own_n, all_dp)
    all_dp[d] = own_n[...]
    for kx in range(1, r.n_x):
        one.forward(kx)
        two.forward(kx)
    ex.wait(lambda p: own_n, all_dp)
    summed = total_of(all_dp, n_dp)
    head = summed[1:2]
    own_sum[...] = jnp.zeros_like(own_sum)
    own_sum[0:1, :] = summed[0:1] + head * head
    ex = mp_ex(2)
    ex.start(lambda p: own_sum, all_mp)
    all_mp[m] = own_sum[...]
    for kx in range(r.n_x):
        one.arrived(kx)
        two.arrived(kx)
    ex.wait(lambda p: own_sum, all_mp)
    norm = jnp.sqrt(jnp.sum(total_of(all_mp, n_mp)[0:1], axis=-1, keepdims=True))
    norm_ref[0:1, :] = jnp.broadcast_to(norm, (1, 128))
    norm_ref[1:2, :] = head
    norm_ref[2:8, :] = jnp.zeros((6, 128), F32)
    red.drain()
    one.drain()
    two.drain()


def back(n_dp, n_mp, lengths, labels, grads, amod, fmod, mid, gin, feats, gd, gu, gscale, emb, hid, gated, mixed, map_states, gffn, ffgated, wd):
    images, part = feats.shape
    units_map = map_states[0].shape[3]
    rows = mid.shape[0]
    tokens = rows * n_mp
    heads = H // n_mp
    slab = (4, grads.shape[1] // n_dp, grads.shape[2])
    shard, units = slab[1], gffn.shape[2]
    small = shard // cuts(shard)
    pieces = 3 * cuts(shard) - scatter_split(shard)[1]
    shape = lambda *dims: jax.ShapeDtypeStruct(dims, F32)
    block = pltpu.VMEM((8, 128), F32)
    return pl.pallas_call(
        functools.partial(back_kernel, n_dp, n_mp, heads),
        out_shape=(
            shape(*slab),
            shape(pieces, small, units),
            jax.ShapeDtypeStruct((tokens, D), BF16),
            jax.ShapeDtypeStruct((tokens, D), BF16),
            shape(part, 2, D),
            shape(part, units_map),
            shape(part, 2, units_map),
            shape(part, DM),
            shape(part, NCLASS),
            shape(8, part),
            shape(8, 128),
        ),
        in_specs=[SMEM_SPEC] * 2 + vmem_specs(13) + any_specs(6),
        out_specs=tuple(vmem_specs(11)),
        scratch_shapes=[pltpu.VMEM(state.shape[1:], F32) for state in map_states]
        + [
            pltpu.VMEM((1, D, units), BF16),
            pltpu.VMEM((tokens, units), BF16),
            pltpu.VMEM((D, units), BF16),
            pltpu.SemaphoreType.DMA((6,)),
            pltpu.VMEM((2, D), F32),
            pltpu.VMEM((images, DM), F32),
            pltpu.VMEM((images, NCLASS), F32),
            gather_sems(n_mp),
            gather_sems(n_mp),
            pltpu.VMEM((n_mp, 2, D), F32),
            pltpu.VMEM((2 * IMG_DEV, D), F32),
            pltpu.VMEM((4 * IMG_DEV, D // 2), BF16),
            pltpu.VMEM((n_dp, 4 * IMG_DEV, D // 2), BF16),
            pltpu.VMEM((2, images, D), F32),
            pltpu.VMEM((images, part), F32),
            pltpu.VMEM((n_dp, images, part), F32),
            pltpu.VMEM((n_dp, IMG_DEV, units_map), F32),
            pltpu.VMEM((n_dp, IMG_DEV, units_map), F32),
            pltpu.VMEM((2, IMG_DEV, units_map), F32),
            pltpu.VMEM((n_dp, 2, IMG_DEV, units_map), F32),
            pltpu.VMEM((2, images, units_map), F32),
            pltpu.VMEM((images, part), F32),
            pltpu.VMEM((n_mp, images, part), F32),
            pltpu.VMEM((images, part), F32),
            pltpu.VMEM((n_dp, images, part), F32),
            block,
            pltpu.VMEM((n_dp, 8, 128), F32),
            block,
            pltpu.VMEM((n_mp, 8, 128), F32),
            pltpu.SemaphoreType.DMA((6, n_dp)),
            pltpu.SemaphoreType.DMA((6, n_dp)),
            pltpu.SemaphoreType.DMA((3, n_mp)),
            pltpu.SemaphoreType.DMA((3, n_mp)),
        ]
        + reduce_scratch(n_mp, rows)
        + scatter_scratch(n_dp, 8, slab[1] // 2, slab[2])
        + scatter_scratch(n_dp, pieces, small, units),
        compiler_params=pltpu.CompilerParams(
            collective_id=1, has_side_effects=True, vmem_limit_bytes=VMEM_BYTES
        ),
        name="back",
    )(lengths, labels, grads, amod, fmod, mid, gin, feats, gd, gu, gscale, emb, hid, gated, mixed, *map_states, gffn, ffgated, wd)


def update_kernel(heads, *refs):
    states, refs = refs[:11], refs[11:]
    norm_ref, gattn_ref, gtime_ref, gclass_ref, gmu_ref, gmd_ref, gmod_ref, ggain_ref = refs[:8]
    ffn_refs, out_ref, gin_ref, refs = refs[8:11], refs[11], refs[12], refs[13:]
    outs, out_final, gin_final, refs = refs[:33], refs[33], refs[34], refs[35:]
    kept, new, first, second = refs[:11], refs[11:22], refs[22:33], refs[33:44]
    gup_s, gdown_s, gin_s, out_s, load_sem, store_sem, out_sem = refs[44:]
    order = (2, 8, 0, 6, 3, 5, 4, 7, 1, 9, 10)
    copies = {i: pltpu.make_async_copy(states[i], kept[i], load_sem.at[i]) for i in order}
    for i in order:
        copies[i].start()
    out_load = pltpu.make_async_copy(out_ref, out_s, out_sem.at[2])
    out_load.start()
    out_copies = [pltpu.make_async_copy(out_s, out_final, out_sem.at[0])]
    out_copies.append(pltpu.make_async_copy(gin_s, gin_final, out_sem.at[1]))
    gin_s[...] = gin_ref[...].astype(F32)
    out_copies[1].start()
    out_load.wait()
    out_copies[0].start()
    parts = cuts(gdown_s.shape[0])
    small = gdown_s.shape[0] // parts
    pieces = [ref.at[i] for ref in ffn_refs for i in range(ref.shape[0])]
    for i, piece in enumerate(pieces):
        rows = slice(i % parts * small, (i % parts + 1) * small)
        if i < parts:
            gdown_s[rows, :] = piece[...]
        else:
            gup_s[rows, i // parts - 1, :] = piece[...]
    factor = CLIP_NORM / jnp.maximum(norm_ref[0:1, 0:1], CLIP_NORM)
    head = norm_ref[1:2, :]
    rates, decays = learn_rates(), decay_rates()
    stores = []

    def store(i):
        for k, (source, target) in enumerate(((new[i], outs[3 * i]), (first[i], outs[3 * i + 1]), (second[i], outs[3 * i + 2]))):
            stores.append(pltpu.make_async_copy(source, target, store_sem.at[i, k]))
            stores[-1].start()

    def step(i, gradient, pick=lambda ref, k: ref.at[k]):
        copies[i].wait()
        new_weight, average, m_new, v_new = adamw_step(lambda k: pick(kept[i], k)[...], gradient, rates[i], decays[i])
        pick(new[i], 0)[...] = new_weight
        pick(new[i], 1)[...] = average
        first[i][...] = m_new
        second[i][...] = v_new
        store(i)

    step(2, gup_s[...] * factor[:, None, :])
    step(8, gmod_ref[...] * factor[:, None, :])
    copies[0].wait()
    for c in range(3):
        results = adamw_step(lambda k: kept[0][k, c], gattn_ref[c] * factor, rates[0], decays[0])
        new[0][0, c], new[0][1, c], first[0][c], second[0][c] = results
    store(0)
    step(6, gmu_ref[...] * factor[:, None, :])
    step(3, gdown_s[...].T * factor)
    step(5, gclass_ref[...] * factor)
    step(4, gtime_ref[...] * factor)
    step(7, gmd_ref[...] * factor)
    step(1, gattn_ref[3].T * factor)
    copies[9].wait()
    copies[10].wait()
    for g in range(3):
        results = adamw_step(lambda k: kept[9][g, k : k + 1, :], ggain_ref[g : g + 1, :] * factor, rates[9], decays[9])
        new[9][g, 0:1, :], new[9][g, 1:2, :], first[9][g : g + 1, :], second[9][g : g + 1, :] = results
    store(9)
    results = adamw_step(lambda k: kept[10][k : k + 1, :], head[:, 0:heads] * factor, rates[10], decays[10])
    new[10][0:1, :], new[10][1:2, :], first[10][...], second[10][...] = results
    store(10)
    for copy in stores + out_copies:
        copy.wait()


def update(states, norm, grads, ffn_parts, out_all, gin_all):
    heads = states[10].shape[1]
    rows, _, units = states[2].shape[1:]
    news, moments = [], []
    for i, state in enumerate(states):
        if i == 9:
            news.append((state.shape[0], 2, state.shape[2]))
            moments.append((state.shape[0], state.shape[2]))
        else:
            news.append((2,) + state.shape[1:])
            moments.append(state.shape[1:] if i < 10 else (1, heads))
    outs = []
    for new, moment in zip(news, moments):
        outs += [new, moment, moment]
    shape = lambda dims: jax.ShapeDtypeStruct(dims, F32)
    return pl.pallas_call(
        functools.partial(update_kernel, heads),
        out_shape=tuple(shape(o) for o in outs)
        + (jax.ShapeDtypeStruct(out_all.shape, BF16), shape(gin_all.shape)),
        in_specs=any_specs(11) + vmem_specs(11) + any_specs(1) + vmem_specs(1),
        out_specs=tuple(any_specs(35)),
        scratch_shapes=[pltpu.VMEM(state.shape, F32) for state in states]
        + [pltpu.VMEM(dims, F32) for dims in news]
        + [pltpu.VMEM(dims, F32) for dims in moments]
        + [pltpu.VMEM(dims, F32) for dims in moments]
        + [
            pltpu.VMEM((rows, 2, units), F32),
            pltpu.VMEM((rows, units), F32),
            pltpu.VMEM(gin_all.shape, F32),
            pltpu.VMEM(out_all.shape, BF16),
            pltpu.SemaphoreType.DMA((11,)),
            pltpu.SemaphoreType.DMA((11, 3)),
            pltpu.SemaphoreType.DMA((3,)),
        ],
        compiler_params=pltpu.CompilerParams(vmem_limit_bytes=VMEM_BYTES),
        name="update",
    )(*states, norm, *grads, *ffn_parts, out_all, gin_all)


def per_device(
    block_input,
    out_cotangent,
    sigmas,
    class_labels,
    image_lengths,
    fourier_freqs,
    inproj_state,
    outproj_state,
    upproj_state,
    downproj_state,
    timeproj_state,
    classemb_state,
    mapup_state,
    mapdown_state,
    modproj_state,
    gains_state,
    headscale_state,
):
    n_dp, n_mp = lax.axis_size("dp"), lax.axis_size("mp")
    in_state = jnp.transpose(inproj_state, (0, 2, 1, 3))
    class_state = jnp.transpose(classemb_state, (0, 2, 1))
    down_map_state = jnp.transpose(mapdown_state, (0, 2, 1))
    gain_state = jnp.transpose(gains_state, (1, 0, 2))
    mods, emb, hid, gated, mixed, feats, wg, wf, q, k, v, normed, att, stats, mid, nm = forward_part(
        n_dp, n_mp, image_lengths, sigmas, class_labels, headscale_state, fourier_freqs[None, :], block_input,
        (in_state, outproj_state, upproj_state),
        (timeproj_state, class_state, mapup_state, down_map_state, modproj_state), gain_state,
    )
    gd, dmid, fmod, ffgated, wd, gw_ffn = ffn(
        n_dp, n_mp, image_lengths, nm, mods, mid, out_cotangent, wf, downproj_state
    )
    gw_attn, gu, gin, amod, gscale = attn_backward(
        n_dp, n_mp, image_lengths, headscale_state, dmid, mods, q, k, stats, gw_ffn, wg, v, normed, att, block_input
    )
    g_attn, gb, out_all, gin_all, g_mod, g_md, g_mu, g_time, g_class, g_gain, norm = back(
        n_dp, n_mp, image_lengths, class_labels, gw_attn, amod, fmod, mid, gin, feats, gd, gu, gscale,
        emb, hid, gated, mixed, (mapup_state, down_map_state, modproj_state), gw_ffn, ffgated, wd,
    )
    states = (
        in_state,
        outproj_state,
        upproj_state,
        downproj_state,
        timeproj_state,
        class_state,
        mapup_state,
        down_map_state,
        modproj_state,
        gain_state,
        headscale_state,
    )
    grads = (g_attn, g_time, g_class, g_mu, g_md, g_mod, g_gain)
    *new, layer_out, input_grad = update(states, norm, grads, (gd, gu, gb), out_all, gin_all)
    orders = {0: (0, 2, 1, 3), 5: (0, 2, 1), 7: (0, 2, 1), 9: (1, 0, 2)}
    moment_orders = {0: (1, 0, 2), 5: (1, 0), 7: (1, 0)}
    results = [layer_out, input_grad, norm[0, 0]]
    for i in range(11):
        stacked, first, second = new[3 * i : 3 * i + 3]
        if i in orders:
            stacked = jnp.transpose(stacked, orders[i])
        if i in moment_orders:
            first, second = jnp.transpose(first, moment_orders[i]), jnp.transpose(second, moment_orders[i])
        if i == 10:
            first, second = first[0], second[0]
        results += [stacked, first, second]
    return tuple(results)


def solution(mesh):
    return jax.shard_map(
        per_device,
        mesh=mesh,
        in_specs=(
            P("dp", None),
            P("dp", None),
            P(),
            P(),
            P(),
            P(),
            P(None, "dp", None, "mp"),
            P(None, "mp", "dp"),
            P(None, "dp", None, "mp"),
            P(None, "mp", "dp"),
            P(None, "dp", None),
            P(None, None, "dp"),
            P(None, "dp", None, "mp"),
            P(None, "mp", "dp"),
            P(None, "dp", None, None),
            P(None, None, "dp"),
            P(None, "mp"),
        ),
        out_specs=(
            P("dp", None),
            P("dp", None),
            P(),
            P(None, "dp", None, "mp"),
            P("dp", None, "mp"),
            P("dp", None, "mp"),
            P(None, "mp", "dp"),
            P("mp", "dp"),
            P("mp", "dp"),
            P(None, "dp", None, "mp"),
            P("dp", None, "mp"),
            P("dp", None, "mp"),
            P(None, "mp", "dp"),
            P("mp", "dp"),
            P("mp", "dp"),
            P(None, "dp", None),
            P("dp", None),
            P("dp", None),
            P(None, None, "dp"),
            P(None, "dp"),
            P(None, "dp"),
            P(None, "dp", None, "mp"),
            P("dp", None, "mp"),
            P("dp", None, "mp"),
            P(None, "mp", "dp"),
            P("mp", "dp"),
            P("mp", "dp"),
            P(None, "dp", None, None),
            P("dp", None, None),
            P("dp", None, None),
            P(None, None, "dp"),
            P(None, "dp"),
            P(None, "dp"),
            P(None, "mp"),
            P("mp"),
            P("mp"),
        ),
        check_vma=False,
    )
```

```python
import functools
import math

import jax
import jax.numpy as jnp
from jax import lax
from jax.experimental import pallas as pl
from jax.experimental.pallas import tpu as pltpu
from jax.sharding import PartitionSpec as P

D = 1024
H = 16
FF = 3072
DM = 768
MFF = 2304
NCLASS = 1000
IMG_DEV = 4
STEP = 10

EPSILON = 1e-06
BETA_ONE = 0.9
BETA_TWO = 0.95
ADAM_EPSILON = 1e-08
CLIP_NORM = 1.0
MASKED = -1e30
MESH = pl.DeviceIdType.MESH
FORWARD_VMEM = 60 * 2**20
FFN_VMEM = 60 * 2**20
ATTN_VMEM = 60 * 2**20
BACK_VMEM = 60 * 2**20
UPDATE_VMEM = 60 * 2**20
F32 = jnp.float32
BF16 = jnp.bfloat16


def minor_size(count):
    return 1 << ((count.bit_length() - 1) // 2)


def learn_rates():
    return (
        2.5 * D ** (-0.5),
        2.5 * (D // 64) ** (-0.5),
        2.5 * D ** (-0.5),
        2.5 * FF ** (-0.5),
        2.5 * DM ** (-0.5),
        2.5,
        2.5 * DM ** (-0.5),
        2.5 * MFF ** (-0.5),
        1.25 * DM ** (-0.5),
        0.25,
        7.5,
    )


def decay_rates():
    return (0.01, 0.01, 0.01, 0.01, 0.01, 0.01, 0.01, 0.01, 0.01, 0.0, 0.0)


def adamw_step(state, gradient, rate, decay):
    keep_rate = 1.0 - (1.0 + STEP) ** (-0.75)
    first = BETA_ONE * state(1) + (1.0 - BETA_ONE) * gradient
    second = BETA_TWO * state(2) + (1.0 - BETA_TWO) * gradient * gradient
    first_hat = first / (1.0 - BETA_ONE**STEP)
    second_hat = second / (1.0 - BETA_TWO**STEP)
    weight = state(0) * (1.0 - rate * decay) - rate * first_hat / (
        jnp.sqrt(second_hat) + ADAM_EPSILON
    )
    average = keep_rate * state(3) + (1.0 - keep_rate) * weight
    return weight, average, first, second


def dot_nn(a, b):
    return lax.dot_general(a, b, (((1,), (0,)), ((), ())), preferred_element_type=F32)


def dot_nt(a, b):
    return lax.dot_general(a, b, (((1,), (1,)), ((), ())), preferred_element_type=F32)


def dot_tn(a, b):
    return lax.dot_general(a, b, (((0,), (0,)), ((), ())), preferred_element_type=F32)


def two_part(dot, exact, wide):
    high = wide.astype(BF16)
    low = (wide - high.astype(F32)).astype(BF16)
    return dot(exact, high) + dot(exact, low)


def two_part_left(dot, wide, exact):
    high = wide.astype(BF16)
    low = (wide - high.astype(F32)).astype(BF16)
    return dot(high, exact) + dot(low, exact)


def gelu_parts(b):
    cdf = 0.5 * (1.0 + lax.erf(b * (1.0 / math.sqrt(2.0))))
    pdf = jnp.exp(-0.5 * b * b) * (1.0 / math.sqrt(2.0 * math.pi))
    return b * cdf, cdf + b * pdf


def greet(peers):
    barrier = pltpu.get_barrier_semaphore()
    total = 0
    for count, peer_of in peers:

        def say(k, carry, peer_of=peer_of):
            pl.semaphore_signal(barrier, inc=1, device_id=peer_of(k), device_id_type=MESH)
            return carry

        lax.fori_loop(1, count, say, 0)
        total += count - 1
    pl.semaphore_wait(barrier, total)


class Exchange:
    def __init__(self, count, me, device_of, send_sem, recv_sem):
        self.count, self.me, self.device_of = count, me, device_of
        self.send_sem, self.recv_sem = send_sem, recv_sem

    def _copy(self, k, src_of, dst, slot):
        peer = lax.rem(self.me + k, self.count)
        return pltpu.make_async_remote_copy(
            src_ref=src_of(peer),
            dst_ref=dst.at[slot],
            send_sem=self.send_sem.at[k],
            recv_sem=self.recv_sem.at[k],
            device_id=self.device_of(peer),
            device_id_type=MESH,
        )

    def start(self, src_of, dst):
        def body(k, carry):
            self._copy(k, src_of, dst, self.me).start()
            return carry

        lax.fori_loop(1, self.count, body, 0)

    def wait(self, src_of, dst):
        def body(k, carry):
            self._copy(k, src_of, dst, lax.rem(self.me + self.count - k, self.count)).wait()
            return carry

        lax.fori_loop(1, self.count, body, 0)

    def run(self, src_of, dst):
        self.start(src_of, dst)
        self.wait(src_of, dst)


def vmem_specs(count):
    return [pl.BlockSpec(memory_space=pltpu.VMEM)] * count


def any_specs(count):
    return [pl.BlockSpec(memory_space=pl.ANY)] * count


SMEM_SPEC = pl.BlockSpec(memory_space=pltpu.SMEM)
SHORT = 256


def total_of(ref, count):
    value = ref[0]
    for index in range(1, count):
        value = value + ref[index]
    return value


def pack_rows(rows):
    half = rows.shape[1] // 2
    return jnp.concatenate([rows[:, :half], rows[:, half:]], axis=0).astype(BF16)


def mean_square(blocks):
    sums = jnp.sum(jnp.sum(blocks, axis=0), axis=-1, keepdims=True)
    return sums * (1.0 / DM)


def rms_blocks(blocks):
    factor = lax.rsqrt(mean_square(blocks * blocks) + EPSILON)
    return factor


def rms_blocks_back(blocks, factor, gain_grad):
    inner = mean_square(blocks * gain_grad)
    return factor[None] * gain_grad - blocks * (factor * factor * factor * inner)[None]


class Grid:
    def __init__(self, n_dp):
        self.d, self.m = lax.axis_index("dp"), lax.axis_index("mp")
        self.n_y = minor_size(n_dp)
        self.n_z = n_dp // self.n_y
        self.z, self.y = lax.div(self.d, self.n_y), lax.rem(self.d, self.n_y)

    def at(self, kz, ky):
        return lax.rem(self.z + kz, self.n_z) * self.n_y + lax.rem(self.y + ky, self.n_y)

    def before(self, kz, ky):
        return lax.rem(self.z + self.n_z - kz, self.n_z) * self.n_y + lax.rem(self.y + self.n_y - ky, self.n_y)


def bulk_sems(n_dp, pieces):
    n_y = minor_size(n_dp)
    z_sem = pltpu.SemaphoreType.DMA((n_dp // n_y, pieces))
    y_sem = pltpu.SemaphoreType.DMA((n_dp // n_y, n_y, pieces))
    return [z_sem, z_sem, y_sem, y_sem]


def if_piece(act, i, low, high):
    @pl.when((i >= low) & (i < high))
    def _():
        act(i)


def each_piece(act, low, high):
    def body(i, carry):
        act(i)
        return carry

    lax.fori_loop(low, high, body, 0)


class Paced:
    def paced_send(self, u, first, num, den):
        self._at(self.send, u, first, num, den)

    def paced_forward(self, u, first, num, den):
        self._at(self.forward, u, first, num, den)

    def _at(self, act, u, first, num, den):
        far = 64 * num
        done = lambda t: lax.div((t - first) * den + far, num)
        new, old = done(u), done(u - 1)
        for step in range(-(-den // num)):
            i = old + 1 + step - 64

            @pl.when((new - 64 >= i) & (i >= 0) & (i < self.pieces))
            def _(i=i):
                act(i)

    @staticmethod
    def after(pieces, first, num, den, ticks):
        return min(pieces, max(0, (ticks - 1 - first) * den // num + 1)) if ticks > first else 0


class BulkGather(Paced):
    def __init__(self, grid, pieces, piece, z_ss, z_rs, y_ss, y_rs):
        self.g, self.pieces, self.piece = grid, pieces, piece
        self.z_ss, self.z_rs, self.y_ss, self.y_rs = z_ss, z_rs, y_ss, y_rs

    def z_copy(self, kz, i, owner):
        return pltpu.make_async_remote_copy(
            src_ref=self.piece(self.g.d, i), dst_ref=self.piece(owner, i), send_sem=self.z_ss.at[kz, i],
            recv_sem=self.z_rs.at[kz, i], device_id=(self.g.at(kz, 0), self.g.m), device_id_type=MESH)

    def y_copy(self, kz, ky, i, owner):
        return pltpu.make_async_remote_copy(
            src_ref=self.piece(self.g.before(kz, 0), i), dst_ref=self.piece(owner, i),
            send_sem=self.y_ss.at[kz, ky, i], recv_sem=self.y_rs.at[kz, ky, i],
            device_id=(self.g.at(0, ky), self.g.m), device_id_type=MESH)

    def send(self, i):
        for kz in range(1, self.g.n_z):
            self.z_copy(kz, i, self.g.d).start()
        for ky in range(1, self.g.n_y):
            self.y_copy(0, ky, i, self.g.d).start()

    def forward(self, i):
        for kz in range(1, self.g.n_z):
            self.z_copy(kz, i, self.g.before(kz, 0)).wait_recv()
            for ky in range(1, self.g.n_y):
                self.y_copy(kz, ky, i, self.g.before(kz, 0)).start()

    def finish_piece(self, i):
        for kz in range(1, self.g.n_z):
            self.z_copy(kz, i, self.g.d).wait_send()
        for kz in range(self.g.n_z):
            for ky in range(1, self.g.n_y):
                self.y_copy(kz, ky, i, self.g.before(kz, ky)).wait()

    def finish(self):
        each_piece(self.finish_piece, 0, self.pieces)


def line_sems(n_dp, pieces):
    n_y = minor_size(n_dp)
    n_z = n_dp // n_y
    return [pltpu.SemaphoreType.DMA((n_z, pieces))] * 4 + [pltpu.SemaphoreType.DMA((n_z, n_y, pieces))] * 2


class LineGather:
    def __init__(self, grid, pieces, piece, up_ss, up_rs, down_ss, down_rs, y_ss, y_rs):
        self.g, self.pieces, self.piece = grid, pieces, piece
        self.up, self.down, self.y_ss, self.y_rs = (up_ss, up_rs), (down_ss, down_rs), y_ss, y_rs
        self.ticks = pieces + grid.n_z - 1

    def block(self, z, y):
        return z * self.g.n_y + y

    def other_y(self, ky):
        return lax.rem(self.g.y + ky, self.g.n_y)

    def before_y(self, ky):
        return lax.rem(self.g.y + self.g.n_y - ky, self.g.n_y)

    def above(self):
        return (self.block(jnp.minimum(self.g.z + 1, self.g.n_z - 1), self.g.y), self.g.m)

    def below(self):
        return (self.block(jnp.maximum(self.g.z - 1, 0), self.g.y), self.g.m)

    def z_copy(self, sems, owner_z, i, target):
        block = self.piece(self.block(owner_z, self.g.y), i)
        return pltpu.make_async_remote_copy(
            src_ref=block, dst_ref=block, send_sem=sems[0].at[owner_z, i], recv_sem=sems[1].at[owner_z, i],
            device_id=target, device_id_type=MESH)

    def up_copy(self, owner_z, i):
        return self.z_copy(self.up, owner_z, i, self.above())

    def down_copy(self, owner_z, i):
        return self.z_copy(self.down, owner_z, i, self.below())

    def y_copy(self, owner_z, ky, i, in_y):
        return pltpu.make_async_remote_copy(
            src_ref=self.piece(self.block(owner_z, self.g.y), i), dst_ref=self.piece(self.block(owner_z, in_y), i),
            send_sem=self.y_ss.at[owner_z, ky, i], recv_sem=self.y_rs.at[owner_z, ky, i],
            device_id=(self.block(self.g.z, self.other_y(ky)), self.g.m), device_id_type=MESH)

    def along_y(self, owner_z, i):
        for ky in range(1, self.g.n_y):
            self.y_copy(owner_z, ky, i, self.g.y).start()

    def send(self, i):
        z, n_z = self.g.z, self.g.n_z

        @pl.when(z < n_z - 1)
        def _():
            self.up_copy(z, i).start()

        @pl.when(z > 0)
        def _():
            self.down_copy(z, i).start()

        self.along_y(z, i)

    def arrival(self, hop, i):
        z, n_z = self.g.z, self.g.n_z

        @pl.when(z - 1 - hop >= 0)
        def _():
            owner = jnp.maximum(z - 1 - hop, 0)
            self.up_copy(owner, i).wait_recv()

            @pl.when(z < n_z - 1)
            def _():
                self.up_copy(owner, i).start()

            self.along_y(owner, i)

        @pl.when(z + 1 + hop < n_z)
        def _():
            owner = jnp.minimum(z + 1 + hop, n_z - 1)
            self.down_copy(owner, i).wait_recv()

            @pl.when(z > 0)
            def _():
                self.down_copy(owner, i).start()

            self.along_y(owner, i)

    def tick(self, t):
        if_piece(self.send, t, 0, self.pieces)
        for hop in range(self.g.n_z - 1):
            if_piece(functools.partial(self.arrival, hop), t - 1 - hop, 0, self.pieces)

    def finish(self):
        z, n_z = self.g.z, self.g.n_z

        def piece_done(i):
            for owner in range(n_z):

                @pl.when((z >= owner) & (z < n_z - 1))
                def _():
                    self.up_copy(owner, i).wait_send()

                @pl.when((z <= owner) & (z > 0))
                def _():
                    self.down_copy(owner, i).wait_send()

                for ky in range(1, self.g.n_y):
                    self.y_copy(owner, ky, i, self.before_y(ky)).wait()

        each_piece(piece_done, 0, self.pieces)


def scatter_scratch(n_dp, pieces, rows, columns):
    n_y = minor_size(n_dp)
    n_z = n_dp // n_y
    slot = (pieces, rows, columns)
    return [
        pltpu.VMEM((n_z, max(n_y - 1, 1)) + slot, BF16),
        pltpu.VMEM((max(n_z - 1, 1),) + slot, BF16),
        pltpu.VMEM((max(n_z - 1, 1),) + slot, BF16),
    ] + bulk_sems(n_dp, pieces)


class BulkScatter(Paced):
    def __init__(self, grid, pieces, piece, out, recv_y, send_z, recv_z, z_ss, z_rs, y_ss, y_rs, sent=None):
        self.g, self.pieces, self.piece, self.out, self.sent = grid, pieces, piece, out, sent or piece
        self.recv_y, self.send_z, self.recv_z = recv_y, send_z, recv_z
        self.z_ss, self.z_rs, self.y_ss, self.y_rs = z_ss, z_rs, y_ss, y_rs

    def y_copy(self, kz, ky, i):
        return pltpu.make_async_remote_copy(
            src_ref=self.sent(self.g.at(kz, ky), i), dst_ref=self.recv_y.at[kz, ky - 1, i],
            send_sem=self.y_ss.at[kz, ky, i], recv_sem=self.y_rs.at[kz, ky, i],
            device_id=(self.g.at(0, ky), self.g.m), device_id_type=MESH)

    def z_copy(self, kz, i):
        return pltpu.make_async_remote_copy(
            src_ref=self.send_z.at[kz - 1, i], dst_ref=self.recv_z.at[kz - 1, i], send_sem=self.z_ss.at[kz, i],
            recv_sem=self.z_rs.at[kz, i], device_id=(self.g.at(kz, 0), self.g.m), device_id_type=MESH)

    def send(self, i):
        for kz in list(range(1, self.g.n_z)) + [0]:
            for ky in range(1, self.g.n_y):
                self.y_copy(kz, ky, i).start()

    def forward(self, i):
        for kz in list(range(1, self.g.n_z)) + [0]:
            value = self.piece(self.g.at(kz, 0), i)[...].astype(F32)
            for ky in range(1, self.g.n_y):
                self.y_copy(kz, ky, i).wait_recv()
                value = value + self.recv_y[kz, ky - 1, i].astype(F32)
            if kz == 0:
                self.out(i)[...] = value
            else:
                self.send_z[kz - 1, i] = value.astype(BF16)
                self.z_copy(kz, i).start()

    def finish_piece(self, i):
        total = self.out(i)[...]
        for kz in range(1, self.g.n_z):
            self.z_copy(kz, i).wait_recv()
            total = total + self.recv_z[kz - 1, i].astype(F32)
        self.out(i)[...] = total
        for kz in range(1, self.g.n_z):
            self.z_copy(kz, i).wait_send()
        for kz in range(self.g.n_z):
            for ky in range(1, self.g.n_y):
                self.y_copy(kz, ky, i).wait_send()

    def finish(self):
        each_piece(self.finish_piece, 0, self.pieces)


def cuts(rows):
    return max(rows // 32, min(rows // 16, 2))


def scatter_split(shard):
    parts = cuts(shard)
    return parts // 2 + 1, min(parts // 2 + 2 * parts + 1, 3 * parts - 1)


def cut_rows(ref, shard, first=0):
    parts = cuts(shard)
    small = shard // parts

    def piece(owner, i):
        rows = pl.ds(pl.multiple_of(owner * shard + lax.rem(i + first, parts) * small, small), small)
        return ref.at[lax.div(i + first, parts), rows, :]

    return piece


class Images:
    def __init__(self, lengths_ref):
        start = lax.axis_index("dp") * IMG_DEV
        self.is_long = jnp.where(lengths_ref[start] > SHORT, 1.0, 0.0)
        self.bias = (1.0 - self.is_long) * MASKED
        live = lengths_ref[start]
        for j in range(1, IMG_DEV):
            live = live + lengths_ref[start + j]
        self.live = live.astype(F32)


def fill_onehot(target, labels_ref):
    classes = lax.broadcasted_iota(jnp.int32, (1, NCLASS), 1)

    def body(i, carry):
        target[pl.ds(i, 1), :] = jnp.where(classes == labels_ref[i], 1.0, 0.0)
        return carry

    lax.fori_loop(0, target.shape[0], body, 0)


def own_features(target, sigmas_ref, freqs_ref, d):
    count, part = freqs_ref.shape[0], target.shape[1]

    def body(i, carry):
        target[pl.ds(i, 1), :] = jnp.full((1, part), sigmas_ref[i], F32)
        return carry

    lax.fori_loop(0, target.shape[0], body, 0)
    slices = count // part
    every = freqs_ref[...].reshape(1, count)
    freqs = every[:, 0:part]
    for k in range(1, slices):
        freqs = jnp.where(lax.rem(d, slices) == k, every[:, k * part : (k + 1) * part], freqs)
    angles = 2.0 * math.pi * (jnp.log(target[...]) / 4.0) * freqs
    target[...] = jnp.where(d < slices, jnp.cos(angles), jnp.sin(angles))


def head_ones(width, heads):
    size = width // heads
    row = lax.div(lax.broadcasted_iota(jnp.int32, (width, 1), 0), size)
    column = lax.div(lax.broadcasted_iota(jnp.int32, (1, width), 1), size)
    return (row == column).astype(F32).astype(BF16)


def head_scales(scales_ref, width, heads):
    column = lax.div(lax.broadcasted_iota(jnp.int32, (1, width), 1), width // heads)
    row = jnp.full((1, width), scales_ref[0, 0], F32)
    for h in range(1, heads):
        row = jnp.where(column == h, scales_ref[0, h], row)
    return row


def loads(pairs, sems):
    copies = [pltpu.make_async_copy(source, target, sems.at[i]) for i, (source, target) in enumerate(pairs)]
    for copy in copies:
        copy.start()
    return copies


class Ranks:
    def __init__(self, n_mp):
        self.d, self.m = lax.axis_index("dp"), lax.axis_index("mp")
        self.n_x = n_mp // 2
        self.x, self.c = lax.div(self.m, 2), lax.rem(self.m, 2)
        self.sibling = (self.d, self.x * 2 + 1 - self.c)

    def rank(self, kx, same):
        core = jnp.where(same == 1, self.c, 1 - self.c)
        return lax.rem(self.x + kx, self.n_x) * 2 + core

    def chip(self, kx):
        return (self.d, lax.rem(self.x + kx, self.n_x) * 2 + self.c)

    def greet(self):
        greet([(2, lambda k: self.sibling), (self.n_x, self.chip)])


class Reduce:
    def __init__(self, ranks, core_send, core_recv, x_send, x_recv, sems):
        self.r = ranks
        self.core_send, self.core_recv, self.x_send, self.x_recv = core_send, core_recv, x_send, x_recv
        self.sems = sems

    def core_copy(self, kx):
        return pltpu.make_async_remote_copy(
            src_ref=self.core_send.at[kx], dst_ref=self.core_recv.at[kx], send_sem=self.sems.at[0, kx],
            recv_sem=self.sems.at[1, kx], device_id=self.r.sibling, device_id_type=MESH)

    def x_copy(self, kx):
        return pltpu.make_async_remote_copy(
            src_ref=self.x_send.at[kx], dst_ref=self.x_recv.at[kx], send_sem=self.sems.at[2, kx],
            recv_sem=self.sems.at[3, kx], device_id=self.r.chip(kx), device_id_type=MESH)

    def other(self, kx, part):
        self.core_send[kx] = part.astype(BF16)
        self.core_copy(kx).start()

    def same(self, kx, part):
        self.core_copy(kx).wait_recv()
        self.x_send[kx] = (part + self.core_recv[kx].astype(F32)).astype(BF16)
        self.x_copy(kx).start()

    def finish(self, part):
        self.core_copy(0).wait_recv()
        total = part + self.core_recv[0].astype(F32)
        for kx in range(1, self.r.n_x):
            self.x_copy(kx).wait_recv()
            total = total + self.x_recv[kx].astype(F32)
        return total

    def drain(self):
        self.core_copy(0).wait_send()
        for kx in range(1, self.r.n_x):
            self.core_copy(kx).wait_send()
            self.x_copy(kx).wait_send()


def reduce_scratch(n_mp, rows):
    slots = pltpu.VMEM((n_mp // 2, rows, D), BF16)
    return [slots, slots, slots, slots, pltpu.SemaphoreType.DMA((4, n_mp // 2))]


class Gather:
    def __init__(self, ranks, rows, buffer, sems):
        self.r, self.rows, self.buffer, self.sems = ranks, rows, buffer, sems

    def at(self, rank):
        return self.buffer.at[pl.ds(pl.multiple_of(rank * self.rows, self.rows), self.rows), :]

    def x_copy(self, kx, slot):
        return pltpu.make_async_remote_copy(
            src_ref=self.at(self.r.m), dst_ref=self.at(slot), send_sem=self.sems.at[0, kx],
            recv_sem=self.sems.at[1, kx], device_id=self.r.chip(kx), device_id_type=MESH)

    def core_copy(self, kx, out_slot, in_slot):
        return pltpu.make_async_remote_copy(
            src_ref=self.at(out_slot), dst_ref=self.at(in_slot), send_sem=self.sems.at[2, kx],
            recv_sem=self.sems.at[3, kx], device_id=self.r.sibling, device_id_type=MESH)

    def start(self):
        for kx in range(1, self.r.n_x):
            self.x_copy(kx, self.r.m).start()
        self.core_copy(0, self.r.m, self.r.m).start()

    def from_chip(self, kx):
        return lax.rem(self.r.x + self.r.n_x - kx, self.r.n_x) * 2 + self.r.c

    def from_core(self, kx):
        return lax.rem(self.r.x + self.r.n_x - kx, self.r.n_x) * 2 + 1 - self.r.c

    def forward(self, kx):
        slot = self.from_chip(kx)
        self.x_copy(kx, slot).wait_recv()
        self.core_copy(kx, slot, slot).start()

    def arrived(self, kx):
        self.core_copy(kx, self.r.m, self.from_core(kx)).wait_recv()

    def drain(self):
        for kx in range(1, self.r.n_x):
            self.x_copy(kx, self.r.m).wait_send()
        for kx in range(self.r.n_x):
            self.core_copy(kx, self.r.m, self.r.m).wait_send()


def gather_sems(n_mp):
    return pltpu.SemaphoreType.DMA((4, n_mp // 2))


def head_sums(values, ones):
    return two_part_left(dot_nn, values, ones)


def row_sums_factor(values):
    return lax.rsqrt(jnp.mean(values * values, axis=-1, keepdims=True) + EPSILON)


def image_scale(info, mods_ref, which, image):
    is_long = info.is_long
    row = mods_ref[which, pl.ds(image, 1), :]
    return 1.0 + (is_long * mods_ref[which, 0:1, :] + (1.0 - is_long) * row)


def column_bias(info, image, columns_shape, short):
    keys = lax.broadcasted_iota(jnp.int32, columns_shape, 0)
    own = (keys >= image * short) & (keys < (image + 1) * short)
    return jnp.where(own, 0.0, info.bias)


def forward_kernel(
    n_dp, n_mp, heads,
    lengths_ref, sigmas_ref, labels_ref, scales_ref, freqs_ref, x_ref,
    in_ref, out_ref, up_ref, time_ref, class_ref, mapup_ref, mapdown_ref, mod_ref, gains_ref,
    mods_ref, emb_ref, hid_ref, gated_ref, mixed_ref, feats_ref, wg_out, wf_out,
    q_out, k_out, v_out, normed_out, qu_out, ku_out, att_ref, stats_ref, mid_ref, nm_ref,
    wg_ref, q_ref, k_ref, v_ref, normed_ref, wf_ref, onehot_s, ones_ref, store_sem,
    in_s, out_s, up_s, time_s, class_s, mapup_s, mapdown_s, mod_s, gains_s, load_sem,
    send_a, recv_a, own_a, send_h, recv_h, own_g, recv_g, own_x, recv_x, own_m, send_o, recv_o,
    dp_ss, dp_rs, mp_ss, mp_rs, a_us, a_ur, a_ds, a_dr, a_ys, a_yr, f_us, f_ur, f_ds, f_dr, f_ys, f_yr,
    qu_s, ku_s, vt_s, part_s, core_send, core_recv, x_send, x_recv, sems,
):
    r = Ranks(n_mp)
    grid = Grid(n_dp)
    d, m = r.d, r.m
    images, part = feats_ref.shape
    info = Images(lengths_ref)
    copies = loads(
        (
            (time_ref.at[0], time_s),
            (in_ref.at[0], in_s),
            (out_ref.at[0], out_s),
            (class_ref.at[0], class_s),
            (gains_ref, gains_s),
            (up_ref.at[0], up_s),
            (mapup_ref.at[0], mapup_s),
            (mapdown_ref.at[0], mapdown_s),
            (mod_ref.at[0], mod_s),
        ),
        load_sem,
    )
    map_copies = [copies[0]] + copies[3:5] + copies[6:]
    greet(
        [
            (n_dp, lambda k: (lax.rem(d + k, n_dp), m)),
            (n_mp, lambda k: (d, lax.rem(m + k, n_mp))),
        ]
    )
    own_features(feats_ref, sigmas_ref, freqs_ref, d)
    shard = in_s.shape[1]
    mine = pl.ds(pl.multiple_of(d * shard, shard), shard)
    attn = LineGather(
        grid, 4, lambda dd, i: wg_ref.at[i, pl.ds(pl.multiple_of(dd * shard, shard), shard), :],
        a_us, a_ur, a_ds, a_dr, a_ys, a_yr)
    up_w = LineGather(
        grid, 2 * cuts(shard), cut_rows(wf_ref, shard), f_us, f_ur, f_ds, f_dr, f_ys, f_yr
    )

    def dp_ex(stage):
        return Exchange(n_dp, d, lambda p: (p, m), dp_ss.at[stage], dp_rs.at[stage])

    map_copies[0].wait()
    partial = dot_nn(feats_ref[...].astype(BF16), time_s[...].astype(BF16))
    for p in range(n_dp):
        send_a[p] = partial[:, p * part : (p + 1) * part]
    ex = dp_ex(0)
    ex.start(lambda p: send_a.at[p], recv_a)
    copies[1].wait()
    for c in range(3):
        wg_ref[c, mine, :] = in_s[c].astype(BF16)
    copies[2].wait()
    wg_ref[3, mine, :] = out_s[...].T.astype(BF16)
    attn.tick(0)
    recv_a[d] = send_a[d]
    copies[5].wait()
    for c in range(2):
        wf_ref[c, mine, :] = up_s[:, c, :].astype(BF16)
    fill_onehot(onehot_s, labels_ref)
    ones_ref[...] = head_ones(q_ref.shape[1], heads)
    for copy in map_copies[1:]:
        copy.wait()
    e_cols = dot_nt(onehot_s[...].astype(BF16), class_s[...].astype(BF16))
    own_a[images:, :] = jnp.zeros((8, part), F32)
    for g in range(3):
        own_a[images + g : images + g + 1, :] = gains_s[g, 0:1, :].astype(BF16).astype(F32)
    ex.wait(lambda p: send_a.at[p], recv_a)
    own_a[0:images, :] = total_of(recv_a, n_dp) + e_cols
    ex = dp_ex(1)
    ex.start(lambda p: own_a, emb_ref)
    attn.tick(1)
    emb_ref[d] = own_a[...]
    ex.wait(lambda p: own_a, emb_ref)
    gains = emb_ref[:, images:, :]
    emb = emb_ref[:, 0:images, :]
    unit = emb * rms_blocks(emb)[None] * gains[:, 0:1, :]
    unit_factor = rms_blocks(unit)
    own_x[0] = (emb_ref[d][0:images] * rms_blocks(emb)) * emb_ref[d][images : images + 1]
    unit_own = own_x[0]
    pre_own = (unit_own * unit_factor * emb_ref[d][images + 1 : images + 2]).astype(BF16)
    for c in range(2):
        part = dot_nn(pre_own, mapup_s[:, c, :].astype(BF16))
        for p in range(n_dp):
            send_h[p, c] = part[p * IMG_DEV : (p + 1) * IMG_DEV, :]
    ex = dp_ex(2)
    ex.start(lambda p: send_h.at[p], recv_h)
    attn.tick(2)
    recv_h[d] = send_h[d]
    ex.wait(lambda p: send_h.at[p], recv_h)
    hidden = total_of(recv_h, n_dp)
    hid_ref[...] = hidden
    own_g[...] = (hidden[0] * gelu_parts(hidden[1])[0]).astype(BF16).astype(F32)
    ex = dp_ex(3)
    ex.start(lambda p: own_g, recv_g)
    attn.tick(3)
    recv_g[d] = own_g[...]
    ex.wait(lambda p: own_g, recv_g)
    for p in range(n_dp):
        gated_ref[p * IMG_DEV : (p + 1) * IMG_DEV, :] = recv_g[p]
    own_x[0] = dot_nt(gated_ref[...].astype(BF16), mapdown_s[...].astype(BF16))
    ex = Exchange(n_mp, m, lambda p: (d, p), mp_ss.at[0], mp_rs.at[0])
    ex.start(lambda p: own_x.at[0], recv_x)
    attn.tick(4)
    up_w.tick(0)
    recv_x[m] = own_x[0]
    ex.wait(lambda p: own_x.at[0], recv_x)
    own_m[...] = total_of(recv_x, n_mp) + unit_own
    ex = dp_ex(4)
    ex.start(lambda p: own_m, mixed_ref)
    attn.tick(5)
    up_w.tick(1)
    mixed_ref[d] = own_m[...]
    ex.wait(lambda p: own_m, mixed_ref)
    mixed_factor = rms_blocks(mixed_ref[...])
    cond_own = (own_m[...] * mixed_factor * emb_ref[d][images + 2 : images + 3]).astype(BF16)
    for c in range(2):
        part = dot_nn(cond_own, mod_s[:, c, :].astype(BF16))
        for p in range(n_dp):
            send_o[p, c] = part[p * IMG_DEV : (p + 1) * IMG_DEV, :]
    ex = dp_ex(5)
    ex.start(lambda p: send_o.at[p], recv_o)
    attn.tick(6)
    up_w.tick(2)
    recv_o[d] = send_o[d]
    ex.wait(lambda p: send_o.at[p], recv_o)
    mods_ref[...] = total_of(recv_o, n_dp)
    each_piece(attn.tick, 7, attn.ticks)
    attn.finish()
    tokens = x_ref.shape[0]
    rows = tokens // n_mp
    width = q_ref.shape[1]
    size = width // heads
    red = Reduce(r, core_send, core_recv, x_send, x_recv, sems)
    at = lambda b: pl.ds(pl.multiple_of(b * rows, rows), rows)
    image_of = lambda b: lax.div(b * rows, SHORT)

    scale_row = head_scales(scales_ref, q_ref.shape[1], heads)

    def project(b, carry):
        xb = x_ref[at(b), :].astype(F32)
        normed = (xb * row_sums_factor(xb) * image_scale(info, mods_ref, 0, image_of(b))).astype(BF16)
        normed_ref[at(b), :] = normed
        q = dot_nn(normed, wg_ref[0])
        q_ref[at(b), :] = q
        qu_s[at(b), :] = (q * lax.rsqrt(head_sums(q * q, ones_ref[...]) + EPSILON) * scale_row).astype(BF16)
        k = dot_nn(normed, wg_ref[1])
        k_ref[at(b), :] = k
        ku_s[at(b), :] = (k * lax.rsqrt(head_sums(k * k, ones_ref[...]) + EPSILON)).astype(BF16)
        v = dot_nn(normed, wg_ref[2])
        v_ref[at(b), :] = v.astype(BF16)
        vt_s[:, at(b)] = v.T.astype(BF16)

        @pl.when(lax.rem(b, 2) == 0)
        def _():
            up_w.tick(3 + lax.div(b, 2))

        return carry

    lax.fori_loop(0, n_mp, project, 0)
    stores = [
        pltpu.make_async_copy(source, target, store_sem.at[n])
        for n, (source, target) in enumerate(
            ((wg_ref, wg_out), (q_ref, q_out), (k_ref, k_out), (v_ref, v_out), (normed_ref, normed_out), (qu_s, qu_out), (ku_s, ku_out))
        )
    ]
    for copy in stores:
        copy.start()
    first_tick = 3 + (n_mp + 1) // 2
    ticks_left = max(up_w.ticks - first_tick, 0)

    def tick_at(u):
        span = heads * n_mp
        count = lambda v: lax.div(v * ticks_left + span, span)

        @pl.when(count(u) != count(u - 1))
        def _():
            up_w.tick(first_tick + count(u) - 1)

    lanes = lax.broadcasted_iota(jnp.int32, (1, width), 1)

    def block(j, carry):
        kx, same = lax.rem(1 + lax.div(j, 2), r.n_x), lax.rem(j, 2)
        b = r.rank(kx, same)
        bias = column_bias(info, image_of(b), (tokens, 1), SHORT)
        qu = qu_s[at(b), :]
        outs = []
        for h in range(heads):
            mask = ((lanes >= h * size) & (lanes < (h + 1) * size)).astype(F32).astype(BF16)
            scores = dot_nt(ku_s[...], qu * mask) + bias
            top = jnp.max(scores, axis=0, keepdims=True)
            expon = jnp.exp(scores - top)
            total = jnp.sum(expon, axis=0, keepdims=True)
            stats_ref[h : h + 1, at(b)] = top + jnp.log(total)
            tick_at(heads * j + h)
            outs.append(dot_nn(vt_s[h * size : (h + 1) * size, :], expon.astype(BF16)) / total)
        att = jnp.concatenate(outs, axis=0).T.astype(BF16)
        att_ref[at(b), :] = att
        part_s[...] = dot_nt(att, wg_ref[3])

        @pl.when(same == 0)
        def _():
            red.other(kx, part_s[...])

        @pl.when((same == 1) & (kx > 0))
        def _():
            red.same(kx, part_s[...])

        return carry

    lax.fori_loop(0, n_mp, block, 0)
    if heads < 8:
        stats_ref[heads:8, :] = jnp.zeros((8 - heads, tokens), F32)
    middle = x_ref[at(r.m), :].astype(F32) + red.finish(part_s[...])
    mid_ref[...] = middle
    nm_ref[...] = (middle * row_sums_factor(middle) * image_scale(info, mods_ref, 1, image_of(r.m))).astype(BF16)
    red.drain()
    up_w.finish()
    stores.append(pltpu.make_async_copy(wf_ref, wf_out, store_sem.at[7]))
    stores[-1].start()
    for copy in stores:
        copy.wait()


def forward_part(n_dp, n_mp, lengths, sigmas, labels, scales, freqs, x, layer_states, map_states, gains_state):
    images, part = sigmas.shape[0], map_states[0].shape[1]
    units_map = map_states[2].shape[3]
    shard, _, units = layer_states[2].shape[1:]
    width, heads = layer_states[0].shape[3], scales.shape[1]
    tokens = x.shape[0]
    rows = tokens // n_mp
    states = (*layer_states, *map_states)
    f32 = lambda *dims: jax.ShapeDtypeStruct(dims, F32)
    bf16 = lambda *dims: jax.ShapeDtypeStruct(dims, BF16)
    return pl.pallas_call(
        functools.partial(forward_kernel, n_dp, n_mp, heads),
        out_shape=(
            f32(2, IMG_DEV, D),
            f32(n_dp, images + 8, part),
            f32(2, IMG_DEV, units_map),
            f32(images, units_map),
            f32(n_dp, images, part),
            f32(images, part),
            bf16(4, D, width),
            bf16(2, D, units),
            f32(tokens, width),
            f32(tokens, width),
            bf16(tokens, width),
            bf16(tokens, D),
            bf16(tokens, width),
            bf16(tokens, width),
            bf16(tokens, width),
            f32(8, tokens),
            f32(rows, D),
            bf16(rows, D),
        ),
        in_specs=[SMEM_SPEC] * 4 + vmem_specs(2) + any_specs(9),
        out_specs=tuple(vmem_specs(6) + any_specs(8) + vmem_specs(4)),
        scratch_shapes=[
            pltpu.VMEM((4, D, width), BF16),
            pltpu.VMEM((tokens, width), F32),
            pltpu.VMEM((tokens, width), F32),
            pltpu.VMEM((tokens, width), BF16),
            pltpu.VMEM((tokens, D), BF16),
            pltpu.VMEM((2, D, units), BF16),
            pltpu.VMEM((images, NCLASS), F32),
            pltpu.VMEM((width, width), BF16),
            pltpu.SemaphoreType.DMA((8,)),
        ]
        + [pltpu.VMEM(state.shape[1:], F32) for state in states]
        + [
            pltpu.VMEM(gains_state.shape, F32),
            pltpu.SemaphoreType.DMA((9,)),
            pltpu.VMEM((n_dp, images, part), F32),
            pltpu.VMEM((n_dp, images, part), F32),
            pltpu.VMEM((images + 8, part), F32),
            pltpu.VMEM((n_dp, 2, IMG_DEV, units_map), F32),
            pltpu.VMEM((n_dp, 2, IMG_DEV, units_map), F32),
            pltpu.VMEM((IMG_DEV, units_map), F32),
            pltpu.VMEM((n_dp, IMG_DEV, units_map), F32),
            pltpu.VMEM((1, images, part), F32),
            pltpu.VMEM((n_mp, images, part), F32),
            pltpu.VMEM((images, part), F32),
            pltpu.VMEM((n_dp, 2, IMG_DEV, D), F32),
            pltpu.VMEM((n_dp, 2, IMG_DEV, D), F32),
            pltpu.SemaphoreType.DMA((6, n_dp)),
            pltpu.SemaphoreType.DMA((6, n_dp)),
            pltpu.SemaphoreType.DMA((1, n_mp)),
            pltpu.SemaphoreType.DMA((1, n_mp)),
        ]
        + line_sems(n_dp, 4)
        + line_sems(n_dp, 2 * cuts(shard))
        + [
            pltpu.VMEM((tokens, width), BF16),
            pltpu.VMEM((tokens, width), BF16),
            pltpu.VMEM((width, tokens), BF16),
            pltpu.VMEM((rows, D), F32),
        ]
        + reduce_scratch(n_mp, rows),
        compiler_params=pltpu.CompilerParams(
            collective_id=0, has_side_effects=True, vmem_limit_bytes=FORWARD_VMEM
        ),
        name="forward_part",
    )(lengths, sigmas, labels, scales, freqs, x, *states, gains_state)


def ffn_kernel(
    n_dp, n_mp, lengths_ref, nm_ref, mods_ref, mid_ref, cot_ref, wf_ref, down_ref,
    gd_ref, dmid_ref, fmod_ref, gated_out, wd_out, gw_out,
    w_s, cot_s, nm_s, gated_s, gate_s, slope_s, dh_s, dz_s, part_s, gw_s, gather_sem,
    b_core_send, b_core_recv, b_x_send, b_x_recv, b_sems,
    down_s, wd_s, load_sem, store_sem, w_zs, w_zr, w_ys, w_yr,
    recv_y, send_z, recv_z, g_zs, g_zr, g_ys, g_yr,
):
    r = Ranks(n_mp)
    grid = Grid(n_dp)
    info = Images(lengths_ref)
    copies = loads(((down_ref.at[0], down_s), (wf_ref, w_s), (cot_ref, cot_s)), load_sem)
    rows = nm_ref.shape[0]
    tokens = rows * n_mp
    at = lambda b: pl.ds(pl.multiple_of(b * rows, rows), rows)
    image_of = lambda b: lax.div(b * rows, SHORT)

    greet(
        [
            (n_dp, lambda k: (lax.rem(r.d + k, n_dp), r.m)),
            (2, lambda k: r.sibling),
            (r.n_x, r.chip),
        ]
    )
    shard = D // n_dp
    parts = cuts(shard)
    small = shard // parts
    copies[0].wait()
    wd_s[0, pl.ds(pl.multiple_of(r.d * shard, shard), shard), :] = down_s[...].T.astype(BF16)
    down_w = BulkGather(grid, parts, cut_rows(wd_s, shard), w_zs, w_zr, w_ys, w_yr)
    first = scatter_split(shard)[0]
    down_g = BulkScatter(
        grid, first, cut_rows(gw_s, shard), lambda i: gd_ref.at[i],
        recv_y, send_z, recv_z, g_zs, g_zr, g_ys, g_yr)
    each_piece(down_w.send, 0, parts)
    nm_s[at(r.m), :] = nm_ref[...]
    gather = Gather(r, rows, nm_s, gather_sem)
    gather.start()
    copies[1].wait()
    bwd = Reduce(r, b_core_send, b_core_recv, b_x_send, b_x_recv, b_sems)

    def forward(j, carry):
        kx = lax.div(j, 2)
        same = jnp.where(kx == 0, 1 - lax.rem(j, 2), lax.rem(j, 2))
        b = r.rank(kx, same)
        back_kx = lax.rem(r.n_x - kx, r.n_x)

        if_piece(down_w.forward, j - 1, 0, min(2, parts))

        @pl.when((same == 0) & (kx > 0))
        def _():
            gather.forward(back_kx)

        @pl.when(same == 0)
        def _():
            gather.arrived(back_kx)

        nm = nm_s[at(b), :]
        hidden = dot_nn(nm, w_s[0])
        gate = dot_nn(nm, w_s[1])
        value, slope = gelu_parts(gate)
        gated = (hidden * value).astype(BF16)
        gated_s[at(b), :] = gated
        gate_s[at(b), :] = value
        slope_s[at(b), :] = hidden * slope
        if_piece(down_w.forward, j, 2, parts)
        return carry

    lax.fori_loop(0, n_mp, forward, 0)
    copies[2].wait()

    def live_rows(b):
        position = lax.broadcasted_iota(jnp.int32, (rows, 1), 0) + b * rows
        return (position.astype(F32) < info.live).astype(F32)

    def live_cotangent(b, carry):
        dz_s[at(b), :] = (cot_s[at(b), :].astype(F32) * live_rows(b)).astype(BF16)
        return carry

    lax.fori_loop(0, n_mp, live_cotangent, 0)
    step = 512

    def down_gradient(i, carry):
        cols = pl.ds(pl.multiple_of(i * step, step), step)
        gw_s[0, cols, :] = dot_tn(dz_s[:, cols], gated_s[...]).astype(BF16)
        return carry

    lax.fori_loop(0, D // step, down_gradient, 0)
    each_piece(down_g.send, 0, first)
    each_piece(down_w.forward, n_mp, parts)
    down_w.finish()
    stores = [
        pltpu.make_async_copy(source, target, store_sem.at[n])
        for n, (source, target) in enumerate(((gated_s, gated_out), (wd_s.at[0], wd_out), (gw_s.at[0], gw_out.at[0])))
    ]
    for copy in stores:
        copy.start()

    def backward(j, carry):
        kx, same = lax.rem(1 + lax.div(j, 2), r.n_x), lax.rem(j, 2)
        b = r.rank(kx, same)
        if_piece(down_g.forward, j - (n_mp - 2), 0, first)
        d_gated = dot_nn(dz_s[at(b), :], wd_s[0])
        d_value = (d_gated * gate_s[at(b), :]).astype(BF16)
        d_gate = (d_gated * slope_s[at(b), :]).astype(BF16)
        dh_s[0, at(b), :] = d_value
        dh_s[1, at(b), :] = d_gate
        part_s[...] = dot_nt(d_value, w_s[0]) + dot_nt(d_gate, w_s[1])

        @pl.when(same == 0)
        def _():
            bwd.other(kx, part_s[...])

        @pl.when((same == 1) & (kx > 0))
        def _():
            bwd.same(kx, part_s[...])

        return carry

    lax.fori_loop(0, n_mp, backward, 0)

    def up_gradient(i, carry):
        if_piece(down_g.forward, i + 2, 2, first)
        cols = pl.ds(pl.multiple_of(i * step, step), step)
        left = nm_s[:, cols]
        for c in range(2):
            gw_s[1 + c, cols, :] = dot_tn(left, dh_s[c]).astype(BF16)
        return carry

    lax.fori_loop(0, D // step, up_gradient, 0)

    each_piece(down_g.forward, D // step + 2, first)
    up_store = pltpu.make_async_copy(gw_s.at[pl.ds(1, 2)], gw_out.at[pl.ds(1, 2)], store_sem.at[3])
    up_store.start()
    d_nm = bwd.finish(part_s[...])
    middle = mid_ref[...]
    live = live_rows(r.m)
    scale = image_scale(info, mods_ref, 1, image_of(r.m))
    factor = row_sums_factor(middle)
    inner = jnp.mean(middle * scale * d_nm, axis=-1, keepdims=True)
    dmid_ref[...] = cot_s[at(r.m), :].astype(F32) * live + (
        factor * scale * d_nm - middle * (factor * factor * factor * inner)
    )
    fmod_ref[...] = jnp.sum(d_nm * middle * factor, axis=0, keepdims=True)
    gather.drain()
    bwd.drain()
    down_g.finish()
    for copy in stores + [up_store]:
        copy.wait()


def ffn(n_dp, n_mp, lengths, nm, mods, mid, cot, wf, down_state):
    rows = nm.shape[0]
    tokens = rows * n_mp
    units = wf.shape[2]
    shard = D // n_dp
    parts = cuts(shard)
    first = scatter_split(shard)[0]
    shape = jax.ShapeDtypeStruct
    return pl.pallas_call(
        functools.partial(ffn_kernel, n_dp, n_mp),
        out_shape=(
            shape((first, shard // parts, units), F32),
            shape((rows, D), F32),
            shape((1, D), F32),
            shape((tokens, units), BF16),
            shape((D, units), BF16),
            shape((3, D, units), BF16),
        ),
        in_specs=[SMEM_SPEC] + vmem_specs(3) + any_specs(3),
        out_specs=tuple(vmem_specs(3) + any_specs(3)),
        scratch_shapes=[
            pltpu.VMEM((2, D, units), BF16),
            pltpu.VMEM((tokens, D), BF16),
            pltpu.VMEM((tokens, D), BF16),
            pltpu.VMEM((tokens, units), BF16),
            pltpu.VMEM((tokens, units), F32),
            pltpu.VMEM((tokens, units), F32),
            pltpu.VMEM((2, tokens, units), BF16),
            pltpu.VMEM((tokens, D), BF16),
            pltpu.VMEM((rows, D), F32),
            pltpu.VMEM((3, D, units), BF16),
            gather_sems(n_mp),
        ]
        + reduce_scratch(n_mp, rows)
        + [
            pltpu.VMEM(down_state.shape[1:], F32),
            pltpu.VMEM((1, D, units), BF16),
            pltpu.SemaphoreType.DMA((3,)),
            pltpu.SemaphoreType.DMA((4,)),
        ]
        + bulk_sems(n_dp, parts)
        + scatter_scratch(n_dp, first, shard // parts, units),
        compiler_params=pltpu.CompilerParams(
            collective_id=4, has_side_effects=True, vmem_limit_bytes=FFN_VMEM
        ),
        name="ffn",
    )(lengths, nm, mods, mid, cot, wf, down_state)


def attn_backward_kernel(
    n_dp, n_mp, heads, lengths_ref, scales_ref, dmid_ref, mods_ref, stats_ref,
    qu_any, ku_any, gffn_ref, wg_any, v_any, q_any, k_any, normed_any, att_any, x_any,
    gw_ref, gf_ref, gin_ref, amod_ref, gscale_ref,
    gffn_s, wg_ref, v_ref, q_ref, k_ref, normed_ref, att_ref, x_ref, ones_ref, load_sem,
    qu_s, ku_s, kt_s, dy_s, dq_s, dk_s, dv_s, low_s, part_s, gather_sem,
    core_send, core_recv, x_send, x_recv, sems,
    recv_y, send_z, recv_z, f_zs, f_zr, f_ys, f_yr,
):
    r = Ranks(n_mp)
    info = Images(lengths_ref)
    rows = dmid_ref.shape[0]
    tokens = rows * n_mp
    width = q_ref.shape[1]
    size = width // heads
    at = lambda b: pl.ds(pl.multiple_of(b * rows, rows), rows)
    image_of = lambda b: lax.div(b * rows, SHORT)
    copies = loads(
        (
            (ku_any, ku_s),
            (qu_any, qu_s),
            (wg_any, wg_ref),
            (v_any, v_ref),
            (gffn_ref, gffn_s),
            (q_any, q_ref),
            (k_any, k_ref),
            (normed_any, normed_ref),
            (att_any, att_ref),
            (x_any.at[at(r.m), :], x_ref),
        ),
        load_sem,
    )
    dy_s[at(r.m), :] = dmid_ref[...].astype(BF16)
    grid = Grid(n_dp)
    greet(
        [
            (n_dp, lambda k: (lax.rem(r.d + k, n_dp), r.m)),
            (2, lambda k: r.sibling),
            (r.n_x, r.chip),
        ]
    )
    gather = Gather(r, rows, dy_s, gather_sem)
    gather.start()
    shard = D // n_dp
    start, end = scatter_split(shard)
    ffn_g = BulkScatter(
        grid, end - start, cut_rows(gffn_s, shard, start), lambda i: gf_ref.at[i],
        recv_y, send_z, recv_z, f_zs, f_zr, f_ys, f_yr, sent=cut_rows(gffn_ref, shard, start))
    each_piece(ffn_g.send, 0, ffn_g.pieces)
    ones_ref[...] = head_ones(width, heads)
    scale_row = head_scales(scales_ref, width, heads)
    red = Reduce(r, core_send, core_recv, x_send, x_recv, sems)

    copies[0].wait()

    def units(b, carry):
        kt_s[:, at(b)] = ku_s[at(b), :].astype(F32).T.astype(BF16)
        return carry

    lax.fori_loop(0, n_mp, units, 0)
    for copy in copies[1:5]:
        copy.wait()
    dk_s[...] = jnp.zeros_like(dk_s)
    dv_s[...] = jnp.zeros_like(dv_s)
    lanes = lax.broadcasted_iota(jnp.int32, (1, width), 1)

    pace = (2, 3, 1)

    def block(j, carry):
        kx = lax.div(j, 2)
        same = 1 - lax.rem(j, 2)
        b = r.rank(kx, same)
        back_kx = lax.rem(r.n_x - kx, r.n_x)

        @pl.when((same == 1) & (kx > 0))
        def _():
            gather.forward(back_kx)

        @pl.when(same == 0)
        def _():
            gather.arrived(back_kx)

        d_att = dot_nn(dy_s[at(b), :], wg_ref[3]).astype(BF16)
        bias = column_bias(info, image_of(b), (tokens, 1), SHORT)
        qu = qu_s[at(b), :]
        outs = []
        for h in range(heads):
            mask = ((lanes >= h * size) & (lanes < (h + 1) * size)).astype(F32).astype(BF16)
            qh = qu * mask
            dh = d_att * mask
            probs = jnp.exp(dot_nt(ku_s[...], qh) + bias - stats_ref[h : h + 1, at(b)])
            ffn_g.paced_forward(heads * j + h, *pace)
            d_probs = dot_nt(v_ref[...], dh)
            inner = jnp.sum(probs * d_probs, axis=0, keepdims=True)
            d_scores = (probs * (d_probs - inner)).astype(BF16)
            dv_s[...] = dv_s[...] + dot_nn(probs.astype(BF16), dh)
            dk_s[...] = dk_s[...] + dot_nn(d_scores, qh)
            outs.append(dot_nn(kt_s[h * size : (h + 1) * size, :], d_scores))
        dq_s[at(b), :] = jnp.concatenate(outs, axis=0).T
        return carry

    lax.fori_loop(0, n_mp, block, 0)

    def inputs(j, scale_grad):
        kx, same = lax.rem(1 + lax.div(j, 2), r.n_x), lax.rem(j, 2)
        b = r.rank(kx, same)
        q, k = q_ref[at(b), :], k_ref[at(b), :]
        q_factor = lax.rsqrt(head_sums(q * q, ones_ref[...]) + EPSILON)
        k_factor = lax.rsqrt(head_sums(k * k, ones_ref[...]) + EPSILON)
        dqu, dku = dq_s[at(b), :], dk_s[at(b), :]
        q_unit, k_unit = q * q_factor, k * k_factor
        q_along = dqu * q_unit
        d_q = (scale_row * q_factor * (dqu - q_unit * head_sums(q_along, ones_ref[...]))).astype(BF16)
        d_k = (k_factor * (dku - k_unit * head_sums(dku * k_unit, ones_ref[...]))).astype(BF16)
        d_v = dv_s[at(b), :].astype(BF16)
        low_s[at(b), 0:width] = d_q
        low_s[at(b), width : 2 * width] = d_k
        low_s[at(b), 2 * width : 3 * width] = d_v
        part_s[...] = dot_nt(d_q, wg_ref[0]) + dot_nt(d_k, wg_ref[1]) + dot_nt(d_v, wg_ref[2])

        @pl.when(same == 0)
        def _():
            red.other(kx, part_s[...])

        @pl.when((same == 1) & (kx > 0))
        def _():
            red.same(kx, part_s[...])

        ffn_g.paced_forward(heads * n_mp + j, *pace)
        return scale_grad + jnp.sum(q_along, axis=0, keepdims=True)

    for copy in copies[5:7]:
        copy.wait()
    gscale_ref[...] = lax.fori_loop(0, n_mp, inputs, jnp.zeros((1, width), F32))

    for copy in copies[7:]:
        copy.wait()
    step = 512

    def weights(i, carry):
        ffn_g.paced_forward(heads * n_mp + n_mp + i, *pace)
        cols = pl.ds(pl.multiple_of(i * step, step), step)
        value = dot_tn(normed_ref[:, cols], low_s[...]).astype(BF16)
        for c in range(3):
            gw_ref[c, cols, :] = value[:, c * width : (c + 1) * width]
        gw_ref[3, cols, :] = dot_tn(dy_s[:, cols], att_ref[...]).astype(BF16)
        return carry

    lax.fori_loop(0, D // step, weights, 0)
    each_piece(ffn_g.forward, ffn_g.after(ffn_g.pieces, *pace, heads * n_mp + n_mp + D // step), ffn_g.pieces)

    d_normed = red.finish(part_s[...])
    x = x_ref[...].astype(F32)
    scale = image_scale(info, mods_ref, 0, image_of(r.m))
    factor = row_sums_factor(x)
    inner = jnp.mean(x * scale * d_normed, axis=-1, keepdims=True)
    gin_ref[...] = dmid_ref[...] + (factor * scale * d_normed - x * (factor * factor * factor * inner))
    amod_ref[...] = jnp.sum(d_normed * x * factor, axis=0, keepdims=True)
    gather.drain()
    red.drain()
    ffn_g.finish()


def attn_backward(n_dp, n_mp, lengths, scales, dmid, mods, stats, qu, ku, gffn, wg, v, q, k, normed, att, x):
    rows = dmid.shape[0]
    tokens = rows * n_mp
    width, heads = q.shape[1], scales.shape[1]
    shard = D // n_dp
    small = shard // cuts(shard)
    start, end = scatter_split(shard)
    shape = jax.ShapeDtypeStruct
    return pl.pallas_call(
        functools.partial(attn_backward_kernel, n_dp, n_mp, heads),
        out_shape=(
            shape(wg.shape, BF16),
            shape((end - start, small, gffn.shape[2]), F32),
            shape((rows, D), F32),
            shape((1, D), F32),
            shape((1, width), F32),
        ),
        in_specs=[SMEM_SPEC] * 2 + vmem_specs(3) + any_specs(10),
        out_specs=tuple(vmem_specs(5)),
        scratch_shapes=[
            pltpu.VMEM(gffn.shape, BF16),
            pltpu.VMEM(wg.shape, BF16),
            pltpu.VMEM((tokens, width), BF16),
            pltpu.VMEM((tokens, width), F32),
            pltpu.VMEM((tokens, width), F32),
            pltpu.VMEM((tokens, D), BF16),
            pltpu.VMEM((tokens, width), BF16),
            pltpu.VMEM((rows, D), BF16),
            pltpu.VMEM((width, width), BF16),
            pltpu.SemaphoreType.DMA((10,)),
            pltpu.VMEM((tokens, width), BF16),
            pltpu.VMEM((tokens, width), BF16),
            pltpu.VMEM((width, tokens), BF16),
            pltpu.VMEM((tokens, D), BF16),
            pltpu.VMEM((tokens, width), F32),
            pltpu.VMEM((tokens, width), F32),
            pltpu.VMEM((tokens, width), F32),
            pltpu.VMEM((tokens, 3 * width), BF16),
            pltpu.VMEM((rows, D), F32),
            gather_sems(n_mp),
        ]
        + reduce_scratch(n_mp, rows)
        + scatter_scratch(n_dp, end - start, small, gffn.shape[2]),
        compiler_params=pltpu.CompilerParams(
            collective_id=5, has_side_effects=True, vmem_limit_bytes=ATTN_VMEM
        ),
        name="attn_backward",
    )(lengths, scales, dmid, mods, stats, qu, ku, gffn, wg, v, q, k, normed, att, x)


def squares(value):
    return jnp.sum(jnp.sum(value * value, axis=0, keepdims=True), axis=-1, keepdims=True)


def back_kernel(
    n_dp, n_mp, heads,
    lengths_ref, labels_ref, grads_ref, amod_ref, fmod_ref, mid_ref, gin_ref, feats_ref, gd_ref, gu_ref, gscale_ref,
    emb_ref, hid_ref, gated_ref, mixed_ref,
    mapup_ref, mapdown_ref, mod_ref, gffn_ref, ffgated_ref, wd_ref,
    gattn_ref, gf_ref, out_all, gin_s, gmod_ref, gmd_ref, gmu_ref, gtime_ref, gclass_ref, ggain_ref, norm_ref,
    mapup_s, mapdown_s, mod_s, gffn_s, ffgated_s, wd_s, load_sem, own_r, full_e, onehot_s, out_sem, gin_sem,
    recv_q, stage_q, own_q, recv_d, full_d, own_c, recv_c, send_g, recv_g, own_h, recv_h, full_h,
    own_p, recv_p, own_s, recv_s, own_n, all_dp, own_sum, all_mp,
    dp_ss, dp_rs, mp_ss, mp_rs,
    core_send, core_recv, x_send, x_recv, sems,
    recv_y, send_z, recv_z, a_zs, a_zr, a_ys, a_yr,
    f_recv_y, f_send_z, f_recv_z, f_zs, f_zr, f_ys, f_yr,
):
    r = Ranks(n_mp)
    d, m = r.d, r.m
    info = Images(lengths_ref)
    grid = Grid(n_dp)
    shard = gattn_ref.shape[1]
    start = scatter_split(shard)[1]
    tall = shard // 2
    attn_g = BulkScatter(
        grid, 8,
        lambda dd, i: grads_ref.at[
            lax.div(i, 2), pl.ds(pl.multiple_of(dd * shard + lax.rem(i, 2) * tall, tall), tall), :
        ],
        lambda i: gattn_ref.at[lax.div(i, 2), pl.ds(pl.multiple_of(lax.rem(i, 2) * tall, tall), tall), :],
        recv_y, send_z, recv_z, a_zs, a_zr, a_ys, a_yr)
    ffn_g = BulkScatter(
        grid, 3 * cuts(shard) - start, cut_rows(gffn_s, shard, start - 2 * cuts(shard)), lambda i: gf_ref.at[i],
        f_recv_y, f_send_z, f_recv_z, f_zs, f_zr, f_ys, f_yr)
    images, own_cols = feats_ref.shape
    rows = mid_ref.shape[0]
    copies = loads(
        (
            (mod_ref.at[0], mod_s),
            (mapdown_ref.at[0], mapdown_s),
            (mapup_ref.at[0], mapup_s),
            (ffgated_ref, ffgated_s),
            (wd_ref, wd_s),
            (gffn_ref.at[pl.ds(2, 1)], gffn_s),
        ),
        load_sem,
    )
    greet(
        [
            (n_dp, lambda k: (lax.rem(d + k, n_dp), m)),
            (n_mp, lambda k: (d, lax.rem(m + k, n_mp))),
        ]
    )
    at = lambda b: pl.ds(pl.multiple_of(b * rows, rows), rows)
    gin_s[at(m), :] = gin_ref[...].astype(BF16)
    one = Gather(r, rows, out_all, out_sem)
    two = Gather(r, rows, gin_s, gin_sem)
    red = Reduce(r, core_send, core_recv, x_send, x_recv, sems)

    def branch(j):
        kx, same = (1 + j // 2) % r.n_x, j % 2
        part = dot_nt(ffgated_s[at(r.rank(kx, same)), :], wd_s[...])
        if same == 0:
            red.other(kx, part)
        elif kx > 0:
            red.same(kx, part)
        else:
            position = lax.broadcasted_iota(jnp.int32, (rows, 1), 0) + m * rows
            live = (position.astype(F32) < info.live).astype(F32)
            out_all[at(m), :] = ((mid_ref[...] + red.finish(part)) * live).astype(BF16)

    def branches(quarter):
        for j in range(quarter * n_mp // 4, (quarter + 1) * n_mp // 4):
            branch(j)

    own_r[0:1, :] = amod_ref[...]
    own_r[1:2, :] = fmod_ref[...]

    def dp_ex(stage):
        return Exchange(n_dp, d, lambda p: (p, m), dp_ss.at[stage], dp_rs.at[stage])

    def mp_ex(stage):
        return Exchange(n_mp, m, lambda p: (d, p), mp_ss.at[stage], mp_rs.at[stage])

    def local_squares():
        value = jnp.zeros((1, 1), F32)
        for i in range(gd_ref.shape[0]):
            value = value + squares(gd_ref[i])
        for i in range(gu_ref.shape[0]):
            value = value + squares(gu_ref[i])
        return value

    ex = mp_ex(0)
    ex.start(lambda p: own_r, recv_q)
    attn_g.send(0)
    copies[5].wait()
    ffn_g.send(0)
    fill_onehot(onehot_s, labels_ref)
    recv_q[m] = own_r[...]
    ex.wait(lambda p: own_r, recv_q)
    for image in range(IMG_DEV):
        for c in range(2):
            row = jnp.zeros((1, D), F32)
            for rank in range(n_mp):
                share = 1.0 - info.is_long if rank * rows // SHORT == image else 0.0
                if image == 0:
                    share = share + info.is_long
                row = row + share * recv_q[rank, c : c + 1, :]
            stage_q[c * IMG_DEV + image : c * IMG_DEV + image + 1, :] = row
    own_q[...] = pack_rows(stage_q[...])
    two.start()
    ex = dp_ex(0)
    ex.start(lambda p: own_q, recv_d)
    attn_g.send(1)
    for copy in copies[:5]:
        copy.wait()
    branches(0)
    ffn_g.forward(0)
    recv_d[d] = own_q[...]
    gains_own = emb_ref[d][images:]
    emb = emb_ref[:, 0:images, :]
    emb_factor = rms_blocks(emb)
    unit = emb * emb_factor[None] * emb_ref[:, images : images + 1, :]
    unit_factor = rms_blocks(unit)
    emb_own = emb_ref[d][0:images]
    unit_own = emb_own * emb_factor * gains_own[0:1]
    pre_own = (unit_own * unit_factor * gains_own[1:2]).astype(BF16)
    mixed = mixed_ref[...]
    mixed_factor = rms_blocks(mixed)
    mixed_own = mixed_ref[d]
    cond_own = (mixed_own * mixed_factor * gains_own[2:3]).astype(BF16)
    ex.wait(lambda p: own_q, recv_d)
    for p in range(n_dp):
        block = recv_d[p].astype(F32)
        for c in range(2):
            for half in range(2):
                first = (2 * half + c) * IMG_DEV
                full_d[c, p * IMG_DEV : (p + 1) * IMG_DEV, half * D // 2 : (half + 1) * D // 2] = block[
                    first : first + IMG_DEV
                ]
    own_c[...] = two_part_left(dot_nt, full_d[0], mod_s[:, 0, :].astype(BF16)) + two_part_left(
        dot_nt, full_d[1], mod_s[:, 1, :].astype(BF16)
    )
    ex = dp_ex(1)
    ex.start(lambda p: own_c, recv_c)
    attn_g.send(2)
    attn_g.forward(0)
    branches(1)
    recv_c[d] = own_c[...]
    squares_mod = jnp.zeros((1, 1), F32)
    for c in range(2):
        grad = two_part(dot_tn, cond_own, full_d[c])
        gmod_ref[:, c, :] = grad
        squares_mod = squares_mod + squares(grad)
    ex.wait(lambda p: own_c, recv_c)
    ggain_ref[2:3, :] = jnp.sum(own_c[...] * mixed_own * mixed_factor, axis=0, keepdims=True)
    d_mixed = rms_blocks_back(
        mixed, mixed_factor, recv_c[...] * emb_ref[:, images + 2 : images + 3, :]
    )
    recv_c[...] = d_mixed
    mix_own = recv_c[d]
    part = two_part_left(dot_nn, mix_own, mapdown_s[...].astype(BF16))
    for p in range(n_dp):
        send_g[p] = part[p * IMG_DEV : (p + 1) * IMG_DEV, :]
    ex = dp_ex(2)
    ex.start(lambda p: send_g.at[p], recv_g)
    attn_g.send(3)
    attn_g.forward(1)
    branches(2)
    recv_g[d] = send_g[d]
    grad = two_part_left(dot_tn, mix_own, gated_ref[...].astype(BF16))
    gmd_ref[...] = grad
    squares_md = squares(grad)
    ex.wait(lambda p: send_g.at[p], recv_g)
    d_gated = total_of(recv_g, n_dp)
    value, slope = gelu_parts(hid_ref[1])
    own_h[0] = d_gated * value
    own_h[1] = d_gated * hid_ref[0] * slope
    ex = dp_ex(3)
    ex.start(lambda p: own_h, recv_h)
    recv_h[d] = own_h[...]
    attn_g.send(4)
    attn_g.forward(2)
    branches(3)
    ex.wait(lambda p: own_h, recv_h)
    for p in range(n_dp):
        for c in range(2):
            full_h[c, p * IMG_DEV : (p + 1) * IMG_DEV, :] = recv_h[p, c]
    own_p[...] = two_part_left(dot_nt, full_h[0], mapup_s[:, 0, :].astype(BF16)) + two_part_left(
        dot_nt, full_h[1], mapup_s[:, 1, :].astype(BF16)
    )
    ex = mp_ex(1)
    ex.start(lambda p: own_p, recv_p)
    one.start()
    attn_g.send(5)
    attn_g.send(6)
    attn_g.forward(3)
    squares_done = local_squares() + squares_md
    recv_p[m] = own_p[...]
    for c in range(2):
        grad = two_part(dot_tn, pre_own, full_h[c])
        gmu_ref[:, c, :] = grad
        squares_done = squares_done + squares(grad)
    ex.wait(lambda p: own_p, recv_p)
    own_s[...] = total_of(recv_p, n_mp)
    ex = dp_ex(4)
    ex.start(lambda p: own_s, recv_s)
    attn_g.send(7)
    attn_g.forward(4)
    attn_g.forward(5)
    recv_s[d] = own_s[...]
    ex.wait(lambda p: own_s, recv_s)
    ggain_ref[1:2, :] = jnp.sum(own_s[...] * unit_own * unit_factor, axis=0, keepdims=True)
    d_unit = recv_c[...] + rms_blocks_back(
        unit, unit_factor, recv_s[...] * emb_ref[:, images + 1 : images + 2, :]
    )
    recv_s[...] = d_unit
    ggain_ref[0:1, :] = jnp.sum(recv_s[d] * emb_own * emb_factor, axis=0, keepdims=True)
    d_emb = rms_blocks_back(emb, emb_factor, d_unit * emb_ref[:, images : images + 1, :])
    recv_s[...] = d_emb
    ggain_ref[3:8, :] = jnp.zeros_like(ggain_ref[3:8, :])
    for p in range(n_dp):
        full_e[:, p * own_cols : (p + 1) * own_cols] = recv_s[p]
    attn_g.forward(6)
    attn_g.forward(7)
    gtime_ref[...] = two_part(dot_tn, feats_ref[...].astype(BF16), full_e[...])
    gclass_ref[...] = two_part_left(dot_tn, recv_s[d], onehot_s[...].astype(BF16))
    attn_g.finish()
    ffn_g.finish()
    split = squares_done
    for c in range(4):
        split = split + squares(gattn_ref[c])
    for i in range(ffn_g.pieces):
        split = split + squares(gf_ref[i])
    shared = squares_mod + squares(gtime_ref[...]) + squares(gclass_ref[...]) + squares(ggain_ref[...])
    lane = lax.broadcasted_iota(jnp.int32, (1, 128), 1)
    own_n[...] = jnp.zeros_like(own_n)
    own_n[0:1, :] = jnp.where(lane == 0, split + shared * (1.0 / n_mp), 0.0)
    width = gscale_ref.shape[1]
    column = lax.div(lax.broadcasted_iota(jnp.int32, (1, width), 1), width // heads)
    scale_row = jnp.zeros((1, 128), F32)
    for h in range(heads):
        head_part = jnp.sum(jnp.where(column == h, gscale_ref[...], 0.0), axis=-1, keepdims=True)
        scale_row = jnp.where(lane == h, head_part, scale_row)
    own_n[1:2, :] = scale_row
    ex = dp_ex(5)
    ex.start(lambda p: own_n, all_dp)
    all_dp[d] = own_n[...]
    for kx in range(1, r.n_x):
        one.forward(kx)
        two.forward(kx)
    ex.wait(lambda p: own_n, all_dp)
    summed = total_of(all_dp, n_dp)
    head = summed[1:2]
    own_sum[...] = jnp.zeros_like(own_sum)
    own_sum[0:1, :] = summed[0:1] + head * head
    ex = mp_ex(2)
    ex.start(lambda p: own_sum, all_mp)
    all_mp[m] = own_sum[...]
    for kx in range(r.n_x):
        one.arrived(kx)
        two.arrived(kx)
    ex.wait(lambda p: own_sum, all_mp)
    norm = jnp.sqrt(jnp.sum(total_of(all_mp, n_mp)[0:1], axis=-1, keepdims=True))
    norm_ref[0:1, :] = jnp.broadcast_to(norm, (1, 128))
    norm_ref[1:2, :] = head
    norm_ref[2:8, :] = jnp.zeros((6, 128), F32)
    red.drain()
    one.drain()
    two.drain()


def back(n_dp, n_mp, lengths, labels, grads, amod, fmod, mid, gin, feats, gd, gu, gscale, emb, hid, gated, mixed, map_states, gffn, ffgated, wd):
    images, part = feats.shape
    units_map = map_states[0].shape[3]
    rows = mid.shape[0]
    tokens = rows * n_mp
    heads = H // n_mp
    slab = (4, grads.shape[1] // n_dp, grads.shape[2])
    shard, units = slab[1], gffn.shape[2]
    small = shard // cuts(shard)
    pieces = 3 * cuts(shard) - scatter_split(shard)[1]
    shape = lambda *dims: jax.ShapeDtypeStruct(dims, F32)
    block = pltpu.VMEM((8, 128), F32)
    return pl.pallas_call(
        functools.partial(back_kernel, n_dp, n_mp, heads),
        out_shape=(
            shape(*slab),
            shape(pieces, small, units),
            jax.ShapeDtypeStruct((tokens, D), BF16),
            jax.ShapeDtypeStruct((tokens, D), BF16),
            shape(part, 2, D),
            shape(part, units_map),
            shape(part, 2, units_map),
            shape(part, DM),
            shape(part, NCLASS),
            shape(8, part),
            shape(8, 128),
        ),
        in_specs=[SMEM_SPEC] * 2 + vmem_specs(13) + any_specs(6),
        out_specs=tuple(vmem_specs(11)),
        scratch_shapes=[pltpu.VMEM(state.shape[1:], F32) for state in map_states]
        + [
            pltpu.VMEM((1, D, units), BF16),
            pltpu.VMEM((tokens, units), BF16),
            pltpu.VMEM((D, units), BF16),
            pltpu.SemaphoreType.DMA((6,)),
            pltpu.VMEM((2, D), F32),
            pltpu.VMEM((images, DM), F32),
            pltpu.VMEM((images, NCLASS), F32),
            gather_sems(n_mp),
            gather_sems(n_mp),
            pltpu.VMEM((n_mp, 2, D), F32),
            pltpu.VMEM((2 * IMG_DEV, D), F32),
            pltpu.VMEM((4 * IMG_DEV, D // 2), BF16),
            pltpu.VMEM((n_dp, 4 * IMG_DEV, D // 2), BF16),
            pltpu.VMEM((2, images, D), F32),
            pltpu.VMEM((images, part), F32),
            pltpu.VMEM((n_dp, images, part), F32),
            pltpu.VMEM((n_dp, IMG_DEV, units_map), F32),
            pltpu.VMEM((n_dp, IMG_DEV, units_map), F32),
            pltpu.VMEM((2, IMG_DEV, units_map), F32),
            pltpu.VMEM((n_dp, 2, IMG_DEV, units_map), F32),
            pltpu.VMEM((2, images, units_map), F32),
            pltpu.VMEM((images, part), F32),
            pltpu.VMEM((n_mp, images, part), F32),
            pltpu.VMEM((images, part), F32),
            pltpu.VMEM((n_dp, images, part), F32),
            block,
            pltpu.VMEM((n_dp, 8, 128), F32),
            block,
            pltpu.VMEM((n_mp, 8, 128), F32),
            pltpu.SemaphoreType.DMA((6, n_dp)),
            pltpu.SemaphoreType.DMA((6, n_dp)),
            pltpu.SemaphoreType.DMA((3, n_mp)),
            pltpu.SemaphoreType.DMA((3, n_mp)),
        ]
        + reduce_scratch(n_mp, rows)
        + scatter_scratch(n_dp, 8, slab[1] // 2, slab[2])
        + scatter_scratch(n_dp, pieces, small, units),
        compiler_params=pltpu.CompilerParams(
            collective_id=1, has_side_effects=True, vmem_limit_bytes=BACK_VMEM
        ),
        name="back",
    )(lengths, labels, grads, amod, fmod, mid, gin, feats, gd, gu, gscale, emb, hid, gated, mixed, *map_states, gffn, ffgated, wd)


def update_kernel(heads, *refs):
    states, refs = refs[:11], refs[11:]
    norm_ref, gattn_ref, gtime_ref, gclass_ref, gmu_ref, gmd_ref, gmod_ref, ggain_ref = refs[:8]
    ffn_refs, out_ref, gin_ref, refs = refs[8:11], refs[11], refs[12], refs[13:]
    outs, out_final, gin_final, norm_out, refs = refs[:33], refs[33], refs[34], refs[35], refs[36:]
    kept, new, first, second = refs[:11], refs[11:22], refs[22:33], refs[33:44]
    gup_s, gdown_s, gin_s, out_s, load_sem, store_sem, out_sem = refs[44:]
    order = (2, 8, 0, 6, 3, 5, 4, 7, 1, 9, 10)
    copies = {i: pltpu.make_async_copy(states[i], kept[i], load_sem.at[i]) for i in order}
    for i in order:
        copies[i].start()
    out_load = pltpu.make_async_copy(out_ref, out_s, out_sem.at[2])
    out_load.start()
    out_copies = [pltpu.make_async_copy(out_s, out_final, out_sem.at[0])]
    out_copies.append(pltpu.make_async_copy(gin_s, gin_final, out_sem.at[1]))
    gin_s[...] = gin_ref[...].astype(F32)
    out_copies[1].start()
    out_load.wait()
    out_copies[0].start()
    parts = cuts(gdown_s.shape[0])
    small = gdown_s.shape[0] // parts
    pieces = [ref.at[i] for ref in ffn_refs for i in range(ref.shape[0])]
    for i, piece in enumerate(pieces):
        rows = slice(i % parts * small, (i % parts + 1) * small)
        if i < parts:
            gdown_s[rows, :] = piece[...]
        else:
            gup_s[rows, i // parts - 1, :] = piece[...]
    factor = CLIP_NORM / jnp.maximum(norm_ref[0:1, 0:1], CLIP_NORM)
    norm_out[...] = norm_ref[0:1, 0:1]
    head = norm_ref[1:2, :]
    rates, decays = learn_rates(), decay_rates()
    stores = []

    def store(i):
        for k, (source, target) in enumerate(((new[i], outs[3 * i]), (first[i], outs[3 * i + 1]), (second[i], outs[3 * i + 2]))):
            stores.append(pltpu.make_async_copy(source, target, store_sem.at[i, k]))
            stores[-1].start()

    def step(i, gradient, pick=lambda ref, k: ref.at[k]):
        copies[i].wait()
        new_weight, average, m_new, v_new = adamw_step(lambda k: pick(kept[i], k)[...], gradient, rates[i], decays[i])
        pick(new[i], 0)[...] = new_weight
        pick(new[i], 1)[...] = average
        first[i][...] = m_new
        second[i][...] = v_new
        store(i)

    step(2, gup_s[...] * factor[:, None, :])
    step(8, gmod_ref[...] * factor[:, None, :])
    copies[0].wait()
    for c in range(3):
        results = adamw_step(lambda k: kept[0][k, c], gattn_ref[c] * factor, rates[0], decays[0])
        new[0][0, c], new[0][1, c], first[0][c], second[0][c] = results
    store(0)
    step(6, gmu_ref[...] * factor[:, None, :])
    step(3, gdown_s[...].T * factor)
    step(5, gclass_ref[...] * factor)
    step(4, gtime_ref[...] * factor)
    step(7, gmd_ref[...] * factor)
    step(1, gattn_ref[3].T * factor)
    copies[9].wait()
    copies[10].wait()
    for g in range(3):
        results = adamw_step(lambda k: kept[9][g, k : k + 1, :], ggain_ref[g : g + 1, :] * factor, rates[9], decays[9])
        new[9][g, 0:1, :], new[9][g, 1:2, :], first[9][g : g + 1, :], second[9][g : g + 1, :] = results
    store(9)
    results = adamw_step(lambda k: kept[10][k : k + 1, :], head[:, 0:heads] * factor, rates[10], decays[10])
    new[10][0:1, :], new[10][1:2, :], first[10][...], second[10][...] = results
    store(10)
    for copy in stores + out_copies:
        copy.wait()


def update(states, norm, grads, ffn_parts, out_all, gin_all):
    heads = states[10].shape[1]
    rows, _, units = states[2].shape[1:]
    news, moments = [], []
    for i, state in enumerate(states):
        if i == 9:
            news.append((state.shape[0], 2, state.shape[2]))
            moments.append((state.shape[0], state.shape[2]))
        else:
            news.append((2,) + state.shape[1:])
            moments.append(state.shape[1:] if i < 10 else (1, heads))
    outs = []
    for new, moment in zip(news, moments):
        outs += [new, moment, moment]
    shape = lambda dims: jax.ShapeDtypeStruct(dims, F32)
    return pl.pallas_call(
        functools.partial(update_kernel, heads),
        out_shape=tuple(shape(o) for o in outs)
        + (jax.ShapeDtypeStruct(out_all.shape, BF16), shape(gin_all.shape), shape((1, 1))),
        in_specs=any_specs(11) + vmem_specs(11) + any_specs(1) + vmem_specs(1),
        out_specs=tuple(any_specs(35) + vmem_specs(1)),
        scratch_shapes=[pltpu.VMEM(state.shape, F32) for state in states]
        + [pltpu.VMEM(dims, F32) for dims in news]
        + [pltpu.VMEM(dims, F32) for dims in moments]
        + [pltpu.VMEM(dims, F32) for dims in moments]
        + [
            pltpu.VMEM((rows, 2, units), F32),
            pltpu.VMEM((rows, units), F32),
            pltpu.VMEM(gin_all.shape, F32),
            pltpu.VMEM(out_all.shape, BF16),
            pltpu.SemaphoreType.DMA((11,)),
            pltpu.SemaphoreType.DMA((11, 3)),
            pltpu.SemaphoreType.DMA((3,)),
        ],
        compiler_params=pltpu.CompilerParams(vmem_limit_bytes=UPDATE_VMEM),
        name="update",
    )(*states, norm, *grads, *ffn_parts, out_all, gin_all)


def per_device(
    block_input,
    out_cotangent,
    sigmas,
    class_labels,
    image_lengths,
    fourier_freqs,
    inproj_state,
    outproj_state,
    upproj_state,
    downproj_state,
    timeproj_state,
    classemb_state,
    mapup_state,
    mapdown_state,
    modproj_state,
    gains_state,
    headscale_state,
):
    n_dp, n_mp = lax.axis_size("dp"), lax.axis_size("mp")
    in_state = jnp.transpose(inproj_state, (0, 2, 1, 3))
    class_state = jnp.transpose(classemb_state, (0, 2, 1))
    down_map_state = jnp.transpose(mapdown_state, (0, 2, 1))
    gain_state = jnp.transpose(gains_state, (1, 0, 2))
    mods, emb, hid, gated, mixed, feats, wg, wf, q, k, v, normed, qu, ku, att, stats, mid, nm = forward_part(
        n_dp, n_mp, image_lengths, sigmas, class_labels, headscale_state, fourier_freqs, block_input,
        (in_state, outproj_state, upproj_state),
        (timeproj_state, class_state, mapup_state, down_map_state, modproj_state), gain_state,
    )
    gd, dmid, fmod, ffgated, wd, gw_ffn = ffn(
        n_dp, n_mp, image_lengths, nm, mods, mid, out_cotangent, wf, downproj_state
    )
    gw_attn, gu, gin, amod, gscale = attn_backward(
        n_dp, n_mp, image_lengths, headscale_state, dmid, mods, stats, qu, ku, gw_ffn, wg, v, q, k, normed, att, block_input
    )
    g_attn, gb, out_all, gin_all, g_mod, g_md, g_mu, g_time, g_class, g_gain, norm = back(
        n_dp, n_mp, image_lengths, class_labels, gw_attn, amod, fmod, mid, gin, feats, gd, gu, gscale,
        emb, hid, gated, mixed, (mapup_state, down_map_state, modproj_state), gw_ffn, ffgated, wd,
    )
    states = (
        in_state,
        outproj_state,
        upproj_state,
        downproj_state,
        timeproj_state,
        class_state,
        mapup_state,
        down_map_state,
        modproj_state,
        gain_state,
        headscale_state,
    )
    grads = (g_attn, g_time, g_class, g_mu, g_md, g_mod, g_gain)
    *new, layer_out, input_grad, grad_norm = update(states, norm, grads, (gd, gu, gb), out_all, gin_all)
    orders = {0: (0, 2, 1, 3), 5: (0, 2, 1), 7: (0, 2, 1), 9: (1, 0, 2)}
    moment_orders = {0: (1, 0, 2), 5: (1, 0), 7: (1, 0)}
    results = [layer_out, input_grad, grad_norm.reshape(())]
    for i in range(11):
        stacked, first, second = new[3 * i : 3 * i + 3]
        if i in orders:
            stacked = jnp.transpose(stacked, orders[i])
        if i in moment_orders:
            first, second = jnp.transpose(first, moment_orders[i]), jnp.transpose(second, moment_orders[i])
        if i == 10:
            first, second = first[0], second[0]
        results += [stacked, first, second]
    return tuple(results)


def solution(mesh):
    return jax.shard_map(
        per_device,
        mesh=mesh,
        in_specs=(
            P("dp", None),
            P("dp", None),
            P(),
            P(),
            P(),
            P(),
            P(None, "dp", None, "mp"),
            P(None, "mp", "dp"),
            P(None, "dp", None, "mp"),
            P(None, "mp", "dp"),
            P(None, "dp", None),
            P(None, None, "dp"),
            P(None, "dp", None, "mp"),
            P(None, "mp", "dp"),
            P(None, "dp", None, None),
            P(None, None, "dp"),
            P(None, "mp"),
        ),
        out_specs=(
            P("dp", None),
            P("dp", None),
            P(),
            P(None, "dp", None, "mp"),
            P("dp", None, "mp"),
            P("dp", None, "mp"),
            P(None, "mp", "dp"),
            P("mp", "dp"),
            P("mp", "dp"),
            P(None, "dp", None, "mp"),
            P("dp", None, "mp"),
            P("dp", None, "mp"),
            P(None, "mp", "dp"),
            P("mp", "dp"),
            P("mp", "dp"),
            P(None, "dp", None),
            P("dp", None),
            P("dp", None),
            P(None, None, "dp"),
            P(None, "dp"),
            P(None, "dp"),
            P(None, "dp", None, "mp"),
            P("dp", None, "mp"),
            P("dp", None, "mp"),
            P(None, "mp", "dp"),
            P("mp", "dp"),
            P("mp", "dp"),
            P(None, "dp", None, None),
            P("dp", None, None),
            P("dp", None, None),
            P(None, None, "dp"),
            P(None, "dp"),
            P(None, "dp"),
            P(None, "mp"),
            P("mp"),
            P("mp"),
        ),
        check_vma=False,
    )
```

```python
import functools
import math

import jax
import jax.numpy as jnp
from jax import lax
from jax.experimental import pallas as pl
from jax.experimental.pallas import tpu as pltpu
from jax.sharding import PartitionSpec as P

D = 1024
H = 16
FF = 3072
DM = 768
MFF = 2304
NCLASS = 1000
IMG_DEV = 4
STEP = 10

EPSILON = 1e-06
BETA_ONE = 0.9
BETA_TWO = 0.95
ADAM_EPSILON = 1e-08
CLIP_NORM = 1.0
MASKED = -1e30
MESH = pl.DeviceIdType.MESH
FORWARD_VMEM = 60 * 2**20
FFN_VMEM = 60 * 2**20
ATTN_VMEM = 60 * 2**20
BACK_VMEM = 60 * 2**20
UPDATE_VMEM = 60 * 2**20
F32 = jnp.float32
BF16 = jnp.bfloat16


def minor_size(count):
    return 1 << ((count.bit_length() - 1) // 2)


def learn_rates():
    return (
        2.5 * D ** (-0.5),
        2.5 * (D // 64) ** (-0.5),
        2.5 * D ** (-0.5),
        2.5 * FF ** (-0.5),
        2.5 * DM ** (-0.5),
        2.5,
        2.5 * DM ** (-0.5),
        2.5 * MFF ** (-0.5),
        1.25 * DM ** (-0.5),
        0.25,
        7.5,
    )


def decay_rates():
    return (0.01, 0.01, 0.01, 0.01, 0.01, 0.01, 0.01, 0.01, 0.01, 0.0, 0.0)


def adamw_step(state, gradient, rate, decay):
    keep_rate = 1.0 - (1.0 + STEP) ** (-0.75)
    first = BETA_ONE * state(1) + (1.0 - BETA_ONE) * gradient
    second = BETA_TWO * state(2) + (1.0 - BETA_TWO) * gradient * gradient
    first_hat = first / (1.0 - BETA_ONE**STEP)
    second_hat = second / (1.0 - BETA_TWO**STEP)
    weight = state(0) * (1.0 - rate * decay) - rate * first_hat / (
        jnp.sqrt(second_hat) + ADAM_EPSILON
    )
    average = keep_rate * state(3) + (1.0 - keep_rate) * weight
    return weight, average, first, second


def dot_nn(a, b):
    return lax.dot_general(a, b, (((1,), (0,)), ((), ())), preferred_element_type=F32)


def dot_nt(a, b):
    return lax.dot_general(a, b, (((1,), (1,)), ((), ())), preferred_element_type=F32)


def dot_tn(a, b):
    return lax.dot_general(a, b, (((0,), (0,)), ((), ())), preferred_element_type=F32)


def two_part(dot, exact, wide):
    high = wide.astype(BF16)
    low = (wide - high.astype(F32)).astype(BF16)
    return dot(exact, high) + dot(exact, low)


def two_part_left(dot, wide, exact):
    high = wide.astype(BF16)
    low = (wide - high.astype(F32)).astype(BF16)
    return dot(high, exact) + dot(low, exact)


def gelu_parts(b):
    cdf = 0.5 * (1.0 + lax.erf(b * (1.0 / math.sqrt(2.0))))
    pdf = jnp.exp(-0.5 * b * b) * (1.0 / math.sqrt(2.0 * math.pi))
    return b * cdf, cdf + b * pdf


def greet(peers):
    barrier = pltpu.get_barrier_semaphore()
    total = 0
    for count, peer_of in peers:

        def say(k, carry, peer_of=peer_of):
            pl.semaphore_signal(barrier, inc=1, device_id=peer_of(k), device_id_type=MESH)
            return carry

        lax.fori_loop(1, count, say, 0)
        total += count - 1
    pl.semaphore_wait(barrier, total)


class Exchange:
    def __init__(self, count, me, device_of, send_sem, recv_sem):
        self.count, self.me, self.device_of = count, me, device_of
        self.send_sem, self.recv_sem = send_sem, recv_sem

    def _copy(self, k, src_of, dst, slot):
        peer = lax.rem(self.me + k, self.count)
        return pltpu.make_async_remote_copy(
            src_ref=src_of(peer),
            dst_ref=dst.at[slot],
            send_sem=self.send_sem.at[k],
            recv_sem=self.recv_sem.at[k],
            device_id=self.device_of(peer),
            device_id_type=MESH,
        )

    def start(self, src_of, dst):
        def body(k, carry):
            self._copy(k, src_of, dst, self.me).start()
            return carry

        lax.fori_loop(1, self.count, body, 0)

    def wait(self, src_of, dst):
        def body(k, carry):
            self._copy(k, src_of, dst, lax.rem(self.me + self.count - k, self.count)).wait()
            return carry

        lax.fori_loop(1, self.count, body, 0)

    def run(self, src_of, dst):
        self.start(src_of, dst)
        self.wait(src_of, dst)


def vmem_specs(count):
    return [pl.BlockSpec(memory_space=pltpu.VMEM)] * count


def any_specs(count):
    return [pl.BlockSpec(memory_space=pl.ANY)] * count


SMEM_SPEC = pl.BlockSpec(memory_space=pltpu.SMEM)
SHORT = 256


def total_of(ref, count):
    value = ref[0]
    for index in range(1, count):
        value = value + ref[index]
    return value


def pack_rows(rows):
    half = rows.shape[1] // 2
    return jnp.concatenate([rows[:, :half], rows[:, half:]], axis=0).astype(BF16)


def mean_square(blocks):
    sums = jnp.sum(jnp.sum(blocks, axis=0), axis=-1, keepdims=True)
    return sums * (1.0 / DM)


def rms_blocks(blocks):
    factor = lax.rsqrt(mean_square(blocks * blocks) + EPSILON)
    return factor


def rms_blocks_back(blocks, factor, gain_grad):
    inner = mean_square(blocks * gain_grad)
    return factor[None] * gain_grad - blocks * (factor * factor * factor * inner)[None]


class Grid:
    def __init__(self, n_dp):
        self.d, self.m = lax.axis_index("dp"), lax.axis_index("mp")
        self.n_y = minor_size(n_dp)
        self.n_z = n_dp // self.n_y
        self.z, self.y = lax.div(self.d, self.n_y), lax.rem(self.d, self.n_y)

    def at(self, kz, ky):
        return lax.rem(self.z + kz, self.n_z) * self.n_y + lax.rem(self.y + ky, self.n_y)

    def before(self, kz, ky):
        return lax.rem(self.z + self.n_z - kz, self.n_z) * self.n_y + lax.rem(self.y + self.n_y - ky, self.n_y)


def bulk_sems(n_dp, pieces):
    n_y = minor_size(n_dp)
    z_sem = pltpu.SemaphoreType.DMA((n_dp // n_y, pieces))
    y_sem = pltpu.SemaphoreType.DMA((n_dp // n_y, n_y, pieces))
    return [z_sem, z_sem, y_sem, y_sem]


def if_piece(act, i, low, high):
    @pl.when((i >= low) & (i < high))
    def _():
        act(i)


def each_piece(act, low, high):
    def body(i, carry):
        act(i)
        return carry

    lax.fori_loop(low, high, body, 0)


class Paced:
    def paced_send(self, u, first, num, den):
        self._at(self.send, u, first, num, den)

    def paced_forward(self, u, first, num, den):
        self._at(self.forward, u, first, num, den)

    def _at(self, act, u, first, num, den):
        far = 64 * num
        done = lambda t: lax.div((t - first) * den + far, num)
        new, old = done(u), done(u - 1)
        for step in range(-(-den // num)):
            i = old + 1 + step - 64

            @pl.when((new - 64 >= i) & (i >= 0) & (i < self.pieces))
            def _(i=i):
                act(i)

    @staticmethod
    def after(pieces, first, num, den, ticks):
        return min(pieces, max(0, (ticks - 1 - first) * den // num + 1)) if ticks > first else 0


class BulkGather(Paced):
    def __init__(self, grid, pieces, piece, z_ss, z_rs, y_ss, y_rs):
        self.g, self.pieces, self.piece = grid, pieces, piece
        self.z_ss, self.z_rs, self.y_ss, self.y_rs = z_ss, z_rs, y_ss, y_rs

    def z_copy(self, kz, i, owner):
        return pltpu.make_async_remote_copy(
            src_ref=self.piece(self.g.d, i), dst_ref=self.piece(owner, i), send_sem=self.z_ss.at[kz, i],
            recv_sem=self.z_rs.at[kz, i], device_id=(self.g.at(kz, 0), self.g.m), device_id_type=MESH)

    def y_copy(self, kz, ky, i, owner):
        return pltpu.make_async_remote_copy(
            src_ref=self.piece(self.g.before(kz, 0), i), dst_ref=self.piece(owner, i),
            send_sem=self.y_ss.at[kz, ky, i], recv_sem=self.y_rs.at[kz, ky, i],
            device_id=(self.g.at(0, ky), self.g.m), device_id_type=MESH)

    def send(self, i):
        for kz in range(1, self.g.n_z):
            self.z_copy(kz, i, self.g.d).start()
        for ky in range(1, self.g.n_y):
            self.y_copy(0, ky, i, self.g.d).start()

    def forward(self, i):
        for kz in range(1, self.g.n_z):
            self.z_copy(kz, i, self.g.before(kz, 0)).wait_recv()
            for ky in range(1, self.g.n_y):
                self.y_copy(kz, ky, i, self.g.before(kz, 0)).start()

    def finish_piece(self, i):
        for kz in range(1, self.g.n_z):
            self.z_copy(kz, i, self.g.d).wait_send()
        for kz in range(self.g.n_z):
            for ky in range(1, self.g.n_y):
                self.y_copy(kz, ky, i, self.g.before(kz, ky)).wait()

    def finish(self):
        each_piece(self.finish_piece, 0, self.pieces)


def line_sems(n_dp, pieces):
    n_y = minor_size(n_dp)
    n_z = n_dp // n_y
    return [pltpu.SemaphoreType.DMA((n_z, pieces))] * 4 + [pltpu.SemaphoreType.DMA((n_z, n_y, pieces))] * 2


class LineGather:
    def __init__(self, grid, pieces, piece, up_ss, up_rs, down_ss, down_rs, y_ss, y_rs):
        self.g, self.pieces, self.piece = grid, pieces, piece
        self.up, self.down, self.y_ss, self.y_rs = (up_ss, up_rs), (down_ss, down_rs), y_ss, y_rs
        self.ticks = pieces + grid.n_z - 1

    def block(self, z, y):
        return z * self.g.n_y + y

    def other_y(self, ky):
        return lax.rem(self.g.y + ky, self.g.n_y)

    def before_y(self, ky):
        return lax.rem(self.g.y + self.g.n_y - ky, self.g.n_y)

    def above(self):
        return (self.block(jnp.minimum(self.g.z + 1, self.g.n_z - 1), self.g.y), self.g.m)

    def below(self):
        return (self.block(jnp.maximum(self.g.z - 1, 0), self.g.y), self.g.m)

    def z_copy(self, sems, owner_z, i, target):
        block = self.piece(self.block(owner_z, self.g.y), i)
        return pltpu.make_async_remote_copy(
            src_ref=block, dst_ref=block, send_sem=sems[0].at[owner_z, i], recv_sem=sems[1].at[owner_z, i],
            device_id=target, device_id_type=MESH)

    def up_copy(self, owner_z, i):
        return self.z_copy(self.up, owner_z, i, self.above())

    def down_copy(self, owner_z, i):
        return self.z_copy(self.down, owner_z, i, self.below())

    def y_copy(self, owner_z, ky, i, in_y):
        return pltpu.make_async_remote_copy(
            src_ref=self.piece(self.block(owner_z, self.g.y), i), dst_ref=self.piece(self.block(owner_z, in_y), i),
            send_sem=self.y_ss.at[owner_z, ky, i], recv_sem=self.y_rs.at[owner_z, ky, i],
            device_id=(self.block(self.g.z, self.other_y(ky)), self.g.m), device_id_type=MESH)

    def along_y(self, owner_z, i):
        for ky in range(1, self.g.n_y):
            self.y_copy(owner_z, ky, i, self.g.y).start()

    def send(self, i):
        z, n_z = self.g.z, self.g.n_z

        @pl.when(z < n_z - 1)
        def _():
            self.up_copy(z, i).start()

        @pl.when(z > 0)
        def _():
            self.down_copy(z, i).start()

        self.along_y(z, i)

    def arrival(self, hop, i):
        z, n_z = self.g.z, self.g.n_z

        @pl.when(z - 1 - hop >= 0)
        def _():
            owner = jnp.maximum(z - 1 - hop, 0)
            self.up_copy(owner, i).wait_recv()

            @pl.when(z < n_z - 1)
            def _():
                self.up_copy(owner, i).start()

            self.along_y(owner, i)

        @pl.when(z + 1 + hop < n_z)
        def _():
            owner = jnp.minimum(z + 1 + hop, n_z - 1)
            self.down_copy(owner, i).wait_recv()

            @pl.when(z > 0)
            def _():
                self.down_copy(owner, i).start()

            self.along_y(owner, i)

    def tick(self, t):
        if_piece(self.send, t, 0, self.pieces)
        for hop in range(self.g.n_z - 1):
            if_piece(functools.partial(self.arrival, hop), t - 1 - hop, 0, self.pieces)

    def finish(self):
        z, n_z = self.g.z, self.g.n_z

        def piece_done(i):
            for owner in range(n_z):

                @pl.when((z >= owner) & (z < n_z - 1))
                def _():
                    self.up_copy(owner, i).wait_send()

                @pl.when((z <= owner) & (z > 0))
                def _():
                    self.down_copy(owner, i).wait_send()

                for ky in range(1, self.g.n_y):
                    self.y_copy(owner, ky, i, self.before_y(ky)).wait()

        each_piece(piece_done, 0, self.pieces)


def scatter_scratch(n_dp, pieces, rows, columns):
    n_y = minor_size(n_dp)
    n_z = n_dp // n_y
    slot = (pieces, rows, columns)
    return [
        pltpu.VMEM((n_z, max(n_y - 1, 1)) + slot, BF16),
        pltpu.VMEM((max(n_z - 1, 1),) + slot, BF16),
        pltpu.VMEM((max(n_z - 1, 1),) + slot, BF16),
    ] + bulk_sems(n_dp, pieces)


class BulkScatter(Paced):
    def __init__(self, grid, pieces, piece, out, recv_y, send_z, recv_z, z_ss, z_rs, y_ss, y_rs, sent=None):
        self.g, self.pieces, self.piece, self.out, self.sent = grid, pieces, piece, out, sent or piece
        self.recv_y, self.send_z, self.recv_z = recv_y, send_z, recv_z
        self.z_ss, self.z_rs, self.y_ss, self.y_rs = z_ss, z_rs, y_ss, y_rs

    def y_copy(self, kz, ky, i):
        return pltpu.make_async_remote_copy(
            src_ref=self.sent(self.g.at(kz, ky), i), dst_ref=self.recv_y.at[kz, ky - 1, i],
            send_sem=self.y_ss.at[kz, ky, i], recv_sem=self.y_rs.at[kz, ky, i],
            device_id=(self.g.at(0, ky), self.g.m), device_id_type=MESH)

    def z_copy(self, kz, i):
        return pltpu.make_async_remote_copy(
            src_ref=self.send_z.at[kz - 1, i], dst_ref=self.recv_z.at[kz - 1, i], send_sem=self.z_ss.at[kz, i],
            recv_sem=self.z_rs.at[kz, i], device_id=(self.g.at(kz, 0), self.g.m), device_id_type=MESH)

    def send(self, i):
        for kz in list(range(1, self.g.n_z)) + [0]:
            for ky in range(1, self.g.n_y):
                self.y_copy(kz, ky, i).start()

    def forward(self, i):
        for kz in list(range(1, self.g.n_z)) + [0]:
            value = self.piece(self.g.at(kz, 0), i)[...].astype(F32)
            for ky in range(1, self.g.n_y):
                self.y_copy(kz, ky, i).wait_recv()
                value = value + self.recv_y[kz, ky - 1, i].astype(F32)
            if kz == 0:
                self.out(i)[...] = value
            else:
                self.send_z[kz - 1, i] = value.astype(BF16)
                self.z_copy(kz, i).start()

    def finish_piece(self, i):
        total = self.out(i)[...]
        for kz in range(1, self.g.n_z):
            self.z_copy(kz, i).wait_recv()
            total = total + self.recv_z[kz - 1, i].astype(F32)
        self.out(i)[...] = total
        for kz in range(1, self.g.n_z):
            self.z_copy(kz, i).wait_send()
        for kz in range(self.g.n_z):
            for ky in range(1, self.g.n_y):
                self.y_copy(kz, ky, i).wait_send()

    def finish(self):
        each_piece(self.finish_piece, 0, self.pieces)


def cuts(rows):
    return max(rows // 32, min(rows // 16, 2))


def scatter_split(shard):
    parts = cuts(shard)
    return parts // 2 + 1, min(parts // 2 + 2 * parts + 1, 3 * parts - 1)


def cut_rows(ref, shard, first=0):
    parts = cuts(shard)
    small = shard // parts

    def piece(owner, i):
        rows = pl.ds(pl.multiple_of(owner * shard + lax.rem(i + first, parts) * small, small), small)
        return ref.at[lax.div(i + first, parts), rows, :]

    return piece


class Images:
    def __init__(self, lengths_ref):
        start = lax.axis_index("dp") * IMG_DEV
        self.is_long = jnp.where(lengths_ref[start] > SHORT, 1.0, 0.0)
        self.bias = (1.0 - self.is_long) * MASKED
        live = lengths_ref[start]
        for j in range(1, IMG_DEV):
            live = live + lengths_ref[start + j]
        self.live = live.astype(F32)


def fill_onehot(target, labels_ref):
    classes = lax.broadcasted_iota(jnp.int32, (1, NCLASS), 1)

    def body(i, carry):
        target[pl.ds(i, 1), :] = jnp.where(classes == labels_ref[i], 1.0, 0.0)
        return carry

    lax.fori_loop(0, target.shape[0], body, 0)


def own_features(target, sigmas_ref, freqs_ref, d):
    count, part = freqs_ref.shape[0], target.shape[1]

    def body(i, carry):
        target[pl.ds(i, 1), :] = jnp.full((1, part), sigmas_ref[i], F32)
        return carry

    lax.fori_loop(0, target.shape[0], body, 0)
    slices = count // part
    every = freqs_ref[...].reshape(1, count)
    freqs = every[:, 0:part]
    for k in range(1, slices):
        freqs = jnp.where(lax.rem(d, slices) == k, every[:, k * part : (k + 1) * part], freqs)
    angles = 2.0 * math.pi * (jnp.log(target[...]) / 4.0) * freqs
    target[...] = jnp.where(d < slices, jnp.cos(angles), jnp.sin(angles))


def head_ones(width, heads):
    size = width // heads
    row = lax.div(lax.broadcasted_iota(jnp.int32, (width, 1), 0), size)
    column = lax.div(lax.broadcasted_iota(jnp.int32, (1, width), 1), size)
    return (row == column).astype(F32).astype(BF16)


def head_scales(scales_ref, width, heads):
    column = lax.div(lax.broadcasted_iota(jnp.int32, (1, width), 1), width // heads)
    row = jnp.full((1, width), scales_ref[0, 0], F32)
    for h in range(1, heads):
        row = jnp.where(column == h, scales_ref[0, h], row)
    return row


def loads(pairs, sems):
    copies = [pltpu.make_async_copy(source, target, sems.at[i]) for i, (source, target) in enumerate(pairs)]
    for copy in copies:
        copy.start()
    return copies


class Ranks:
    def __init__(self, n_mp):
        self.d, self.m = lax.axis_index("dp"), lax.axis_index("mp")
        self.n_x = n_mp // 2
        self.x, self.c = lax.div(self.m, 2), lax.rem(self.m, 2)
        self.sibling = (self.d, self.x * 2 + 1 - self.c)

    def rank(self, kx, same):
        core = jnp.where(same == 1, self.c, 1 - self.c)
        return lax.rem(self.x + kx, self.n_x) * 2 + core

    def chip(self, kx):
        return (self.d, lax.rem(self.x + kx, self.n_x) * 2 + self.c)

    def greet(self):
        greet([(2, lambda k: self.sibling), (self.n_x, self.chip)])


class Reduce:
    def __init__(self, ranks, core_send, core_recv, x_send, x_recv, sems):
        self.r = ranks
        self.core_send, self.core_recv, self.x_send, self.x_recv = core_send, core_recv, x_send, x_recv
        self.sems = sems

    def core_copy(self, kx):
        return pltpu.make_async_remote_copy(
            src_ref=self.core_send.at[kx], dst_ref=self.core_recv.at[kx], send_sem=self.sems.at[0, kx],
            recv_sem=self.sems.at[1, kx], device_id=self.r.sibling, device_id_type=MESH)

    def x_copy(self, kx):
        return pltpu.make_async_remote_copy(
            src_ref=self.x_send.at[kx], dst_ref=self.x_recv.at[kx], send_sem=self.sems.at[2, kx],
            recv_sem=self.sems.at[3, kx], device_id=self.r.chip(kx), device_id_type=MESH)

    def other(self, kx, part):
        self.core_send[kx] = part.astype(BF16)
        self.core_copy(kx).start()

    def same(self, kx, part):
        self.core_copy(kx).wait_recv()
        self.x_send[kx] = (part + self.core_recv[kx].astype(F32)).astype(BF16)
        self.x_copy(kx).start()

    def finish(self, part):
        self.core_copy(0).wait_recv()
        total = part + self.core_recv[0].astype(F32)
        for kx in range(1, self.r.n_x):
            self.x_copy(kx).wait_recv()
            total = total + self.x_recv[kx].astype(F32)
        return total

    def drain(self):
        self.core_copy(0).wait_send()
        for kx in range(1, self.r.n_x):
            self.core_copy(kx).wait_send()
            self.x_copy(kx).wait_send()


def reduce_scratch(n_mp, rows):
    slots = pltpu.VMEM((n_mp // 2, rows, D), BF16)
    return [slots, slots, slots, slots, pltpu.SemaphoreType.DMA((4, n_mp // 2))]


class Gather:
    def __init__(self, ranks, rows, buffer, sems):
        self.r, self.rows, self.buffer, self.sems = ranks, rows, buffer, sems

    def at(self, rank):
        return self.buffer.at[pl.ds(pl.multiple_of(rank * self.rows, self.rows), self.rows), :]

    def x_copy(self, kx, slot):
        return pltpu.make_async_remote_copy(
            src_ref=self.at(self.r.m), dst_ref=self.at(slot), send_sem=self.sems.at[0, kx],
            recv_sem=self.sems.at[1, kx], device_id=self.r.chip(kx), device_id_type=MESH)

    def core_copy(self, kx, out_slot, in_slot):
        return pltpu.make_async_remote_copy(
            src_ref=self.at(out_slot), dst_ref=self.at(in_slot), send_sem=self.sems.at[2, kx],
            recv_sem=self.sems.at[3, kx], device_id=self.r.sibling, device_id_type=MESH)

    def start(self):
        for kx in range(1, self.r.n_x):
            self.x_copy(kx, self.r.m).start()
        self.core_copy(0, self.r.m, self.r.m).start()

    def from_chip(self, kx):
        return lax.rem(self.r.x + self.r.n_x - kx, self.r.n_x) * 2 + self.r.c

    def from_core(self, kx):
        return lax.rem(self.r.x + self.r.n_x - kx, self.r.n_x) * 2 + 1 - self.r.c

    def forward(self, kx):
        slot = self.from_chip(kx)
        self.x_copy(kx, slot).wait_recv()
        self.core_copy(kx, slot, slot).start()

    def arrived(self, kx):
        self.core_copy(kx, self.r.m, self.from_core(kx)).wait_recv()

    def drain(self):
        for kx in range(1, self.r.n_x):
            self.x_copy(kx, self.r.m).wait_send()
        for kx in range(self.r.n_x):
            self.core_copy(kx, self.r.m, self.r.m).wait_send()


def gather_sems(n_mp):
    return pltpu.SemaphoreType.DMA((4, n_mp // 2))


def head_sums(values, ones):
    return two_part_left(dot_nn, values, ones)


def row_sums_factor(values):
    return lax.rsqrt(jnp.mean(values * values, axis=-1, keepdims=True) + EPSILON)


def image_scale(info, mods_ref, which, image):
    is_long = info.is_long
    row = mods_ref[which, pl.ds(image, 1), :]
    return 1.0 + (is_long * mods_ref[which, 0:1, :] + (1.0 - is_long) * row)


def column_bias(info, image, columns_shape, short):
    keys = lax.broadcasted_iota(jnp.int32, columns_shape, 0)
    own = (keys >= image * short) & (keys < (image + 1) * short)
    return jnp.where(own, 0.0, info.bias)


def forward_kernel(
    n_dp, n_mp, heads,
    lengths_ref, sigmas_ref, labels_ref, scales_ref, freqs_ref, x_any,
    in_ref, out_ref, up_ref, time_ref, class_ref, mapup_ref, mapdown_ref, mod_ref, gains_ref,
    mods_ref, emb_ref, hid_ref, gated_ref, mixed_ref, feats_ref, wg_out, wf_out,
    q_out, k_out, v_out, normed_out, qu_out, ku_out, att_ref, stats_ref, mid_ref, nm_ref,
    x_ref, wg_ref, q_ref, k_ref, v_ref, normed_ref, wf_ref, onehot_s, ones_ref, store_sem,
    in_s, out_s, up_s, time_s, class_s, mapup_s, mapdown_s, mod_s, gains_s, load_sem,
    send_a, recv_a, own_a, send_h, recv_h, own_g, recv_g, own_x, recv_x, own_m, send_o, recv_o,
    dp_ss, dp_rs, mp_ss, mp_rs, a_us, a_ur, a_ds, a_dr, a_ys, a_yr, f_us, f_ur, f_ds, f_dr, f_ys, f_yr,
    qu_s, ku_s, vt_s, part_s, core_send, core_recv, x_send, x_recv, sems,
):
    r = Ranks(n_mp)
    grid = Grid(n_dp)
    d, m = r.d, r.m
    images, part = feats_ref.shape
    info = Images(lengths_ref)
    copies = loads(
        (
            (time_ref.at[0], time_s),
            (in_ref.at[0], in_s),
            (out_ref.at[0], out_s),
            (class_ref.at[0], class_s),
            (gains_ref, gains_s),
            (up_ref.at[0], up_s),
            (mapup_ref.at[0], mapup_s),
            (mapdown_ref.at[0], mapdown_s),
            (mod_ref.at[0], mod_s),
            (x_any, x_ref),
        ),
        load_sem,
    )
    map_copies = [copies[0]] + copies[3:5] + copies[6:]
    greet(
        [
            (n_dp, lambda k: (lax.rem(d + k, n_dp), m)),
            (n_mp, lambda k: (d, lax.rem(m + k, n_mp))),
        ]
    )
    own_features(feats_ref, sigmas_ref, freqs_ref, d)
    shard = in_s.shape[1]
    mine = pl.ds(pl.multiple_of(d * shard, shard), shard)
    attn = LineGather(
        grid, 4, lambda dd, i: wg_ref.at[i, pl.ds(pl.multiple_of(dd * shard, shard), shard), :],
        a_us, a_ur, a_ds, a_dr, a_ys, a_yr)
    up_w = LineGather(
        grid, 2 * cuts(shard), cut_rows(wf_ref, shard), f_us, f_ur, f_ds, f_dr, f_ys, f_yr
    )

    def dp_ex(stage):
        return Exchange(n_dp, d, lambda p: (p, m), dp_ss.at[stage], dp_rs.at[stage])

    map_copies[0].wait()
    partial = dot_nn(feats_ref[...].astype(BF16), time_s[...].astype(BF16))
    for p in range(n_dp):
        send_a[p] = partial[:, p * part : (p + 1) * part]
    ex = dp_ex(0)
    ex.start(lambda p: send_a.at[p], recv_a)
    copies[1].wait()
    for c in range(3):
        wg_ref[c, mine, :] = in_s[c].astype(BF16)
    copies[2].wait()
    wg_ref[3, mine, :] = out_s[...].T.astype(BF16)
    attn.tick(0)
    recv_a[d] = send_a[d]
    copies[5].wait()
    for c in range(2):
        wf_ref[c, mine, :] = up_s[:, c, :].astype(BF16)
    fill_onehot(onehot_s, labels_ref)
    ones_ref[...] = head_ones(q_ref.shape[1], heads)
    for copy in map_copies[1:]:
        copy.wait()
    e_cols = dot_nt(onehot_s[...].astype(BF16), class_s[...].astype(BF16))
    own_a[images:, :] = jnp.zeros((8, part), F32)
    for g in range(3):
        own_a[images + g : images + g + 1, :] = gains_s[g, 0:1, :].astype(BF16).astype(F32)
    ex.wait(lambda p: send_a.at[p], recv_a)
    own_a[0:images, :] = total_of(recv_a, n_dp) + e_cols
    ex = dp_ex(1)
    ex.start(lambda p: own_a, emb_ref)
    attn.tick(1)
    emb_ref[d] = own_a[...]
    ex.wait(lambda p: own_a, emb_ref)
    gains = emb_ref[:, images:, :]
    emb = emb_ref[:, 0:images, :]
    unit = emb * rms_blocks(emb)[None] * gains[:, 0:1, :]
    unit_factor = rms_blocks(unit)
    own_x[0] = (emb_ref[d][0:images] * rms_blocks(emb)) * emb_ref[d][images : images + 1]
    unit_own = own_x[0]
    pre_own = (unit_own * unit_factor * emb_ref[d][images + 1 : images + 2]).astype(BF16)
    for c in range(2):
        part = dot_nn(pre_own, mapup_s[:, c, :].astype(BF16))
        for p in range(n_dp):
            send_h[p, c] = part[p * IMG_DEV : (p + 1) * IMG_DEV, :]
    ex = dp_ex(2)
    ex.start(lambda p: send_h.at[p], recv_h)
    attn.tick(2)
    recv_h[d] = send_h[d]
    ex.wait(lambda p: send_h.at[p], recv_h)
    hidden = total_of(recv_h, n_dp)
    hid_ref[...] = hidden
    own_g[...] = (hidden[0] * gelu_parts(hidden[1])[0]).astype(BF16).astype(F32)
    ex = dp_ex(3)
    ex.start(lambda p: own_g, recv_g)
    attn.tick(3)
    recv_g[d] = own_g[...]
    ex.wait(lambda p: own_g, recv_g)
    for p in range(n_dp):
        gated_ref[p * IMG_DEV : (p + 1) * IMG_DEV, :] = recv_g[p]
    own_x[0] = dot_nt(gated_ref[...].astype(BF16), mapdown_s[...].astype(BF16))
    ex = Exchange(n_mp, m, lambda p: (d, p), mp_ss.at[0], mp_rs.at[0])
    ex.start(lambda p: own_x.at[0], recv_x)
    attn.tick(4)
    up_w.tick(0)
    recv_x[m] = own_x[0]
    ex.wait(lambda p: own_x.at[0], recv_x)
    own_m[...] = total_of(recv_x, n_mp) + unit_own
    ex = dp_ex(4)
    ex.start(lambda p: own_m, mixed_ref)
    attn.tick(5)
    up_w.tick(1)
    mixed_ref[d] = own_m[...]
    ex.wait(lambda p: own_m, mixed_ref)
    mixed_factor = rms_blocks(mixed_ref[...])
    cond_own = (own_m[...] * mixed_factor * emb_ref[d][images + 2 : images + 3]).astype(BF16)
    for c in range(2):
        part = dot_nn(cond_own, mod_s[:, c, :].astype(BF16))
        for p in range(n_dp):
            send_o[p, c] = part[p * IMG_DEV : (p + 1) * IMG_DEV, :]
    ex = dp_ex(5)
    ex.start(lambda p: send_o.at[p], recv_o)
    attn.tick(6)
    up_w.tick(2)
    recv_o[d] = send_o[d]
    ex.wait(lambda p: send_o.at[p], recv_o)
    mods_ref[...] = total_of(recv_o, n_dp)
    each_piece(attn.tick, 7, attn.ticks)
    attn.finish()
    tokens = x_ref.shape[0]
    rows = tokens // n_mp
    width = q_ref.shape[1]
    size = width // heads
    red = Reduce(r, core_send, core_recv, x_send, x_recv, sems)
    at = lambda b: pl.ds(pl.multiple_of(b * rows, rows), rows)
    image_of = lambda b: lax.div(b * rows, SHORT)

    scale_row = head_scales(scales_ref, q_ref.shape[1], heads)

    def project(b, carry):
        xb = x_ref[at(b), :].astype(F32)
        normed = (xb * row_sums_factor(xb) * image_scale(info, mods_ref, 0, image_of(b))).astype(BF16)
        normed_ref[at(b), :] = normed
        q = dot_nn(normed, wg_ref[0])
        q_ref[at(b), :] = q
        qu_s[at(b), :] = (q * lax.rsqrt(head_sums(q * q, ones_ref[...]) + EPSILON) * scale_row).astype(BF16)
        k = dot_nn(normed, wg_ref[1])
        k_ref[at(b), :] = k
        ku_s[at(b), :] = (k * lax.rsqrt(head_sums(k * k, ones_ref[...]) + EPSILON)).astype(BF16)
        v = dot_nn(normed, wg_ref[2])
        v_ref[at(b), :] = v.astype(BF16)
        vt_s[:, at(b)] = v.T.astype(BF16)

        @pl.when(lax.rem(b, 2) == 0)
        def _():
            up_w.tick(3 + lax.div(b, 2))

        return carry

    lax.fori_loop(0, n_mp, project, 0)
    stores = [
        pltpu.make_async_copy(source, target, store_sem.at[n])
        for n, (source, target) in enumerate(
            ((wg_ref, wg_out), (q_ref, q_out), (k_ref, k_out), (v_ref, v_out), (normed_ref, normed_out), (qu_s, qu_out), (ku_s, ku_out))
        )
    ]
    for copy in stores:
        copy.start()
    first_tick = 3 + (n_mp + 1) // 2
    ticks_left = max(up_w.ticks - first_tick, 0)

    def tick_at(u):
        span = heads * n_mp
        count = lambda v: lax.div(v * ticks_left + span, span)

        @pl.when(count(u) != count(u - 1))
        def _():
            up_w.tick(first_tick + count(u) - 1)

    lanes = lax.broadcasted_iota(jnp.int32, (1, width), 1)

    def block(j, carry):
        kx, same = lax.rem(1 + lax.div(j, 2), r.n_x), lax.rem(j, 2)
        b = r.rank(kx, same)
        bias = column_bias(info, image_of(b), (tokens, 1), SHORT)
        qu = qu_s[at(b), :]
        outs = []
        for h in range(heads):
            mask = ((lanes >= h * size) & (lanes < (h + 1) * size)).astype(F32).astype(BF16)
            scores = dot_nt(ku_s[...], qu * mask) + bias
            top = jnp.max(scores, axis=0, keepdims=True)
            expon = jnp.exp(scores - top)
            total = jnp.sum(expon, axis=0, keepdims=True)
            stats_ref[h : h + 1, at(b)] = top + jnp.log(total)
            tick_at(heads * j + h)
            outs.append(dot_nn(vt_s[h * size : (h + 1) * size, :], expon.astype(BF16)) / total)
        att = jnp.concatenate(outs, axis=0).T.astype(BF16)
        att_ref[at(b), :] = att
        part_s[...] = dot_nt(att, wg_ref[3])

        @pl.when(same == 0)
        def _():
            red.other(kx, part_s[...])

        @pl.when((same == 1) & (kx > 0))
        def _():
            red.same(kx, part_s[...])

        return carry

    lax.fori_loop(0, n_mp, block, 0)
    if heads < 8:
        stats_ref[heads:8, :] = jnp.zeros((8 - heads, tokens), F32)
    middle = x_ref[at(r.m), :].astype(F32) + red.finish(part_s[...])
    mid_ref[...] = middle
    nm_ref[...] = (middle * row_sums_factor(middle) * image_scale(info, mods_ref, 1, image_of(r.m))).astype(BF16)
    red.drain()
    up_w.finish()
    stores.append(pltpu.make_async_copy(wf_ref, wf_out, store_sem.at[7]))
    stores[-1].start()
    for copy in stores:
        copy.wait()


def forward_part(n_dp, n_mp, lengths, sigmas, labels, scales, freqs, x, layer_states, map_states, gains_state):
    images, part = sigmas.shape[0], map_states[0].shape[1]
    units_map = map_states[2].shape[3]
    shard, _, units = layer_states[2].shape[1:]
    width, heads = layer_states[0].shape[3], scales.shape[1]
    tokens = x.shape[0]
    rows = tokens // n_mp
    states = (*layer_states, *map_states)
    f32 = lambda *dims: jax.ShapeDtypeStruct(dims, F32)
    bf16 = lambda *dims: jax.ShapeDtypeStruct(dims, BF16)
    return pl.pallas_call(
        functools.partial(forward_kernel, n_dp, n_mp, heads),
        out_shape=(
            f32(2, IMG_DEV, D),
            f32(n_dp, images + 8, part),
            f32(2, IMG_DEV, units_map),
            f32(images, units_map),
            f32(n_dp, images, part),
            f32(images, part),
            bf16(4, D, width),
            bf16(2, D, units),
            f32(tokens, width),
            f32(tokens, width),
            bf16(tokens, width),
            bf16(tokens, D),
            bf16(tokens, width),
            bf16(tokens, width),
            bf16(tokens, width),
            f32(8, tokens),
            f32(rows, D),
            bf16(rows, D),
        ),
        in_specs=[SMEM_SPEC] * 4 + vmem_specs(1) + any_specs(10),
        out_specs=tuple(vmem_specs(6) + any_specs(8) + vmem_specs(4)),
        scratch_shapes=[
            pltpu.VMEM((tokens, D), BF16),
            pltpu.VMEM((4, D, width), BF16),
            pltpu.VMEM((tokens, width), F32),
            pltpu.VMEM((tokens, width), F32),
            pltpu.VMEM((tokens, width), BF16),
            pltpu.VMEM((tokens, D), BF16),
            pltpu.VMEM((2, D, units), BF16),
            pltpu.VMEM((images, NCLASS), F32),
            pltpu.VMEM((width, width), BF16),
            pltpu.SemaphoreType.DMA((8,)),
        ]
        + [pltpu.VMEM(state.shape[1:], F32) for state in states]
        + [
            pltpu.VMEM(gains_state.shape, F32),
            pltpu.SemaphoreType.DMA((10,)),
            pltpu.VMEM((n_dp, images, part), F32),
            pltpu.VMEM((n_dp, images, part), F32),
            pltpu.VMEM((images + 8, part), F32),
            pltpu.VMEM((n_dp, 2, IMG_DEV, units_map), F32),
            pltpu.VMEM((n_dp, 2, IMG_DEV, units_map), F32),
            pltpu.VMEM((IMG_DEV, units_map), F32),
            pltpu.VMEM((n_dp, IMG_DEV, units_map), F32),
            pltpu.VMEM((1, images, part), F32),
            pltpu.VMEM((n_mp, images, part), F32),
            pltpu.VMEM((images, part), F32),
            pltpu.VMEM((n_dp, 2, IMG_DEV, D), F32),
            pltpu.VMEM((n_dp, 2, IMG_DEV, D), F32),
            pltpu.SemaphoreType.DMA((6, n_dp)),
            pltpu.SemaphoreType.DMA((6, n_dp)),
            pltpu.SemaphoreType.DMA((1, n_mp)),
            pltpu.SemaphoreType.DMA((1, n_mp)),
        ]
        + line_sems(n_dp, 4)
        + line_sems(n_dp, 2 * cuts(shard))
        + [
            pltpu.VMEM((tokens, width), BF16),
            pltpu.VMEM((tokens, width), BF16),
            pltpu.VMEM((width, tokens), BF16),
            pltpu.VMEM((rows, D), F32),
        ]
        + reduce_scratch(n_mp, rows),
        compiler_params=pltpu.CompilerParams(
            collective_id=0, has_side_effects=True, vmem_limit_bytes=FORWARD_VMEM
        ),
        name="forward_part",
    )(lengths, sigmas, labels, scales, freqs, x, *states, gains_state)


def ffn_kernel(
    n_dp, n_mp, lengths_ref, nm_ref, mods_ref, mid_ref, cot_ref, wf_ref, down_ref,
    gd_ref, dmid_ref, fmod_ref, gated_out, wd_out, gw_out,
    w_s, cot_s, nm_s, gated_s, gate_s, slope_s, dh_s, dz_s, part_s, gw_s, gather_sem,
    b_core_send, b_core_recv, b_x_send, b_x_recv, b_sems,
    down_s, wd_s, load_sem, store_sem, w_zs, w_zr, w_ys, w_yr,
    recv_y, send_z, recv_z, g_zs, g_zr, g_ys, g_yr,
):
    r = Ranks(n_mp)
    grid = Grid(n_dp)
    info = Images(lengths_ref)
    copies = loads(((down_ref.at[0], down_s), (wf_ref, w_s), (cot_ref, cot_s)), load_sem)
    rows = nm_ref.shape[0]
    tokens = rows * n_mp
    at = lambda b: pl.ds(pl.multiple_of(b * rows, rows), rows)
    image_of = lambda b: lax.div(b * rows, SHORT)

    greet(
        [
            (n_dp, lambda k: (lax.rem(r.d + k, n_dp), r.m)),
            (2, lambda k: r.sibling),
            (r.n_x, r.chip),
        ]
    )
    shard = D // n_dp
    parts = cuts(shard)
    small = shard // parts
    copies[0].wait()
    wd_s[0, pl.ds(pl.multiple_of(r.d * shard, shard), shard), :] = down_s[...].T.astype(BF16)
    down_w = BulkGather(grid, parts, cut_rows(wd_s, shard), w_zs, w_zr, w_ys, w_yr)
    first = scatter_split(shard)[0]
    down_g = BulkScatter(
        grid, first, cut_rows(gw_s, shard), lambda i: gd_ref.at[i],
        recv_y, send_z, recv_z, g_zs, g_zr, g_ys, g_yr)
    each_piece(down_w.send, 0, parts)
    nm_s[at(r.m), :] = nm_ref[...]
    gather = Gather(r, rows, nm_s, gather_sem)
    gather.start()
    copies[1].wait()
    bwd = Reduce(r, b_core_send, b_core_recv, b_x_send, b_x_recv, b_sems)

    def forward(j, carry):
        kx = lax.div(j, 2)
        same = jnp.where(kx == 0, 1 - lax.rem(j, 2), lax.rem(j, 2))
        b = r.rank(kx, same)
        back_kx = lax.rem(r.n_x - kx, r.n_x)

        if_piece(down_w.forward, j - 1, 0, min(2, parts))

        @pl.when((same == 0) & (kx > 0))
        def _():
            gather.forward(back_kx)

        @pl.when(same == 0)
        def _():
            gather.arrived(back_kx)

        nm = nm_s[at(b), :]
        hidden = dot_nn(nm, w_s[0])
        gate = dot_nn(nm, w_s[1])
        value, slope = gelu_parts(gate)
        gated = (hidden * value).astype(BF16)
        gated_s[at(b), :] = gated
        gate_s[at(b), :] = value
        slope_s[at(b), :] = hidden * slope
        if_piece(down_w.forward, j, 2, parts)
        return carry

    lax.fori_loop(0, n_mp, forward, 0)
    copies[2].wait()

    def live_rows(b):
        position = lax.broadcasted_iota(jnp.int32, (rows, 1), 0) + b * rows
        return (position.astype(F32) < info.live).astype(F32)

    def live_cotangent(b, carry):
        dz_s[at(b), :] = (cot_s[at(b), :].astype(F32) * live_rows(b)).astype(BF16)
        return carry

    lax.fori_loop(0, n_mp, live_cotangent, 0)
    step = 512

    def down_gradient(i, carry):
        cols = pl.ds(pl.multiple_of(i * step, step), step)
        gw_s[0, cols, :] = dot_tn(dz_s[:, cols], gated_s[...]).astype(BF16)
        return carry

    lax.fori_loop(0, D // step, down_gradient, 0)
    each_piece(down_g.send, 0, first)
    each_piece(down_w.forward, n_mp, parts)
    down_w.finish()
    stores = [
        pltpu.make_async_copy(source, target, store_sem.at[n])
        for n, (source, target) in enumerate(((gated_s, gated_out), (wd_s.at[0], wd_out), (gw_s.at[0], gw_out.at[0])))
    ]
    for copy in stores:
        copy.start()

    def backward(j, carry):
        kx, same = lax.rem(1 + lax.div(j, 2), r.n_x), lax.rem(j, 2)
        b = r.rank(kx, same)
        if_piece(down_g.forward, j - (n_mp - 2), 0, first)
        d_gated = dot_nn(dz_s[at(b), :], wd_s[0])
        d_value = (d_gated * gate_s[at(b), :]).astype(BF16)
        d_gate = (d_gated * slope_s[at(b), :]).astype(BF16)
        dh_s[0, at(b), :] = d_value
        dh_s[1, at(b), :] = d_gate
        part_s[...] = dot_nt(d_value, w_s[0]) + dot_nt(d_gate, w_s[1])

        @pl.when(same == 0)
        def _():
            bwd.other(kx, part_s[...])

        @pl.when((same == 1) & (kx > 0))
        def _():
            bwd.same(kx, part_s[...])

        return carry

    lax.fori_loop(0, n_mp, backward, 0)

    def up_gradient(i, carry):
        if_piece(down_g.forward, i + 2, 2, first)
        cols = pl.ds(pl.multiple_of(i * step, step), step)
        left = nm_s[:, cols]
        for c in range(2):
            gw_s[1 + c, cols, :] = dot_tn(left, dh_s[c]).astype(BF16)
        return carry

    lax.fori_loop(0, D // step, up_gradient, 0)

    each_piece(down_g.forward, D // step + 2, first)
    up_store = pltpu.make_async_copy(gw_s.at[pl.ds(1, 2)], gw_out.at[pl.ds(1, 2)], store_sem.at[3])
    up_store.start()
    d_nm = bwd.finish(part_s[...])
    middle = mid_ref[...]
    live = live_rows(r.m)
    scale = image_scale(info, mods_ref, 1, image_of(r.m))
    factor = row_sums_factor(middle)
    inner = jnp.mean(middle * scale * d_nm, axis=-1, keepdims=True)
    dmid_ref[...] = cot_s[at(r.m), :].astype(F32) * live + (
        factor * scale * d_nm - middle * (factor * factor * factor * inner)
    )
    fmod_ref[...] = jnp.sum(d_nm * middle * factor, axis=0, keepdims=True)
    gather.drain()
    bwd.drain()
    down_g.finish()
    for copy in stores + [up_store]:
        copy.wait()


def ffn(n_dp, n_mp, lengths, nm, mods, mid, cot, wf, down_state):
    rows = nm.shape[0]
    tokens = rows * n_mp
    units = wf.shape[2]
    shard = D // n_dp
    parts = cuts(shard)
    first = scatter_split(shard)[0]
    shape = jax.ShapeDtypeStruct
    return pl.pallas_call(
        functools.partial(ffn_kernel, n_dp, n_mp),
        out_shape=(
            shape((first, shard // parts, units), F32),
            shape((rows, D), F32),
            shape((1, D), F32),
            shape((tokens, units), BF16),
            shape((D, units), BF16),
            shape((3, D, units), BF16),
        ),
        in_specs=[SMEM_SPEC] + vmem_specs(3) + any_specs(3),
        out_specs=tuple(vmem_specs(3) + any_specs(3)),
        scratch_shapes=[
            pltpu.VMEM((2, D, units), BF16),
            pltpu.VMEM((tokens, D), BF16),
            pltpu.VMEM((tokens, D), BF16),
            pltpu.VMEM((tokens, units), BF16),
            pltpu.VMEM((tokens, units), F32),
            pltpu.VMEM((tokens, units), F32),
            pltpu.VMEM((2, tokens, units), BF16),
            pltpu.VMEM((tokens, D), BF16),
            pltpu.VMEM((rows, D), F32),
            pltpu.VMEM((3, D, units), BF16),
            gather_sems(n_mp),
        ]
        + reduce_scratch(n_mp, rows)
        + [
            pltpu.VMEM(down_state.shape[1:], F32),
            pltpu.VMEM((1, D, units), BF16),
            pltpu.SemaphoreType.DMA((3,)),
            pltpu.SemaphoreType.DMA((4,)),
        ]
        + bulk_sems(n_dp, parts)
        + scatter_scratch(n_dp, first, shard // parts, units),
        compiler_params=pltpu.CompilerParams(
            collective_id=4, has_side_effects=True, vmem_limit_bytes=FFN_VMEM
        ),
        name="ffn",
    )(lengths, nm, mods, mid, cot, wf, down_state)


def attn_backward_kernel(
    n_dp, n_mp, heads, lengths_ref, scales_ref, dmid_ref, mods_ref, stats_ref,
    qu_any, ku_any, gffn_ref, wg_any, v_any, q_any, k_any, normed_any, att_any, x_any,
    gw_out, gf_ref, gin_ref, amod_ref, gscale_ref,
    gw_ref, store_sem, gffn_s, wg_ref, v_ref, q_ref, k_ref, normed_ref, att_ref, x_ref, ones_ref, load_sem,
    qu_s, ku_s, kt_s, dy_s, dq_s, dk_s, dv_s, low_s, part_s, gather_sem,
    core_send, core_recv, x_send, x_recv, sems,
    recv_y, send_z, recv_z, f_zs, f_zr, f_ys, f_yr,
):
    r = Ranks(n_mp)
    info = Images(lengths_ref)
    rows = dmid_ref.shape[0]
    tokens = rows * n_mp
    width = q_ref.shape[1]
    size = width // heads
    at = lambda b: pl.ds(pl.multiple_of(b * rows, rows), rows)
    image_of = lambda b: lax.div(b * rows, SHORT)
    copies = loads(
        (
            (ku_any, ku_s),
            (qu_any, qu_s),
            (wg_any, wg_ref),
            (v_any, v_ref),
            (gffn_ref, gffn_s),
            (q_any, q_ref),
            (k_any, k_ref),
            (normed_any, normed_ref),
            (att_any, att_ref),
            (x_any.at[at(r.m), :], x_ref),
        ),
        load_sem,
    )
    dy_s[at(r.m), :] = dmid_ref[...].astype(BF16)
    grid = Grid(n_dp)
    greet(
        [
            (n_dp, lambda k: (lax.rem(r.d + k, n_dp), r.m)),
            (2, lambda k: r.sibling),
            (r.n_x, r.chip),
        ]
    )
    gather = Gather(r, rows, dy_s, gather_sem)
    gather.start()
    shard = D // n_dp
    start, end = scatter_split(shard)
    ffn_g = BulkScatter(
        grid, end - start, cut_rows(gffn_s, shard, start), lambda i: gf_ref.at[i],
        recv_y, send_z, recv_z, f_zs, f_zr, f_ys, f_yr, sent=cut_rows(gffn_ref, shard, start))
    each_piece(ffn_g.send, 0, ffn_g.pieces)
    ones_ref[...] = head_ones(width, heads)
    scale_row = head_scales(scales_ref, width, heads)
    red = Reduce(r, core_send, core_recv, x_send, x_recv, sems)

    copies[0].wait()

    def units(b, carry):
        kt_s[:, at(b)] = ku_s[at(b), :].astype(F32).T.astype(BF16)
        return carry

    lax.fori_loop(0, n_mp, units, 0)
    for copy in copies[1:5]:
        copy.wait()
    dk_s[...] = jnp.zeros_like(dk_s)
    dv_s[...] = jnp.zeros_like(dv_s)
    lanes = lax.broadcasted_iota(jnp.int32, (1, width), 1)

    pace = (2, 3, 1)

    def block(j, carry):
        kx = lax.div(j, 2)
        same = 1 - lax.rem(j, 2)
        b = r.rank(kx, same)
        back_kx = lax.rem(r.n_x - kx, r.n_x)

        @pl.when((same == 1) & (kx > 0))
        def _():
            gather.forward(back_kx)

        @pl.when(same == 0)
        def _():
            gather.arrived(back_kx)

        d_att = dot_nn(dy_s[at(b), :], wg_ref[3]).astype(BF16)
        bias = column_bias(info, image_of(b), (tokens, 1), SHORT)
        qu = qu_s[at(b), :]
        outs = []
        for h in range(heads):
            mask = ((lanes >= h * size) & (lanes < (h + 1) * size)).astype(F32).astype(BF16)
            qh = qu * mask
            dh = d_att * mask
            probs = jnp.exp(dot_nt(ku_s[...], qh) + bias - stats_ref[h : h + 1, at(b)])
            ffn_g.paced_forward(heads * j + h, *pace)
            d_probs = dot_nt(v_ref[...], dh)
            inner = jnp.sum(probs * d_probs, axis=0, keepdims=True)
            d_scores = (probs * (d_probs - inner)).astype(BF16)
            dv_s[...] = dv_s[...] + dot_nn(probs.astype(BF16), dh)
            dk_s[...] = dk_s[...] + dot_nn(d_scores, qh)
            outs.append(dot_nn(kt_s[h * size : (h + 1) * size, :], d_scores))
        dq_s[at(b), :] = jnp.concatenate(outs, axis=0).T
        return carry

    lax.fori_loop(0, n_mp, block, 0)

    def inputs(j, scale_grad):
        kx, same = lax.rem(1 + lax.div(j, 2), r.n_x), lax.rem(j, 2)
        b = r.rank(kx, same)
        q, k = q_ref[at(b), :], k_ref[at(b), :]
        q_factor = lax.rsqrt(head_sums(q * q, ones_ref[...]) + EPSILON)
        k_factor = lax.rsqrt(head_sums(k * k, ones_ref[...]) + EPSILON)
        dqu, dku = dq_s[at(b), :], dk_s[at(b), :]
        q_unit, k_unit = q * q_factor, k * k_factor
        q_along = dqu * q_unit
        d_q = (scale_row * q_factor * (dqu - q_unit * head_sums(q_along, ones_ref[...]))).astype(BF16)
        d_k = (k_factor * (dku - k_unit * head_sums(dku * k_unit, ones_ref[...]))).astype(BF16)
        d_v = dv_s[at(b), :].astype(BF16)
        low_s[at(b), 0:width] = d_q
        low_s[at(b), width : 2 * width] = d_k
        low_s[at(b), 2 * width : 3 * width] = d_v
        part_s[...] = dot_nt(d_q, wg_ref[0]) + dot_nt(d_k, wg_ref[1]) + dot_nt(d_v, wg_ref[2])

        @pl.when(same == 0)
        def _():
            red.other(kx, part_s[...])

        @pl.when((same == 1) & (kx > 0))
        def _():
            red.same(kx, part_s[...])

        ffn_g.paced_forward(heads * n_mp + j, *pace)
        return scale_grad + jnp.sum(q_along, axis=0, keepdims=True)

    for copy in copies[5:7]:
        copy.wait()
    gscale_ref[...] = lax.fori_loop(0, n_mp, inputs, jnp.zeros((1, width), F32))

    for copy in copies[7:]:
        copy.wait()
    step = 512

    def weights(i, carry):
        ffn_g.paced_forward(heads * n_mp + n_mp + i, *pace)
        cols = pl.ds(pl.multiple_of(i * step, step), step)
        value = dot_tn(normed_ref[:, cols], low_s[...]).astype(BF16)
        for c in range(3):
            gw_ref[c, cols, :] = value[:, c * width : (c + 1) * width]
        gw_ref[3, cols, :] = dot_tn(dy_s[:, cols], att_ref[...]).astype(BF16)
        return carry

    lax.fori_loop(0, D // step, weights, 0)
    each_piece(ffn_g.forward, ffn_g.after(ffn_g.pieces, *pace, heads * n_mp + n_mp + D // step), ffn_g.pieces)

    gw_store = pltpu.make_async_copy(gw_ref, gw_out, store_sem.at[0])
    gw_store.start()
    d_normed = red.finish(part_s[...])
    x = x_ref[...].astype(F32)
    scale = image_scale(info, mods_ref, 0, image_of(r.m))
    factor = row_sums_factor(x)
    inner = jnp.mean(x * scale * d_normed, axis=-1, keepdims=True)
    gin_ref[...] = dmid_ref[...] + (factor * scale * d_normed - x * (factor * factor * factor * inner))
    amod_ref[...] = jnp.sum(d_normed * x * factor, axis=0, keepdims=True)
    gather.drain()
    red.drain()
    ffn_g.finish()
    gw_store.wait()


def attn_backward(n_dp, n_mp, lengths, scales, dmid, mods, stats, qu, ku, gffn, wg, v, q, k, normed, att, x):
    rows = dmid.shape[0]
    tokens = rows * n_mp
    width, heads = q.shape[1], scales.shape[1]
    shard = D // n_dp
    small = shard // cuts(shard)
    start, end = scatter_split(shard)
    shape = jax.ShapeDtypeStruct
    return pl.pallas_call(
        functools.partial(attn_backward_kernel, n_dp, n_mp, heads),
        out_shape=(
            shape(wg.shape, BF16),
            shape((end - start, small, gffn.shape[2]), F32),
            shape((rows, D), F32),
            shape((1, D), F32),
            shape((1, width), F32),
        ),
        in_specs=[SMEM_SPEC] * 2 + vmem_specs(3) + any_specs(10),
        out_specs=tuple(any_specs(1) + vmem_specs(4)),
        scratch_shapes=[
            pltpu.VMEM(wg.shape, BF16),
            pltpu.SemaphoreType.DMA((1,)),
            pltpu.VMEM(gffn.shape, BF16),
            pltpu.VMEM(wg.shape, BF16),
            pltpu.VMEM((tokens, width), BF16),
            pltpu.VMEM((tokens, width), F32),
            pltpu.VMEM((tokens, width), F32),
            pltpu.VMEM((tokens, D), BF16),
            pltpu.VMEM((tokens, width), BF16),
            pltpu.VMEM((rows, D), BF16),
            pltpu.VMEM((width, width), BF16),
            pltpu.SemaphoreType.DMA((10,)),
            pltpu.VMEM((tokens, width), BF16),
            pltpu.VMEM((tokens, width), BF16),
            pltpu.VMEM((width, tokens), BF16),
            pltpu.VMEM((tokens, D), BF16),
            pltpu.VMEM((tokens, width), F32),
            pltpu.VMEM((tokens, width), F32),
            pltpu.VMEM((tokens, width), F32),
            pltpu.VMEM((tokens, 3 * width), BF16),
            pltpu.VMEM((rows, D), F32),
            gather_sems(n_mp),
        ]
        + reduce_scratch(n_mp, rows)
        + scatter_scratch(n_dp, end - start, small, gffn.shape[2]),
        compiler_params=pltpu.CompilerParams(
            collective_id=5, has_side_effects=True, vmem_limit_bytes=ATTN_VMEM
        ),
        name="attn_backward",
    )(lengths, scales, dmid, mods, stats, qu, ku, gffn, wg, v, q, k, normed, att, x)


def squares(value):
    return jnp.sum(jnp.sum(value * value, axis=0, keepdims=True), axis=-1, keepdims=True)


def back_kernel(
    n_dp, n_mp, heads,
    lengths_ref, labels_ref, grads_ref, amod_ref, fmod_ref, gin_ref, feats_ref, gd_ref, gscale_ref,
    emb_ref, hid_ref, gated_ref, mixed_ref,
    mapup_ref, mapdown_ref, mod_ref, gffn_ref, ffgated_ref, wd_ref, mid_any, gu_any,
    gattn_ref, gf_ref, out_all, gin_s, gmod_ref, gmd_ref, gmu_ref, gtime_ref, gclass_ref, ggain_ref, norm_ref,
    mapup_s, mapdown_s, mod_s, gffn_s, ffgated_s, wd_s, mid_ref, gu_ref, load_sem, own_r, full_e, onehot_s, out_sem, gin_sem,
    recv_q, stage_q, own_q, recv_d, full_d, own_c, recv_c, send_g, recv_g, own_h, recv_h, full_h,
    own_p, recv_p, own_s, recv_s, own_n, all_dp, own_sum, all_mp,
    dp_ss, dp_rs, mp_ss, mp_rs,
    core_send, core_recv, x_send, x_recv, sems,
    recv_y, send_z, recv_z, a_zs, a_zr, a_ys, a_yr,
    f_recv_y, f_send_z, f_recv_z, f_zs, f_zr, f_ys, f_yr,
):
    r = Ranks(n_mp)
    d, m = r.d, r.m
    info = Images(lengths_ref)
    grid = Grid(n_dp)
    shard = gattn_ref.shape[1]
    start = scatter_split(shard)[1]
    tall = shard // 2
    attn_g = BulkScatter(
        grid, 8,
        lambda dd, i: grads_ref.at[
            lax.div(i, 2), pl.ds(pl.multiple_of(dd * shard + lax.rem(i, 2) * tall, tall), tall), :
        ],
        lambda i: gattn_ref.at[lax.div(i, 2), pl.ds(pl.multiple_of(lax.rem(i, 2) * tall, tall), tall), :],
        recv_y, send_z, recv_z, a_zs, a_zr, a_ys, a_yr)
    ffn_g = BulkScatter(
        grid, 3 * cuts(shard) - start, cut_rows(gffn_s, shard, start - 2 * cuts(shard)), lambda i: gf_ref.at[i],
        f_recv_y, f_send_z, f_recv_z, f_zs, f_zr, f_ys, f_yr)
    images, own_cols = feats_ref.shape
    rows = mid_ref.shape[0]
    copies = loads(
        (
            (mod_ref.at[0], mod_s),
            (mapdown_ref.at[0], mapdown_s),
            (mapup_ref.at[0], mapup_s),
            (ffgated_ref, ffgated_s),
            (wd_ref, wd_s),
            (gffn_ref.at[pl.ds(2, 1)], gffn_s),
            (mid_any, mid_ref),
            (gu_any, gu_ref),
        ),
        load_sem,
    )
    greet(
        [
            (n_dp, lambda k: (lax.rem(d + k, n_dp), m)),
            (n_mp, lambda k: (d, lax.rem(m + k, n_mp))),
        ]
    )
    at = lambda b: pl.ds(pl.multiple_of(b * rows, rows), rows)
    gin_s[at(m), :] = gin_ref[...].astype(BF16)
    one = Gather(r, rows, out_all, out_sem)
    two = Gather(r, rows, gin_s, gin_sem)
    red = Reduce(r, core_send, core_recv, x_send, x_recv, sems)

    def branch(j):
        kx, same = (1 + j // 2) % r.n_x, j % 2
        part = dot_nt(ffgated_s[at(r.rank(kx, same)), :], wd_s[...])
        if same == 0:
            red.other(kx, part)
        elif kx > 0:
            red.same(kx, part)
        else:
            position = lax.broadcasted_iota(jnp.int32, (rows, 1), 0) + m * rows
            live = (position.astype(F32) < info.live).astype(F32)
            out_all[at(m), :] = ((mid_ref[...] + red.finish(part)) * live).astype(BF16)

    def branches(quarter):
        for j in range(quarter * n_mp // 4, (quarter + 1) * n_mp // 4):
            branch(j)

    own_r[0:1, :] = amod_ref[...]
    own_r[1:2, :] = fmod_ref[...]

    def dp_ex(stage):
        return Exchange(n_dp, d, lambda p: (p, m), dp_ss.at[stage], dp_rs.at[stage])

    def mp_ex(stage):
        return Exchange(n_mp, m, lambda p: (d, p), mp_ss.at[stage], mp_rs.at[stage])

    def local_squares():
        value = jnp.zeros((1, 1), F32)
        for i in range(gd_ref.shape[0]):
            value = value + squares(gd_ref[i])
        for i in range(gu_ref.shape[0]):
            value = value + squares(gu_ref[i])
        return value

    ex = mp_ex(0)
    ex.start(lambda p: own_r, recv_q)
    attn_g.send(0)
    copies[5].wait()
    ffn_g.send(0)
    fill_onehot(onehot_s, labels_ref)
    recv_q[m] = own_r[...]
    ex.wait(lambda p: own_r, recv_q)
    for image in range(IMG_DEV):
        for c in range(2):
            row = jnp.zeros((1, D), F32)
            for rank in range(n_mp):
                share = 1.0 - info.is_long if rank * rows // SHORT == image else 0.0
                if image == 0:
                    share = share + info.is_long
                row = row + share * recv_q[rank, c : c + 1, :]
            stage_q[c * IMG_DEV + image : c * IMG_DEV + image + 1, :] = row
    own_q[...] = pack_rows(stage_q[...])
    two.start()
    ex = dp_ex(0)
    ex.start(lambda p: own_q, recv_d)
    attn_g.send(1)
    for copy in copies[:5] + copies[6:]:
        copy.wait()
    branches(0)
    ffn_g.forward(0)
    recv_d[d] = own_q[...]
    gains_own = emb_ref[d][images:]
    emb = emb_ref[:, 0:images, :]
    emb_factor = rms_blocks(emb)
    unit = emb * emb_factor[None] * emb_ref[:, images : images + 1, :]
    unit_factor = rms_blocks(unit)
    emb_own = emb_ref[d][0:images]
    unit_own = emb_own * emb_factor * gains_own[0:1]
    pre_own = (unit_own * unit_factor * gains_own[1:2]).astype(BF16)
    mixed = mixed_ref[...]
    mixed_factor = rms_blocks(mixed)
    mixed_own = mixed_ref[d]
    cond_own = (mixed_own * mixed_factor * gains_own[2:3]).astype(BF16)
    ex.wait(lambda p: own_q, recv_d)
    for p in range(n_dp):
        block = recv_d[p].astype(F32)
        for c in range(2):
            for half in range(2):
                first = (2 * half + c) * IMG_DEV
                full_d[c, p * IMG_DEV : (p + 1) * IMG_DEV, half * D // 2 : (half + 1) * D // 2] = block[
                    first : first + IMG_DEV
                ]
    own_c[...] = two_part_left(dot_nt, full_d[0], mod_s[:, 0, :].astype(BF16)) + two_part_left(
        dot_nt, full_d[1], mod_s[:, 1, :].astype(BF16)
    )
    ex = dp_ex(1)
    ex.start(lambda p: own_c, recv_c)
    attn_g.send(2)
    attn_g.forward(0)
    branches(1)
    recv_c[d] = own_c[...]
    squares_mod = jnp.zeros((1, 1), F32)
    for c in range(2):
        grad = two_part(dot_tn, cond_own, full_d[c])
        gmod_ref[:, c, :] = grad
        squares_mod = squares_mod + squares(grad)
    ex.wait(lambda p: own_c, recv_c)
    ggain_ref[2:3, :] = jnp.sum(own_c[...] * mixed_own * mixed_factor, axis=0, keepdims=True)
    d_mixed = rms_blocks_back(
        mixed, mixed_factor, recv_c[...] * emb_ref[:, images + 2 : images + 3, :]
    )
    recv_c[...] = d_mixed
    mix_own = recv_c[d]
    part = two_part_left(dot_nn, mix_own, mapdown_s[...].astype(BF16))
    for p in range(n_dp):
        send_g[p] = part[p * IMG_DEV : (p + 1) * IMG_DEV, :]
    ex = dp_ex(2)
    ex.start(lambda p: send_g.at[p], recv_g)
    attn_g.send(3)
    attn_g.forward(1)
    branches(2)
    recv_g[d] = send_g[d]
    grad = two_part_left(dot_tn, mix_own, gated_ref[...].astype(BF16))
    gmd_ref[...] = grad
    squares_md = squares(grad)
    ex.wait(lambda p: send_g.at[p], recv_g)
    d_gated = total_of(recv_g, n_dp)
    value, slope = gelu_parts(hid_ref[1])
    own_h[0] = d_gated * value
    own_h[1] = d_gated * hid_ref[0] * slope
    ex = dp_ex(3)
    ex.start(lambda p: own_h, recv_h)
    recv_h[d] = own_h[...]
    attn_g.send(4)
    attn_g.forward(2)
    branches(3)
    ex.wait(lambda p: own_h, recv_h)
    for p in range(n_dp):
        for c in range(2):
            full_h[c, p * IMG_DEV : (p + 1) * IMG_DEV, :] = recv_h[p, c]
    own_p[...] = two_part_left(dot_nt, full_h[0], mapup_s[:, 0, :].astype(BF16)) + two_part_left(
        dot_nt, full_h[1], mapup_s[:, 1, :].astype(BF16)
    )
    ex = mp_ex(1)
    ex.start(lambda p: own_p, recv_p)
    one.start()
    attn_g.send(5)
    attn_g.send(6)
    attn_g.forward(3)
    squares_done = local_squares() + squares_md
    recv_p[m] = own_p[...]
    for c in range(2):
        grad = two_part(dot_tn, pre_own, full_h[c])
        gmu_ref[:, c, :] = grad
        squares_done = squares_done + squares(grad)
    ex.wait(lambda p: own_p, recv_p)
    own_s[...] = total_of(recv_p, n_mp)
    ex = dp_ex(4)
    ex.start(lambda p: own_s, recv_s)
    attn_g.send(7)
    attn_g.forward(4)
    attn_g.forward(5)
    recv_s[d] = own_s[...]
    ex.wait(lambda p: own_s, recv_s)
    ggain_ref[1:2, :] = jnp.sum(own_s[...] * unit_own * unit_factor, axis=0, keepdims=True)
    d_unit = recv_c[...] + rms_blocks_back(
        unit, unit_factor, recv_s[...] * emb_ref[:, images + 1 : images + 2, :]
    )
    recv_s[...] = d_unit
    ggain_ref[0:1, :] = jnp.sum(recv_s[d] * emb_own * emb_factor, axis=0, keepdims=True)
    d_emb = rms_blocks_back(emb, emb_factor, d_unit * emb_ref[:, images : images + 1, :])
    recv_s[...] = d_emb
    ggain_ref[3:8, :] = jnp.zeros_like(ggain_ref[3:8, :])
    for p in range(n_dp):
        full_e[:, p * own_cols : (p + 1) * own_cols] = recv_s[p]
    attn_g.forward(6)
    attn_g.forward(7)
    gtime_ref[...] = two_part(dot_tn, feats_ref[...].astype(BF16), full_e[...])
    gclass_ref[...] = two_part_left(dot_tn, recv_s[d], onehot_s[...].astype(BF16))
    attn_g.finish()
    ffn_g.finish()
    split = squares_done
    for c in range(4):
        split = split + squares(gattn_ref[c])
    for i in range(ffn_g.pieces):
        split = split + squares(gf_ref[i])
    shared = squares_mod + squares(gtime_ref[...]) + squares(gclass_ref[...]) + squares(ggain_ref[...])
    lane = lax.broadcasted_iota(jnp.int32, (1, 128), 1)
    own_n[...] = jnp.zeros_like(own_n)
    own_n[0:1, :] = jnp.where(lane == 0, split + shared * (1.0 / n_mp), 0.0)
    width = gscale_ref.shape[1]
    column = lax.div(lax.broadcasted_iota(jnp.int32, (1, width), 1), width // heads)
    scale_row = jnp.zeros((1, 128), F32)
    for h in range(heads):
        head_part = jnp.sum(jnp.where(column == h, gscale_ref[...], 0.0), axis=-1, keepdims=True)
        scale_row = jnp.where(lane == h, head_part, scale_row)
    own_n[1:2, :] = scale_row
    ex = dp_ex(5)
    ex.start(lambda p: own_n, all_dp)
    all_dp[d] = own_n[...]
    for kx in range(1, r.n_x):
        one.forward(kx)
        two.forward(kx)
    ex.wait(lambda p: own_n, all_dp)
    summed = total_of(all_dp, n_dp)
    head = summed[1:2]
    own_sum[...] = jnp.zeros_like(own_sum)
    own_sum[0:1, :] = summed[0:1] + head * head
    ex = mp_ex(2)
    ex.start(lambda p: own_sum, all_mp)
    all_mp[m] = own_sum[...]
    for kx in range(r.n_x):
        one.arrived(kx)
        two.arrived(kx)
    ex.wait(lambda p: own_sum, all_mp)
    norm = jnp.sqrt(jnp.sum(total_of(all_mp, n_mp)[0:1], axis=-1, keepdims=True))
    norm_ref[0:1, :] = jnp.broadcast_to(norm, (1, 128))
    norm_ref[1:2, :] = head
    norm_ref[2:8, :] = jnp.zeros((6, 128), F32)
    red.drain()
    one.drain()
    two.drain()


def back(n_dp, n_mp, lengths, labels, grads, amod, fmod, mid, gin, feats, gd, gu, gscale, emb, hid, gated, mixed, map_states, gffn, ffgated, wd):
    images, part = feats.shape
    units_map = map_states[0].shape[3]
    rows = mid.shape[0]
    tokens = rows * n_mp
    heads = H // n_mp
    slab = (4, grads.shape[1] // n_dp, grads.shape[2])
    shard, units = slab[1], gffn.shape[2]
    small = shard // cuts(shard)
    pieces = 3 * cuts(shard) - scatter_split(shard)[1]
    shape = lambda *dims: jax.ShapeDtypeStruct(dims, F32)
    block = pltpu.VMEM((8, 128), F32)
    return pl.pallas_call(
        functools.partial(back_kernel, n_dp, n_mp, heads),
        out_shape=(
            shape(*slab),
            shape(pieces, small, units),
            jax.ShapeDtypeStruct((tokens, D), BF16),
            jax.ShapeDtypeStruct((tokens, D), BF16),
            shape(part, 2, D),
            shape(part, units_map),
            shape(part, 2, units_map),
            shape(part, DM),
            shape(part, NCLASS),
            shape(8, part),
            shape(8, 128),
        ),
        in_specs=[SMEM_SPEC] * 2 + vmem_specs(11) + any_specs(8),
        out_specs=tuple(vmem_specs(11)),
        scratch_shapes=[pltpu.VMEM(state.shape[1:], F32) for state in map_states]
        + [
            pltpu.VMEM((1, D, units), BF16),
            pltpu.VMEM((tokens, units), BF16),
            pltpu.VMEM((D, units), BF16),
            pltpu.VMEM(mid.shape, F32),
            pltpu.VMEM(gu.shape, F32),
            pltpu.SemaphoreType.DMA((8,)),
            pltpu.VMEM((2, D), F32),
            pltpu.VMEM((images, DM), F32),
            pltpu.VMEM((images, NCLASS), F32),
            gather_sems(n_mp),
            gather_sems(n_mp),
            pltpu.VMEM((n_mp, 2, D), F32),
            pltpu.VMEM((2 * IMG_DEV, D), F32),
            pltpu.VMEM((4 * IMG_DEV, D // 2), BF16),
            pltpu.VMEM((n_dp, 4 * IMG_DEV, D // 2), BF16),
            pltpu.VMEM((2, images, D), F32),
            pltpu.VMEM((images, part), F32),
            pltpu.VMEM((n_dp, images, part), F32),
            pltpu.VMEM((n_dp, IMG_DEV, units_map), F32),
            pltpu.VMEM((n_dp, IMG_DEV, units_map), F32),
            pltpu.VMEM((2, IMG_DEV, units_map), F32),
            pltpu.VMEM((n_dp, 2, IMG_DEV, units_map), F32),
            pltpu.VMEM((2, images, units_map), F32),
            pltpu.VMEM((images, part), F32),
            pltpu.VMEM((n_mp, images, part), F32),
            pltpu.VMEM((images, part), F32),
            pltpu.VMEM((n_dp, images, part), F32),
            block,
            pltpu.VMEM((n_dp, 8, 128), F32),
            block,
            pltpu.VMEM((n_mp, 8, 128), F32),
            pltpu.SemaphoreType.DMA((6, n_dp)),
            pltpu.SemaphoreType.DMA((6, n_dp)),
            pltpu.SemaphoreType.DMA((3, n_mp)),
            pltpu.SemaphoreType.DMA((3, n_mp)),
        ]
        + reduce_scratch(n_mp, rows)
        + scatter_scratch(n_dp, 8, slab[1] // 2, slab[2])
        + scatter_scratch(n_dp, pieces, small, units),
        compiler_params=pltpu.CompilerParams(
            collective_id=1, has_side_effects=True, vmem_limit_bytes=BACK_VMEM
        ),
        name="back",
    )(lengths, labels, grads, amod, fmod, gin, feats, gd, gscale, emb, hid, gated, mixed, *map_states, gffn, ffgated, wd, mid, gu)


def update_kernel(heads, *refs):
    states, refs = refs[:11], refs[11:]
    norm_ref, gattn_ref, gtime_ref, gclass_ref, gmu_ref, gmd_ref, gmod_ref, ggain_ref = refs[:8]
    ffn_refs, out_ref, gin_ref, refs = refs[8:11], refs[11], refs[12], refs[13:]
    outs, out_final, gin_final, norm_out, refs = refs[:33], refs[33], refs[34], refs[35], refs[36:]
    kept, new, first, second = refs[:11], refs[11:22], refs[22:33], refs[33:44]
    gup_s, gdown_s, gin_s, out_s, load_sem, store_sem, out_sem = refs[44:]
    order = (2, 8, 0, 6, 3, 5, 4, 7, 1, 9, 10)
    copies = {i: pltpu.make_async_copy(states[i], kept[i], load_sem.at[i]) for i in order}
    for i in order:
        copies[i].start()
    out_load = pltpu.make_async_copy(out_ref, out_s, out_sem.at[2])
    out_load.start()
    out_copies = [pltpu.make_async_copy(out_s, out_final, out_sem.at[0])]
    out_copies.append(pltpu.make_async_copy(gin_s, gin_final, out_sem.at[1]))
    parts = cuts(gdown_s.shape[0])
    small = gdown_s.shape[0] // parts
    pieces = [ref.at[i] for ref in ffn_refs for i in range(ref.shape[0])]
    for i, piece in enumerate(pieces):
        rows = slice(i % parts * small, (i % parts + 1) * small)
        if i < parts:
            gdown_s[rows, :] = piece[...]
        else:
            gup_s[rows, i // parts - 1, :] = piece[...]
    factor = CLIP_NORM / jnp.maximum(norm_ref[0:1, 0:1], CLIP_NORM)
    norm_out[...] = norm_ref[0:1, 0:1]
    head = norm_ref[1:2, :]
    rates, decays = learn_rates(), decay_rates()
    stores = []

    def store(i):
        for k, (source, target) in enumerate(((new[i], outs[3 * i]), (first[i], outs[3 * i + 1]), (second[i], outs[3 * i + 2]))):
            stores.append(pltpu.make_async_copy(source, target, store_sem.at[i, k]))
            stores[-1].start()

    def step(i, gradient, pick=lambda ref, k: ref.at[k]):
        copies[i].wait()
        new_weight, average, m_new, v_new = adamw_step(lambda k: pick(kept[i], k)[...], gradient, rates[i], decays[i])
        pick(new[i], 0)[...] = new_weight
        pick(new[i], 1)[...] = average
        first[i][...] = m_new
        second[i][...] = v_new
        store(i)

    step(2, gup_s[...] * factor[:, None, :])
    step(8, gmod_ref[...] * factor[:, None, :])
    copies[0].wait()
    for c in range(3):
        results = adamw_step(lambda k: kept[0][k, c], gattn_ref[c] * factor, rates[0], decays[0])
        new[0][0, c], new[0][1, c], first[0][c], second[0][c] = results
    store(0)
    step(6, gmu_ref[...] * factor[:, None, :])
    gin_s[...] = gin_ref[...].astype(F32)
    out_copies[1].start()
    step(3, gdown_s[...].T * factor)
    step(5, gclass_ref[...] * factor)
    step(4, gtime_ref[...] * factor)
    step(7, gmd_ref[...] * factor)
    step(1, gattn_ref[3].T * factor)
    copies[9].wait()
    copies[10].wait()
    for g in range(3):
        results = adamw_step(lambda k: kept[9][g, k : k + 1, :], ggain_ref[g : g + 1, :] * factor, rates[9], decays[9])
        new[9][g, 0:1, :], new[9][g, 1:2, :], first[9][g : g + 1, :], second[9][g : g + 1, :] = results
    store(9)
    results = adamw_step(lambda k: kept[10][k : k + 1, :], head[:, 0:heads] * factor, rates[10], decays[10])
    new[10][0:1, :], new[10][1:2, :], first[10][...], second[10][...] = results
    store(10)
    out_load.wait()
    out_copies[0].start()
    for copy in stores + out_copies:
        copy.wait()


def update(states, norm, grads, ffn_parts, out_all, gin_all):
    heads = states[10].shape[1]
    rows, _, units = states[2].shape[1:]
    news, moments = [], []
    for i, state in enumerate(states):
        if i == 9:
            news.append((state.shape[0], 2, state.shape[2]))
            moments.append((state.shape[0], state.shape[2]))
        else:
            news.append((2,) + state.shape[1:])
            moments.append(state.shape[1:] if i < 10 else (1, heads))
    outs = []
    for new, moment in zip(news, moments):
        outs += [new, moment, moment]
    shape = lambda dims: jax.ShapeDtypeStruct(dims, F32)
    return pl.pallas_call(
        functools.partial(update_kernel, heads),
        out_shape=tuple(shape(o) for o in outs)
        + (jax.ShapeDtypeStruct(out_all.shape, BF16), shape(gin_all.shape), shape((1, 1))),
        in_specs=any_specs(11) + vmem_specs(11) + any_specs(1) + vmem_specs(1),
        out_specs=tuple(any_specs(35) + vmem_specs(1)),
        scratch_shapes=[pltpu.VMEM(state.shape, F32) for state in states]
        + [pltpu.VMEM(dims, F32) for dims in news]
        + [pltpu.VMEM(dims, F32) for dims in moments]
        + [pltpu.VMEM(dims, F32) for dims in moments]
        + [
            pltpu.VMEM((rows, 2, units), F32),
            pltpu.VMEM((rows, units), F32),
            pltpu.VMEM(gin_all.shape, F32),
            pltpu.VMEM(out_all.shape, BF16),
            pltpu.SemaphoreType.DMA((11,)),
            pltpu.SemaphoreType.DMA((11, 3)),
            pltpu.SemaphoreType.DMA((3,)),
        ],
        compiler_params=pltpu.CompilerParams(vmem_limit_bytes=UPDATE_VMEM),
        name="update",
    )(*states, norm, *grads, *ffn_parts, out_all, gin_all)


def per_device(
    block_input,
    out_cotangent,
    sigmas,
    class_labels,
    image_lengths,
    fourier_freqs,
    inproj_state,
    outproj_state,
    upproj_state,
    downproj_state,
    timeproj_state,
    classemb_state,
    mapup_state,
    mapdown_state,
    modproj_state,
    gains_state,
    headscale_state,
):
    n_dp, n_mp = lax.axis_size("dp"), lax.axis_size("mp")
    in_state = jnp.transpose(inproj_state, (0, 2, 1, 3))
    class_state = jnp.transpose(classemb_state, (0, 2, 1))
    down_map_state = jnp.transpose(mapdown_state, (0, 2, 1))
    gain_state = jnp.transpose(gains_state, (1, 0, 2))
    mods, emb, hid, gated, mixed, feats, wg, wf, q, k, v, normed, qu, ku, att, stats, mid, nm = forward_part(
        n_dp, n_mp, image_lengths, sigmas, class_labels, headscale_state, fourier_freqs, block_input,
        (in_state, outproj_state, upproj_state),
        (timeproj_state, class_state, mapup_state, down_map_state, modproj_state), gain_state,
    )
    gd, dmid, fmod, ffgated, wd, gw_ffn = ffn(
        n_dp, n_mp, image_lengths, nm, mods, mid, out_cotangent, wf, downproj_state
    )
    gw_attn, gu, gin, amod, gscale = attn_backward(
        n_dp, n_mp, image_lengths, headscale_state, dmid, mods, stats, qu, ku, gw_ffn, wg, v, q, k, normed, att, block_input
    )
    g_attn, gb, out_all, gin_all, g_mod, g_md, g_mu, g_time, g_class, g_gain, norm = back(
        n_dp, n_mp, image_lengths, class_labels, gw_attn, amod, fmod, mid, gin, feats, gd, gu, gscale,
        emb, hid, gated, mixed, (mapup_state, down_map_state, modproj_state), gw_ffn, ffgated, wd,
    )
    states = (
        in_state,
        outproj_state,
        upproj_state,
        downproj_state,
        timeproj_state,
        class_state,
        mapup_state,
        down_map_state,
        modproj_state,
        gain_state,
        headscale_state,
    )
    grads = (g_attn, g_time, g_class, g_mu, g_md, g_mod, g_gain)
    *new, layer_out, input_grad, grad_norm = update(states, norm, grads, (gd, gu, gb), out_all, gin_all)
    orders = {0: (0, 2, 1, 3), 5: (0, 2, 1), 7: (0, 2, 1), 9: (1, 0, 2)}
    moment_orders = {0: (1, 0, 2), 5: (1, 0), 7: (1, 0)}
    results = [layer_out, input_grad, grad_norm.reshape(())]
    for i in range(11):
        stacked, first, second = new[3 * i : 3 * i + 3]
        if i in orders:
            stacked = jnp.transpose(stacked, orders[i])
        if i in moment_orders:
            first, second = jnp.transpose(first, moment_orders[i]), jnp.transpose(second, moment_orders[i])
        if i == 10:
            first, second = first[0], second[0]
        results += [stacked, first, second]
    return tuple(results)


def solution(mesh):
    return jax.shard_map(
        per_device,
        mesh=mesh,
        in_specs=(
            P("dp", None),
            P("dp", None),
            P(),
            P(),
            P(),
            P(),
            P(None, "dp", None, "mp"),
            P(None, "mp", "dp"),
            P(None, "dp", None, "mp"),
            P(None, "mp", "dp"),
            P(None, "dp", None),
            P(None, None, "dp"),
            P(None, "dp", None, "mp"),
            P(None, "mp", "dp"),
            P(None, "dp", None, None),
            P(None, None, "dp"),
            P(None, "mp"),
        ),
        out_specs=(
            P("dp", None),
            P("dp", None),
            P(),
            P(None, "dp", None, "mp"),
            P("dp", None, "mp"),
            P("dp", None, "mp"),
            P(None, "mp", "dp"),
            P("mp", "dp"),
            P("mp", "dp"),
            P(None, "dp", None, "mp"),
            P("dp", None, "mp"),
            P("dp", None, "mp"),
            P(None, "mp", "dp"),
            P("mp", "dp"),
            P("mp", "dp"),
            P(None, "dp", None),
            P("dp", None),
            P("dp", None),
            P(None, None, "dp"),
            P(None, "dp"),
            P(None, "dp"),
            P(None, "dp", None, "mp"),
            P("dp", None, "mp"),
            P("dp", None, "mp"),
            P(None, "mp", "dp"),
            P("mp", "dp"),
            P("mp", "dp"),
            P(None, "dp", None, None),
            P("dp", None, None),
            P("dp", None, None),
            P(None, None, "dp"),
            P(None, "dp"),
            P(None, "dp"),
            P(None, "mp"),
            P("mp"),
            P("mp"),
        ),
        check_vma=False,
    )
```

```python
import functools
import math

import jax
import jax.numpy as jnp
from jax import lax
from jax.experimental import pallas as pl
from jax.experimental.pallas import tpu as pltpu
from jax.sharding import PartitionSpec as P

D = 1024
H = 16
FF = 3072
DM = 768
MFF = 2304
NCLASS = 1000
IMG_DEV = 4
STEP = 10

EPSILON = 1e-06
BETA_ONE = 0.9
BETA_TWO = 0.95
ADAM_EPSILON = 1e-08
CLIP_NORM = 1.0
MASKED = -1e30
MESH = pl.DeviceIdType.MESH
FORWARD_VMEM = 60 * 2**20
FFN_VMEM = 60 * 2**20
ATTN_VMEM = 60 * 2**20
BACK_VMEM = 60 * 2**20
UPDATE_VMEM = 60 * 2**20
F32 = jnp.float32
BF16 = jnp.bfloat16


def minor_size(count):
    return 1 << ((count.bit_length() - 1) // 2)


def learn_rates():
    return (
        2.5 * D ** (-0.5),
        2.5 * (D // 64) ** (-0.5),
        2.5 * D ** (-0.5),
        2.5 * FF ** (-0.5),
        2.5 * DM ** (-0.5),
        2.5,
        2.5 * DM ** (-0.5),
        2.5 * MFF ** (-0.5),
        1.25 * DM ** (-0.5),
        0.25,
        7.5,
    )


def decay_rates():
    return (0.01, 0.01, 0.01, 0.01, 0.01, 0.01, 0.01, 0.01, 0.01, 0.0, 0.0)


def adamw_step(state, gradient, rate, decay):
    keep_rate = 1.0 - (1.0 + STEP) ** (-0.75)
    first = BETA_ONE * state(1) + (1.0 - BETA_ONE) * gradient
    second = BETA_TWO * state(2) + (1.0 - BETA_TWO) * gradient * gradient
    first_hat = first / (1.0 - BETA_ONE**STEP)
    second_hat = second / (1.0 - BETA_TWO**STEP)
    weight = state(0) * (1.0 - rate * decay) - rate * first_hat / (
        jnp.sqrt(second_hat) + ADAM_EPSILON
    )
    average = keep_rate * state(3) + (1.0 - keep_rate) * weight
    return weight, average, first, second


def dot_nn(a, b):
    return lax.dot_general(a, b, (((1,), (0,)), ((), ())), preferred_element_type=F32)


def dot_nt(a, b):
    return lax.dot_general(a, b, (((1,), (1,)), ((), ())), preferred_element_type=F32)


def dot_tn(a, b):
    return lax.dot_general(a, b, (((0,), (0,)), ((), ())), preferred_element_type=F32)


def two_part(dot, exact, wide):
    high = wide.astype(BF16)
    low = (wide - high.astype(F32)).astype(BF16)
    return dot(exact, high) + dot(exact, low)


def two_part_left(dot, wide, exact):
    high = wide.astype(BF16)
    low = (wide - high.astype(F32)).astype(BF16)
    return dot(high, exact) + dot(low, exact)


def gelu_parts(b):
    cdf = 0.5 * (1.0 + lax.erf(b * (1.0 / math.sqrt(2.0))))
    pdf = jnp.exp(-0.5 * b * b) * (1.0 / math.sqrt(2.0 * math.pi))
    return b * cdf, cdf + b * pdf


def greet(peers):
    barrier = pltpu.get_barrier_semaphore()
    total = 0
    for count, peer_of in peers:

        def say(k, carry, peer_of=peer_of):
            pl.semaphore_signal(barrier, inc=1, device_id=peer_of(k), device_id_type=MESH)
            return carry

        lax.fori_loop(1, count, say, 0)
        total += count - 1
    pl.semaphore_wait(barrier, total)


class Exchange:
    def __init__(self, count, me, device_of, send_sem, recv_sem):
        self.count, self.me, self.device_of = count, me, device_of
        self.send_sem, self.recv_sem = send_sem, recv_sem

    def _copy(self, k, src_of, dst, slot):
        peer = lax.rem(self.me + k, self.count)
        return pltpu.make_async_remote_copy(
            src_ref=src_of(peer),
            dst_ref=dst.at[slot],
            send_sem=self.send_sem.at[k],
            recv_sem=self.recv_sem.at[k],
            device_id=self.device_of(peer),
            device_id_type=MESH,
        )

    def start(self, src_of, dst):
        def body(k, carry):
            self._copy(k, src_of, dst, self.me).start()
            return carry

        lax.fori_loop(1, self.count, body, 0)

    def wait(self, src_of, dst):
        def body(k, carry):
            self._copy(k, src_of, dst, lax.rem(self.me + self.count - k, self.count)).wait()
            return carry

        lax.fori_loop(1, self.count, body, 0)

    def run(self, src_of, dst):
        self.start(src_of, dst)
        self.wait(src_of, dst)


def vmem_specs(count):
    return [pl.BlockSpec(memory_space=pltpu.VMEM)] * count


def any_specs(count):
    return [pl.BlockSpec(memory_space=pl.ANY)] * count


SMEM_SPEC = pl.BlockSpec(memory_space=pltpu.SMEM)
SHORT = 256


def total_of(ref, count):
    value = ref[0]
    for index in range(1, count):
        value = value + ref[index]
    return value


def pack_rows(rows):
    half = rows.shape[1] // 2
    return jnp.concatenate([rows[:, :half], rows[:, half:]], axis=0).astype(BF16)


def mean_square(blocks):
    sums = jnp.sum(jnp.sum(blocks, axis=0), axis=-1, keepdims=True)
    return sums * (1.0 / DM)


def rms_blocks(blocks):
    factor = lax.rsqrt(mean_square(blocks * blocks) + EPSILON)
    return factor


def rms_blocks_back(blocks, factor, gain_grad):
    inner = mean_square(blocks * gain_grad)
    return factor[None] * gain_grad - blocks * (factor * factor * factor * inner)[None]


class Grid:
    def __init__(self, n_dp):
        self.d, self.m = lax.axis_index("dp"), lax.axis_index("mp")
        self.n_y = minor_size(n_dp)
        self.n_z = n_dp // self.n_y
        self.z, self.y = lax.div(self.d, self.n_y), lax.rem(self.d, self.n_y)

    def at(self, kz, ky):
        return lax.rem(self.z + kz, self.n_z) * self.n_y + lax.rem(self.y + ky, self.n_y)

    def before(self, kz, ky):
        return lax.rem(self.z + self.n_z - kz, self.n_z) * self.n_y + lax.rem(self.y + self.n_y - ky, self.n_y)


def bulk_sems(n_dp, pieces):
    n_y = minor_size(n_dp)
    z_sem = pltpu.SemaphoreType.DMA((n_dp // n_y, pieces))
    y_sem = pltpu.SemaphoreType.DMA((n_dp // n_y, n_y, pieces))
    return [z_sem, z_sem, y_sem, y_sem]


def if_piece(act, i, low, high):
    @pl.when((i >= low) & (i < high))
    def _():
        act(i)


def each_piece(act, low, high):
    def body(i, carry):
        act(i)
        return carry

    lax.fori_loop(low, high, body, 0)


class Paced:
    def paced_send(self, u, first, num, den):
        self._at(self.send, u, first, num, den)

    def paced_forward(self, u, first, num, den):
        self._at(self.forward, u, first, num, den)

    def _at(self, act, u, first, num, den):
        far = 64 * num
        done = lambda t: lax.div((t - first) * den + far, num)
        new, old = done(u), done(u - 1)
        for step in range(-(-den // num)):
            i = old + 1 + step - 64

            @pl.when((new - 64 >= i) & (i >= 0) & (i < self.pieces))
            def _(i=i):
                act(i)

    @staticmethod
    def after(pieces, first, num, den, ticks):
        return min(pieces, max(0, (ticks - 1 - first) * den // num + 1)) if ticks > first else 0


class BulkGather(Paced):
    def __init__(self, grid, pieces, piece, z_ss, z_rs, y_ss, y_rs):
        self.g, self.pieces, self.piece = grid, pieces, piece
        self.z_ss, self.z_rs, self.y_ss, self.y_rs = z_ss, z_rs, y_ss, y_rs

    def z_copy(self, kz, i, owner):
        return pltpu.make_async_remote_copy(
            src_ref=self.piece(self.g.d, i), dst_ref=self.piece(owner, i), send_sem=self.z_ss.at[kz, i],
            recv_sem=self.z_rs.at[kz, i], device_id=(self.g.at(kz, 0), self.g.m), device_id_type=MESH)

    def y_copy(self, kz, ky, i, owner):
        return pltpu.make_async_remote_copy(
            src_ref=self.piece(self.g.before(kz, 0), i), dst_ref=self.piece(owner, i),
            send_sem=self.y_ss.at[kz, ky, i], recv_sem=self.y_rs.at[kz, ky, i],
            device_id=(self.g.at(0, ky), self.g.m), device_id_type=MESH)

    def send(self, i):
        for kz in range(1, self.g.n_z):
            self.z_copy(kz, i, self.g.d).start()
        for ky in range(1, self.g.n_y):
            self.y_copy(0, ky, i, self.g.d).start()

    def forward(self, i):
        for kz in range(1, self.g.n_z):
            self.z_copy(kz, i, self.g.before(kz, 0)).wait_recv()
            for ky in range(1, self.g.n_y):
                self.y_copy(kz, ky, i, self.g.before(kz, 0)).start()

    def finish_piece(self, i):
        for kz in range(1, self.g.n_z):
            self.z_copy(kz, i, self.g.d).wait_send()
        for kz in range(self.g.n_z):
            for ky in range(1, self.g.n_y):
                self.y_copy(kz, ky, i, self.g.before(kz, ky)).wait()

    def finish(self):
        each_piece(self.finish_piece, 0, self.pieces)


def line_sems(n_dp, pieces):
    n_y = minor_size(n_dp)
    n_z = n_dp // n_y
    return [pltpu.SemaphoreType.DMA((n_z, pieces))] * 4 + [pltpu.SemaphoreType.DMA((n_z, n_y, pieces))] * 2


class LineGather:
    def __init__(self, grid, pieces, piece, up_ss, up_rs, down_ss, down_rs, y_ss, y_rs):
        self.g, self.pieces, self.piece = grid, pieces, piece
        self.up, self.down, self.y_ss, self.y_rs = (up_ss, up_rs), (down_ss, down_rs), y_ss, y_rs
        self.ticks = pieces + grid.n_z - 1

    def block(self, z, y):
        return z * self.g.n_y + y

    def other_y(self, ky):
        return lax.rem(self.g.y + ky, self.g.n_y)

    def before_y(self, ky):
        return lax.rem(self.g.y + self.g.n_y - ky, self.g.n_y)

    def above(self):
        return (self.block(jnp.minimum(self.g.z + 1, self.g.n_z - 1), self.g.y), self.g.m)

    def below(self):
        return (self.block(jnp.maximum(self.g.z - 1, 0), self.g.y), self.g.m)

    def z_copy(self, sems, owner_z, i, target):
        block = self.piece(self.block(owner_z, self.g.y), i)
        return pltpu.make_async_remote_copy(
            src_ref=block, dst_ref=block, send_sem=sems[0].at[owner_z, i], recv_sem=sems[1].at[owner_z, i],
            device_id=target, device_id_type=MESH)

    def up_copy(self, owner_z, i):
        return self.z_copy(self.up, owner_z, i, self.above())

    def down_copy(self, owner_z, i):
        return self.z_copy(self.down, owner_z, i, self.below())

    def y_copy(self, owner_z, ky, i, in_y):
        return pltpu.make_async_remote_copy(
            src_ref=self.piece(self.block(owner_z, self.g.y), i), dst_ref=self.piece(self.block(owner_z, in_y), i),
            send_sem=self.y_ss.at[owner_z, ky, i], recv_sem=self.y_rs.at[owner_z, ky, i],
            device_id=(self.block(self.g.z, self.other_y(ky)), self.g.m), device_id_type=MESH)

    def along_y(self, owner_z, i):
        for ky in range(1, self.g.n_y):
            self.y_copy(owner_z, ky, i, self.g.y).start()

    def send(self, i):
        z, n_z = self.g.z, self.g.n_z

        @pl.when(z < n_z - 1)
        def _():
            self.up_copy(z, i).start()

        @pl.when(z > 0)
        def _():
            self.down_copy(z, i).start()

        self.along_y(z, i)

    def arrival(self, hop, i):
        z, n_z = self.g.z, self.g.n_z

        @pl.when(z - 1 - hop >= 0)
        def _():
            owner = jnp.maximum(z - 1 - hop, 0)
            self.up_copy(owner, i).wait_recv()

            @pl.when(z < n_z - 1)
            def _():
                self.up_copy(owner, i).start()

            self.along_y(owner, i)

        @pl.when(z + 1 + hop < n_z)
        def _():
            owner = jnp.minimum(z + 1 + hop, n_z - 1)
            self.down_copy(owner, i).wait_recv()

            @pl.when(z > 0)
            def _():
                self.down_copy(owner, i).start()

            self.along_y(owner, i)

    def tick(self, t):
        if_piece(self.send, t, 0, self.pieces)
        for hop in range(self.g.n_z - 1):
            if_piece(functools.partial(self.arrival, hop), t - 1 - hop, 0, self.pieces)

    def finish(self):
        z, n_z = self.g.z, self.g.n_z

        def piece_done(i):
            for owner in range(n_z):

                @pl.when((z >= owner) & (z < n_z - 1))
                def _():
                    self.up_copy(owner, i).wait_send()

                @pl.when((z <= owner) & (z > 0))
                def _():
                    self.down_copy(owner, i).wait_send()

                for ky in range(1, self.g.n_y):
                    self.y_copy(owner, ky, i, self.before_y(ky)).wait()

        each_piece(piece_done, 0, self.pieces)


def scatter_scratch(n_dp, pieces, rows, columns):
    n_y = minor_size(n_dp)
    n_z = n_dp // n_y
    slot = (pieces, rows, columns)
    return [
        pltpu.VMEM((n_z, max(n_y - 1, 1)) + slot, BF16),
        pltpu.VMEM((max(n_z - 1, 1),) + slot, BF16),
        pltpu.VMEM((max(n_z - 1, 1),) + slot, BF16),
    ] + bulk_sems(n_dp, pieces)


class BulkScatter(Paced):
    def __init__(self, grid, pieces, piece, out, recv_y, send_z, recv_z, z_ss, z_rs, y_ss, y_rs, sent=None):
        self.g, self.pieces, self.piece, self.out, self.sent = grid, pieces, piece, out, sent or piece
        self.recv_y, self.send_z, self.recv_z = recv_y, send_z, recv_z
        self.z_ss, self.z_rs, self.y_ss, self.y_rs = z_ss, z_rs, y_ss, y_rs

    def y_copy(self, kz, ky, i):
        return pltpu.make_async_remote_copy(
            src_ref=self.sent(self.g.at(kz, ky), i), dst_ref=self.recv_y.at[kz, ky - 1, i],
            send_sem=self.y_ss.at[kz, ky, i], recv_sem=self.y_rs.at[kz, ky, i],
            device_id=(self.g.at(0, ky), self.g.m), device_id_type=MESH)

    def z_copy(self, kz, i):
        return pltpu.make_async_remote_copy(
            src_ref=self.send_z.at[kz - 1, i], dst_ref=self.recv_z.at[kz - 1, i], send_sem=self.z_ss.at[kz, i],
            recv_sem=self.z_rs.at[kz, i], device_id=(self.g.at(kz, 0), self.g.m), device_id_type=MESH)

    def send(self, i):
        for kz in list(range(1, self.g.n_z)) + [0]:
            for ky in range(1, self.g.n_y):
                self.y_copy(kz, ky, i).start()

    def forward(self, i):
        for kz in list(range(1, self.g.n_z)) + [0]:
            value = self.piece(self.g.at(kz, 0), i)[...].astype(F32)
            for ky in range(1, self.g.n_y):
                self.y_copy(kz, ky, i).wait_recv()
                value = value + self.recv_y[kz, ky - 1, i].astype(F32)
            if kz == 0:
                self.out(i)[...] = value
            else:
                self.send_z[kz - 1, i] = value.astype(BF16)
                self.z_copy(kz, i).start()

    def finish_piece(self, i):
        total = self.out(i)[...]
        for kz in range(1, self.g.n_z):
            self.z_copy(kz, i).wait_recv()
            total = total + self.recv_z[kz - 1, i].astype(F32)
        self.out(i)[...] = total
        for kz in range(1, self.g.n_z):
            self.z_copy(kz, i).wait_send()
        for kz in range(self.g.n_z):
            for ky in range(1, self.g.n_y):
                self.y_copy(kz, ky, i).wait_send()

    def finish(self):
        each_piece(self.finish_piece, 0, self.pieces)


def cuts(rows):
    return max(rows // 32, min(rows // 16, 2))


def scatter_split(shard):
    parts = cuts(shard)
    return parts // 2 + 1, min(parts // 2 + 2 * parts + 1, 3 * parts - 1)


def cut_rows(ref, shard, first=0):
    parts = cuts(shard)
    small = shard // parts

    def piece(owner, i):
        rows = pl.ds(pl.multiple_of(owner * shard + lax.rem(i + first, parts) * small, small), small)
        return ref.at[lax.div(i + first, parts), rows, :]

    return piece


class Images:
    def __init__(self, lengths_ref):
        start = lax.axis_index("dp") * IMG_DEV
        self.is_long = jnp.where(lengths_ref[start] > SHORT, 1.0, 0.0)
        self.bias = (1.0 - self.is_long) * MASKED
        live = lengths_ref[start]
        for j in range(1, IMG_DEV):
            live = live + lengths_ref[start + j]
        self.live = live.astype(F32)


def fill_onehot(target, labels_ref):
    classes = lax.broadcasted_iota(jnp.int32, (1, NCLASS), 1)

    def body(i, carry):
        target[pl.ds(i, 1), :] = jnp.where(classes == labels_ref[i], 1.0, 0.0)
        return carry

    lax.fori_loop(0, target.shape[0], body, 0)


def own_features(target, sigmas_ref, freqs_ref, d):
    count, part = freqs_ref.shape[0], target.shape[1]

    def body(i, carry):
        target[pl.ds(i, 1), :] = jnp.full((1, part), sigmas_ref[i], F32)
        return carry

    lax.fori_loop(0, target.shape[0], body, 0)
    slices = count // part
    every = freqs_ref[...].reshape(1, count)
    freqs = every[:, 0:part]
    for k in range(1, slices):
        freqs = jnp.where(lax.rem(d, slices) == k, every[:, k * part : (k + 1) * part], freqs)
    angles = 2.0 * math.pi * (jnp.log(target[...]) / 4.0) * freqs
    target[...] = jnp.where(d < slices, jnp.cos(angles), jnp.sin(angles))


def head_ones(width, heads):
    size = width // heads
    row = lax.div(lax.broadcasted_iota(jnp.int32, (width, 1), 0), size)
    column = lax.div(lax.broadcasted_iota(jnp.int32, (1, width), 1), size)
    return (row == column).astype(F32).astype(BF16)


def head_scales(scales_ref, width, heads):
    column = lax.div(lax.broadcasted_iota(jnp.int32, (1, width), 1), width // heads)
    row = jnp.full((1, width), scales_ref[0, 0], F32)
    for h in range(1, heads):
        row = jnp.where(column == h, scales_ref[0, h], row)
    return row


def loads(pairs, sems):
    copies = [pltpu.make_async_copy(source, target, sems.at[i]) for i, (source, target) in enumerate(pairs)]
    for copy in copies:
        copy.start()
    return copies


class Ranks:
    def __init__(self, n_mp):
        self.d, self.m = lax.axis_index("dp"), lax.axis_index("mp")
        self.n_x = n_mp // 2
        self.x, self.c = lax.div(self.m, 2), lax.rem(self.m, 2)
        self.sibling = (self.d, self.x * 2 + 1 - self.c)

    def rank(self, kx, same):
        core = jnp.where(same == 1, self.c, 1 - self.c)
        return lax.rem(self.x + kx, self.n_x) * 2 + core

    def chip(self, kx):
        return (self.d, lax.rem(self.x + kx, self.n_x) * 2 + self.c)

    def greet(self):
        greet([(2, lambda k: self.sibling), (self.n_x, self.chip)])


class Reduce:
    def __init__(self, ranks, core_send, core_recv, x_send, x_recv, sems):
        self.r = ranks
        self.core_send, self.core_recv, self.x_send, self.x_recv = core_send, core_recv, x_send, x_recv
        self.sems = sems

    def core_copy(self, kx):
        return pltpu.make_async_remote_copy(
            src_ref=self.core_send.at[kx], dst_ref=self.core_recv.at[kx], send_sem=self.sems.at[0, kx],
            recv_sem=self.sems.at[1, kx], device_id=self.r.sibling, device_id_type=MESH)

    def x_copy(self, kx):
        return pltpu.make_async_remote_copy(
            src_ref=self.x_send.at[kx], dst_ref=self.x_recv.at[kx], send_sem=self.sems.at[2, kx],
            recv_sem=self.sems.at[3, kx], device_id=self.r.chip(kx), device_id_type=MESH)

    def other(self, kx, part):
        self.core_send[kx] = part.astype(BF16)
        self.core_copy(kx).start()

    def same(self, kx, part):
        self.core_copy(kx).wait_recv()
        self.x_send[kx] = (part + self.core_recv[kx].astype(F32)).astype(BF16)
        self.x_copy(kx).start()

    def finish(self, part):
        self.core_copy(0).wait_recv()
        total = part + self.core_recv[0].astype(F32)
        for kx in range(1, self.r.n_x):
            self.x_copy(kx).wait_recv()
            total = total + self.x_recv[kx].astype(F32)
        return total

    def drain(self):
        self.core_copy(0).wait_send()
        for kx in range(1, self.r.n_x):
            self.core_copy(kx).wait_send()
            self.x_copy(kx).wait_send()


def reduce_scratch(n_mp, rows):
    slots = pltpu.VMEM((n_mp // 2, rows, D), BF16)
    return [slots, slots, slots, slots, pltpu.SemaphoreType.DMA((4, n_mp // 2))]


class Gather:
    def __init__(self, ranks, rows, buffer, sems):
        self.r, self.rows, self.buffer, self.sems = ranks, rows, buffer, sems

    def at(self, rank):
        return self.buffer.at[pl.ds(pl.multiple_of(rank * self.rows, self.rows), self.rows), :]

    def x_copy(self, kx, slot):
        return pltpu.make_async_remote_copy(
            src_ref=self.at(self.r.m), dst_ref=self.at(slot), send_sem=self.sems.at[0, kx],
            recv_sem=self.sems.at[1, kx], device_id=self.r.chip(kx), device_id_type=MESH)

    def core_copy(self, kx, out_slot, in_slot):
        return pltpu.make_async_remote_copy(
            src_ref=self.at(out_slot), dst_ref=self.at(in_slot), send_sem=self.sems.at[2, kx],
            recv_sem=self.sems.at[3, kx], device_id=self.r.sibling, device_id_type=MESH)

    def start(self):
        for kx in range(1, self.r.n_x):
            self.x_copy(kx, self.r.m).start()
        self.core_copy(0, self.r.m, self.r.m).start()

    def from_chip(self, kx):
        return lax.rem(self.r.x + self.r.n_x - kx, self.r.n_x) * 2 + self.r.c

    def from_core(self, kx):
        return lax.rem(self.r.x + self.r.n_x - kx, self.r.n_x) * 2 + 1 - self.r.c

    def forward(self, kx):
        slot = self.from_chip(kx)
        self.x_copy(kx, slot).wait_recv()
        self.core_copy(kx, slot, slot).start()

    def arrived(self, kx):
        self.core_copy(kx, self.r.m, self.from_core(kx)).wait_recv()

    def drain(self):
        for kx in range(1, self.r.n_x):
            self.x_copy(kx, self.r.m).wait_send()
        for kx in range(self.r.n_x):
            self.core_copy(kx, self.r.m, self.r.m).wait_send()


def gather_sems(n_mp):
    return pltpu.SemaphoreType.DMA((4, n_mp // 2))


def head_sums(values, ones):
    return two_part_left(dot_nn, values, ones)


def row_sums_factor(values):
    return lax.rsqrt(jnp.mean(values * values, axis=-1, keepdims=True) + EPSILON)


def image_scale(info, mods_ref, which, image):
    is_long = info.is_long
    row = mods_ref[which, pl.ds(image, 1), :]
    return 1.0 + (is_long * mods_ref[which, 0:1, :] + (1.0 - is_long) * row)


def column_bias(info, image, columns_shape, short):
    keys = lax.broadcasted_iota(jnp.int32, columns_shape, 0)
    own = (keys >= image * short) & (keys < (image + 1) * short)
    return jnp.where(own, 0.0, info.bias)


def forward_kernel(
    n_dp, n_mp, heads,
    lengths_ref, sigmas_ref, labels_ref, scales_ref, freqs_ref, x_any,
    in_ref, out_ref, up_ref, time_ref, class_ref, mapup_ref, mapdown_ref, mod_ref, gains_ref,
    mods_ref, emb_ref, hid_ref, gated_ref, mixed_ref, feats_ref, wg_out, wf_out,
    q_out, k_out, v_out, normed_out, qu_out, ku_out, att_ref, stats_ref, mid_ref, nm_ref,
    x_ref, wg_ref, q_ref, k_ref, v_ref, normed_ref, wf_ref, onehot_s, ones_ref, store_sem,
    in_s, out_s, up_s, time_s, class_s, mapup_s, mapdown_s, mod_s, gains_s, load_sem,
    send_a, recv_a, own_a, send_h, recv_h, own_g, recv_g, own_x, recv_x, own_m, send_o, recv_o,
    dp_ss, dp_rs, mp_ss, mp_rs, a_us, a_ur, a_ds, a_dr, a_ys, a_yr, f_us, f_ur, f_ds, f_dr, f_ys, f_yr,
    qu_s, ku_s, vt_s, part_s, core_send, core_recv, x_send, x_recv, sems,
):
    r = Ranks(n_mp)
    grid = Grid(n_dp)
    d, m = r.d, r.m
    images, part = feats_ref.shape
    info = Images(lengths_ref)
    copies = loads(
        (
            (time_ref.at[0], time_s),
            (in_ref.at[0], in_s),
            (out_ref.at[0], out_s),
            (class_ref.at[0], class_s),
            (gains_ref, gains_s),
            (up_ref.at[0], up_s),
            (mapup_ref.at[0], mapup_s),
            (mapdown_ref.at[0], mapdown_s),
            (mod_ref.at[0], mod_s),
            (x_any, x_ref),
        ),
        load_sem,
    )
    map_copies = [copies[0]] + copies[3:5] + copies[6:]
    greet(
        [
            (n_dp, lambda k: (lax.rem(d + k, n_dp), m)),
            (n_mp, lambda k: (d, lax.rem(m + k, n_mp))),
        ]
    )
    own_features(feats_ref, sigmas_ref, freqs_ref, d)
    shard = in_s.shape[1]
    mine = pl.ds(pl.multiple_of(d * shard, shard), shard)
    attn = LineGather(
        grid, 4, lambda dd, i: wg_ref.at[i, pl.ds(pl.multiple_of(dd * shard, shard), shard), :],
        a_us, a_ur, a_ds, a_dr, a_ys, a_yr)
    up_w = LineGather(
        grid, 2 * cuts(shard), cut_rows(wf_ref, shard), f_us, f_ur, f_ds, f_dr, f_ys, f_yr
    )

    def dp_ex(stage):
        return Exchange(n_dp, d, lambda p: (p, m), dp_ss.at[stage], dp_rs.at[stage])

    map_copies[0].wait()
    partial = dot_nn(feats_ref[...].astype(BF16), time_s[...].astype(BF16))
    for p in range(n_dp):
        send_a[p] = partial[:, p * part : (p + 1) * part]
    ex = dp_ex(0)
    ex.start(lambda p: send_a.at[p], recv_a)
    copies[1].wait()
    for c in range(3):
        wg_ref[c, mine, :] = in_s[c].astype(BF16)
    copies[2].wait()
    wg_ref[3, mine, :] = out_s[...].T.astype(BF16)
    attn.tick(0)
    recv_a[d] = send_a[d]
    copies[5].wait()
    for c in range(2):
        wf_ref[c, mine, :] = up_s[:, c, :].astype(BF16)
    fill_onehot(onehot_s, labels_ref)
    ones_ref[...] = head_ones(q_ref.shape[1], heads)
    for copy in map_copies[1:]:
        copy.wait()
    e_cols = dot_nt(onehot_s[...].astype(BF16), class_s[...].astype(BF16))
    own_a[images:, :] = jnp.zeros((8, part), F32)
    for g in range(3):
        own_a[images + g : images + g + 1, :] = gains_s[g, 0:1, :].astype(BF16).astype(F32)
    ex.wait(lambda p: send_a.at[p], recv_a)
    own_a[0:images, :] = total_of(recv_a, n_dp) + e_cols
    ex = dp_ex(1)
    ex.start(lambda p: own_a, emb_ref)
    attn.tick(1)
    emb_ref[d] = own_a[...]
    ex.wait(lambda p: own_a, emb_ref)
    gains = emb_ref[:, images:, :]
    emb = emb_ref[:, 0:images, :]
    unit = emb * rms_blocks(emb)[None] * gains[:, 0:1, :]
    unit_factor = rms_blocks(unit)
    own_x[0] = (emb_ref[d][0:images] * rms_blocks(emb)) * emb_ref[d][images : images + 1]
    unit_own = own_x[0]
    pre_own = (unit_own * unit_factor * emb_ref[d][images + 1 : images + 2]).astype(BF16)
    for c in range(2):
        part = dot_nn(pre_own, mapup_s[:, c, :].astype(BF16))
        for p in range(n_dp):
            send_h[p, c] = part[p * IMG_DEV : (p + 1) * IMG_DEV, :]
    ex = dp_ex(2)
    ex.start(lambda p: send_h.at[p], recv_h)
    attn.tick(2)
    recv_h[d] = send_h[d]
    ex.wait(lambda p: send_h.at[p], recv_h)
    hidden = total_of(recv_h, n_dp)
    hid_ref[...] = hidden
    own_g[...] = (hidden[0] * gelu_parts(hidden[1])[0]).astype(BF16).astype(F32)
    ex = dp_ex(3)
    ex.start(lambda p: own_g, recv_g)
    attn.tick(3)
    recv_g[d] = own_g[...]
    ex.wait(lambda p: own_g, recv_g)
    for p in range(n_dp):
        gated_ref[p * IMG_DEV : (p + 1) * IMG_DEV, :] = recv_g[p]
    own_x[0] = dot_nt(gated_ref[...].astype(BF16), mapdown_s[...].astype(BF16))
    ex = Exchange(n_mp, m, lambda p: (d, p), mp_ss.at[0], mp_rs.at[0])
    ex.start(lambda p: own_x.at[0], recv_x)
    attn.tick(4)
    up_w.tick(0)
    recv_x[m] = own_x[0]
    ex.wait(lambda p: own_x.at[0], recv_x)
    own_m[...] = total_of(recv_x, n_mp) + unit_own
    ex = dp_ex(4)
    ex.start(lambda p: own_m, mixed_ref)
    attn.tick(5)
    up_w.tick(1)
    mixed_ref[d] = own_m[...]
    ex.wait(lambda p: own_m, mixed_ref)
    mixed_factor = rms_blocks(mixed_ref[...])
    cond_own = (own_m[...] * mixed_factor * emb_ref[d][images + 2 : images + 3]).astype(BF16)
    for c in range(2):
        part = dot_nn(cond_own, mod_s[:, c, :].astype(BF16))
        for p in range(n_dp):
            send_o[p, c] = part[p * IMG_DEV : (p + 1) * IMG_DEV, :]
    ex = dp_ex(5)
    ex.start(lambda p: send_o.at[p], recv_o)
    attn.tick(6)
    up_w.tick(2)
    recv_o[d] = send_o[d]
    ex.wait(lambda p: send_o.at[p], recv_o)
    mods_ref[...] = total_of(recv_o, n_dp)
    each_piece(attn.tick, 7, attn.ticks)
    attn.finish()
    tokens = x_ref.shape[0]
    rows = tokens // n_mp
    width = q_ref.shape[1]
    size = width // heads
    red = Reduce(r, core_send, core_recv, x_send, x_recv, sems)
    at = lambda b: pl.ds(pl.multiple_of(b * rows, rows), rows)
    image_of = lambda b: lax.div(b * rows, SHORT)

    scale_row = head_scales(scales_ref, q_ref.shape[1], heads)

    def project(b, carry):
        xb = x_ref[at(b), :].astype(F32)
        normed = (xb * row_sums_factor(xb) * image_scale(info, mods_ref, 0, image_of(b))).astype(BF16)
        normed_ref[at(b), :] = normed
        q = dot_nn(normed, wg_ref[0])
        q_ref[at(b), :] = q
        qu_s[at(b), :] = (q * lax.rsqrt(head_sums(q * q, ones_ref[...]) + EPSILON) * scale_row).astype(BF16)
        k = dot_nn(normed, wg_ref[1])
        k_ref[at(b), :] = k
        ku_s[at(b), :] = (k * lax.rsqrt(head_sums(k * k, ones_ref[...]) + EPSILON)).astype(BF16)
        v = dot_nn(normed, wg_ref[2])
        v_ref[at(b), :] = v.astype(BF16)
        vt_s[:, at(b)] = v.T.astype(BF16)

        @pl.when(lax.rem(b, 2) == 0)
        def _():
            up_w.tick(3 + lax.div(b, 2))

        return carry

    lax.fori_loop(0, n_mp, project, 0)
    stores = [
        pltpu.make_async_copy(source, target, store_sem.at[n])
        for n, (source, target) in enumerate(
            ((wg_ref, wg_out), (q_ref, q_out), (k_ref, k_out), (v_ref, v_out), (normed_ref, normed_out), (qu_s, qu_out), (ku_s, ku_out))
        )
    ]
    for copy in stores:
        copy.start()
    first_tick = 3 + (n_mp + 1) // 2
    ticks_left = max(up_w.ticks - first_tick, 0)

    def tick_at(u):
        span = heads * n_mp
        count = lambda v: lax.div(v * ticks_left + span, span)

        @pl.when(count(u) != count(u - 1))
        def _():
            up_w.tick(first_tick + count(u) - 1)

    lanes = lax.broadcasted_iota(jnp.int32, (1, width), 1)

    def block(j, carry):
        kx, same = lax.rem(1 + lax.div(j, 2), r.n_x), lax.rem(j, 2)
        b = r.rank(kx, same)
        bias = column_bias(info, image_of(b), (tokens, 1), SHORT)
        qu = qu_s[at(b), :]
        outs = []
        for h in range(heads):
            mask = ((lanes >= h * size) & (lanes < (h + 1) * size)).astype(F32).astype(BF16)
            scores = dot_nt(ku_s[...], qu * mask) + bias
            top = jnp.max(scores, axis=0, keepdims=True)
            expon = jnp.exp(scores - top)
            total = jnp.sum(expon, axis=0, keepdims=True)
            stats_ref[h : h + 1, at(b)] = top + jnp.log(total)
            tick_at(heads * j + h)
            outs.append(dot_nn(vt_s[h * size : (h + 1) * size, :], expon.astype(BF16)) / total)
        att = jnp.concatenate(outs, axis=0).T.astype(BF16)
        att_ref[at(b), :] = att
        part_s[...] = dot_nt(att, wg_ref[3])

        @pl.when(same == 0)
        def _():
            red.other(kx, part_s[...])

        @pl.when((same == 1) & (kx > 0))
        def _():
            red.same(kx, part_s[...])

        return carry

    lax.fori_loop(0, n_mp, block, 0)
    if heads < 8:
        stats_ref[heads:8, :] = jnp.zeros((8 - heads, tokens), F32)
    middle = x_ref[at(r.m), :].astype(F32) + red.finish(part_s[...])
    mid_ref[...] = middle
    nm_ref[...] = (middle * row_sums_factor(middle) * image_scale(info, mods_ref, 1, image_of(r.m))).astype(BF16)
    red.drain()
    up_w.finish()
    stores.append(pltpu.make_async_copy(wf_ref, wf_out, store_sem.at[7]))
    stores[-1].start()
    for copy in stores:
        copy.wait()


def forward_part(n_dp, n_mp, lengths, sigmas, labels, scales, freqs, x, layer_states, map_states, gains_state):
    images, part = sigmas.shape[0], map_states[0].shape[1]
    units_map = map_states[2].shape[3]
    shard, _, units = layer_states[2].shape[1:]
    width, heads = layer_states[0].shape[3], scales.shape[1]
    tokens = x.shape[0]
    rows = tokens // n_mp
    states = (*layer_states, *map_states)
    f32 = lambda *dims: jax.ShapeDtypeStruct(dims, F32)
    bf16 = lambda *dims: jax.ShapeDtypeStruct(dims, BF16)
    return pl.pallas_call(
        functools.partial(forward_kernel, n_dp, n_mp, heads),
        out_shape=(
            f32(2, IMG_DEV, D),
            f32(n_dp, images + 8, part),
            f32(2, IMG_DEV, units_map),
            f32(images, units_map),
            f32(n_dp, images, part),
            f32(images, part),
            bf16(4, D, width),
            bf16(2, D, units),
            f32(tokens, width),
            f32(tokens, width),
            bf16(tokens, width),
            bf16(tokens, D),
            bf16(tokens, width),
            bf16(tokens, width),
            bf16(tokens, width),
            f32(8, tokens),
            f32(rows, D),
            bf16(rows, D),
        ),
        in_specs=[SMEM_SPEC] * 4 + vmem_specs(1) + any_specs(10),
        out_specs=tuple(vmem_specs(6) + any_specs(8) + vmem_specs(4)),
        scratch_shapes=[
            pltpu.VMEM((tokens, D), BF16),
            pltpu.VMEM((4, D, width), BF16),
            pltpu.VMEM((tokens, width), F32),
            pltpu.VMEM((tokens, width), F32),
            pltpu.VMEM((tokens, width), BF16),
            pltpu.VMEM((tokens, D), BF16),
            pltpu.VMEM((2, D, units), BF16),
            pltpu.VMEM((images, NCLASS), F32),
            pltpu.VMEM((width, width), BF16),
            pltpu.SemaphoreType.DMA((8,)),
        ]
        + [pltpu.VMEM(state.shape[1:], F32) for state in states]
        + [
            pltpu.VMEM(gains_state.shape, F32),
            pltpu.SemaphoreType.DMA((10,)),
            pltpu.VMEM((n_dp, images, part), F32),
            pltpu.VMEM((n_dp, images, part), F32),
            pltpu.VMEM((images + 8, part), F32),
            pltpu.VMEM((n_dp, 2, IMG_DEV, units_map), F32),
            pltpu.VMEM((n_dp, 2, IMG_DEV, units_map), F32),
            pltpu.VMEM((IMG_DEV, units_map), F32),
            pltpu.VMEM((n_dp, IMG_DEV, units_map), F32),
            pltpu.VMEM((1, images, part), F32),
            pltpu.VMEM((n_mp, images, part), F32),
            pltpu.VMEM((images, part), F32),
            pltpu.VMEM((n_dp, 2, IMG_DEV, D), F32),
            pltpu.VMEM((n_dp, 2, IMG_DEV, D), F32),
            pltpu.SemaphoreType.DMA((6, n_dp)),
            pltpu.SemaphoreType.DMA((6, n_dp)),
            pltpu.SemaphoreType.DMA((1, n_mp)),
            pltpu.SemaphoreType.DMA((1, n_mp)),
        ]
        + line_sems(n_dp, 4)
        + line_sems(n_dp, 2 * cuts(shard))
        + [
            pltpu.VMEM((tokens, width), BF16),
            pltpu.VMEM((tokens, width), BF16),
            pltpu.VMEM((width, tokens), BF16),
            pltpu.VMEM((rows, D), F32),
        ]
        + reduce_scratch(n_mp, rows),
        compiler_params=pltpu.CompilerParams(
            collective_id=0, has_side_effects=True, vmem_limit_bytes=FORWARD_VMEM
        ),
        name="forward_part",
    )(lengths, sigmas, labels, scales, freqs, x, *states, gains_state)


def ffn_kernel(
    n_dp, n_mp, lengths_ref, nm_ref, mods_ref, mid_ref, cot_ref, wf_ref, down_ref,
    gd_ref, dmid_ref, fmod_ref, gated_out, wd_out, gw_out,
    w_s, cot_s, nm_s, gated_s, gate_s, slope_s, dh_s, dz_s, part_s, gw_s, gather_sem,
    b_core_send, b_core_recv, b_x_send, b_x_recv, b_sems,
    down_s, wd_s, load_sem, store_sem, w_zs, w_zr, w_ys, w_yr,
    recv_y, send_z, recv_z, g_zs, g_zr, g_ys, g_yr,
):
    r = Ranks(n_mp)
    grid = Grid(n_dp)
    info = Images(lengths_ref)
    copies = loads(((down_ref.at[0], down_s), (wf_ref, w_s), (cot_ref, cot_s)), load_sem)
    rows = nm_ref.shape[0]
    tokens = rows * n_mp
    at = lambda b: pl.ds(pl.multiple_of(b * rows, rows), rows)
    image_of = lambda b: lax.div(b * rows, SHORT)

    greet(
        [
            (n_dp, lambda k: (lax.rem(r.d + k, n_dp), r.m)),
            (2, lambda k: r.sibling),
            (r.n_x, r.chip),
        ]
    )
    shard = D // n_dp
    parts = cuts(shard)
    small = shard // parts
    copies[0].wait()
    wd_s[0, pl.ds(pl.multiple_of(r.d * shard, shard), shard), :] = down_s[...].T.astype(BF16)
    down_w = BulkGather(grid, parts, cut_rows(wd_s, shard), w_zs, w_zr, w_ys, w_yr)
    first = scatter_split(shard)[0]
    down_g = BulkScatter(
        grid, first, cut_rows(gw_s, shard), lambda i: gd_ref.at[i],
        recv_y, send_z, recv_z, g_zs, g_zr, g_ys, g_yr)
    each_piece(down_w.send, 0, parts)
    nm_s[at(r.m), :] = nm_ref[...]
    gather = Gather(r, rows, nm_s, gather_sem)
    gather.start()
    copies[1].wait()
    bwd = Reduce(r, b_core_send, b_core_recv, b_x_send, b_x_recv, b_sems)

    copies[2].wait()

    def live_rows(b):
        position = lax.broadcasted_iota(jnp.int32, (rows, 1), 0) + b * rows
        return (position.astype(F32) < info.live).astype(F32)

    def live_cotangent(b, carry):
        dz_s[at(b), :] = (cot_s[at(b), :].astype(F32) * live_rows(b)).astype(BF16)
        return carry

    lax.fori_loop(0, n_mp, live_cotangent, 0)
    def forward(j, carry):
        kx = lax.div(j, 2)
        same = jnp.where(kx == 0, 1 - lax.rem(j, 2), lax.rem(j, 2))
        b = r.rank(kx, same)
        back_kx = lax.rem(r.n_x - kx, r.n_x)

        if_piece(down_w.forward, j - 1, 0, min(2, parts))

        @pl.when((same == 0) & (kx > 0))
        def _():
            gather.forward(back_kx)

        @pl.when(same == 0)
        def _():
            gather.arrived(back_kx)

        nm = nm_s[at(b), :]
        hidden = dot_nn(nm, w_s[0])
        gate = dot_nn(nm, w_s[1])
        value, slope = gelu_parts(gate)
        gated = (hidden * value).astype(BF16)
        gated_s[at(b), :] = gated
        gate_s[at(b), :] = value
        slope_s[at(b), :] = hidden * slope
        if_piece(down_w.forward, j, 2, parts)
        return carry

    lax.fori_loop(0, n_mp, forward, 0)

    step = 512

    def down_gradient(i, carry):
        cols = pl.ds(pl.multiple_of(i * step, step), step)
        gw_s[0, cols, :] = dot_tn(dz_s[:, cols], gated_s[...]).astype(BF16)
        return carry

    lax.fori_loop(0, D // step, down_gradient, 0)
    each_piece(down_g.send, 0, first)
    each_piece(down_w.forward, n_mp, parts)
    down_w.finish()
    stores = [
        pltpu.make_async_copy(source, target, store_sem.at[n])
        for n, (source, target) in enumerate(((gated_s, gated_out), (wd_s.at[0], wd_out), (gw_s.at[0], gw_out.at[0])))
    ]
    for copy in stores:
        copy.start()

    def backward(j, carry):
        kx, same = lax.rem(1 + lax.div(j, 2), r.n_x), lax.rem(j, 2)
        b = r.rank(kx, same)
        if_piece(down_g.forward, j - (n_mp - 2), 0, first)
        d_gated = dot_nn(dz_s[at(b), :], wd_s[0])
        d_value = (d_gated * gate_s[at(b), :]).astype(BF16)
        d_gate = (d_gated * slope_s[at(b), :]).astype(BF16)
        dh_s[0, at(b), :] = d_value
        dh_s[1, at(b), :] = d_gate
        part_s[...] = dot_nt(d_value, w_s[0]) + dot_nt(d_gate, w_s[1])

        @pl.when(same == 0)
        def _():
            bwd.other(kx, part_s[...])

        @pl.when((same == 1) & (kx > 0))
        def _():
            bwd.same(kx, part_s[...])

        return carry

    lax.fori_loop(0, n_mp, backward, 0)

    def up_gradient(i, carry):
        if_piece(down_g.forward, i + 2, 2, first)
        cols = pl.ds(pl.multiple_of(i * step, step), step)
        left = nm_s[:, cols]
        for c in range(2):
            gw_s[1 + c, cols, :] = dot_tn(left, dh_s[c]).astype(BF16)
        return carry

    lax.fori_loop(0, D // step, up_gradient, 0)

    each_piece(down_g.forward, D // step + 2, first)
    up_store = pltpu.make_async_copy(gw_s.at[pl.ds(1, 2)], gw_out.at[pl.ds(1, 2)], store_sem.at[3])
    up_store.start()
    d_nm = bwd.finish(part_s[...])
    middle = mid_ref[...]
    live = live_rows(r.m)
    scale = image_scale(info, mods_ref, 1, image_of(r.m))
    factor = row_sums_factor(middle)
    inner = jnp.mean(middle * scale * d_nm, axis=-1, keepdims=True)
    dmid_ref[...] = cot_s[at(r.m), :].astype(F32) * live + (
        factor * scale * d_nm - middle * (factor * factor * factor * inner)
    )
    fmod_ref[...] = jnp.sum(d_nm * middle * factor, axis=0, keepdims=True)
    gather.drain()
    bwd.drain()
    down_g.finish()
    for copy in stores + [up_store]:
        copy.wait()


def ffn(n_dp, n_mp, lengths, nm, mods, mid, cot, wf, down_state):
    rows = nm.shape[0]
    tokens = rows * n_mp
    units = wf.shape[2]
    shard = D // n_dp
    parts = cuts(shard)
    first = scatter_split(shard)[0]
    shape = jax.ShapeDtypeStruct
    return pl.pallas_call(
        functools.partial(ffn_kernel, n_dp, n_mp),
        out_shape=(
            shape((first, shard // parts, units), F32),
            shape((rows, D), F32),
            shape((1, D), F32),
            shape((tokens, units), BF16),
            shape((D, units), BF16),
            shape((3, D, units), BF16),
        ),
        in_specs=[SMEM_SPEC] + vmem_specs(3) + any_specs(3),
        out_specs=tuple(vmem_specs(3) + any_specs(3)),
        scratch_shapes=[
            pltpu.VMEM((2, D, units), BF16),
            pltpu.VMEM((tokens, D), BF16),
            pltpu.VMEM((tokens, D), BF16),
            pltpu.VMEM((tokens, units), BF16),
            pltpu.VMEM((tokens, units), F32),
            pltpu.VMEM((tokens, units), F32),
            pltpu.VMEM((2, tokens, units), BF16),
            pltpu.VMEM((tokens, D), BF16),
            pltpu.VMEM((rows, D), F32),
            pltpu.VMEM((3, D, units), BF16),
            gather_sems(n_mp),
        ]
        + reduce_scratch(n_mp, rows)
        + [
            pltpu.VMEM(down_state.shape[1:], F32),
            pltpu.VMEM((1, D, units), BF16),
            pltpu.SemaphoreType.DMA((3,)),
            pltpu.SemaphoreType.DMA((4,)),
        ]
        + bulk_sems(n_dp, parts)
        + scatter_scratch(n_dp, first, shard // parts, units),
        compiler_params=pltpu.CompilerParams(
            collective_id=4, has_side_effects=True, vmem_limit_bytes=FFN_VMEM
        ),
        name="ffn",
    )(lengths, nm, mods, mid, cot, wf, down_state)


def attn_backward_kernel(
    n_dp, n_mp, heads, lengths_ref, scales_ref, dmid_ref, mods_ref, stats_ref,
    qu_any, ku_any, gffn_ref, wg_any, v_any, q_any, k_any, normed_any, att_any, x_any,
    gw_out, gf_ref, gin_ref, amod_ref, gscale_ref,
    gw_ref, store_sem, gffn_s, wg_ref, v_ref, q_ref, k_ref, normed_ref, att_ref, x_ref, ones_ref, load_sem,
    qu_s, ku_s, kt_s, dy_s, dq_s, dk_s, dv_s, low_s, part_s, gather_sem,
    core_send, core_recv, x_send, x_recv, sems,
    recv_y, send_z, recv_z, f_zs, f_zr, f_ys, f_yr,
):
    r = Ranks(n_mp)
    info = Images(lengths_ref)
    rows = dmid_ref.shape[0]
    tokens = rows * n_mp
    width = q_ref.shape[1]
    size = width // heads
    at = lambda b: pl.ds(pl.multiple_of(b * rows, rows), rows)
    image_of = lambda b: lax.div(b * rows, SHORT)
    copies = loads(
        (
            (ku_any, ku_s),
            (qu_any, qu_s),
            (wg_any, wg_ref),
            (v_any, v_ref),
            (gffn_ref, gffn_s),
            (q_any, q_ref),
            (k_any, k_ref),
            (normed_any, normed_ref),
            (att_any, att_ref),
            (x_any.at[at(r.m), :], x_ref),
        ),
        load_sem,
    )
    dy_s[at(r.m), :] = dmid_ref[...].astype(BF16)
    grid = Grid(n_dp)
    greet(
        [
            (n_dp, lambda k: (lax.rem(r.d + k, n_dp), r.m)),
            (2, lambda k: r.sibling),
            (r.n_x, r.chip),
        ]
    )
    gather = Gather(r, rows, dy_s, gather_sem)
    gather.start()
    shard = D // n_dp
    start, end = scatter_split(shard)
    ffn_g = BulkScatter(
        grid, end - start, cut_rows(gffn_s, shard, start), lambda i: gf_ref.at[i],
        recv_y, send_z, recv_z, f_zs, f_zr, f_ys, f_yr, sent=cut_rows(gffn_ref, shard, start))
    each_piece(ffn_g.send, 0, ffn_g.pieces)
    ones_ref[...] = head_ones(width, heads)
    scale_row = head_scales(scales_ref, width, heads)
    red = Reduce(r, core_send, core_recv, x_send, x_recv, sems)

    copies[0].wait()

    def units(b, carry):
        kt_s[:, at(b)] = ku_s[at(b), :].astype(F32).T.astype(BF16)
        return carry

    lax.fori_loop(0, n_mp, units, 0)
    for copy in copies[1:5]:
        copy.wait()
    dk_s[...] = jnp.zeros_like(dk_s)
    dv_s[...] = jnp.zeros_like(dv_s)
    lanes = lax.broadcasted_iota(jnp.int32, (1, width), 1)

    pace = (2, 3, 1)

    def block(j, carry):
        kx = lax.div(j, 2)
        same = 1 - lax.rem(j, 2)
        b = r.rank(kx, same)
        back_kx = lax.rem(r.n_x - kx, r.n_x)

        @pl.when((same == 1) & (kx > 0))
        def _():
            gather.forward(back_kx)

        @pl.when(same == 0)
        def _():
            gather.arrived(back_kx)

        d_att = dot_nn(dy_s[at(b), :], wg_ref[3]).astype(BF16)
        bias = column_bias(info, image_of(b), (tokens, 1), SHORT)
        qu = qu_s[at(b), :]
        outs = []
        for h in range(heads):
            mask = ((lanes >= h * size) & (lanes < (h + 1) * size)).astype(F32).astype(BF16)
            qh = qu * mask
            dh = d_att * mask
            probs = jnp.exp(dot_nt(ku_s[...], qh) + bias - stats_ref[h : h + 1, at(b)])
            ffn_g.paced_forward(heads * j + h, *pace)
            d_probs = dot_nt(v_ref[...], dh)
            inner = jnp.sum(probs * d_probs, axis=0, keepdims=True)
            d_scores = (probs * (d_probs - inner)).astype(BF16)
            dv_s[...] = dv_s[...] + dot_nn(probs.astype(BF16), dh)
            dk_s[...] = dk_s[...] + dot_nn(d_scores, qh)
            outs.append(dot_nn(kt_s[h * size : (h + 1) * size, :], d_scores))
        dq_s[at(b), :] = jnp.concatenate(outs, axis=0).T
        return carry

    lax.fori_loop(0, n_mp, block, 0)

    def inputs(j, scale_grad):
        kx, same = lax.rem(1 + lax.div(j, 2), r.n_x), lax.rem(j, 2)
        b = r.rank(kx, same)
        q, k = q_ref[at(b), :], k_ref[at(b), :]
        q_factor = lax.rsqrt(head_sums(q * q, ones_ref[...]) + EPSILON)
        k_factor = lax.rsqrt(head_sums(k * k, ones_ref[...]) + EPSILON)
        dqu, dku = dq_s[at(b), :], dk_s[at(b), :]
        q_unit, k_unit = q * q_factor, k * k_factor
        q_along = dqu * q_unit
        d_q = (scale_row * q_factor * (dqu - q_unit * head_sums(q_along, ones_ref[...]))).astype(BF16)
        d_k = (k_factor * (dku - k_unit * head_sums(dku * k_unit, ones_ref[...]))).astype(BF16)
        d_v = dv_s[at(b), :].astype(BF16)
        low_s[at(b), 0:width] = d_q
        low_s[at(b), width : 2 * width] = d_k
        low_s[at(b), 2 * width : 3 * width] = d_v
        part_s[...] = dot_nt(d_q, wg_ref[0]) + dot_nt(d_k, wg_ref[1]) + dot_nt(d_v, wg_ref[2])

        @pl.when(same == 0)
        def _():
            red.other(kx, part_s[...])

        @pl.when((same == 1) & (kx > 0))
        def _():
            red.same(kx, part_s[...])

        ffn_g.paced_forward(heads * n_mp + j, *pace)
        return scale_grad + jnp.sum(q_along, axis=0, keepdims=True)

    for copy in copies[5:7]:
        copy.wait()
    gscale_ref[...] = lax.fori_loop(0, n_mp, inputs, jnp.zeros((1, width), F32))

    for copy in copies[7:]:
        copy.wait()
    step = 512

    def weights(i, carry):
        ffn_g.paced_forward(heads * n_mp + n_mp + i, *pace)
        cols = pl.ds(pl.multiple_of(i * step, step), step)
        value = dot_tn(normed_ref[:, cols], low_s[...]).astype(BF16)
        for c in range(3):
            gw_ref[c, cols, :] = value[:, c * width : (c + 1) * width]
        gw_ref[3, cols, :] = dot_tn(dy_s[:, cols], att_ref[...]).astype(BF16)
        return carry

    lax.fori_loop(0, D // step, weights, 0)
    each_piece(ffn_g.forward, ffn_g.after(ffn_g.pieces, *pace, heads * n_mp + n_mp + D // step), ffn_g.pieces)

    gw_store = pltpu.make_async_copy(gw_ref, gw_out, store_sem.at[0])
    gw_store.start()
    d_normed = red.finish(part_s[...])
    x = x_ref[...].astype(F32)
    scale = image_scale(info, mods_ref, 0, image_of(r.m))
    factor = row_sums_factor(x)
    inner = jnp.mean(x * scale * d_normed, axis=-1, keepdims=True)
    gin_ref[...] = dmid_ref[...] + (factor * scale * d_normed - x * (factor * factor * factor * inner))
    amod_ref[...] = jnp.sum(d_normed * x * factor, axis=0, keepdims=True)
    gather.drain()
    red.drain()
    ffn_g.finish()
    gw_store.wait()


def attn_backward(n_dp, n_mp, lengths, scales, dmid, mods, stats, qu, ku, gffn, wg, v, q, k, normed, att, x):
    rows = dmid.shape[0]
    tokens = rows * n_mp
    width, heads = q.shape[1], scales.shape[1]
    shard = D // n_dp
    small = shard // cuts(shard)
    start, end = scatter_split(shard)
    shape = jax.ShapeDtypeStruct
    return pl.pallas_call(
        functools.partial(attn_backward_kernel, n_dp, n_mp, heads),
        out_shape=(
            shape(wg.shape, BF16),
            shape((end - start, small, gffn.shape[2]), F32),
            shape((rows, D), F32),
            shape((1, D), F32),
            shape((1, width), F32),
        ),
        in_specs=[SMEM_SPEC] * 2 + vmem_specs(3) + any_specs(10),
        out_specs=tuple(any_specs(1) + vmem_specs(4)),
        scratch_shapes=[
            pltpu.VMEM(wg.shape, BF16),
            pltpu.SemaphoreType.DMA((1,)),
            pltpu.VMEM(gffn.shape, BF16),
            pltpu.VMEM(wg.shape, BF16),
            pltpu.VMEM((tokens, width), BF16),
            pltpu.VMEM((tokens, width), F32),
            pltpu.VMEM((tokens, width), F32),
            pltpu.VMEM((tokens, D), BF16),
            pltpu.VMEM((tokens, width), BF16),
            pltpu.VMEM((rows, D), BF16),
            pltpu.VMEM((width, width), BF16),
            pltpu.SemaphoreType.DMA((10,)),
            pltpu.VMEM((tokens, width), BF16),
            pltpu.VMEM((tokens, width), BF16),
            pltpu.VMEM((width, tokens), BF16),
            pltpu.VMEM((tokens, D), BF16),
            pltpu.VMEM((tokens, width), F32),
            pltpu.VMEM((tokens, width), F32),
            pltpu.VMEM((tokens, width), F32),
            pltpu.VMEM((tokens, 3 * width), BF16),
            pltpu.VMEM((rows, D), F32),
            gather_sems(n_mp),
        ]
        + reduce_scratch(n_mp, rows)
        + scatter_scratch(n_dp, end - start, small, gffn.shape[2]),
        compiler_params=pltpu.CompilerParams(
            collective_id=5, has_side_effects=True, vmem_limit_bytes=ATTN_VMEM
        ),
        name="attn_backward",
    )(lengths, scales, dmid, mods, stats, qu, ku, gffn, wg, v, q, k, normed, att, x)


def squares(value):
    return jnp.sum(jnp.sum(value * value, axis=0, keepdims=True), axis=-1, keepdims=True)


def back_kernel(
    n_dp, n_mp, heads,
    lengths_ref, labels_ref, grads_ref, amod_ref, fmod_ref, gin_ref, feats_ref, gd_ref, gscale_ref,
    emb_ref, hid_ref, gated_ref, mixed_ref,
    mapup_ref, mapdown_ref, mod_ref, gffn_ref, ffgated_ref, wd_ref, mid_any, gu_any,
    gattn_ref, gf_ref, out_all, gin_s, gmod_ref, gmd_ref, gmu_ref, gtime_ref, gclass_ref, ggain_ref, norm_ref,
    mapup_s, mapdown_s, mod_s, gffn_s, ffgated_s, wd_s, mid_ref, gu_ref, load_sem, own_r, full_e, onehot_s, out_sem, gin_sem,
    recv_q, stage_q, own_q, recv_d, full_d, own_c, recv_c, send_g, recv_g, own_h, recv_h, full_h,
    own_p, recv_p, own_s, recv_s, own_n, all_dp, own_sum, all_mp,
    dp_ss, dp_rs, mp_ss, mp_rs,
    core_send, core_recv, x_send, x_recv, sems,
    recv_y, send_z, recv_z, a_zs, a_zr, a_ys, a_yr,
    f_recv_y, f_send_z, f_recv_z, f_zs, f_zr, f_ys, f_yr,
):
    r = Ranks(n_mp)
    d, m = r.d, r.m
    info = Images(lengths_ref)
    grid = Grid(n_dp)
    shard = gattn_ref.shape[1]
    start = scatter_split(shard)[1]
    tall = shard // 2
    attn_g = BulkScatter(
        grid, 8,
        lambda dd, i: grads_ref.at[
            lax.div(i, 2), pl.ds(pl.multiple_of(dd * shard + lax.rem(i, 2) * tall, tall), tall), :
        ],
        lambda i: gattn_ref.at[lax.div(i, 2), pl.ds(pl.multiple_of(lax.rem(i, 2) * tall, tall), tall), :],
        recv_y, send_z, recv_z, a_zs, a_zr, a_ys, a_yr)
    ffn_g = BulkScatter(
        grid, 3 * cuts(shard) - start, cut_rows(gffn_s, shard, start - 2 * cuts(shard)), lambda i: gf_ref.at[i],
        f_recv_y, f_send_z, f_recv_z, f_zs, f_zr, f_ys, f_yr)
    images, own_cols = feats_ref.shape
    rows = mid_ref.shape[0]
    copies = loads(
        (
            (mod_ref.at[0], mod_s),
            (mapdown_ref.at[0], mapdown_s),
            (mapup_ref.at[0], mapup_s),
            (ffgated_ref, ffgated_s),
            (wd_ref, wd_s),
            (gffn_ref.at[pl.ds(2, 1)], gffn_s),
            (mid_any, mid_ref),
            (gu_any, gu_ref),
        ),
        load_sem,
    )
    greet(
        [
            (n_dp, lambda k: (lax.rem(d + k, n_dp), m)),
            (n_mp, lambda k: (d, lax.rem(m + k, n_mp))),
        ]
    )
    at = lambda b: pl.ds(pl.multiple_of(b * rows, rows), rows)
    gin_s[at(m), :] = gin_ref[...].astype(BF16)
    one = Gather(r, rows, out_all, out_sem)
    two = Gather(r, rows, gin_s, gin_sem)
    red = Reduce(r, core_send, core_recv, x_send, x_recv, sems)

    def branch(j):
        kx, same = (1 + j // 2) % r.n_x, j % 2
        part = dot_nt(ffgated_s[at(r.rank(kx, same)), :], wd_s[...])
        if same == 0:
            red.other(kx, part)
        elif kx > 0:
            red.same(kx, part)
        else:
            position = lax.broadcasted_iota(jnp.int32, (rows, 1), 0) + m * rows
            live = (position.astype(F32) < info.live).astype(F32)
            out_all[at(m), :] = ((mid_ref[...] + red.finish(part)) * live).astype(BF16)

    def branches(quarter):
        for j in range(quarter * n_mp // 4, (quarter + 1) * n_mp // 4):
            branch(j)

    own_r[0:1, :] = amod_ref[...]
    own_r[1:2, :] = fmod_ref[...]

    def dp_ex(stage):
        return Exchange(n_dp, d, lambda p: (p, m), dp_ss.at[stage], dp_rs.at[stage])

    def mp_ex(stage):
        return Exchange(n_mp, m, lambda p: (d, p), mp_ss.at[stage], mp_rs.at[stage])

    def local_squares():
        value = jnp.zeros((1, 1), F32)
        for i in range(gd_ref.shape[0]):
            value = value + squares(gd_ref[i])
        for i in range(gu_ref.shape[0]):
            value = value + squares(gu_ref[i])
        return value

    ex = mp_ex(0)
    ex.start(lambda p: own_r, recv_q)
    attn_g.send(0)
    copies[5].wait()
    ffn_g.send(0)
    fill_onehot(onehot_s, labels_ref)
    recv_q[m] = own_r[...]
    ex.wait(lambda p: own_r, recv_q)
    for image in range(IMG_DEV):
        for c in range(2):
            row = jnp.zeros((1, D), F32)
            for rank in range(n_mp):
                share = 1.0 - info.is_long if rank * rows // SHORT == image else 0.0
                if image == 0:
                    share = share + info.is_long
                row = row + share * recv_q[rank, c : c + 1, :]
            stage_q[c * IMG_DEV + image : c * IMG_DEV + image + 1, :] = row
    own_q[...] = pack_rows(stage_q[...])
    two.start()
    ex = dp_ex(0)
    ex.start(lambda p: own_q, recv_d)
    attn_g.send(1)
    for copy in copies[:5] + copies[6:]:
        copy.wait()
    branches(0)
    ffn_g.forward(0)
    recv_d[d] = own_q[...]
    gains_own = emb_ref[d][images:]
    emb = emb_ref[:, 0:images, :]
    emb_factor = rms_blocks(emb)
    unit = emb * emb_factor[None] * emb_ref[:, images : images + 1, :]
    unit_factor = rms_blocks(unit)
    emb_own = emb_ref[d][0:images]
    unit_own = emb_own * emb_factor * gains_own[0:1]
    pre_own = (unit_own * unit_factor * gains_own[1:2]).astype(BF16)
    mixed = mixed_ref[...]
    mixed_factor = rms_blocks(mixed)
    mixed_own = mixed_ref[d]
    cond_own = (mixed_own * mixed_factor * gains_own[2:3]).astype(BF16)
    ex.wait(lambda p: own_q, recv_d)
    for p in range(n_dp):
        block = recv_d[p].astype(F32)
        for c in range(2):
            for half in range(2):
                first = (2 * half + c) * IMG_DEV
                full_d[c, p * IMG_DEV : (p + 1) * IMG_DEV, half * D // 2 : (half + 1) * D // 2] = block[
                    first : first + IMG_DEV
                ]
    own_c[...] = two_part_left(dot_nt, full_d[0], mod_s[:, 0, :].astype(BF16)) + two_part_left(
        dot_nt, full_d[1], mod_s[:, 1, :].astype(BF16)
    )
    ex = dp_ex(1)
    ex.start(lambda p: own_c, recv_c)
    attn_g.send(2)
    attn_g.forward(0)
    branches(1)
    recv_c[d] = own_c[...]
    squares_mod = jnp.zeros((1, 1), F32)
    for c in range(2):
        grad = two_part(dot_tn, cond_own, full_d[c])
        gmod_ref[:, c, :] = grad
        squares_mod = squares_mod + squares(grad)
    ex.wait(lambda p: own_c, recv_c)
    ggain_ref[2:3, :] = jnp.sum(own_c[...] * mixed_own * mixed_factor, axis=0, keepdims=True)
    d_mixed = rms_blocks_back(
        mixed, mixed_factor, recv_c[...] * emb_ref[:, images + 2 : images + 3, :]
    )
    recv_c[...] = d_mixed
    mix_own = recv_c[d]
    part = two_part_left(dot_nn, mix_own, mapdown_s[...].astype(BF16))
    for p in range(n_dp):
        send_g[p] = part[p * IMG_DEV : (p + 1) * IMG_DEV, :]
    ex = dp_ex(2)
    ex.start(lambda p: send_g.at[p], recv_g)
    attn_g.send(3)
    attn_g.forward(1)
    branches(2)
    recv_g[d] = send_g[d]
    grad = two_part_left(dot_tn, mix_own, gated_ref[...].astype(BF16))
    gmd_ref[...] = grad
    squares_md = squares(grad)
    ex.wait(lambda p: send_g.at[p], recv_g)
    d_gated = total_of(recv_g, n_dp)
    value, slope = gelu_parts(hid_ref[1])
    own_h[0] = d_gated * value
    own_h[1] = d_gated * hid_ref[0] * slope
    ex = dp_ex(3)
    ex.start(lambda p: own_h, recv_h)
    recv_h[d] = own_h[...]
    attn_g.send(4)
    attn_g.forward(2)
    branches(3)
    ex.wait(lambda p: own_h, recv_h)
    for p in range(n_dp):
        for c in range(2):
            full_h[c, p * IMG_DEV : (p + 1) * IMG_DEV, :] = recv_h[p, c]
    own_p[...] = two_part_left(dot_nt, full_h[0], mapup_s[:, 0, :].astype(BF16)) + two_part_left(
        dot_nt, full_h[1], mapup_s[:, 1, :].astype(BF16)
    )
    ex = mp_ex(1)
    ex.start(lambda p: own_p, recv_p)
    one.start()
    attn_g.send(5)
    attn_g.send(6)
    attn_g.forward(3)
    squares_done = local_squares() + squares_md
    recv_p[m] = own_p[...]
    for c in range(2):
        grad = two_part(dot_tn, pre_own, full_h[c])
        gmu_ref[:, c, :] = grad
        squares_done = squares_done + squares(grad)
    ex.wait(lambda p: own_p, recv_p)
    own_s[...] = total_of(recv_p, n_mp)
    ex = dp_ex(4)
    ex.start(lambda p: own_s, recv_s)
    attn_g.send(7)
    attn_g.forward(4)
    attn_g.forward(5)
    recv_s[d] = own_s[...]
    ex.wait(lambda p: own_s, recv_s)
    ggain_ref[1:2, :] = jnp.sum(own_s[...] * unit_own * unit_factor, axis=0, keepdims=True)
    d_unit = recv_c[...] + rms_blocks_back(
        unit, unit_factor, recv_s[...] * emb_ref[:, images + 1 : images + 2, :]
    )
    recv_s[...] = d_unit
    ggain_ref[0:1, :] = jnp.sum(recv_s[d] * emb_own * emb_factor, axis=0, keepdims=True)
    d_emb = rms_blocks_back(emb, emb_factor, d_unit * emb_ref[:, images : images + 1, :])
    recv_s[...] = d_emb
    ggain_ref[3:8, :] = jnp.zeros_like(ggain_ref[3:8, :])
    for p in range(n_dp):
        full_e[:, p * own_cols : (p + 1) * own_cols] = recv_s[p]
    attn_g.forward(6)
    attn_g.forward(7)
    gtime_ref[...] = two_part(dot_tn, feats_ref[...].astype(BF16), full_e[...])
    gclass_ref[...] = two_part_left(dot_tn, recv_s[d], onehot_s[...].astype(BF16))
    attn_g.finish()
    ffn_g.finish()
    split = squares_done
    for c in range(4):
        split = split + squares(gattn_ref[c])
    for i in range(ffn_g.pieces):
        split = split + squares(gf_ref[i])
    shared = squares_mod + squares(gtime_ref[...]) + squares(gclass_ref[...]) + squares(ggain_ref[...])
    lane = lax.broadcasted_iota(jnp.int32, (1, 128), 1)
    own_n[...] = jnp.zeros_like(own_n)
    own_n[0:1, :] = jnp.where(lane == 0, split + shared * (1.0 / n_mp), 0.0)
    width = gscale_ref.shape[1]
    column = lax.div(lax.broadcasted_iota(jnp.int32, (1, width), 1), width // heads)
    scale_row = jnp.zeros((1, 128), F32)
    for h in range(heads):
        head_part = jnp.sum(jnp.where(column == h, gscale_ref[...], 0.0), axis=-1, keepdims=True)
        scale_row = jnp.where(lane == h, head_part, scale_row)
    own_n[1:2, :] = scale_row
    ex = dp_ex(5)
    ex.start(lambda p: own_n, all_dp)
    all_dp[d] = own_n[...]
    for kx in range(1, r.n_x):
        one.forward(kx)
        two.forward(kx)
    ex.wait(lambda p: own_n, all_dp)
    summed = total_of(all_dp, n_dp)
    head = summed[1:2]
    own_sum[...] = jnp.zeros_like(own_sum)
    own_sum[0:1, :] = summed[0:1] + head * head
    ex = mp_ex(2)
    ex.start(lambda p: own_sum, all_mp)
    all_mp[m] = own_sum[...]
    for kx in range(r.n_x):
        one.arrived(kx)
        two.arrived(kx)
    ex.wait(lambda p: own_sum, all_mp)
    norm = jnp.sqrt(jnp.sum(total_of(all_mp, n_mp)[0:1], axis=-1, keepdims=True))
    norm_ref[0:1, :] = jnp.broadcast_to(norm, (1, 128))
    norm_ref[1:2, :] = head
    norm_ref[2:8, :] = jnp.zeros((6, 128), F32)
    red.drain()
    one.drain()
    two.drain()


def back(n_dp, n_mp, lengths, labels, grads, amod, fmod, mid, gin, feats, gd, gu, gscale, emb, hid, gated, mixed, map_states, gffn, ffgated, wd):
    images, part = feats.shape
    units_map = map_states[0].shape[3]
    rows = mid.shape[0]
    tokens = rows * n_mp
    heads = H // n_mp
    slab = (4, grads.shape[1] // n_dp, grads.shape[2])
    shard, units = slab[1], gffn.shape[2]
    small = shard // cuts(shard)
    pieces = 3 * cuts(shard) - scatter_split(shard)[1]
    shape = lambda *dims: jax.ShapeDtypeStruct(dims, F32)
    block = pltpu.VMEM((8, 128), F32)
    return pl.pallas_call(
        functools.partial(back_kernel, n_dp, n_mp, heads),
        out_shape=(
            shape(*slab),
            shape(pieces, small, units),
            jax.ShapeDtypeStruct((tokens, D), BF16),
            jax.ShapeDtypeStruct((tokens, D), BF16),
            shape(part, 2, D),
            shape(part, units_map),
            shape(part, 2, units_map),
            shape(part, DM),
            shape(part, NCLASS),
            shape(8, part),
            shape(8, 128),
        ),
        in_specs=[SMEM_SPEC] * 2 + vmem_specs(11) + any_specs(8),
        out_specs=tuple(vmem_specs(11)),
        scratch_shapes=[pltpu.VMEM(state.shape[1:], F32) for state in map_states]
        + [
            pltpu.VMEM((1, D, units), BF16),
            pltpu.VMEM((tokens, units), BF16),
            pltpu.VMEM((D, units), BF16),
            pltpu.VMEM(mid.shape, F32),
            pltpu.VMEM(gu.shape, F32),
            pltpu.SemaphoreType.DMA((8,)),
            pltpu.VMEM((2, D), F32),
            pltpu.VMEM((images, DM), F32),
            pltpu.VMEM((images, NCLASS), F32),
            gather_sems(n_mp),
            gather_sems(n_mp),
            pltpu.VMEM((n_mp, 2, D), F32),
            pltpu.VMEM((2 * IMG_DEV, D), F32),
            pltpu.VMEM((4 * IMG_DEV, D // 2), BF16),
            pltpu.VMEM((n_dp, 4 * IMG_DEV, D // 2), BF16),
            pltpu.VMEM((2, images, D), F32),
            pltpu.VMEM((images, part), F32),
            pltpu.VMEM((n_dp, images, part), F32),
            pltpu.VMEM((n_dp, IMG_DEV, units_map), F32),
            pltpu.VMEM((n_dp, IMG_DEV, units_map), F32),
            pltpu.VMEM((2, IMG_DEV, units_map), F32),
            pltpu.VMEM((n_dp, 2, IMG_DEV, units_map), F32),
            pltpu.VMEM((2, images, units_map), F32),
            pltpu.VMEM((images, part), F32),
            pltpu.VMEM((n_mp, images, part), F32),
            pltpu.VMEM((images, part), F32),
            pltpu.VMEM((n_dp, images, part), F32),
            block,
            pltpu.VMEM((n_dp, 8, 128), F32),
            block,
            pltpu.VMEM((n_mp, 8, 128), F32),
            pltpu.SemaphoreType.DMA((6, n_dp)),
            pltpu.SemaphoreType.DMA((6, n_dp)),
            pltpu.SemaphoreType.DMA((3, n_mp)),
            pltpu.SemaphoreType.DMA((3, n_mp)),
        ]
        + reduce_scratch(n_mp, rows)
        + scatter_scratch(n_dp, 8, slab[1] // 2, slab[2])
        + scatter_scratch(n_dp, pieces, small, units),
        compiler_params=pltpu.CompilerParams(
            collective_id=1, has_side_effects=True, vmem_limit_bytes=BACK_VMEM
        ),
        name="back",
    )(lengths, labels, grads, amod, fmod, gin, feats, gd, gscale, emb, hid, gated, mixed, *map_states, gffn, ffgated, wd, mid, gu)


def update_kernel(heads, *refs):
    states, refs = refs[:11], refs[11:]
    norm_ref, gattn_ref, gtime_ref, gclass_ref, gmu_ref, gmd_ref, gmod_ref, ggain_ref = refs[:8]
    ffn_refs, out_ref, gin_ref, refs = refs[8:11], refs[11], refs[12], refs[13:]
    outs, out_final, gin_final, norm_out, refs = refs[:33], refs[33], refs[34], refs[35], refs[36:]
    kept, new, first, second = refs[:11], refs[11:22], refs[22:33], refs[33:44]
    gup_s, gdown_s, gin_s, out_s, load_sem, store_sem, out_sem = refs[44:]
    order = (2, 8, 0, 6, 3, 5, 4, 7, 1, 9, 10)
    copies = {i: pltpu.make_async_copy(states[i], kept[i], load_sem.at[i]) for i in order}
    for i in order:
        copies[i].start()
    out_load = pltpu.make_async_copy(out_ref, out_s, out_sem.at[2])
    out_load.start()
    out_copies = [pltpu.make_async_copy(out_s, out_final, out_sem.at[0])]
    out_copies.append(pltpu.make_async_copy(gin_s, gin_final, out_sem.at[1]))
    parts = cuts(gdown_s.shape[0])
    small = gdown_s.shape[0] // parts
    pieces = [ref.at[i] for ref in ffn_refs for i in range(ref.shape[0])]
    for i, piece in enumerate(pieces):
        rows = slice(i % parts * small, (i % parts + 1) * small)
        if i < parts:
            gdown_s[rows, :] = piece[...]
        else:
            gup_s[rows, i // parts - 1, :] = piece[...]
    factor = CLIP_NORM / jnp.maximum(norm_ref[0:1, 0:1], CLIP_NORM)
    norm_out[...] = norm_ref[0:1, 0:1]
    head = norm_ref[1:2, :]
    rates, decays = learn_rates(), decay_rates()
    stores = []

    def store(i):
        for k, (source, target) in enumerate(((new[i], outs[3 * i]), (first[i], outs[3 * i + 1]), (second[i], outs[3 * i + 2]))):
            stores.append(pltpu.make_async_copy(source, target, store_sem.at[i, k]))
            stores[-1].start()

    def step(i, gradient, pick=lambda ref, k: ref.at[k]):
        copies[i].wait()
        new_weight, average, m_new, v_new = adamw_step(lambda k: pick(kept[i], k)[...], gradient, rates[i], decays[i])
        pick(new[i], 0)[...] = new_weight
        pick(new[i], 1)[...] = average
        first[i][...] = m_new
        second[i][...] = v_new
        store(i)

    step(2, gup_s[...] * factor[:, None, :])
    step(8, gmod_ref[...] * factor[:, None, :])
    copies[0].wait()
    for c in range(3):
        results = adamw_step(lambda k: kept[0][k, c], gattn_ref[c] * factor, rates[0], decays[0])
        new[0][0, c], new[0][1, c], first[0][c], second[0][c] = results
    store(0)
    step(6, gmu_ref[...] * factor[:, None, :])
    gin_s[...] = gin_ref[...].astype(F32)
    out_copies[1].start()
    step(3, gdown_s[...].T * factor)
    step(5, gclass_ref[...] * factor)
    step(4, gtime_ref[...] * factor)
    step(7, gmd_ref[...] * factor)
    step(1, gattn_ref[3].T * factor)
    copies[9].wait()
    copies[10].wait()
    for g in range(3):
        results = adamw_step(lambda k: kept[9][g, k : k + 1, :], ggain_ref[g : g + 1, :] * factor, rates[9], decays[9])
        new[9][g, 0:1, :], new[9][g, 1:2, :], first[9][g : g + 1, :], second[9][g : g + 1, :] = results
    store(9)
    results = adamw_step(lambda k: kept[10][k : k + 1, :], head[:, 0:heads] * factor, rates[10], decays[10])
    new[10][0:1, :], new[10][1:2, :], first[10][...], second[10][...] = results
    store(10)
    out_load.wait()
    out_copies[0].start()
    for copy in stores + out_copies:
        copy.wait()


def update(states, norm, grads, ffn_parts, out_all, gin_all):
    heads = states[10].shape[1]
    rows, _, units = states[2].shape[1:]
    news, moments = [], []
    for i, state in enumerate(states):
        if i == 9:
            news.append((state.shape[0], 2, state.shape[2]))
            moments.append((state.shape[0], state.shape[2]))
        else:
            news.append((2,) + state.shape[1:])
            moments.append(state.shape[1:] if i < 10 else (1, heads))
    outs = []
    for new, moment in zip(news, moments):
        outs += [new, moment, moment]
    shape = lambda dims: jax.ShapeDtypeStruct(dims, F32)
    return pl.pallas_call(
        functools.partial(update_kernel, heads),
        out_shape=tuple(shape(o) for o in outs)
        + (jax.ShapeDtypeStruct(out_all.shape, BF16), shape(gin_all.shape), shape((1, 1))),
        in_specs=any_specs(11) + vmem_specs(11) + any_specs(1) + vmem_specs(1),
        out_specs=tuple(any_specs(35) + vmem_specs(1)),
        scratch_shapes=[pltpu.VMEM(state.shape, F32) for state in states]
        + [pltpu.VMEM(dims, F32) for dims in news]
        + [pltpu.VMEM(dims, F32) for dims in moments]
        + [pltpu.VMEM(dims, F32) for dims in moments]
        + [
            pltpu.VMEM((rows, 2, units), F32),
            pltpu.VMEM((rows, units), F32),
            pltpu.VMEM(gin_all.shape, F32),
            pltpu.VMEM(out_all.shape, BF16),
            pltpu.SemaphoreType.DMA((11,)),
            pltpu.SemaphoreType.DMA((11, 3)),
            pltpu.SemaphoreType.DMA((3,)),
        ],
        compiler_params=pltpu.CompilerParams(vmem_limit_bytes=UPDATE_VMEM),
        name="update",
    )(*states, norm, *grads, *ffn_parts, out_all, gin_all)


def per_device(
    block_input,
    out_cotangent,
    sigmas,
    class_labels,
    image_lengths,
    fourier_freqs,
    inproj_state,
    outproj_state,
    upproj_state,
    downproj_state,
    timeproj_state,
    classemb_state,
    mapup_state,
    mapdown_state,
    modproj_state,
    gains_state,
    headscale_state,
):
    n_dp, n_mp = lax.axis_size("dp"), lax.axis_size("mp")
    in_state = jnp.transpose(inproj_state, (0, 2, 1, 3))
    class_state = jnp.transpose(classemb_state, (0, 2, 1))
    down_map_state = jnp.transpose(mapdown_state, (0, 2, 1))
    gain_state = jnp.transpose(gains_state, (1, 0, 2))
    mods, emb, hid, gated, mixed, feats, wg, wf, q, k, v, normed, qu, ku, att, stats, mid, nm = forward_part(
        n_dp, n_mp, image_lengths, sigmas, class_labels, headscale_state, fourier_freqs, block_input,
        (in_state, outproj_state, upproj_state),
        (timeproj_state, class_state, mapup_state, down_map_state, modproj_state), gain_state,
    )
    gd, dmid, fmod, ffgated, wd, gw_ffn = ffn(
        n_dp, n_mp, image_lengths, nm, mods, mid, out_cotangent, wf, downproj_state
    )
    gw_attn, gu, gin, amod, gscale = attn_backward(
        n_dp, n_mp, image_lengths, headscale_state, dmid, mods, stats, qu, ku, gw_ffn, wg, v, q, k, normed, att, block_input
    )
    g_attn, gb, out_all, gin_all, g_mod, g_md, g_mu, g_time, g_class, g_gain, norm = back(
        n_dp, n_mp, image_lengths, class_labels, gw_attn, amod, fmod, mid, gin, feats, gd, gu, gscale,
        emb, hid, gated, mixed, (mapup_state, down_map_state, modproj_state), gw_ffn, ffgated, wd,
    )
    states = (
        in_state,
        outproj_state,
        upproj_state,
        downproj_state,
        timeproj_state,
        class_state,
        mapup_state,
        down_map_state,
        modproj_state,
        gain_state,
        headscale_state,
    )
    grads = (g_attn, g_time, g_class, g_mu, g_md, g_mod, g_gain)
    *new, layer_out, input_grad, grad_norm = update(states, norm, grads, (gd, gu, gb), out_all, gin_all)
    orders = {0: (0, 2, 1, 3), 5: (0, 2, 1), 7: (0, 2, 1), 9: (1, 0, 2)}
    moment_orders = {0: (1, 0, 2), 5: (1, 0), 7: (1, 0)}
    results = [layer_out, input_grad, grad_norm.reshape(())]
    for i in range(11):
        stacked, first, second = new[3 * i : 3 * i + 3]
        if i in orders:
            stacked = jnp.transpose(stacked, orders[i])
        if i in moment_orders:
            first, second = jnp.transpose(first, moment_orders[i]), jnp.transpose(second, moment_orders[i])
        if i == 10:
            first, second = first[0], second[0]
        results += [stacked, first, second]
    return tuple(results)


def solution(mesh):
    return jax.shard_map(
        per_device,
        mesh=mesh,
        in_specs=(
            P("dp", None),
            P("dp", None),
            P(),
            P(),
            P(),
            P(),
            P(None, "dp", None, "mp"),
            P(None, "mp", "dp"),
            P(None, "dp", None, "mp"),
            P(None, "mp", "dp"),
            P(None, "dp", None),
            P(None, None, "dp"),
            P(None, "dp", None, "mp"),
            P(None, "mp", "dp"),
            P(None, "dp", None, None),
            P(None, None, "dp"),
            P(None, "mp"),
        ),
        out_specs=(
            P("dp", None),
            P("dp", None),
            P(),
            P(None, "dp", None, "mp"),
            P("dp", None, "mp"),
            P("dp", None, "mp"),
            P(None, "mp", "dp"),
            P("mp", "dp"),
            P("mp", "dp"),
            P(None, "dp", None, "mp"),
            P("dp", None, "mp"),
            P("dp", None, "mp"),
            P(None, "mp", "dp"),
            P("mp", "dp"),
            P("mp", "dp"),
            P(None, "dp", None),
            P("dp", None),
            P("dp", None),
            P(None, None, "dp"),
            P(None, "dp"),
            P(None, "dp"),
            P(None, "dp", None, "mp"),
            P("dp", None, "mp"),
            P("dp", None, "mp"),
            P(None, "mp", "dp"),
            P("mp", "dp"),
            P("mp", "dp"),
            P(None, "dp", None, None),
            P("dp", None, None),
            P("dp", None, None),
            P(None, None, "dp"),
            P(None, "dp"),
            P(None, "dp"),
            P(None, "mp"),
            P("mp"),
            P("mp"),
        ),
        check_vma=False,
    )
```
